32 devices in a mesh: space: 4 (over z), ens: 8 (over y, x, core).
Axes of the slice: x: 2, y: 2, z: 4, core: 2. Of those that a mesh axis runs over, the one named last changes fastest.
Arguments:
- starting_speed_field: float32 [64, 64, 2048], P('ens', 'space'), may hold values from -6 to 6
- sample_fluidity_exponent: float32 [64, 64, 2048], P('ens', 'space'), may hold values from -1.5 to 0.5
- observed: float32 [1024], P('space'), may hold values from -6 to 6
- obs_noise: float32 [64, 1024], P('ens', 'space'), may hold values from -3 to 3
- obs_var: float32 [1024], P('space'), may hold values from 0.5 to 4
- probe_cells: int32 [1024], P('space'), may hold values from 0 to 32767
- pair_cells: int32 [4, 32], P('space'), may hold values from 0 to 255
- pair_probes: int32 [4, 32], P('space'), may hold values from 0 to 5, as said below
- pair_taper: int32 [4, 32], P('space'), may hold values from 1 to 256
- pair_counts: int32 [4], P('space'), may hold values from 8 to 32, as said below
- probe_taper: int32 [4, 2, 6], P('space'), may hold values from 1 to 256
Outputs:
- prior_speed_prediction: float32 [64, 64, 2048], P('ens', 'space')
- posterior_fluidity_exponent: float32 [64, 64, 2048], P('ens', 'space')
- weighted_innovation_matrix: float32 [64, 1024], P('ens', 'space')
The draws below stay inside these ranges and needn't reach their ends.
Inputs may be any that keep to these rules, and one draw needn't show every extreme that they name: `pair_probes`: each pair slot names a probe block of the slab or of a neighbour slab, never one outside the channel: slab 0 uses 2 to 5 and the last slab 0 to 3. `pair_counts`: slots at or beyond a slab's count are padding; some slab has all 32 slots live.
All inputs are finite; a program needn't handle non-finite values.
Results may differ from the reference program's by a relative error of at most 0.000096.
Values sent between devices are 32-bit elements; how exact they have to be, the bound alone decides.
No kernel may reach another device: no remote copies, remote signals or barrier semaphores. Data moves between devices by JAX's collectives and lax.ppermute only.
A program may use at most 64 MiB of HBM per device.

```python
import math
import jax
import jax.numpy as jnp
from jax import lax

BLK = 128
SX = 16
NY = 32
NZ = 64
PBD = 2
PAIR_MAX = 32
STEPS = 2
LAYER_NUMBER = 4
SAMPLE_NUMBER = 64
NX = 64
PLANE = 2048
GRID_POINTS_PER = 32768
CB = 256
PROBE_DEV = 256
NPROBE = 1024


def draw_pair_probes(key, part):
    slab_rows = jnp.arange(LAYER_NUMBER, dtype=jnp.int32)[:, None]
    slot_cols = jnp.arange(PAIR_MAX, dtype=jnp.int32)[None, :]
    low_block = jnp.where(slab_rows == 0, PBD, 0)
    high_block = jnp.where(slab_rows == LAYER_NUMBER - 1, 2 * PBD, 3 * PBD)
    random_bits = jax.random.randint(key, (LAYER_NUMBER, PAIR_MAX), 0, 1 << 20)
    general = low_block + random_bits % (high_block - low_block)
    inside = random_bits % PBD
    lower_side = jnp.where(slab_rows == 0, 2 * PBD + inside, inside)
    upper_side = jnp.where(slab_rows == LAYER_NUMBER - 1, inside, 2 * PBD + inside)
    chosen = jnp.where(slot_cols == 0, lower_side, jnp.where(slot_cols == 1, upper_side, general))
    return chosen.astype(jnp.int32)


def draw_pair_counts(key, part):
    least = max(2, PAIR_MAX // 4)
    counts = jax.random.randint(key, (LAYER_NUMBER,), least, PAIR_MAX + 1)
    fullest = jax.random.randint(jax.random.fold_in(key, 11), (), 0, LAYER_NUMBER)
    return jnp.where(jnp.arange(LAYER_NUMBER, dtype=jnp.int32) == fullest, PAIR_MAX, counts).astype(jnp.int32)


def set_ends(values, rng, low, largest):
    longest = values.shape.index(max(values.shape))
    spots = []
    for shift in (0, 1):
        where = [jax.random.randint(jax.random.fold_in(rng, axis), (), 0, length) for axis, length in enumerate(values.shape)]
        where[longest] = (where[longest] + shift) % values.shape[longest]
        spots.append(tuple(where))
    return values.at[spots[0]].set(low).at[spots[1]].set(largest)


def block_scale(stream_key, extent, pieces, low, high):
    factor_of = 1.0
    for axis_at, shards_of in pieces:
        draws = jax.random.uniform(jax.random.fold_in(jax.random.fold_in(stream_key, 6), axis_at), (shards_of,), jnp.float32, low / len(pieces), high / len(pieces))
        factor_of = factor_of * jnp.repeat(jnp.exp(draws), extent[axis_at] // shards_of).reshape((-1,) + (1,) * (len(extent) - 1 - axis_at))
    return factor_of


def gaussian(stream_key, extent, scale, most, cuts=(), held_as=jnp.bfloat16):
    level = block_scale(stream_key, extent, cuts, -0.22, 0.18) if cuts else 1.0
    result = jax.random.normal(stream_key, extent, jnp.float32) * scale * level
    return jnp.minimum(jnp.maximum(result, -most), most).astype(held_as)


def setup_inputs(seed: int = 0) -> dict:
    arg_keys = jax.random.split(jax.random.key(seed), 12)
    starting_speed_field = gaussian(arg_keys[0], (SAMPLE_NUMBER, NX, PLANE), 1.0, 6.0, ((0, 8), (1, 4)), jnp.float32)
    sample_fluidity_exponent = jnp.clip(-1.5 + 2.0 * jax.random.uniform(arg_keys[1], (SAMPLE_NUMBER, NX, PLANE), jnp.float32) ** block_scale(arg_keys[1], (SAMPLE_NUMBER, NX, PLANE), ((0, 8), (1, 4)), -0.2, 0.2), -1.5, 0.5)
    observed = gaussian(arg_keys[2], (NPROBE,), 1.0, 6.0, ((0, 4),), jnp.float32)
    obs_noise = gaussian(arg_keys[3], (SAMPLE_NUMBER, NPROBE), 0.5, 3.0, ((0, 8), (1, 4)), jnp.float32)
    obs_var = jnp.clip(jnp.exp(math.log(4.0) - 2.0794415 * jax.random.uniform(arg_keys[4], (NPROBE,), jnp.float32) ** block_scale(arg_keys[4], (NPROBE,), ((0, 4),), -0.2, 0.2)), 0.5, 4.0)
    probe_cells = set_ends(jax.random.randint(arg_keys[5], (NPROBE,), 0, SX * NY * NZ), jax.random.fold_in(arg_keys[5], 1), 0, (SX * NY * NZ) - 1).astype(jnp.int32)
    pair_cells = set_ends(jax.random.randint(arg_keys[6], (LAYER_NUMBER, PAIR_MAX), 0, SX * NY * NZ // BLK), jax.random.fold_in(arg_keys[6], 1), 0, (SX * NY * NZ // BLK) - 1).astype(jnp.int32)
    pair_probes = draw_pair_probes(jax.random.fold_in(arg_keys[11], 71), 0)
    pair_taper = set_ends(jax.random.randint(arg_keys[8], (LAYER_NUMBER, PAIR_MAX), 1, 257), jax.random.fold_in(arg_keys[8], 1), 1, 256).astype(jnp.int32)
    pair_counts = draw_pair_counts(jax.random.fold_in(arg_keys[11], 71), 0)
    probe_taper = set_ends(jax.random.randint(arg_keys[10], (LAYER_NUMBER, PBD, 3 * PBD), 1, 257), jax.random.fold_in(arg_keys[10], 1), 1, 256).astype(jnp.int32)
    return dict(starting_speed_field=starting_speed_field, sample_fluidity_exponent=sample_fluidity_exponent, observed=observed, obs_noise=obs_noise, obs_var=obs_var, probe_cells=probe_cells, pair_cells=pair_cells, pair_probes=pair_probes, pair_taper=pair_taper, pair_counts=pair_counts, probe_taper=probe_taper)


DT_STEP = 0.08


def advance(padded_u, padded_t):
    inner_u = padded_u[:, 1:-1]
    inner_t = padded_t[:, 1:-1]
    viscous = jnp.exp(inner_t)
    viscosity_halo_padding = jnp.exp(padded_t)
    running = 0.5 * (viscous + viscosity_halo_padding[:, 2:]) * (padded_u[:, 2:] - inner_u)
    running = running + 0.5 * (viscous + viscosity_halo_padding[:, :-2]) * (padded_u[:, :-2] - inner_u)
    for offset in (NZ, -NZ):
        running = running + 0.5 * (viscous + jnp.roll(viscous, offset, axis=2)) * (jnp.roll(inner_u, offset, axis=2) - inner_u)
    height = lax.broadcasted_iota(jnp.int32, inner_u.shape, 2) % NZ
    for offset, wall_cell in ((1, 0), (-1, NZ - 1)):
        at_wall = height == wall_cell
        beside_u = jnp.where(at_wall, 0.0, jnp.roll(inner_u, offset, axis=2))
        beside_v = jnp.where(at_wall, 1.0, jnp.roll(viscous, offset, axis=2))
        running = running + 0.5 * (viscous + beside_v) * (beside_u - inner_u)
    return inner_u + DT_STEP * running


def reference(starting_speed_field, sample_fluidity_exponent, observed, obs_noise, obs_var, probe_cells, pair_cells, pair_probes, pair_taper, pair_counts, probe_taper):
    highest = lax.Precision.HIGHEST

    def sample_number_current(pair_in):
        current, visc_field = pair_in
        for repeat in range(STEPS):
            padded_u = jnp.pad(current, ((1, 1), (0, 0)))
            padded_t = jnp.pad(visc_field, ((1, 1), (0, 0)))
            current = advance(padded_u[None], padded_t[None])[0]
        return current

    prior_speed_prediction = lax.map(sample_number_current, (starting_speed_field, sample_fluidity_exponent))
    raveled_speed_field = prior_speed_prediction.reshape(SAMPLE_NUMBER, LAYER_NUMBER * GRID_POINTS_PER)
    global_cell = (jnp.arange(NPROBE, dtype=jnp.int32) // PROBE_DEV) * GRID_POINTS_PER + probe_cells
    predicted = raveled_speed_field[:, global_cell]
    anomaly = predicted - jnp.sum(predicted, axis=0) / SAMPLE_NUMBER
    scaled = (observed + obs_noise - predicted) / obs_var

    def extend(values):
        padded = jnp.pad(values, ((0, 0), (PROBE_DEV, PROBE_DEV)))
        window = jnp.arange(LAYER_NUMBER, dtype=jnp.int32)[:, None] * PROBE_DEV + jnp.arange(3 * PROBE_DEV, dtype=jnp.int32)[None, :]
        return padded[:, window].reshape(SAMPLE_NUMBER, LAYER_NUMBER, 3 * PBD, BLK)

    anom_wide = extend(anomaly)
    scaled_wide = extend(scaled)
    own_blocks = anom_wide[:, :, PBD:2 * PBD]
    probe_cov = jnp.einsum('msip,msjq->sijpq', own_blocks, anom_wide, precision=highest)
    probe_cov = probe_cov * (probe_taper.astype(jnp.float32) / 256.0 / (SAMPLE_NUMBER - 1))[:, :, :, None, None]
    correction = jnp.einsum('sijpq,msjq->msip', probe_cov, scaled_wide, precision=highest)
    var_blocks = obs_var.reshape(LAYER_NUMBER, PBD, BLK)
    gain_blocks = scaled_wide[:, :, PBD:2 * PBD] - correction / var_blocks[None]
    weighted_innovation_matrix = gain_blocks.reshape(SAMPLE_NUMBER, NPROBE)
    gain_wide = extend(weighted_innovation_matrix)
    slab_rows = jnp.arange(LAYER_NUMBER, dtype=jnp.int32)[:, None]
    theta_blocks = sample_fluidity_exponent.reshape(SAMPLE_NUMBER, LAYER_NUMBER, CB, BLK)
    theta_pick = theta_blocks[:, slab_rows, pair_cells]
    anom_pick = anom_wide[:, slab_rows, pair_probes]
    gain_pick = gain_wide[:, slab_rows, pair_probes]
    cross_cov = jnp.einsum('mskr,mskq->skrq', theta_pick, anom_pick, precision=highest)
    active_pairs = jnp.arange(PAIR_MAX, dtype=jnp.int32)[None, :] < pair_counts[:, None]
    weight = jnp.where(active_pairs, pair_taper.astype(jnp.float32) / 256.0, 0.0) / (SAMPLE_NUMBER - 1)
    updates = jnp.einsum('skrq,mskq->mskr', cross_cov, gain_pick, precision=highest) * weight[None, :, :, None]
    one_hot = (pair_cells[:, :, None] == jnp.arange(CB, dtype=jnp.int32)[None, None, :]).astype(jnp.float32)
    increment = jnp.einsum('skc,mskr->mscr', one_hot, updates, precision=highest)
    posterior_fluidity_exponent = sample_fluidity_exponent + increment.reshape(sample_fluidity_exponent.shape)
    return prior_speed_prediction, posterior_fluidity_exponent, weighted_innovation_matrix
```

```python
import functools

import jax
import jax.numpy as jnp
from jax import lax
from jax.experimental import pallas as pl
from jax.experimental.pallas import tpu as pltpu
from jax.sharding import PartitionSpec as P

LANES = 128
ROWS = 8
NZ = 64
HALF_DT = 0.5 * 0.08

VMEM = pl.BlockSpec(memory_space=pltpu.VMEM)
SMEM = pl.BlockSpec(memory_space=pltpu.SMEM)


def to_rows(array):
    members, planes, cells = array.shape
    split = array.reshape(members, planes // ROWS, ROWS, cells // LANES, LANES)
    return split.transpose(0, 1, 3, 2, 4).reshape(-1, LANES)


def from_rows(rows, shape):
    members, planes, cells = shape
    split = rows.reshape(members, planes // ROWS, cells // LANES, ROWS, LANES)
    return split.transpose(0, 1, 3, 2, 4).reshape(shape)


def row_of(plane, tile, tiles):
    return (plane // ROWS * tiles + tile) * ROWS + plane % ROWS


def pack_kernel(planes, tiles, cells_ref, taper_ref, u_ref, t_ref, noise_ref, observed_ref, var_ref,
                low_ref, high_ref, pick_ref, obs_ref):
    stride = planes * tiles
    for out_ref, first in ((low_ref, 0), (high_ref, planes - 2)):
        for kind, source in enumerate((u_ref, t_ref)):
            for depth in range(2):
                for tile in range(tiles):
                    out_ref[(kind * 2 + depth) * tiles + tile] = source[
                        pl.ds(row_of(first + depth, tile, tiles), ROWS, stride=stride), :
                    ]
        out_ref[4 * tiles] = jnp.ones((ROWS, LANES), jnp.float32)
    for slot in range(pick_ref.shape[0]):
        block = cells_ref[0, slot]
        row = row_of(block // tiles, block % tiles, tiles)
        pick_ref[slot] = t_ref[pl.ds(row, ROWS, stride=stride), :]
    width = obs_ref.shape[1]
    obs_ref[0:ROWS, :] = noise_ref[...]
    obs_ref[ROWS : ROWS + 1, :] = observed_ref[...]
    obs_ref[ROWS + 1 : ROWS + 2, :] = var_ref[...]
    own, window = taper_ref.shape[1:]
    for i in range(own):
        for j in range(window):
            at = ROWS + 2 + i * window + j
            level = taper_ref[0, i, j].astype(jnp.float32)
            obs_ref[at : at + 1, :] = jnp.full((1, width), level, jnp.float32)


def forecast_kernel(planes, tiles, probe_ref, u_ref, t_ref, before_ref, after_ref,
                    out_ref, sent_ref, u0, hv, u1, u2, diag, ax, near, far, zp, zm):
    stride = planes * tiles
    lane = lax.broadcasted_iota(jnp.int32, (ROWS, LANES), 1)
    first_half = lane < NZ
    height = lane % NZ
    floor, roof = height == 0, height == NZ - 1

    def rot(value, by):
        return pltpu.roll(value, by % LANES, 1)

    def load(x, _):
        base = (x // ROWS) * tiles * ROWS + x % ROWS
        for tile in range(tiles):
            rows = pl.ds(base + tile * ROWS, ROWS, stride=stride)
            u0[x + 2, tile] = u_ref[rows, :]
            hv[x + 2, tile] = HALF_DT * jnp.exp(t_ref[rows, :])
        return 0

    lax.fori_loop(0, planes, load, 0)
    for ref, first in ((before_ref, 0), (after_ref, planes + 2)):
        for depth in range(2):
            for tile in range(tiles):
                u0[first + depth, tile] = ref[depth * tiles + tile]
                hv[first + depth, tile] = HALF_DT * jnp.exp(ref[(2 + depth) * tiles + tile])

    def coefficients(x):
        turned = [rot(hv[x, tile], NZ) for tile in range(tiles)]
        for tile in range(tiles):
            here = hv[x, tile]
            to_near = here + turned[tile]
            to_far = here + jnp.where(first_half, turned[tile - 1], turned[(tile + 1) % tiles])
            up = here + jnp.where(roof, HALF_DT, rot(here, -1))
            down = here + jnp.where(floor, HALF_DT, rot(here, 1))
            low = here + hv[x - 1, tile]
            high = here + hv[x + 1, tile]
            diag[x, tile] = 1.0 - ((to_near + to_far) + (up + down) + (low + high))
            ax[x, tile] = high
            near[x, tile] = to_near
            far[x, tile] = to_far
            zp[x, tile] = jnp.where(roof, 0.0, up)
            zm[x, tile] = jnp.where(floor, 0.0, down)

    def step(source, x):
        turned = [rot(source[x, tile], NZ) for tile in range(tiles)]
        values = []
        for tile in range(tiles):
            here = source[x, tile]
            beyond = jnp.where(first_half, turned[tile - 1], turned[(tile + 1) % tiles])
            value = diag[x, tile] * here
            value = value + ax[x, tile] * source[x + 1, tile]
            value = value + (hv[x, tile] + hv[x - 1, tile]) * source[x - 1, tile]
            value = value + near[x, tile] * turned[tile] + far[x, tile] * beyond
            value = value + zp[x, tile] * rot(here, -1) + zm[x, tile] * rot(here, 1)
            values.append(value)
        return values

    def first_step(x, _):
        coefficients(x)
        for tile, value in enumerate(step(u0, x)):
            u1[x, tile] = value
        return 0

    lax.fori_loop(1, planes + 3, first_step, 0)
    for tile in range(tiles):
        u1[1, tile] = u1[1, tile] * before_ref[4 * tiles]
        u1[planes + 2, tile] = u1[planes + 2, tile] * after_ref[4 * tiles]

    def second_step(x, _):
        base = (x // ROWS) * tiles * ROWS + x % ROWS
        for tile, value in enumerate(step(u1, x + 2)):
            u2[x * tiles + tile] = value
            out_ref[pl.ds(base + tile * ROWS, ROWS, stride=stride), :] = value
        return 0

    lax.fori_loop(0, planes, second_step, 0)

    for part in range(sent_ref.shape[2] // LANES):
        found = jnp.zeros((ROWS, LANES), jnp.float32)
        for p in range(LANES):
            cell = probe_ref[part * LANES + p]
            turned = pltpu.roll(u2[cell // LANES], (p - cell % LANES) % LANES, 1)
            found = jnp.where(lane == p, turned, found)

        def send(device, _):
            sent_ref[device, :, part * LANES : (part + 1) * LANES] = found
            return 0

        lax.fori_loop(0, sent_ref.shape[0], send, 0)


def dot_lanes(left, right):
    return lax.dot_general(left, right, (((1,), (1,)), ((), ())), precision=lax.Precision.HIGHEST,
                           preferred_element_type=jnp.float32)


def dot_rows(left, right):
    return lax.dot_general(left, right, (((1,), (0,)), ((), ())), precision=lax.Precision.HIGHEST,
                           preferred_element_type=jnp.float32)


def update_kernel(slabs, groups, planes, tiles, place_ref, cells_ref, probes_ref, level_ref, count_ref,
                  pred_ref, obs_ref, theta_ref, t_ref, post_ref, gain_ref, reach):
    members = groups * ROWS
    share = 1.0 / (members - 1)
    slab, group = place_ref[0], place_ref[1]
    blocks = gain_ref.shape[1] // LANES
    window = 3 * blocks
    post_ref[...] = t_ref[...]
    anomaly, scaled, variance, matches, observed = [], [], [], [], []
    for offset in range(-2, 3):
        wanted = slab + offset
        at = jnp.clip(wanted, 0, slabs - 1)
        live = jnp.where((wanted >= 0) & (wanted < slabs), 1.0, 0.0)
        predicted = pred_ref[pl.ds(at * groups, groups)].reshape(members, blocks * LANES)
        mean = jnp.sum(predicted, axis=0, keepdims=True) / members
        anomaly.append((predicted - mean) * live)
        seen = obs_ref[at]
        observed.append(seen)
        variance.append(seen[ROWS + 1 : ROWS + 2])
        own = pred_ref[at * groups + group]
        scaled.append((seen[ROWS : ROWS + 1] + seen[:ROWS] - own) / variance[-1] * live)
    for d in range(5):
        for b in range(blocks):
            cut = slice(b * LANES, (b + 1) * LANES)
            matches.append(dot_lanes(scaled[d][:, cut], anomaly[d][:, cut]))
    for d in range(1, 4):
        for i in range(blocks):
            cut = slice(i * LANES, (i + 1) * LANES)
            total = jnp.zeros((ROWS, members), jnp.float32)
            for j in range(window):
                at = ROWS + 2 + i * window + j
                level = observed[d][at : at + 1, :members] / 256.0 * share
                total = total + level * matches[(d - 1) * blocks + j]
            correction = dot_rows(total, anomaly[d][:, cut])
            gain = scaled[d][:, cut] - correction / variance[d][:, cut]
            if d == 2:
                gain_ref[:, cut] = gain
            reach[(d - 1) * blocks + i] = dot_lanes(gain, anomaly[d][:, cut])
    for slot in range(theta_ref.shape[1]):
        weight = jnp.where(slot < count_ref[0], level_ref[0, slot].astype(jnp.float32) / 256.0, 0.0) * share
        change = dot_rows(reach[probes_ref[0, slot]] * weight, theta_ref[:, slot].reshape(members, LANES))
        block = cells_ref[0, slot]
        rows = pl.ds(row_of(block // tiles, block % tiles, tiles), ROWS, stride=planes * tiles)
        post_ref[rows, :] = post_ref[rows, :] + change


def shards(
    starting_speed_field,
    sample_fluidity_exponent,
    observed,
    obs_noise,
    obs_var,
    probe_cells,
    pair_cells,
    pair_probes,
    pair_taper,
    pair_counts,
    probe_taper,
):
    shape = starting_speed_field.shape
    members, planes, cells = shape
    tiles = cells // LANES
    slots = pair_cells.shape[1]
    probes = obs_noise.shape[1]
    slabs, groups = lax.axis_size("space"), lax.axis_size("ens")
    f32 = jnp.float32
    u_rows = to_rows(starting_speed_field)
    t_rows = to_rows(sample_fluidity_exponent)
    obs_rows = -(-(ROWS + 2 + probe_taper.shape[1] * probe_taper.shape[2]) // ROWS) * ROWS
    edge = jax.ShapeDtypeStruct((4 * tiles + 1, ROWS, LANES), f32)
    params = pltpu.CompilerParams(vmem_limit_bytes=48 * 1024 * 1024)
    low, high, picked, obs = pl.pallas_call(
        functools.partial(pack_kernel, planes, tiles),
        out_shape=(
            edge,
            edge,
            jax.ShapeDtypeStruct((slots, ROWS, LANES), f32),
            jax.ShapeDtypeStruct((obs_rows, probes), f32),
        ),
        in_specs=[SMEM, SMEM] + [VMEM] * 5,
        out_specs=(VMEM,) * 4,
        compiler_params=params,
        name="pack",
    )(pair_cells, probe_taper, u_rows, t_rows, obs_noise, observed.reshape(1, -1), obs_var.reshape(1, -1))
    upward = [(i, i + 1) for i in range(slabs - 1)]
    before = lax.ppermute(high, "space", upward)
    after = lax.ppermute(low, "space", [(j, i) for i, j in upward])
    theta_all = lax.all_gather(picked, "ens")
    obs_all = lax.all_gather(obs, "space")
    padded = pltpu.VMEM((planes + 4, tiles, ROWS, LANES), f32)
    u2_rows, sent = pl.pallas_call(
        functools.partial(forecast_kernel, planes, tiles),
        out_shape=(
            jax.ShapeDtypeStruct(u_rows.shape, f32),
            jax.ShapeDtypeStruct((slabs * groups, members, probes), f32),
        ),
        in_specs=[SMEM] + [VMEM] * 4,
        out_specs=(VMEM,) * 2,
        scratch_shapes=[padded] * 3 + [pltpu.VMEM((planes * tiles, ROWS, LANES), f32)] + [padded] * 6,
        compiler_params=params,
        name="forecast",
    )(probe_cells, u_rows, t_rows, before, after)
    pred_all = lax.all_to_all(sent, ("space", "ens"), 0, 0)
    place = jnp.stack([lax.axis_index("space"), lax.axis_index("ens")]).astype(jnp.int32)
    post_rows, gain = pl.pallas_call(
        functools.partial(update_kernel, slabs, groups, planes, tiles),
        out_shape=(
            jax.ShapeDtypeStruct(u_rows.shape, f32),
            jax.ShapeDtypeStruct((members, probes), f32),
        ),
        in_specs=[SMEM] * 5 + [VMEM] * 4,
        out_specs=(VMEM,) * 2,
        scratch_shapes=[pltpu.VMEM((probe_taper.shape[2], ROWS, groups * ROWS), f32)],
        compiler_params=params,
        name="update",
    )(place, pair_cells, pair_probes, pair_taper, pair_counts, pred_all, obs_all, theta_all, t_rows)
    return (from_rows(u2_rows, shape), from_rows(post_rows, shape), gain)


def solution(mesh):
    return jax.shard_map(
        shards,
        mesh=mesh,
        in_specs=(
            P("ens", "space", None),
            P("ens", "space", None),
            P("space"),
            P("ens", "space"),
            P("space"),
            P("space"),
            P("space", None),
            P("space", None),
            P("space", None),
            P("space"),
            P("space", None, None),
        ),
        out_specs=(P("ens", "space", None), P("ens", "space", None), P("ens", "space")),
        check_vma=False,
    )
```

```python
import functools

import jax
import jax.numpy as jnp
from jax import lax
from jax.experimental import pallas as pl
from jax.experimental.pallas import tpu as pltpu
from jax.sharding import PartitionSpec as P

LANES = 128
ROWS = 8
NZ = 64
HALF_DT = 0.5 * 0.08

VMEM = pl.BlockSpec(memory_space=pltpu.VMEM)
SMEM = pl.BlockSpec(memory_space=pltpu.SMEM)
HBM = pl.BlockSpec(memory_space=pltpu.HBM)


def to_rows(array):
    members, planes, cells = array.shape
    split = array.reshape(members, planes // ROWS, ROWS, cells // LANES, LANES)
    return split.transpose(0, 1, 3, 2, 4).reshape(-1, LANES)


def from_rows(rows, shape):
    members, planes, cells = shape
    split = rows.reshape(members, planes // ROWS, cells // LANES, ROWS, LANES)
    return split.transpose(0, 1, 3, 2, 4).reshape(shape)


def row_of(plane, tile, tiles):
    return (plane // ROWS * tiles + tile) * ROWS + plane % ROWS


def pack_kernel(planes, tiles, cells_hbm, taper_hbm, u_hbm, t_hbm, noise_hbm, observed_hbm, var_hbm,
                low_ref, high_ref, obs_ref, pick_hbm,
                cells_ref, taper_ref, u_ref, t_ref, noise_ref, row_ref, pick_ref, sems):
    stride = planes * tiles
    blocks = noise_ref.shape[1] // LANES
    copies = [
        pltpu.make_async_copy(source, target, sems.at[at])
        for at, (source, target) in enumerate((
            (cells_hbm, cells_ref),
            (t_hbm, t_ref),
            (u_hbm, u_ref),
            (taper_hbm, taper_ref),
            (noise_hbm, noise_ref),
            (observed_hbm, row_ref.at[0:1]),
            (var_hbm, row_ref.at[1:2]),
        ))
    ]
    for copy in copies:
        copy.start()
    copies[0].wait()
    copies[1].wait()
    for slot in range(pick_ref.shape[0]):
        block = cells_ref[0, slot]
        pick_ref[slot] = t_ref[pl.ds(row_of(block // tiles, block % tiles, tiles), ROWS, stride=stride), :]
    picked = pltpu.make_async_copy(pick_ref, pick_hbm, sems.at[len(copies)])
    picked.start()
    for kind, source in ((1, t_ref), (0, u_ref)):
        if kind == 0:
            copies[2].wait()
        for out_ref, first in ((high_ref, planes - 2), (low_ref, 0)):
            for depth in range(2):
                for tile in range(tiles):
                    out_ref[(kind * 2 + depth) * tiles + tile] = source[
                        pl.ds(row_of(first + depth, tile, tiles), ROWS, stride=stride), :
                    ]
    for copy in copies[3:]:
        copy.wait()
    own, window = taper_ref.shape[1:]
    rows = [row_ref[kind : kind + 1, b * LANES : (b + 1) * LANES] for kind in range(2) for b in range(blocks)]
    rows.append(jnp.ones((1, LANES), jnp.float32))
    for i in range(own):
        for j in range(window):
            rows.append(jnp.full((1, LANES), taper_ref[0, i, j].astype(jnp.float32), jnp.float32))
    for ref, first in ((low_ref, 4 * tiles), (high_ref, 4 * tiles), (obs_ref, 0)):
        for b in range(blocks):
            ref[first + b] = noise_ref[:, b * LANES : (b + 1) * LANES]
        for at, row in enumerate(rows):
            ref[first + blocks + at // ROWS, at % ROWS : at % ROWS + 1, :] = row
    picked.wait()


def rot(value, by):
    return pltpu.roll(value, by % LANES, 1)


def lane_masks():
    lane = lax.broadcasted_iota(jnp.int32, (ROWS, LANES), 1)
    height = lane & (NZ - 1)
    return lane < NZ, height == 0, height == NZ - 1


def coefficients(masks, low, here, high):
    first_half, floor, roof = masks
    tiles = len(here)
    turned = [rot(value, NZ) for value in here]
    out = []
    for tile in range(tiles):
        mid = here[tile]
        near = mid + turned[tile]
        far = mid + jnp.where(first_half, turned[tile - 1], turned[(tile + 1) % tiles])
        up = mid + jnp.where(roof, HALF_DT, rot(mid, -1))
        down = mid + jnp.where(floor, HALF_DT, rot(mid, 1))
        below = mid + low[tile]
        above = mid + high[tile]
        diag = 1.0 - ((near + far) + (up + down) + (below + above))
        out.append((diag, near, far, jnp.where(roof, 0.0, up), jnp.where(floor, 0.0, down), below, above))
    return out


def step(masks, weights, low, here, high):
    first_half = masks[0]
    tiles = len(here)
    turned = [rot(value, NZ) for value in here]
    out = []
    for tile in range(tiles):
        diag, near, far, up, down, below, above = weights[tile]
        mid = here[tile]
        beyond = jnp.where(first_half, turned[tile - 1], turned[(tile + 1) % tiles])
        out.append(
            (diag * mid + near * turned[tile])
            + (far * beyond + up * rot(mid, -1))
            + (down * rot(mid, 1) + below * low[tile])
            + above * high[tile]
        )
    return out


def plane_of(ref, at, tiles):
    return [ref[at * tiles + tile] for tile in range(tiles)]


def put(ref, at, values):
    for tile, value in enumerate(values):
        ref[at * len(values) + tile] = value


def inner_kernel(planes, tiles, u_hbm, t_hbm, u2_ref, edge_ref,
                 u_ref, t_ref, u0, hv, u1, held, sems):
    stride = planes * tiles
    masks = lane_masks()
    copies = [pltpu.make_async_copy(u_hbm, u_ref, sems.at[0]), pltpu.make_async_copy(t_hbm, t_ref, sems.at[1])]
    for copy in copies:
        copy.start()
    for copy in copies:
        copy.wait()

    def load(x, _):
        base = (x // ROWS) * tiles * ROWS + x % ROWS
        for tile in range(tiles):
            rows = pl.ds(base + tile * ROWS, ROWS, stride=stride)
            u0[x * tiles + tile] = u_ref[rows, :]
            hv[x * tiles + tile] = HALF_DT * jnp.exp(t_ref[rows, :])
        return 0

    lax.fori_loop(0, planes, load, 0)

    def first_step(x, _):
        weights = coefficients(masks, *[plane_of(hv, x + d, tiles) for d in (-1, 0, 1)])
        for tile in range(tiles):
            for kind in range(5):
                held[kind, x * tiles + tile] = weights[tile][kind]
        put(u1, x, step(masks, weights, *[plane_of(u0, x + d, tiles) for d in (-1, 0, 1)]))
        return 0

    lax.fori_loop(1, planes - 1, first_step, 0)

    def second_step(x, _):
        weights = []
        for tile in range(tiles):
            at = x * tiles + tile
            here = hv[at]
            weights.append([held[kind, at] for kind in range(5)] + [here + hv[at - tiles], here + hv[at + tiles]])
        put(u2_ref, x, step(masks, weights, *[plane_of(u1, x + d, tiles) for d in (-1, 0, 1)]))
        return 0

    lax.fori_loop(2, planes - 2, second_step, 0)
    last = planes - 1
    at = 0
    for ref, kept in ((u0, (0, 1, last - 1, last)), (hv, (0, 1, 2, last - 2, last - 1, last)),
                      (u1, (1, 2, last - 2, last - 1))):
        for x in kept:
            put(edge_ref, at, plane_of(ref, x, tiles))
            at += 1


def outer_kernel(planes, tiles, probe_ref, before_ref, after_ref, edge_ref, inner_ref, u2_ref, sent_ref):
    masks = lane_masks()
    blocks = sent_ref.shape[2] // LANES
    mark = 4 * tiles + blocks + 2 * blocks // ROWS
    mark_row = 2 * blocks % ROWS
    edge = [plane_of(edge_ref, at, tiles) for at in range(14)]
    last = planes - 1
    for ref, own_u, own_v, own_1, where in (
        (before_ref, edge[0:2], edge[4:7], edge[10:12], (0, 1)),
        (after_ref, edge[3:1:-1], edge[9:6:-1], edge[13:11:-1], (last, last - 1)),
    ):
        order = (0, 1) if ref is before_ref else (1, 0)
        u = [plane_of(ref, d, tiles) for d in order] + own_u
        v = [[HALF_DT * jnp.exp(t) for t in plane_of(ref, 2 + d, tiles)] for d in order] + own_v
        live = ref[mark, mark_row : mark_row + 1, :]
        weights = [coefficients(masks, v[d], v[d + 1], v[d + 2]) for d in range(3)]
        next_u = [step(masks, weights[d], u[d], u[d + 1], u[d + 2]) for d in range(2)]
        next_u[0] = [value * live for value in next_u[0]]
        next_u = next_u + own_1
        for d in range(2):
            put(u2_ref, where[d], step(masks, weights[d + 1], next_u[d], next_u[d + 1], next_u[d + 2]))

    lane = lax.broadcasted_iota(jnp.int32, (ROWS, LANES), 1)
    for part in range(blocks):
        found = jnp.zeros((ROWS, LANES), jnp.float32)
        for p in range(LANES):
            cell = probe_ref[part * LANES + p]
            turned = pltpu.roll(u2_ref[cell >> 7], (p - cell) & (LANES - 1), 1)
            found = jnp.where(lane == p, turned, found)

        def send(device, _):
            sent_ref[device, :, part * LANES : (part + 1) * LANES] = found
            return 0

        lax.fori_loop(0, sent_ref.shape[0], send, 0)


def store_kernel(planes, tiles, u2_ref, out_ref):
    stride = planes * tiles

    def store(x, _):
        base = (x // ROWS) * tiles * ROWS + x % ROWS
        for tile in range(tiles):
            out_ref[pl.ds(base + tile * ROWS, ROWS, stride=stride), :] = u2_ref[x * tiles + tile]
        return 0

    lax.fori_loop(0, planes, store, 0)


def dot_lanes(left, right):
    return lax.dot_general(left, right, (((1,), (1,)), ((), ())), precision=lax.Precision.HIGHEST,
                           preferred_element_type=jnp.float32)


def dot_rows(left, right):
    return lax.dot_general(left, right, (((1,), (0,)), ((), ())), precision=lax.Precision.HIGHEST,
                           preferred_element_type=jnp.float32)


def update_kernel(slabs, groups, planes, tiles, own, place_ref, cells_hbm, probes_hbm, level_hbm, count_hbm,
                  pred_ref, obs_refs, theta_ref, t_ref, post_ref, gain_ref,
                  reach, cells_ref, probes_ref, level_ref, count_ref, sems):
    members = groups * ROWS
    share = 1.0 / (members - 1)
    copies = [
        pltpu.make_async_copy(source, target, sems.at[at])
        for at, (source, target) in enumerate((
            (cells_hbm, cells_ref), (probes_hbm, probes_ref), (level_hbm, level_ref), (count_hbm, count_ref)))
    ]
    for copy in copies:
        copy.start()
    slab, group = place_ref[0], place_ref[1]
    blocks = gain_ref.shape[1] // LANES
    window = 3 * blocks
    post_ref[...] = t_ref[...]

    def wide(row):
        return row[:, :members] if members <= LANES else jnp.concatenate([row] * (members // LANES), axis=1)

    anomaly, scaled, variance, matches = [], [], [], []
    for d in range(5):
        wanted = slab + d - 2
        at = jnp.clip(wanted, 0, slabs - 1)
        live = jnp.where((wanted >= 0) & (wanted < slabs), 1.0, 0.0)
        predicted = pred_ref[pl.ds(at * groups, groups)].reshape(members, blocks * LANES)
        mean = jnp.sum(predicted, axis=0, keepdims=True) / members
        anomaly.append((predicted - mean) * live)
        mine = pred_ref[at * groups + group]
        ref, first = obs_refs[d]
        for b in range(blocks):
            cut = slice(b * LANES, (b + 1) * LANES)
            observed = ref[first + blocks, b : b + 1, :]
            variance.append(ref[first + blocks, blocks + b : blocks + b + 1, :] + (1.0 - live))
            scaled.append((observed + ref[first + b] - mine[:, cut]) / variance[-1] * live)
            matches.append(dot_lanes(scaled[-1], anomaly[d][:, cut]))
    for d in range(1, 4):
        ref, first = obs_refs[d]
        for i in range(blocks):
            cut = slice(i * LANES, (i + 1) * LANES)
            total = jnp.zeros((ROWS, members), jnp.float32)
            for j in range(window):
                at = 2 * blocks + 1 + i * window + j
                level = ref[first + blocks + at // ROWS, at % ROWS : at % ROWS + 1, :] / 256.0 * share
                total = total + wide(level) * matches[(d - 1) * blocks + j]
            correction = dot_rows(total, anomaly[d][:, cut])
            gain = scaled[d * blocks + i] - correction / variance[d * blocks + i]
            if d == 2:
                gain_ref[:, cut] = gain
            reach[(d - 1) * blocks + i] = dot_lanes(gain, anomaly[d][:, cut])
    for copy in copies:
        copy.wait()
    for slot in range(theta_ref.shape[1]):
        weight = jnp.where(slot < count_ref[0], level_ref[0, slot].astype(jnp.float32) / 256.0, 0.0) * share
        change = dot_rows(reach[probes_ref[0, slot]] * weight, theta_ref[:, slot].reshape(members, LANES))
        block = cells_ref[0, slot]
        rows = pl.ds(row_of(block // tiles, block % tiles, tiles), ROWS, stride=planes * tiles)
        post_ref[rows, :] = post_ref[rows, :] + change


def shards(
    starting_speed_field,
    sample_fluidity_exponent,
    observed,
    obs_noise,
    obs_var,
    probe_cells,
    pair_cells,
    pair_probes,
    pair_taper,
    pair_counts,
    probe_taper,
):
    shape = starting_speed_field.shape
    members, planes, cells = shape
    tiles = cells // LANES
    slots = pair_cells.shape[1]
    probes = obs_noise.shape[1]
    blocks = probes // LANES
    slabs, groups = lax.axis_size("space"), lax.axis_size("ens")
    f32, i32 = jnp.float32, jnp.int32
    u_rows = to_rows(starting_speed_field)
    t_rows = to_rows(sample_fluidity_exponent)
    obs_tiles = blocks - (-(2 * blocks + 1 + probe_taper.shape[1] * probe_taper.shape[2]) // ROWS)
    edge = jax.ShapeDtypeStruct((4 * tiles + obs_tiles, ROWS, LANES), f32)
    obs_shape = jax.ShapeDtypeStruct((obs_tiles, ROWS, LANES), f32)
    params = pltpu.CompilerParams(vmem_limit_bytes=48 * 1024 * 1024)
    field = pltpu.VMEM(u_rows.shape, f32)
    stack = pltpu.VMEM((planes * tiles, ROWS, LANES), f32)
    low, high, obs, picked = pl.pallas_call(
        functools.partial(pack_kernel, planes, tiles),
        out_shape=(edge, edge, obs_shape, jax.ShapeDtypeStruct((slots, ROWS, LANES), f32)),
        in_specs=[HBM] * 7,
        out_specs=(VMEM, VMEM, VMEM, HBM),
        scratch_shapes=[
            pltpu.SMEM(pair_cells.shape, i32),
            pltpu.SMEM(probe_taper.shape, i32),
            field,
            field,
            pltpu.VMEM((ROWS, probes), f32),
            pltpu.VMEM((2, probes), f32),
            pltpu.VMEM((slots, ROWS, LANES), f32),
            pltpu.SemaphoreType.DMA((8,)),
        ],
        compiler_params=params,
        name="pack",
    )(pair_cells, probe_taper, u_rows, t_rows, obs_noise, observed.reshape(1, -1), obs_var.reshape(1, -1))
    upward = [(i, i + 1) for i in range(slabs - 1)]
    before = lax.ppermute(high, "space", upward)
    after = lax.ppermute(low, "space", [(j, i) for i, j in upward])
    if slabs == 4:
        before_2 = after_2 = lax.ppermute(obs, "space", [(i, (i + 2) % 4) for i in range(4)])
    else:
        upward_2 = [(i, i + 2) for i in range(slabs - 2)]
        before_2 = lax.ppermute(obs, "space", upward_2)
        after_2 = lax.ppermute(obs, "space", [(j, i) for i, j in upward_2])
    theta_all = lax.all_gather(picked, "ens")
    inner, edges = pl.pallas_call(
        functools.partial(inner_kernel, planes, tiles),
        out_shape=(
            jax.ShapeDtypeStruct((planes * tiles, ROWS, LANES), f32),
            jax.ShapeDtypeStruct((14 * tiles, ROWS, LANES), f32),
        ),
        in_specs=[HBM] * 2,
        out_specs=(VMEM,) * 2,
        scratch_shapes=[
            field,
            field,
            stack,
            stack,
            stack,
            pltpu.VMEM((5, planes * tiles, ROWS, LANES), f32),
            pltpu.SemaphoreType.DMA((2,)),
        ],
        compiler_params=params,
        cost_estimate=pl.CostEstimate(flops=20_000_000, bytes_accessed=20_000_000, transcendentals=0),
        name="inner_planes",
    )(u_rows, t_rows)
    u2, sent = pl.pallas_call(
        functools.partial(outer_kernel, planes, tiles),
        out_shape=(
            jax.ShapeDtypeStruct((planes * tiles, ROWS, LANES), f32),
            jax.ShapeDtypeStruct((slabs * groups, members, probes), f32),
        ),
        in_specs=[SMEM] + [VMEM] * 4,
        out_specs=(VMEM,) * 2,
        input_output_aliases={4: 0},
        compiler_params=params,
        name="outer_planes",
    )(probe_cells, before, after, edges, inner)
    pred_all = lax.all_to_all(sent, ("space", "ens"), 0, 0)
    u2_rows = pl.pallas_call(
        functools.partial(store_kernel, planes, tiles),
        out_shape=jax.ShapeDtypeStruct(u_rows.shape, f32),
        in_specs=[VMEM],
        out_specs=VMEM,
        compiler_params=params,
        cost_estimate=pl.CostEstimate(flops=1_000_000, bytes_accessed=8_000_000, transcendentals=0),
        name="store",
    )(u2)
    place = jnp.stack([lax.axis_index("space"), lax.axis_index("ens")]).astype(i32)

    def update(place_ref, cells_ref, probes_ref, level_ref, count_ref, pred_ref, before_2_ref, before_ref, obs_ref,
               after_ref, after_2_ref, *rest):
        seen = ((before_2_ref, 0), (before_ref, 4 * tiles), (obs_ref, 0), (after_ref, 4 * tiles), (after_2_ref, 0))
        update_kernel(slabs, groups, planes, tiles, 0, place_ref, cells_ref, probes_ref, level_ref, count_ref,
                      pred_ref, seen, *rest)

    post_rows, gain = pl.pallas_call(
        update,
        out_shape=(
            jax.ShapeDtypeStruct(u_rows.shape, f32),
            jax.ShapeDtypeStruct((members, probes), f32),
        ),
        in_specs=[SMEM] + [HBM] * 4 + [VMEM] * 8,
        out_specs=(VMEM,) * 2,
        scratch_shapes=[
            pltpu.VMEM((probe_taper.shape[2], ROWS, groups * ROWS), f32),
            pltpu.SMEM(pair_cells.shape, i32),
            pltpu.SMEM(pair_cells.shape, i32),
            pltpu.SMEM(pair_cells.shape, i32),
            pltpu.SMEM(pair_counts.shape, i32),
            pltpu.SemaphoreType.DMA((4,)),
        ],
        compiler_params=params,
        name="update",
    )(place, pair_cells, pair_probes, pair_taper, pair_counts, pred_all, before_2, before, obs, after, after_2,
      theta_all, t_rows)
    return (from_rows(u2_rows, shape), from_rows(post_rows, shape), gain)


def solution(mesh):
    return jax.shard_map(
        shards,
        mesh=mesh,
        in_specs=(
            P("ens", "space", None),
            P("ens", "space", None),
            P("space"),
            P("ens", "space"),
            P("space"),
            P("space"),
            P("space", None),
            P("space", None),
            P("space", None),
            P("space"),
            P("space", None, None),
        ),
        out_specs=(P("ens", "space", None), P("ens", "space", None), P("ens", "space")),
        check_vma=False,
    )
```

```python
import functools

import jax
import jax.numpy as jnp
from jax import lax
from jax.experimental import pallas as pl
from jax.experimental.pallas import tpu as pltpu
from jax.sharding import PartitionSpec as P

LANES = 128
ROWS = 8
NZ = 64
HALF_DT = 0.5 * 0.08

VMEM = pl.BlockSpec(memory_space=pltpu.VMEM)
SMEM = pl.BlockSpec(memory_space=pltpu.SMEM)
HBM = pl.BlockSpec(memory_space=pltpu.HBM)
ANY = pl.BlockSpec(memory_space=pl.ANY)


def stay(array):
    return pltpu.with_memory_space_constraint(array, pltpu.HBM)


def to_rows(array):
    members, planes, cells = array.shape
    split = array.reshape(members, planes // ROWS, ROWS, cells // LANES, LANES)
    return split.transpose(0, 1, 3, 2, 4).reshape(-1, LANES)


def from_rows(rows, shape):
    members, planes, cells = shape
    split = rows.reshape(members, planes // ROWS, cells // LANES, ROWS, LANES)
    return split.transpose(0, 1, 3, 2, 4).reshape(shape)


def row_of(plane, tile, tiles):
    return (plane // ROWS * tiles + tile) * ROWS + plane % ROWS


def pack_kernel(planes, tiles, cells_hbm, taper_hbm, u_hbm, t_hbm, noise_hbm, observed_hbm, var_hbm,
                low_ref, high_ref, obs_ref, pick_hbm,
                cells_ref, taper_ref, u_ref, t_ref, noise_ref, row_ref, pick_ref, sems):
    stride = planes * tiles
    blocks = noise_ref.shape[1] // LANES
    copies = [
        pltpu.make_async_copy(source, target, sems.at[at])
        for at, (source, target) in enumerate((
            (cells_hbm, cells_ref),
            (t_hbm, t_ref),
            (u_hbm, u_ref),
            (taper_hbm, taper_ref),
            (noise_hbm, noise_ref),
            (observed_hbm, row_ref.at[0:1]),
            (var_hbm, row_ref.at[1:2]),
        ))
    ]
    for copy in copies:
        copy.start()
    copies[0].wait()
    copies[1].wait()
    for slot in range(pick_ref.shape[0]):
        block = cells_ref[0, slot]
        pick_ref[slot] = t_ref[pl.ds(row_of(block // tiles, block % tiles, tiles), ROWS, stride=stride), :]
    picked = pltpu.make_async_copy(pick_ref, pick_hbm, sems.at[len(copies)])
    picked.start()
    for kind, source in ((1, t_ref), (0, u_ref)):
        if kind == 0:
            copies[2].wait()
        for out_ref, first in ((high_ref, planes - 2), (low_ref, 0)):
            for depth in range(2):
                for tile in range(tiles):
                    out_ref[(kind * 2 + depth) * tiles + tile] = source[
                        pl.ds(row_of(first + depth, tile, tiles), ROWS, stride=stride), :
                    ]
    for copy in copies[3:]:
        copy.wait()
    own, window = taper_ref.shape[1:]
    rows = [row_ref[kind : kind + 1, b * LANES : (b + 1) * LANES] for kind in range(2) for b in range(blocks)]
    rows.append(jnp.ones((1, LANES), jnp.float32))
    for i in range(own):
        for j in range(window):
            rows.append(jnp.full((1, LANES), taper_ref[0, i, j].astype(jnp.float32), jnp.float32))
    for ref, first in ((low_ref, 4 * tiles), (high_ref, 4 * tiles), (obs_ref, 0)):
        for b in range(blocks):
            ref[first + b] = noise_ref[:, b * LANES : (b + 1) * LANES]
        for at, row in enumerate(rows):
            ref[first + blocks + at // ROWS, at % ROWS : at % ROWS + 1, :] = row
    picked.wait()


def rot(value, by):
    return pltpu.roll(value, by % LANES, 1)


def lane_masks():
    lane = lax.broadcasted_iota(jnp.int32, (ROWS, LANES), 1)
    height = lane & (NZ - 1)
    return lane < NZ, height == 0, height == NZ - 1


def coefficients(masks, low, here, high):
    first_half, floor, roof = masks
    tiles = len(here)
    turned = [rot(value, NZ) for value in here]
    out = []
    for tile in range(tiles):
        mid = here[tile]
        near = mid + turned[tile]
        far = mid + jnp.where(first_half, turned[tile - 1], turned[(tile + 1) % tiles])
        up = mid + jnp.where(roof, HALF_DT, rot(mid, -1))
        down = mid + jnp.where(floor, HALF_DT, rot(mid, 1))
        below = mid + low[tile]
        above = mid + high[tile]
        diag = 1.0 - ((near + far) + (up + down) + (below + above))
        out.append((diag, near, far, jnp.where(roof, 0.0, up), jnp.where(floor, 0.0, down), below, above))
    return out


def step(masks, weights, low, here, high):
    first_half = masks[0]
    tiles = len(here)
    turned = [rot(value, NZ) for value in here]
    out = []
    for tile in range(tiles):
        diag, near, far, up, down, below, above = weights[tile]
        mid = here[tile]
        beyond = jnp.where(first_half, turned[tile - 1], turned[(tile + 1) % tiles])
        out.append(
            (diag * mid + near * turned[tile])
            + (far * beyond + up * rot(mid, -1))
            + (down * rot(mid, 1) + below * low[tile])
            + above * high[tile]
        )
    return out


def plane_of(ref, at, tiles):
    return [ref[at * tiles + tile] for tile in range(tiles)]


def put(ref, at, values):
    for tile, value in enumerate(values):
        ref[at * len(values) + tile] = value


def inner_kernel(planes, tiles, u_hbm, t_hbm, u2_ref, edge_ref,
                 u_ref, t_ref, u0, hv, u1, held, sems):
    stride = planes * tiles
    masks = lane_masks()
    copies = [pltpu.make_async_copy(u_hbm, u_ref, sems.at[0]), pltpu.make_async_copy(t_hbm, t_ref, sems.at[1])]
    for copy in copies:
        copy.start()
    for copy in copies:
        copy.wait()

    def load(x, _):
        base = (x // ROWS) * tiles * ROWS + x % ROWS
        for tile in range(tiles):
            rows = pl.ds(base + tile * ROWS, ROWS, stride=stride)
            u0[x * tiles + tile] = u_ref[rows, :]
            hv[x * tiles + tile] = HALF_DT * jnp.exp(t_ref[rows, :])
        return 0

    lax.fori_loop(0, planes, load, 0)

    def first_step(x, _):
        weights = coefficients(masks, *[plane_of(hv, x + d, tiles) for d in (-1, 0, 1)])
        for tile in range(tiles):
            for kind in range(5):
                held[kind, x * tiles + tile] = weights[tile][kind]
        put(u1, x, step(masks, weights, *[plane_of(u0, x + d, tiles) for d in (-1, 0, 1)]))
        return 0

    lax.fori_loop(1, planes - 1, first_step, 0)

    def second_step(x, _):
        weights = []
        for tile in range(tiles):
            at = x * tiles + tile
            here = hv[at]
            weights.append([held[kind, at] for kind in range(5)] + [here + hv[at - tiles], here + hv[at + tiles]])
        put(u2_ref, x, step(masks, weights, *[plane_of(u1, x + d, tiles) for d in (-1, 0, 1)]))
        return 0

    lax.fori_loop(2, planes - 2, second_step, 0)
    last = planes - 1
    at = 0
    for ref, kept in ((u0, (0, 1, last - 1, last)), (hv, (0, 1, 2, last - 2, last - 1, last)),
                      (u1, (1, 2, last - 2, last - 1))):
        for x in kept:
            put(edge_ref, at, plane_of(ref, x, tiles))
            at += 1


def outer_kernel(planes, tiles, probe_hbm, before_ref, after_ref, edge_ref, inner_ref, before_2_hbm, after_2_hbm,
                 u2_ref, sent_ref, probe_ref, sem):
    probe_copy = pltpu.make_async_copy(probe_hbm, probe_ref, sem)
    probe_copy.start()
    masks = lane_masks()
    blocks = sent_ref.shape[2] // LANES
    mark = 4 * tiles + blocks + 2 * blocks // ROWS
    mark_row = 2 * blocks % ROWS
    edge = [plane_of(edge_ref, at, tiles) for at in range(14)]
    last = planes - 1
    for ref, own_u, own_v, own_1, where in (
        (before_ref, edge[0:2], edge[4:7], edge[10:12], (0, 1)),
        (after_ref, edge[3:1:-1], edge[9:6:-1], edge[13:11:-1], (last, last - 1)),
    ):
        order = (0, 1) if ref is before_ref else (1, 0)
        u = [plane_of(ref, d, tiles) for d in order] + own_u
        v = [[HALF_DT * jnp.exp(t) for t in plane_of(ref, 2 + d, tiles)] for d in order] + own_v
        live = ref[mark, mark_row : mark_row + 1, :]
        weights = [coefficients(masks, v[d], v[d + 1], v[d + 2]) for d in range(3)]
        next_u = [step(masks, weights[d], u[d], u[d + 1], u[d + 2]) for d in range(2)]
        next_u[0] = [value * live for value in next_u[0]]
        next_u = next_u + own_1
        for d in range(2):
            put(u2_ref, where[d], step(masks, weights[d + 1], next_u[d], next_u[d + 1], next_u[d + 2]))

    probe_copy.wait()
    lane = lax.broadcasted_iota(jnp.int32, (ROWS, LANES), 1)
    for part in range(blocks):
        found = jnp.zeros((ROWS, LANES), jnp.float32)
        for p in range(LANES):
            cell = probe_ref[part * LANES + p]
            turned = pltpu.roll(u2_ref[cell >> 7], (p - cell) & (LANES - 1), 1)
            found = jnp.where(lane == p, turned, found)

        def send(device, _):
            sent_ref[device, :, part * LANES : (part + 1) * LANES] = found
            return 0

        lax.fori_loop(0, sent_ref.shape[0], send, 0)


def halves(value):
    high = value.astype(jnp.bfloat16)
    return high, (value - high.astype(jnp.float32)).astype(jnp.bfloat16)


def between_kernel(planes, tiles, u2_ref, theta_hbm, out_ref, split_ref, theta_ref, sem):
    copy = pltpu.make_async_copy(theta_hbm, theta_ref, sem)
    copy.start()
    stride = planes * tiles
    members = theta_ref.shape[0] * ROWS

    def store(x, _):
        base = (x // ROWS) * tiles * ROWS + x % ROWS
        for tile in range(tiles):
            out_ref[pl.ds(base + tile * ROWS, ROWS, stride=stride), :] = u2_ref[x * tiles + tile]
        return 0

    lax.fori_loop(0, planes, store, 0)
    copy.wait()

    def split(slot, _):
        high, low = halves(theta_ref[:, slot].reshape(members, LANES))
        split_ref[slot, :members, :] = high
        split_ref[slot, members:, :] = low
        return 0

    lax.fori_loop(0, split_ref.shape[0], split, 0)


def dot_lanes(left, right):
    return lax.dot_general(left, right, (((1,), (1,)), ((), ())), precision=lax.Precision.HIGHEST,
                           preferred_element_type=jnp.float32)


def dot_rows(left, right):
    return lax.dot_general(left, right, (((1,), (0,)), ((), ())), precision=lax.Precision.HIGHEST,
                           preferred_element_type=jnp.float32)


def update_kernel(slabs, groups, planes, tiles, place_ref, count_ref, cells_hbm, probes_hbm, level_hbm,
                  pred_ref, obs_refs, split_ref, t_ref, post_ref, gain_ref,
                  reach, cells_ref, probes_ref, level_ref, sems):
    members = groups * ROWS
    share = 1.0 / (members - 1)
    copies = [
        pltpu.make_async_copy(source, target, sems.at[at])
        for at, (source, target) in enumerate((
            (cells_hbm, cells_ref), (probes_hbm, probes_ref), (level_hbm, level_ref)))
    ]
    for copy in copies:
        copy.start()
    slab, group = place_ref[0], place_ref[1]
    blocks = gain_ref.shape[1] // LANES
    window = 3 * blocks
    post_ref[...] = t_ref[...]

    def wide(row):
        return row[:, :members] if members <= LANES else jnp.concatenate([row] * (members // LANES), axis=1)

    anomaly, scaled, variance, matches = [], [], [], []
    for d in range(5):
        wanted = slab + d - 2
        at = jnp.clip(wanted, 0, slabs - 1)
        live = jnp.where((wanted >= 0) & (wanted < slabs), 1.0, 0.0)
        predicted = pred_ref[pl.ds(at * groups, groups)].reshape(members, blocks * LANES)
        mean = jnp.sum(predicted, axis=0, keepdims=True) / members
        anomaly.append((predicted - mean) * live)
        mine = pred_ref[at * groups + group]
        ref, first = obs_refs[d]
        for b in range(blocks):
            cut = slice(b * LANES, (b + 1) * LANES)
            observed = ref[first + blocks, b : b + 1, :]
            variance.append(ref[first + blocks, blocks + b : blocks + b + 1, :] + (1.0 - live))
            scaled.append((observed + ref[first + b] - mine[:, cut]) / variance[-1] * live)
            matches.append(dot_lanes(scaled[-1], anomaly[d][:, cut]))
    for d in range(1, 4):
        ref, first = obs_refs[d]
        for i in range(blocks):
            cut = slice(i * LANES, (i + 1) * LANES)
            total = jnp.zeros((ROWS, members), jnp.float32)
            for j in range(window):
                at = 2 * blocks + 1 + i * window + j
                level = ref[first + blocks + at // ROWS, at % ROWS : at % ROWS + 1, :] / 256.0 * share
                total = total + wide(level) * matches[(d - 1) * blocks + j]
            correction = dot_rows(total, anomaly[d][:, cut])
            gain = scaled[d * blocks + i] - correction / variance[d * blocks + i]
            if d == 2:
                gain_ref[:, cut] = gain
            high, low = halves(dot_lanes(gain, anomaly[d][:, cut]))
            both = jnp.concatenate([high.astype(jnp.float32), low.astype(jnp.float32)], axis=0)
            reach[(d - 1) * blocks + i] = jnp.concatenate([both, both], axis=1).astype(jnp.bfloat16)
    for copy in copies:
        copy.wait()
    for slot in range(split_ref.shape[0]):
        weight = jnp.where(slot < count_ref[0], level_ref[0, slot].astype(jnp.float32) / 256.0, 0.0) * share
        both = lax.dot_general(reach[probes_ref[0, slot]], split_ref[slot],
                               (((1,), (0,)), ((), ())), preferred_element_type=jnp.float32)
        change = (both[:ROWS] + both[ROWS:]) * weight
        block = cells_ref[0, slot]
        rows = pl.ds(row_of(block // tiles, block % tiles, tiles), ROWS, stride=planes * tiles)
        post_ref[rows, :] = post_ref[rows, :] + change


def shards(
    starting_speed_field,
    sample_fluidity_exponent,
    observed,
    obs_noise,
    obs_var,
    probe_cells,
    pair_cells,
    pair_probes,
    pair_taper,
    pair_counts,
    probe_taper,
):
    shape = starting_speed_field.shape
    members, planes, cells = shape
    tiles = cells // LANES
    slots = pair_cells.shape[1]
    probes = obs_noise.shape[1]
    blocks = probes // LANES
    slabs, groups = lax.axis_size("space"), lax.axis_size("ens")
    f32, i32 = jnp.float32, jnp.int32
    u_rows = to_rows(starting_speed_field)
    t_rows = to_rows(sample_fluidity_exponent)
    obs_tiles = blocks - (-(2 * blocks + 1 + probe_taper.shape[1] * probe_taper.shape[2]) // ROWS)
    edge = jax.ShapeDtypeStruct((4 * tiles + obs_tiles, ROWS, LANES), f32)
    obs_shape = jax.ShapeDtypeStruct((obs_tiles, ROWS, LANES), f32)
    params = pltpu.CompilerParams(vmem_limit_bytes=48 * 1024 * 1024)
    field = pltpu.VMEM(u_rows.shape, f32)
    stack = pltpu.VMEM((planes * tiles, ROWS, LANES), f32)
    low, high, obs, picked = pl.pallas_call(
        functools.partial(pack_kernel, planes, tiles),
        out_shape=(edge, edge, obs_shape, jax.ShapeDtypeStruct((slots, ROWS, LANES), f32)),
        in_specs=[HBM] * 7,
        out_specs=(VMEM, VMEM, VMEM, HBM),
        scratch_shapes=[
            pltpu.SMEM(pair_cells.shape, i32),
            pltpu.SMEM(probe_taper.shape, i32),
            field,
            field,
            pltpu.VMEM((ROWS, probes), f32),
            pltpu.VMEM((2, probes), f32),
            pltpu.VMEM((slots, ROWS, LANES), f32),
            pltpu.SemaphoreType.DMA((8,)),
        ],
        compiler_params=params,
        name="pack",
    )(*map(stay, (pair_cells, probe_taper, u_rows, t_rows, obs_noise, observed.reshape(1, -1), obs_var.reshape(1, -1))))
    upward = [(i, i + 1) for i in range(slabs - 1)]
    before = lax.ppermute(high, "space", upward)
    after = lax.ppermute(low, "space", [(j, i) for i, j in upward])
    if slabs == 4:
        before_2 = after_2 = lax.ppermute(obs, "space", [(i, (i + 2) % 4) for i in range(4)])
    else:
        upward_2 = [(i, i + 2) for i in range(slabs - 2)]
        before_2 = lax.ppermute(obs, "space", upward_2)
        after_2 = lax.ppermute(obs, "space", [(j, i) for i, j in upward_2])
    theta_all = lax.all_gather(picked, "ens")
    inner, edges = pl.pallas_call(
        functools.partial(inner_kernel, planes, tiles),
        out_shape=(
            jax.ShapeDtypeStruct((planes * tiles, ROWS, LANES), f32),
            jax.ShapeDtypeStruct((14 * tiles, ROWS, LANES), f32),
        ),
        in_specs=[HBM] * 2,
        out_specs=(VMEM,) * 2,
        scratch_shapes=[
            field,
            field,
            stack,
            stack,
            stack,
            pltpu.VMEM((5, planes * tiles, ROWS, LANES), f32),
            pltpu.SemaphoreType.DMA((2,)),
        ],
        compiler_params=params,
        cost_estimate=pl.CostEstimate(flops=20_000_000, bytes_accessed=20_000_000, transcendentals=0),
        name="inner_planes",
    )(stay(u_rows), stay(t_rows))
    u2, sent = pl.pallas_call(
        functools.partial(outer_kernel, planes, tiles),
        out_shape=(
            jax.ShapeDtypeStruct((planes * tiles, ROWS, LANES), f32),
            jax.ShapeDtypeStruct((slabs * groups, members, probes), f32),
        ),
        in_specs=[HBM] + [VMEM] * 4 + [ANY] * 2,
        out_specs=(VMEM,) * 2,
        scratch_shapes=[pltpu.SMEM(probe_cells.shape, i32), pltpu.SemaphoreType.DMA(())],
        input_output_aliases={4: 0},
        compiler_params=params,
        name="outer_planes",
    )(stay(probe_cells), before, after, edges, inner, before_2, after_2)
    pred_all = lax.all_to_all(sent, ("space", "ens"), 0, 0)
    u2_rows, split = pl.pallas_call(
        functools.partial(between_kernel, planes, tiles),
        out_shape=(
            jax.ShapeDtypeStruct(u_rows.shape, f32),
            jax.ShapeDtypeStruct((slots, 2 * groups * ROWS, LANES), jnp.bfloat16),
        ),
        in_specs=[VMEM, HBM],
        out_specs=(VMEM,) * 2,
        scratch_shapes=[pltpu.VMEM(theta_all.shape, f32), pltpu.SemaphoreType.DMA(())],
        compiler_params=params,
        cost_estimate=pl.CostEstimate(flops=1_000_000, bytes_accessed=8_000_000, transcendentals=0),
        name="between",
    )(u2, stay(theta_all))
    place = jnp.stack([lax.axis_index("space"), lax.axis_index("ens")]).astype(i32)

    def update(place_ref, count_ref, cells_ref, probes_ref, level_ref, pred_ref, before_2_ref, before_ref, obs_ref,
               after_ref, after_2_ref, *rest):
        seen = ((before_2_ref, 0), (before_ref, 4 * tiles), (obs_ref, 0), (after_ref, 4 * tiles), (after_2_ref, 0))
        update_kernel(slabs, groups, planes, tiles, place_ref, count_ref, cells_ref, probes_ref, level_ref,
                      pred_ref, seen, *rest)

    post_rows, gain = pl.pallas_call(
        update,
        out_shape=(
            jax.ShapeDtypeStruct(u_rows.shape, f32),
            jax.ShapeDtypeStruct((members, probes), f32),
        ),
        in_specs=[SMEM] * 2 + [HBM] * 3 + [VMEM] * 8,
        out_specs=(VMEM,) * 2,
        scratch_shapes=[
            pltpu.VMEM((probe_taper.shape[2], 2 * ROWS, 2 * groups * ROWS), jnp.bfloat16),
            pltpu.SMEM(pair_cells.shape, i32),
            pltpu.SMEM(pair_cells.shape, i32),
            pltpu.SMEM(pair_cells.shape, i32),
            pltpu.SemaphoreType.DMA((3,)),
        ],
        compiler_params=params,
        name="update",
    )(place, pair_counts, *map(stay, (pair_cells, pair_probes, pair_taper)), pred_all, before_2, before, obs, after,
      after_2, split, t_rows)
    return (from_rows(u2_rows, shape), from_rows(post_rows, shape), gain)


def solution(mesh):
    return jax.shard_map(
        shards,
        mesh=mesh,
        in_specs=(
            P("ens", "space", None),
            P("ens", "space", None),
            P("space"),
            P("ens", "space"),
            P("space"),
            P("space"),
            P("space", None),
            P("space", None),
            P("space", None),
            P("space"),
            P("space", None, None),
        ),
        out_specs=(P("ens", "space", None), P("ens", "space", None), P("ens", "space")),
        check_vma=False,
    )
```

```python
import functools

import jax
import jax.numpy as jnp
from jax import lax
from jax.experimental import pallas as pl
from jax.experimental.pallas import tpu as pltpu
from jax.sharding import PartitionSpec as P

LANES = 128
ROWS = 8
NZ = 64
HALF_DT = 0.5 * 0.08

VMEM = pl.BlockSpec(memory_space=pltpu.VMEM)
SMEM = pl.BlockSpec(memory_space=pltpu.SMEM)
HBM = pl.BlockSpec(memory_space=pltpu.HBM)
ANY = pl.BlockSpec(memory_space=pl.ANY)


def stay(array):
    return pltpu.with_memory_space_constraint(array, pltpu.HBM)


def to_rows(array):
    members, planes, cells = array.shape
    split = array.reshape(members, planes // ROWS, ROWS, cells // LANES, LANES)
    return split.transpose(0, 1, 3, 2, 4).reshape(-1, LANES)


def from_rows(rows, shape):
    members, planes, cells = shape
    split = rows.reshape(members, planes // ROWS, cells // LANES, ROWS, LANES)
    return split.transpose(0, 1, 3, 2, 4).reshape(shape)


def row_of(plane, tile, tiles):
    return (plane // ROWS * tiles + tile) * ROWS + plane % ROWS


def pack_kernel(planes, tiles, cells_hbm, taper_hbm, u_hbm, t_hbm, noise_hbm, observed_hbm, var_hbm,
                low_ref, high_ref, obs_ref, pick_hbm, u_ref, t_ref,
                cells_ref, taper_ref, noise_ref, row_ref, pick_ref, sems):
    stride = planes * tiles
    blocks = noise_ref.shape[1] // LANES
    copies = [
        pltpu.make_async_copy(source, target, sems.at[at])
        for at, (source, target) in enumerate((
            (cells_hbm, cells_ref),
            (t_hbm, t_ref),
            (u_hbm, u_ref),
            (taper_hbm, taper_ref),
            (noise_hbm, noise_ref),
            (observed_hbm, row_ref.at[0:1]),
            (var_hbm, row_ref.at[1:2]),
        ))
    ]
    for copy in copies:
        copy.start()
    copies[0].wait()
    copies[1].wait()
    for slot in range(pick_ref.shape[0]):
        block = cells_ref[0, slot]
        pick_ref[slot] = t_ref[pl.ds(row_of(block // tiles, block % tiles, tiles), ROWS, stride=stride), :]
    picked = [
        pltpu.make_async_copy(pick_ref, pick_hbm.at[device], sems.at[len(copies) + device])
        for device in range(pick_hbm.shape[0])
    ]
    for copy in picked:
        copy.start()
    for kind, source in ((1, t_ref), (0, u_ref)):
        if kind == 0:
            copies[2].wait()
        for out_ref, first in ((high_ref, planes - 2), (low_ref, 0)):
            for depth in range(2):
                for tile in range(tiles):
                    out_ref[(kind * 2 + depth) * tiles + tile] = source[
                        pl.ds(row_of(first + depth, tile, tiles), ROWS, stride=stride), :
                    ]
    for copy in copies[3:]:
        copy.wait()
    own, window = taper_ref.shape[1:]
    rows = [row_ref[kind : kind + 1, b * LANES : (b + 1) * LANES] for kind in range(2) for b in range(blocks)]
    rows.append(jnp.ones((1, LANES), jnp.float32))
    for i in range(own):
        for j in range(window):
            rows.append(jnp.full((1, LANES), taper_ref[0, i, j].astype(jnp.float32), jnp.float32))
    for ref, first in ((low_ref, 4 * tiles), (high_ref, 4 * tiles), (obs_ref, 0)):
        for b in range(blocks):
            ref[first + b] = noise_ref[:, b * LANES : (b + 1) * LANES]
        for at, row in enumerate(rows):
            ref[first + blocks + at // ROWS, at % ROWS : at % ROWS + 1, :] = row
    for copy in picked:
        copy.wait()


def rot(value, by):
    return pltpu.roll(value, by % LANES, 1)


def lane_masks():
    lane = lax.broadcasted_iota(jnp.int32, (ROWS, LANES), 1)
    height = lane & (NZ - 1)
    return lane < NZ, height == 0, height == NZ - 1


def coefficients(masks, low, here, high):
    first_half, floor, roof = masks
    tiles = len(here)
    turned = [rot(value, NZ) for value in here]
    out = []
    for tile in range(tiles):
        mid = here[tile]
        near = mid + turned[tile]
        far = mid + jnp.where(first_half, turned[tile - 1], turned[(tile + 1) % tiles])
        up = mid + jnp.where(roof, HALF_DT, rot(mid, -1))
        down = mid + jnp.where(floor, HALF_DT, rot(mid, 1))
        below = mid + low[tile]
        above = mid + high[tile]
        diag = 1.0 - ((near + far) + (up + down) + (below + above))
        out.append((diag, near, far, jnp.where(roof, 0.0, up), jnp.where(floor, 0.0, down), below, above))
    return out


def step(masks, weights, low, here, high):
    first_half = masks[0]
    tiles = len(here)
    turned = [rot(value, NZ) for value in here]
    out = []
    for tile in range(tiles):
        diag, near, far, up, down, below, above = weights[tile]
        mid = here[tile]
        beyond = jnp.where(first_half, turned[tile - 1], turned[(tile + 1) % tiles])
        out.append(
            (diag * mid + near * turned[tile])
            + (far * beyond + up * rot(mid, -1))
            + (down * rot(mid, 1) + below * low[tile])
            + above * high[tile]
        )
    return out


def plane_of(ref, at, tiles):
    return [ref[at * tiles + tile] for tile in range(tiles)]


def put(ref, at, values):
    for tile, value in enumerate(values):
        ref[at * len(values) + tile] = value


def inner_kernel(planes, tiles, u_ref, t_ref, u2_ref, edge_ref, u0, hv, u1, held):
    stride = planes * tiles
    masks = lane_masks()

    def load(x, _):
        base = (x // ROWS) * tiles * ROWS + x % ROWS
        for tile in range(tiles):
            rows = pl.ds(base + tile * ROWS, ROWS, stride=stride)
            u0[x * tiles + tile] = u_ref[rows, :]
            hv[x * tiles + tile] = HALF_DT * jnp.exp(t_ref[rows, :])
        return 0

    lax.fori_loop(0, planes, load, 0)

    def first_step(x, _):
        weights = coefficients(masks, *[plane_of(hv, x + d, tiles) for d in (-1, 0, 1)])
        for tile in range(tiles):
            for kind in range(5):
                held[kind, x * tiles + tile] = weights[tile][kind]
        put(u1, x, step(masks, weights, *[plane_of(u0, x + d, tiles) for d in (-1, 0, 1)]))
        return 0

    lax.fori_loop(1, planes - 1, first_step, 0)

    def second_step(x, _):
        weights = []
        for tile in range(tiles):
            at = x * tiles + tile
            here = hv[at]
            weights.append([held[kind, at] for kind in range(5)] + [here + hv[at - tiles], here + hv[at + tiles]])
        put(u2_ref, x, step(masks, weights, *[plane_of(u1, x + d, tiles) for d in (-1, 0, 1)]))
        return 0

    lax.fori_loop(2, planes - 2, second_step, 0)
    last = planes - 1
    at = 0
    for ref, kept in ((u0, (0, 1, last - 1, last)), (hv, (0, 1, 2, last - 2, last - 1, last)),
                      (u1, (1, 2, last - 2, last - 1))):
        for x in kept:
            put(edge_ref, at, plane_of(ref, x, tiles))
            at += 1


def outer_kernel(planes, tiles, probe_hbm, before_ref, after_ref, edge_ref, inner_ref, before_2_hbm, after_2_hbm,
                 u2_ref, sent_ref, probe_ref, sem):
    probe_copy = pltpu.make_async_copy(probe_hbm, probe_ref, sem)
    probe_copy.start()
    masks = lane_masks()
    blocks = sent_ref.shape[2] // LANES
    mark = 4 * tiles + blocks + 2 * blocks // ROWS
    mark_row = 2 * blocks % ROWS
    edge = [plane_of(edge_ref, at, tiles) for at in range(14)]
    last = planes - 1
    for ref, own_u, own_v, own_1, where in (
        (before_ref, edge[0:2], edge[4:7], edge[10:12], (0, 1)),
        (after_ref, edge[3:1:-1], edge[9:6:-1], edge[13:11:-1], (last, last - 1)),
    ):
        order = (0, 1) if ref is before_ref else (1, 0)
        u = [plane_of(ref, d, tiles) for d in order] + own_u
        v = [[HALF_DT * jnp.exp(t) for t in plane_of(ref, 2 + d, tiles)] for d in order] + own_v
        live = ref[mark, mark_row : mark_row + 1, :]
        weights = [coefficients(masks, v[d], v[d + 1], v[d + 2]) for d in range(3)]
        next_u = [step(masks, weights[d], u[d], u[d + 1], u[d + 2]) for d in range(2)]
        next_u[0] = [value * live for value in next_u[0]]
        next_u = next_u + own_1
        for d in range(2):
            put(u2_ref, where[d], step(masks, weights[d + 1], next_u[d], next_u[d + 1], next_u[d + 2]))

    probe_copy.wait()
    lane = lax.broadcasted_iota(jnp.int32, (ROWS, LANES), 1)
    for part in range(blocks):
        found = jnp.zeros((ROWS, LANES), jnp.float32)
        for p in range(LANES):
            cell = probe_ref[part * LANES + p]
            turned = pltpu.roll(u2_ref[cell >> 7], (p - cell) & (LANES - 1), 1)
            found = jnp.where(lane == p, turned, found)

        def send(device, _):
            sent_ref[device, :, part * LANES : (part + 1) * LANES] = found
            return 0

        lax.fori_loop(0, sent_ref.shape[0], send, 0)


def halves(value):
    high = value.astype(jnp.bfloat16)
    return high, (value - high.astype(jnp.float32)).astype(jnp.bfloat16)


def between_kernel(planes, tiles, u2_ref, theta_hbm, out_ref, split_ref, theta_ref, sem):
    copy = pltpu.make_async_copy(theta_hbm, theta_ref, sem)
    copy.start()
    stride = planes * tiles
    members = theta_ref.shape[0] * ROWS

    def store(x, _):
        base = (x // ROWS) * tiles * ROWS + x % ROWS
        for tile in range(tiles):
            out_ref[pl.ds(base + tile * ROWS, ROWS, stride=stride), :] = u2_ref[x * tiles + tile]
        return 0

    lax.fori_loop(0, planes, store, 0)
    copy.wait()

    def split(slot, _):
        high, low = halves(theta_ref[:, slot].reshape(members, LANES))
        split_ref[slot, :members, :] = high
        split_ref[slot, members:, :] = low
        return 0

    lax.fori_loop(0, split_ref.shape[0], split, 0)


def dot_lanes(left, right):
    return lax.dot_general(left, right, (((1,), (1,)), ((), ())), precision=lax.Precision.HIGHEST,
                           preferred_element_type=jnp.float32)


def dot_rows(left, right):
    return lax.dot_general(left, right, (((1,), (0,)), ((), ())), precision=lax.Precision.HIGHEST,
                           preferred_element_type=jnp.float32)


def update_kernel(slabs, groups, planes, tiles, place_ref, count_ref, cells_hbm, probes_hbm, level_hbm,
                  pred_ref, obs_refs, split_ref, t_ref, post_ref, gain_ref,
                  reach, cells_ref, probes_ref, level_ref, sems):
    members = groups * ROWS
    share = 1.0 / (members - 1)
    copies = [
        pltpu.make_async_copy(source, target, sems.at[at])
        for at, (source, target) in enumerate((
            (cells_hbm, cells_ref), (probes_hbm, probes_ref), (level_hbm, level_ref)))
    ]
    for copy in copies:
        copy.start()
    slab, group = place_ref[0], place_ref[1]
    blocks = gain_ref.shape[1] // LANES
    window = 3 * blocks
    post_ref[...] = t_ref[...]

    def wide(row):
        return row[:, :members] if members <= LANES else jnp.concatenate([row] * (members // LANES), axis=1)

    anomaly, scaled, variance, matches = [], [], [], []
    for d in range(5):
        wanted = slab + d - 2
        at = jnp.clip(wanted, 0, slabs - 1)
        live = jnp.where((wanted >= 0) & (wanted < slabs), 1.0, 0.0)
        predicted = pred_ref[pl.ds(at * groups, groups)].reshape(members, blocks * LANES)
        mean = jnp.sum(predicted, axis=0, keepdims=True) / members
        anomaly.append((predicted - mean) * live)
        mine = pred_ref[at * groups + group]
        ref, first = obs_refs[d]
        for b in range(blocks):
            cut = slice(b * LANES, (b + 1) * LANES)
            observed = ref[first + blocks, b : b + 1, :]
            variance.append(ref[first + blocks, blocks + b : blocks + b + 1, :] + (1.0 - live))
            scaled.append((observed + ref[first + b] - mine[:, cut]) / variance[-1] * live)
            matches.append(dot_lanes(scaled[-1], anomaly[d][:, cut]))
    for d in range(1, 4):
        ref, first = obs_refs[d]
        for i in range(blocks):
            cut = slice(i * LANES, (i + 1) * LANES)
            total = jnp.zeros((ROWS, members), jnp.float32)
            for j in range(window):
                at = 2 * blocks + 1 + i * window + j
                level = ref[first + blocks + at // ROWS, at % ROWS : at % ROWS + 1, :] / 256.0 * share
                total = total + wide(level) * matches[(d - 1) * blocks + j]
            correction = dot_rows(total, anomaly[d][:, cut])
            gain = scaled[d * blocks + i] - correction / variance[d * blocks + i]
            if d == 2:
                gain_ref[:, cut] = gain
            high, low = halves(dot_lanes(gain, anomaly[d][:, cut]))
            both = jnp.concatenate([high.astype(jnp.float32), low.astype(jnp.float32)], axis=0)
            reach[(d - 1) * blocks + i] = jnp.concatenate([both, both], axis=1).astype(jnp.bfloat16)
    for copy in copies:
        copy.wait()
    for slot in range(split_ref.shape[0]):
        weight = jnp.where(slot < count_ref[0], level_ref[0, slot].astype(jnp.float32) / 256.0, 0.0) * share
        both = lax.dot_general(reach[probes_ref[0, slot]], split_ref[slot],
                               (((1,), (0,)), ((), ())), preferred_element_type=jnp.float32)
        change = (both[:ROWS] + both[ROWS:]) * weight
        block = cells_ref[0, slot]
        rows = pl.ds(row_of(block // tiles, block % tiles, tiles), ROWS, stride=planes * tiles)
        post_ref[rows, :] = post_ref[rows, :] + change


def shards(
    starting_speed_field,
    sample_fluidity_exponent,
    observed,
    obs_noise,
    obs_var,
    probe_cells,
    pair_cells,
    pair_probes,
    pair_taper,
    pair_counts,
    probe_taper,
):
    shape = starting_speed_field.shape
    members, planes, cells = shape
    tiles = cells // LANES
    slots = pair_cells.shape[1]
    probes = obs_noise.shape[1]
    blocks = probes // LANES
    slabs, groups = lax.axis_size("space"), lax.axis_size("ens")
    f32, i32 = jnp.float32, jnp.int32
    u_rows = to_rows(starting_speed_field)
    t_rows = to_rows(sample_fluidity_exponent)
    obs_tiles = blocks - (-(2 * blocks + 1 + probe_taper.shape[1] * probe_taper.shape[2]) // ROWS)
    edge = jax.ShapeDtypeStruct((4 * tiles + obs_tiles, ROWS, LANES), f32)
    obs_shape = jax.ShapeDtypeStruct((obs_tiles, ROWS, LANES), f32)
    params = pltpu.CompilerParams(vmem_limit_bytes=32 * 1024 * 1024)
    stack = pltpu.VMEM((planes * tiles, ROWS, LANES), f32)
    low, high, obs, picked, u_near, t_near = pl.pallas_call(
        functools.partial(pack_kernel, planes, tiles),
        out_shape=(
            edge,
            edge,
            obs_shape,
            jax.ShapeDtypeStruct((groups, slots, ROWS, LANES), f32),
            jax.ShapeDtypeStruct(u_rows.shape, f32),
            jax.ShapeDtypeStruct(u_rows.shape, f32),
        ),
        in_specs=[HBM] * 7,
        out_specs=(VMEM, VMEM, VMEM, HBM, VMEM, VMEM),
        scratch_shapes=[
            pltpu.SMEM(pair_cells.shape, i32),
            pltpu.SMEM(probe_taper.shape, i32),
            pltpu.VMEM((ROWS, probes), f32),
            pltpu.VMEM((2, probes), f32),
            pltpu.VMEM((slots, ROWS, LANES), f32),
            pltpu.SemaphoreType.DMA((7 + groups,)),
        ],
        compiler_params=params,
        name="pack",
    )(*map(stay, (pair_cells, probe_taper, u_rows, t_rows, obs_noise, observed.reshape(1, -1), obs_var.reshape(1, -1))))
    upward = [(i, i + 1) for i in range(slabs - 1)]
    before = lax.ppermute(high, "space", upward)
    after = lax.ppermute(low, "space", [(j, i) for i, j in upward])
    if slabs == 4:
        before_2 = after_2 = lax.ppermute(obs, "space", [(i, (i + 2) % 4) for i in range(4)])
    else:
        upward_2 = [(i, i + 2) for i in range(slabs - 2)]
        before_2 = lax.ppermute(obs, "space", upward_2)
        after_2 = lax.ppermute(obs, "space", [(j, i) for i, j in upward_2])
    theta_all = lax.all_to_all(picked, "ens", 0, 0)
    inner, edges = pl.pallas_call(
        functools.partial(inner_kernel, planes, tiles),
        out_shape=(
            jax.ShapeDtypeStruct((planes * tiles, ROWS, LANES), f32),
            jax.ShapeDtypeStruct((14 * tiles, ROWS, LANES), f32),
        ),
        in_specs=[VMEM] * 2,
        out_specs=(VMEM,) * 2,
        scratch_shapes=[stack, stack, stack, pltpu.VMEM((5, planes * tiles, ROWS, LANES), f32)],
        compiler_params=params,
        cost_estimate=pl.CostEstimate(flops=20_000_000, bytes_accessed=20_000_000, transcendentals=0),
        name="inner_planes",
    )(u_near, t_near)
    u2, sent = pl.pallas_call(
        functools.partial(outer_kernel, planes, tiles),
        out_shape=(
            jax.ShapeDtypeStruct((planes * tiles, ROWS, LANES), f32),
            jax.ShapeDtypeStruct((slabs * groups, members, probes), f32),
        ),
        in_specs=[HBM] + [VMEM] * 4 + [ANY] * 2,
        out_specs=(VMEM,) * 2,
        scratch_shapes=[pltpu.SMEM(probe_cells.shape, i32), pltpu.SemaphoreType.DMA(())],
        input_output_aliases={4: 0},
        compiler_params=params,
        name="outer_planes",
    )(stay(probe_cells), before, after, edges, inner, before_2, after_2)
    pred_all = lax.all_to_all(sent, ("space", "ens"), 0, 0)
    u2_rows, split = pl.pallas_call(
        functools.partial(between_kernel, planes, tiles),
        out_shape=(
            jax.ShapeDtypeStruct(u_rows.shape, f32),
            jax.ShapeDtypeStruct((slots, 2 * groups * ROWS, LANES), jnp.bfloat16),
        ),
        in_specs=[VMEM, HBM],
        out_specs=(VMEM,) * 2,
        scratch_shapes=[pltpu.VMEM(theta_all.shape, f32), pltpu.SemaphoreType.DMA(())],
        compiler_params=params,
        cost_estimate=pl.CostEstimate(flops=1_000_000, bytes_accessed=8_000_000, transcendentals=0),
        name="between",
    )(u2, stay(theta_all))
    place = jnp.stack([lax.axis_index("space"), lax.axis_index("ens")]).astype(i32)

    def update(place_ref, count_ref, cells_ref, probes_ref, level_ref, pred_ref, before_2_ref, before_ref, obs_ref,
               after_ref, after_2_ref, *rest):
        seen = ((before_2_ref, 0), (before_ref, 4 * tiles), (obs_ref, 0), (after_ref, 4 * tiles), (after_2_ref, 0))
        update_kernel(slabs, groups, planes, tiles, place_ref, count_ref, cells_ref, probes_ref, level_ref,
                      pred_ref, seen, *rest)

    post_rows, gain = pl.pallas_call(
        update,
        out_shape=(
            jax.ShapeDtypeStruct(u_rows.shape, f32),
            jax.ShapeDtypeStruct((members, probes), f32),
        ),
        in_specs=[SMEM] * 2 + [HBM] * 3 + [VMEM] * 8,
        out_specs=(VMEM,) * 2,
        scratch_shapes=[
            pltpu.VMEM((probe_taper.shape[2], 2 * ROWS, 2 * groups * ROWS), jnp.bfloat16),
            pltpu.SMEM(pair_cells.shape, i32),
            pltpu.SMEM(pair_cells.shape, i32),
            pltpu.SMEM(pair_cells.shape, i32),
            pltpu.SemaphoreType.DMA((3,)),
        ],
        compiler_params=params,
        name="update",
    )(place, pair_counts, *map(stay, (pair_cells, pair_probes, pair_taper)), pred_all, before_2, before, obs, after,
      after_2, split, t_near)
    return (from_rows(u2_rows, shape), from_rows(post_rows, shape), gain)


def solution(mesh):
    return jax.shard_map(
        shards,
        mesh=mesh,
        in_specs=(
            P("ens", "space", None),
            P("ens", "space", None),
            P("space"),
            P("ens", "space"),
            P("space"),
            P("space"),
            P("space", None),
            P("space", None),
            P("space", None),
            P("space"),
            P("space", None, None),
        ),
        out_specs=(P("ens", "space", None), P("ens", "space", None), P("ens", "space")),
        check_vma=False,
    )
```

```python
import functools

import jax
import jax.numpy as jnp
from jax import lax
from jax.experimental import pallas as pl
from jax.experimental.pallas import tpu as pltpu
from jax.sharding import PartitionSpec as P

LANES = 128
ROWS = 8
NZ = 64
HALF_DT = 0.5 * 0.08

VMEM = pl.BlockSpec(memory_space=pltpu.VMEM)
SMEM = pl.BlockSpec(memory_space=pltpu.SMEM)
HBM = pl.BlockSpec(memory_space=pltpu.HBM)
ANY = pl.BlockSpec(memory_space=pl.ANY)


def stay(array):
    return pltpu.with_memory_space_constraint(array, pltpu.HBM)


def to_rows(array):
    members, planes, cells = array.shape
    split = array.reshape(members, planes // ROWS, ROWS, cells // LANES, LANES)
    return split.transpose(0, 1, 3, 2, 4).reshape(-1, LANES)


def from_rows(rows, shape):
    members, planes, cells = shape
    split = rows.reshape(members, planes // ROWS, cells // LANES, ROWS, LANES)
    return split.transpose(0, 1, 3, 2, 4).reshape(shape)


def row_of(plane, tile, tiles):
    return (plane // ROWS * tiles + tile) * ROWS + plane % ROWS


def pack_kernel(planes, tiles, taper_hbm, u_hbm, t_hbm, noise_hbm, observed_hbm, var_hbm,
                low_ref, high_ref, obs_ref, t_ref, taper_ref, u_ref, noise_ref, row_ref, sems):
    stride = planes * tiles
    blocks = noise_ref.shape[1] // LANES
    copies = [
        pltpu.make_async_copy(source, target, sems.at[at])
        for at, (source, target) in enumerate((
            (t_hbm, t_ref),
            (u_hbm, u_ref),
            (taper_hbm, taper_ref),
            (noise_hbm, noise_ref),
            (observed_hbm, row_ref.at[0:1]),
            (var_hbm, row_ref.at[1:2]),
        ))
    ]
    for copy in copies:
        copy.start()
    for kind, source in ((1, t_ref), (0, u_ref)):
        copies[1 - kind].wait()
        for out_ref, first in ((high_ref, planes - 2), (low_ref, 0)):
            for depth in range(2):
                for tile in range(tiles):
                    out_ref[(kind * 2 + depth) * tiles + tile] = source[
                        pl.ds(row_of(first + depth, tile, tiles), ROWS, stride=stride), :
                    ]
    for copy in copies[2:]:
        copy.wait()
    own, window = taper_ref.shape[1:]
    rows = [row_ref[kind : kind + 1, b * LANES : (b + 1) * LANES] for kind in range(2) for b in range(blocks)]
    rows.append(jnp.ones((1, LANES), jnp.float32))
    for i in range(own):
        for j in range(window):
            rows.append(jnp.full((1, LANES), taper_ref[0, i, j].astype(jnp.float32), jnp.float32))
    for ref, first in ((low_ref, 4 * tiles), (high_ref, 4 * tiles), (obs_ref, 0)):
        for b in range(blocks):
            ref[first + b] = noise_ref[:, b * LANES : (b + 1) * LANES]
        for at, row in enumerate(rows):
            ref[first + blocks + at // ROWS, at % ROWS : at % ROWS + 1, :] = row


def pick_kernel(planes, tiles, cells_hbm, t_ref, pick_hbm, done_ref, cells_ref, pick_ref, sems):
    copy = pltpu.make_async_copy(cells_hbm, cells_ref, sems.at[0])
    copy.start()
    done_ref[...] = jnp.zeros(done_ref.shape, jnp.float32)
    copy.wait()
    for slot in range(pick_ref.shape[0]):
        block = cells_ref[0, slot]
        row = row_of(block // tiles, block % tiles, tiles)
        pick_ref[slot] = t_ref[pl.ds(row, ROWS, stride=planes * tiles), :]
    copies = [
        pltpu.make_async_copy(pick_ref, pick_hbm.at[device], sems.at[1 + device])
        for device in range(pick_hbm.shape[0])
    ]
    for copy in copies:
        copy.start()
    for copy in copies:
        copy.wait()


def rot(value, by):
    return pltpu.roll(value, by % LANES, 1)


def lane_masks():
    lane = lax.broadcasted_iota(jnp.int32, (ROWS, LANES), 1)
    height = lane & (NZ - 1)
    return lane < NZ, height == 0, height == NZ - 1


def coefficients(masks, low, here, high):
    first_half, floor, roof = masks
    tiles = len(here)
    turned = [rot(value, NZ) for value in here]
    out = []
    for tile in range(tiles):
        mid = here[tile]
        near = mid + turned[tile]
        far = mid + jnp.where(first_half, turned[tile - 1], turned[(tile + 1) % tiles])
        up = mid + jnp.where(roof, HALF_DT, rot(mid, -1))
        down = mid + jnp.where(floor, HALF_DT, rot(mid, 1))
        below = mid + low[tile]
        above = mid + high[tile]
        diag = 1.0 - ((near + far) + (up + down) + (below + above))
        out.append((diag, near, far, jnp.where(roof, 0.0, up), jnp.where(floor, 0.0, down), below, above))
    return out


def step(masks, weights, low, here, high):
    first_half = masks[0]
    tiles = len(here)
    turned = [rot(value, NZ) for value in here]
    out = []
    for tile in range(tiles):
        diag, near, far, up, down, below, above = weights[tile]
        mid = here[tile]
        beyond = jnp.where(first_half, turned[tile - 1], turned[(tile + 1) % tiles])
        out.append(
            (diag * mid + near * turned[tile])
            + (far * beyond + up * rot(mid, -1))
            + (down * rot(mid, 1) + below * low[tile])
            + above * high[tile]
        )
    return out


def plane_of(ref, at, tiles):
    return [ref[at * tiles + tile] for tile in range(tiles)]


def put(ref, at, values):
    for tile, value in enumerate(values):
        ref[at * len(values) + tile] = value


def each(first, last, unroll, body):
    count = (last - first) // unroll

    def several(at, _):
        for d in range(unroll):
            body(first + at * unroll + d)
        return 0

    lax.fori_loop(0, count, several, 0)
    for x in range(first + count * unroll, last):
        body(x)


def inner_kernel(planes, tiles, u_hbm, t_ref, after_pick, u2_ref, edge_ref, u_ref, u0, hv, u1, held, sem):
    stride = planes * tiles
    masks = lane_masks()
    copy = pltpu.make_async_copy(u_hbm, u_ref, sem)
    copy.start()

    def rows_at(x, tile):
        return pl.ds((x // ROWS) * tiles * ROWS + x % ROWS + tile * ROWS, ROWS, stride=stride)

    def load_t(x):
        for tile in range(tiles):
            hv[x * tiles + tile] = HALF_DT * jnp.exp(t_ref[rows_at(x, tile), :])

    def load_u(x):
        for tile in range(tiles):
            u0[x * tiles + tile] = u_ref[rows_at(x, tile), :]

    def first_step(x):
        weights = coefficients(masks, *[plane_of(hv, x + d, tiles) for d in (-1, 0, 1)])
        for tile in range(tiles):
            for kind in range(5):
                held[kind, x * tiles + tile] = weights[tile][kind]
        put(u1, x, step(masks, weights, *[plane_of(u0, x + d, tiles) for d in (-1, 0, 1)]))

    def second_step(x):
        weights = []
        for tile in range(tiles):
            at = x * tiles + tile
            here = hv[at]
            weights.append([held[kind, at] for kind in range(5)] + [here + hv[at - tiles], here + hv[at + tiles]])
        put(u2_ref, x, step(masks, weights, *[plane_of(u1, x + d, tiles) for d in (-1, 0, 1)]))

    each(0, planes, 4, load_t)
    copy.wait()
    each(0, planes, 4, load_u)
    each(1, planes - 1, 7, first_step)
    each(2, planes - 2, 6, second_step)
    last = planes - 1
    at = 0
    for ref, kept in ((u0, (0, 1, last - 1, last)), (hv, (0, 1, 2, last - 2, last - 1, last)),
                      (u1, (1, 2, last - 2, last - 1))):
        for x in kept:
            put(edge_ref, at, plane_of(ref, x, tiles))
            at += 1


def outer_kernel(planes, tiles, probe_hbm, before_ref, after_ref, edge_ref, inner_ref, before_2_hbm, after_2_hbm,
                 u2_ref, sent_ref, probe_ref, sem):
    probe_copy = pltpu.make_async_copy(probe_hbm, probe_ref, sem)
    probe_copy.start()
    masks = lane_masks()
    blocks = sent_ref.shape[2] // LANES
    mark = 4 * tiles + blocks + 2 * blocks // ROWS
    mark_row = 2 * blocks % ROWS
    edge = [plane_of(edge_ref, at, tiles) for at in range(14)]
    last = planes - 1
    for ref, own_u, own_v, own_1, where in (
        (before_ref, edge[0:2], edge[4:7], edge[10:12], (0, 1)),
        (after_ref, edge[3:1:-1], edge[9:6:-1], edge[13:11:-1], (last, last - 1)),
    ):
        order = (0, 1) if ref is before_ref else (1, 0)
        u = [plane_of(ref, d, tiles) for d in order] + own_u
        v = [[HALF_DT * jnp.exp(t) for t in plane_of(ref, 2 + d, tiles)] for d in order] + own_v
        live = ref[mark, mark_row : mark_row + 1, :]
        weights = [coefficients(masks, v[d], v[d + 1], v[d + 2]) for d in range(3)]
        next_u = [step(masks, weights[d], u[d], u[d + 1], u[d + 2]) for d in range(2)]
        next_u[0] = [value * live for value in next_u[0]]
        next_u = next_u + own_1
        for d in range(2):
            put(u2_ref, where[d], step(masks, weights[d + 1], next_u[d], next_u[d + 1], next_u[d + 2]))

    probe_copy.wait()
    lane = lax.broadcasted_iota(jnp.int32, (ROWS, LANES), 1)
    for part in range(blocks):
        found = jnp.zeros((ROWS, LANES), jnp.float32)
        for p in range(LANES):
            cell = probe_ref[part * LANES + p]
            turned = pltpu.roll(u2_ref[cell >> 7], (p - cell) & (LANES - 1), 1)
            found = jnp.where(lane == p, turned, found)

        def send(device, _):
            sent_ref[device, :, part * LANES : (part + 1) * LANES] = found
            return 0

        lax.fori_loop(0, sent_ref.shape[0], send, 0)


def halves(value):
    high = value.astype(jnp.bfloat16)
    return high, (value - high.astype(jnp.float32)).astype(jnp.bfloat16)


def between_kernel(planes, tiles, u2_ref, theta_hbm, out_ref, split_ref, theta_ref, sem):
    copy = pltpu.make_async_copy(theta_hbm, theta_ref, sem)
    copy.start()
    stride = planes * tiles
    members = theta_ref.shape[0] * ROWS

    def store(x, _):
        base = (x // ROWS) * tiles * ROWS + x % ROWS
        for tile in range(tiles):
            out_ref[pl.ds(base + tile * ROWS, ROWS, stride=stride), :] = u2_ref[x * tiles + tile]
        return 0

    lax.fori_loop(0, planes, store, 0)
    copy.wait()

    def split(slot, _):
        high, low = halves(theta_ref[:, slot].reshape(members, LANES))
        split_ref[slot, :members, :] = high
        split_ref[slot, members:, :] = low
        return 0

    lax.fori_loop(0, split_ref.shape[0], split, 0)


def dot_lanes(left, right):
    return lax.dot_general(left, right, (((1,), (1,)), ((), ())), precision=lax.Precision.HIGHEST,
                           preferred_element_type=jnp.float32)


def dot_rows(left, right):
    return lax.dot_general(left, right, (((1,), (0,)), ((), ())), precision=lax.Precision.HIGHEST,
                           preferred_element_type=jnp.float32)


def update_kernel(slabs, groups, planes, tiles, place_ref, count_ref, cells_hbm, probes_hbm, level_hbm,
                  pred_ref, obs_refs, split_hbm, t_hbm, post_ref, gain_ref,
                  reach, cells_ref, probes_ref, level_ref, split_ref, sems):
    members = groups * ROWS
    share = 1.0 / (members - 1)
    copies = [
        pltpu.make_async_copy(source, target, sems.at[at])
        for at, (source, target) in enumerate((
            (cells_hbm, cells_ref), (probes_hbm, probes_ref), (level_hbm, level_ref),
            (split_hbm, split_ref), (t_hbm, post_ref)))
    ]
    for copy in copies:
        copy.start()
    slab, group = place_ref[0], place_ref[1]
    blocks = gain_ref.shape[1] // LANES
    window = 3 * blocks

    def wide(row):
        return row[:, :members] if members <= LANES else jnp.concatenate([row] * (members // LANES), axis=1)

    anomaly, scaled, variance, matches = [], [], [], []
    for d in range(5):
        wanted = slab + d - 2
        at = jnp.clip(wanted, 0, slabs - 1)
        live = jnp.where((wanted >= 0) & (wanted < slabs), 1.0, 0.0)
        predicted = pred_ref[pl.ds(at * groups, groups)].reshape(members, blocks * LANES)
        mean = jnp.sum(predicted, axis=0, keepdims=True) / members
        anomaly.append((predicted - mean) * live)
        mine = pred_ref[at * groups + group]
        ref, first = obs_refs[d]
        for b in range(blocks):
            cut = slice(b * LANES, (b + 1) * LANES)
            observed = ref[first + blocks, b : b + 1, :]
            variance.append(ref[first + blocks, blocks + b : blocks + b + 1, :] + (1.0 - live))
            scaled.append((observed + ref[first + b] - mine[:, cut]) / variance[-1] * live)
            matches.append(dot_lanes(scaled[-1], anomaly[d][:, cut]))
    for d in range(1, 4):
        ref, first = obs_refs[d]
        for i in range(blocks):
            cut = slice(i * LANES, (i + 1) * LANES)
            total = jnp.zeros((ROWS, members), jnp.float32)
            for j in range(window):
                at = 2 * blocks + 1 + i * window + j
                level = ref[first + blocks + at // ROWS, at % ROWS : at % ROWS + 1, :] / 256.0 * share
                total = total + wide(level) * matches[(d - 1) * blocks + j]
            correction = dot_rows(total, anomaly[d][:, cut])
            gain = scaled[d * blocks + i] - correction / variance[d * blocks + i]
            if d == 2:
                gain_ref[:, cut] = gain
            high, low = halves(dot_lanes(gain, anomaly[d][:, cut]))
            both = jnp.concatenate([high.astype(jnp.float32), low.astype(jnp.float32)], axis=0)
            reach[(d - 1) * blocks + i] = jnp.concatenate([both, both], axis=1).astype(jnp.bfloat16)
    for copy in copies:
        copy.wait()
    for slot in range(split_ref.shape[0]):
        weight = jnp.where(slot < count_ref[0], level_ref[0, slot].astype(jnp.float32) / 256.0, 0.0) * share
        both = lax.dot_general(reach[probes_ref[0, slot]], split_ref[slot],
                               (((1,), (0,)), ((), ())), preferred_element_type=jnp.float32)
        change = (both[:ROWS] + both[ROWS:]) * weight
        block = cells_ref[0, slot]
        rows = pl.ds(row_of(block // tiles, block % tiles, tiles), ROWS, stride=planes * tiles)
        post_ref[rows, :] = post_ref[rows, :] + change


def shards(
    starting_speed_field,
    sample_fluidity_exponent,
    observed,
    obs_noise,
    obs_var,
    probe_cells,
    pair_cells,
    pair_probes,
    pair_taper,
    pair_counts,
    probe_taper,
):
    shape = starting_speed_field.shape
    members, planes, cells = shape
    tiles = cells // LANES
    slots = pair_cells.shape[1]
    probes = obs_noise.shape[1]
    blocks = probes // LANES
    slabs, groups = lax.axis_size("space"), lax.axis_size("ens")
    f32, i32 = jnp.float32, jnp.int32
    u_rows = to_rows(starting_speed_field)
    t_rows = to_rows(sample_fluidity_exponent)
    obs_tiles = blocks - (-(2 * blocks + 1 + probe_taper.shape[1] * probe_taper.shape[2]) // ROWS)
    edge = jax.ShapeDtypeStruct((4 * tiles + obs_tiles, ROWS, LANES), f32)
    obs_shape = jax.ShapeDtypeStruct((obs_tiles, ROWS, LANES), f32)
    params = pltpu.CompilerParams(vmem_limit_bytes=32 * 1024 * 1024)
    stack = pltpu.VMEM((planes * tiles, ROWS, LANES), f32)
    low, high, obs, t_near = pl.pallas_call(
        functools.partial(pack_kernel, planes, tiles),
        out_shape=(edge, edge, obs_shape, jax.ShapeDtypeStruct(u_rows.shape, f32)),
        in_specs=[HBM] * 6,
        out_specs=(VMEM,) * 4,
        scratch_shapes=[
            pltpu.SMEM(probe_taper.shape, i32),
            pltpu.VMEM(u_rows.shape, f32),
            pltpu.VMEM((ROWS, probes), f32),
            pltpu.VMEM((2, probes), f32),
            pltpu.SemaphoreType.DMA((6,)),
        ],
        compiler_params=params,
        name="pack",
    )(*map(stay, (probe_taper, u_rows, t_rows, obs_noise, observed.reshape(1, -1), obs_var.reshape(1, -1))))
    upward = [(i, i + 1) for i in range(slabs - 1)]
    before = lax.ppermute(high, "space", upward)
    after = lax.ppermute(low, "space", [(j, i) for i, j in upward])
    if slabs == 4:
        before_2 = after_2 = lax.ppermute(obs, "space", [(i, (i + 2) % 4) for i in range(4)])
    else:
        upward_2 = [(i, i + 2) for i in range(slabs - 2)]
        before_2 = lax.ppermute(obs, "space", upward_2)
        after_2 = lax.ppermute(obs, "space", [(j, i) for i, j in upward_2])
    picked, after_pick = pl.pallas_call(
        functools.partial(pick_kernel, planes, tiles),
        out_shape=(
            pltpu.HBM((groups, slots, ROWS, LANES), f32),
            jax.ShapeDtypeStruct((ROWS, LANES), f32),
        ),
        in_specs=[HBM, VMEM],
        out_specs=(HBM, VMEM),
        scratch_shapes=[
            pltpu.SMEM(pair_cells.shape, i32),
            pltpu.VMEM((slots, ROWS, LANES), f32),
            pltpu.SemaphoreType.DMA((1 + groups,)),
        ],
        compiler_params=params,
        name="pick",
    )(stay(pair_cells), t_near)
    theta_all = lax.all_to_all(picked, "ens", 0, 0)
    inner, edges = pl.pallas_call(
        functools.partial(inner_kernel, planes, tiles),
        out_shape=(
            jax.ShapeDtypeStruct((planes * tiles, ROWS, LANES), f32),
            jax.ShapeDtypeStruct((14 * tiles, ROWS, LANES), f32),
        ),
        in_specs=[HBM, VMEM, VMEM],
        out_specs=(VMEM,) * 2,
        scratch_shapes=[
            pltpu.VMEM(u_rows.shape, f32),
            stack,
            stack,
            stack,
            pltpu.VMEM((5, planes * tiles, ROWS, LANES), f32),
            pltpu.SemaphoreType.DMA(()),
        ],
        compiler_params=params,
        cost_estimate=pl.CostEstimate(flops=20_000_000, bytes_accessed=20_000_000, transcendentals=0),
        name="inner_planes",
    )(stay(u_rows), t_near, after_pick)
    u2, sent = pl.pallas_call(
        functools.partial(outer_kernel, planes, tiles),
        out_shape=(
            jax.ShapeDtypeStruct((planes * tiles, ROWS, LANES), f32),
            jax.ShapeDtypeStruct((slabs * groups, members, probes), f32),
        ),
        in_specs=[HBM] + [VMEM] * 4 + [ANY] * 2,
        out_specs=(VMEM,) * 2,
        scratch_shapes=[pltpu.SMEM(probe_cells.shape, i32), pltpu.SemaphoreType.DMA(())],
        input_output_aliases={4: 0},
        compiler_params=params,
        name="outer_planes",
    )(stay(probe_cells), before, after, edges, inner, before_2, after_2)
    pred_all = lax.all_to_all(sent, ("space", "ens"), 0, 0)
    u2_rows, split = pl.pallas_call(
        functools.partial(between_kernel, planes, tiles),
        out_shape=(
            jax.ShapeDtypeStruct(u_rows.shape, f32),
            pltpu.HBM((slots, 2 * groups * ROWS, LANES), jnp.bfloat16),
        ),
        in_specs=[VMEM, HBM],
        out_specs=(VMEM,) * 2,
        scratch_shapes=[pltpu.VMEM(theta_all.shape, f32), pltpu.SemaphoreType.DMA(())],
        compiler_params=params,
        cost_estimate=pl.CostEstimate(flops=1_000_000, bytes_accessed=8_000_000, transcendentals=0),
        name="between",
    )(u2, stay(theta_all))
    place = jnp.stack([lax.axis_index("space"), lax.axis_index("ens")]).astype(i32)

    def update(place_ref, count_ref, cells_ref, probes_ref, level_ref, pred_ref, before_2_ref, before_ref, obs_ref,
               after_ref, after_2_ref, *rest):
        seen = ((before_2_ref, 0), (before_ref, 4 * tiles), (obs_ref, 0), (after_ref, 4 * tiles), (after_2_ref, 0))
        update_kernel(slabs, groups, planes, tiles, place_ref, count_ref, cells_ref, probes_ref, level_ref,
                      pred_ref, seen, *rest)

    post_rows, gain = pl.pallas_call(
        update,
        out_shape=(
            jax.ShapeDtypeStruct(u_rows.shape, f32),
            jax.ShapeDtypeStruct((members, probes), f32),
        ),
        in_specs=[SMEM] * 2 + [HBM] * 3 + [VMEM] * 6 + [HBM] * 2,
        out_specs=(VMEM,) * 2,
        scratch_shapes=[
            pltpu.VMEM((probe_taper.shape[2], 2 * ROWS, 2 * groups * ROWS), jnp.bfloat16),
            pltpu.SMEM(pair_cells.shape, i32),
            pltpu.SMEM(pair_cells.shape, i32),
            pltpu.SMEM(pair_cells.shape, i32),
            pltpu.VMEM(split.shape, jnp.bfloat16),
            pltpu.SemaphoreType.DMA((5,)),
        ],
        compiler_params=params,
        name="update",
    )(place, pair_counts, *map(stay, (pair_cells, pair_probes, pair_taper)), pred_all, before_2, before, obs, after,
      after_2, stay(split), stay(t_rows))
    return (from_rows(u2_rows, shape), from_rows(post_rows, shape), gain)


def solution(mesh):
    return jax.shard_map(
        shards,
        mesh=mesh,
        in_specs=(
            P("ens", "space", None),
            P("ens", "space", None),
            P("space"),
            P("ens", "space"),
            P("space"),
            P("space"),
            P("space", None),
            P("space", None),
            P("space", None),
            P("space"),
            P("space", None, None),
        ),
        out_specs=(P("ens", "space", None), P("ens", "space", None), P("ens", "space")),
        check_vma=False,
    )
```

```python
import functools

import jax
import jax.numpy as jnp
from jax import lax
from jax.experimental import pallas as pl
from jax.experimental.pallas import tpu as pltpu
from jax.sharding import PartitionSpec as P

LANES = 128
ROWS = 8
NZ = 64
HALF_DT = 0.5 * 0.08

VMEM = pl.BlockSpec(memory_space=pltpu.VMEM)
SMEM = pl.BlockSpec(memory_space=pltpu.SMEM)
HBM = pl.BlockSpec(memory_space=pltpu.HBM)


def stay(array):
    return pltpu.with_memory_space_constraint(array, pltpu.HBM)


def to_rows(array):
    members, planes, cells = array.shape
    split = array.reshape(members, planes // ROWS, ROWS, cells // LANES, LANES)
    return split.transpose(0, 1, 3, 2, 4).reshape(-1, LANES)


def from_rows(rows, shape):
    members, planes, cells = shape
    split = rows.reshape(members, planes // ROWS, cells // LANES, ROWS, LANES)
    return split.transpose(0, 1, 3, 2, 4).reshape(shape)


def row_of(plane, tile, tiles):
    return (plane // ROWS * tiles + tile) * ROWS + plane % ROWS


def pack_kernel(planes, tiles, cells_hbm, taper_hbm, u_hbm, t_hbm, noise_hbm, observed_hbm, var_hbm,
                low_ref, high_ref, obs_ref, t_ref, pick_hbm,
                cells_ref, taper_ref, u_ref, noise_ref, row_ref, pick_ref, sems):
    stride = planes * tiles
    blocks = noise_ref.shape[1] // LANES
    copies = [
        pltpu.make_async_copy(source, target, sems.at[at])
        for at, (source, target) in enumerate((
            (cells_hbm, cells_ref),
            (t_hbm, t_ref),
            (u_hbm, u_ref),
            (taper_hbm, taper_ref),
            (noise_hbm, noise_ref),
            (observed_hbm, row_ref.at[0:1]),
            (var_hbm, row_ref.at[1:2]),
        ))
    ]
    for copy in copies:
        copy.start()
    copies[0].wait()
    copies[1].wait()
    for slot in range(pick_ref.shape[0]):
        block = cells_ref[0, slot]
        row = row_of(block // tiles, block % tiles, tiles)
        pick_ref[slot] = t_ref[pl.ds(row, ROWS, stride=stride), :]
    picks = [
        pltpu.make_async_copy(pick_ref, pick_hbm.at[device], sems.at[len(copies) + device])
        for device in range(pick_hbm.shape[0])
    ]
    for copy in picks:
        copy.start()
    for kind, source in ((1, t_ref), (0, u_ref)):
        if kind == 0:
            copies[2].wait()
        for out_ref, first in ((high_ref, planes - 2), (low_ref, 0)):
            for depth in range(2):
                for tile in range(tiles):
                    out_ref[(kind * 2 + depth) * tiles + tile] = source[
                        pl.ds(row_of(first + depth, tile, tiles), ROWS, stride=stride), :
                    ]
    for ref in (low_ref, high_ref):
        ref[4 * tiles] = jnp.ones((ROWS, LANES), jnp.float32)
    for copy in copies[3:]:
        copy.wait()
    own, window = taper_ref.shape[1:]
    rows = [row_ref[kind : kind + 1, b * LANES : (b + 1) * LANES] for kind in range(2) for b in range(blocks)]
    for i in range(own):
        for j in range(window):
            rows.append(jnp.full((1, LANES), taper_ref[0, i, j].astype(jnp.float32), jnp.float32))
    for b in range(blocks):
        obs_ref[b] = noise_ref[:, b * LANES : (b + 1) * LANES]
    for at, row in enumerate(rows):
        obs_ref[blocks + at // ROWS, at % ROWS : at % ROWS + 1, :] = row
    for copy in picks:
        copy.wait()


def rot(value, by):
    return pltpu.roll(value, by % LANES, 1)


def lane_masks():
    lane = lax.broadcasted_iota(jnp.int32, (ROWS, LANES), 1)
    height = lane & (NZ - 1)
    return lane < NZ, height == 0, height == NZ - 1


def coefficients(masks, low, here, high):
    first_half, floor, roof = masks
    tiles = len(here)
    turned = [rot(value, NZ) for value in here]
    out = []
    for tile in range(tiles):
        mid = here[tile]
        near = mid + turned[tile]
        far = mid + jnp.where(first_half, turned[tile - 1], turned[(tile + 1) % tiles])
        up = mid + jnp.where(roof, HALF_DT, rot(mid, -1))
        down = mid + jnp.where(floor, HALF_DT, rot(mid, 1))
        below = mid + low[tile]
        above = mid + high[tile]
        diag = 1.0 - ((near + far) + (up + down) + (below + above))
        out.append((diag, near, far, jnp.where(roof, 0.0, up), jnp.where(floor, 0.0, down), below, above))
    return out


def step(masks, weights, low, here, high):
    first_half = masks[0]
    tiles = len(here)
    turned = [rot(value, NZ) for value in here]
    out = []
    for tile in range(tiles):
        diag, near, far, up, down, below, above = weights[tile]
        mid = here[tile]
        beyond = jnp.where(first_half, turned[tile - 1], turned[(tile + 1) % tiles])
        out.append(
            (diag * mid + near * turned[tile])
            + (far * beyond + up * rot(mid, -1))
            + (down * rot(mid, 1) + below * low[tile])
            + above * high[tile]
        )
    return out


def plane_of(ref, at, tiles):
    return [ref[at * tiles + tile] for tile in range(tiles)]


def put(ref, at, values):
    for tile, value in enumerate(values):
        ref[at * len(values) + tile] = value


def each(first, last, unroll, body):
    count = (last - first) // unroll

    def several(at, _):
        for d in range(unroll):
            body(first + at * unroll + d)
        return 0

    lax.fori_loop(0, count, several, 0)
    for x in range(first + count * unroll, last):
        body(x)


def inner_kernel(planes, tiles, u_hbm, t_ref, u2_ref, edge_ref, u_ref, u0, hv, u1, held, sem):
    stride = planes * tiles
    masks = lane_masks()
    copy = pltpu.make_async_copy(u_hbm, u_ref, sem)
    copy.start()

    def rows_at(x, tile):
        return pl.ds((x // ROWS) * tiles * ROWS + x % ROWS + tile * ROWS, ROWS, stride=stride)

    def load_t(x):
        for tile in range(tiles):
            hv[x * tiles + tile] = HALF_DT * jnp.exp(t_ref[rows_at(x, tile), :])

    def load_u(x):
        for tile in range(tiles):
            u0[x * tiles + tile] = u_ref[rows_at(x, tile), :]

    def first_step(x):
        weights = coefficients(masks, *[plane_of(hv, x + d, tiles) for d in (-1, 0, 1)])
        for tile in range(tiles):
            for kind in range(5):
                held[kind, x * tiles + tile] = weights[tile][kind]
        put(u1, x, step(masks, weights, *[plane_of(u0, x + d, tiles) for d in (-1, 0, 1)]))

    def second_step(x):
        weights = []
        for tile in range(tiles):
            at = x * tiles + tile
            here = hv[at]
            weights.append([held[kind, at] for kind in range(5)] + [here + hv[at - tiles], here + hv[at + tiles]])
        put(u2_ref, x, step(masks, weights, *[plane_of(u1, x + d, tiles) for d in (-1, 0, 1)]))

    each(0, planes, 4, load_t)
    copy.wait()
    each(0, planes, 4, load_u)
    each(1, planes - 1, 7, first_step)
    each(2, planes - 2, 6, second_step)
    last = planes - 1
    at = 0
    for ref, kept in ((u0, (0, 1, last - 1, last)), (hv, (0, 1, 2, last - 2, last - 1, last)),
                      (u1, (1, 2, last - 2, last - 1))):
        for x in kept:
            put(edge_ref, at, plane_of(ref, x, tiles))
            at += 1


def outer_kernel(planes, tiles, probe_hbm, before_ref, after_ref, edge_ref, inner_ref, obs_ref,
                 u2_ref, sent_ref, probe_ref, sem):
    probe_copy = pltpu.make_async_copy(probe_hbm, probe_ref, sem)
    probe_copy.start()
    masks = lane_masks()
    blocks = probe_ref.shape[0] // LANES
    edge = [plane_of(edge_ref, at, tiles) for at in range(14)]
    last = planes - 1
    for ref, own_u, own_v, own_1, where in (
        (before_ref, edge[0:2], edge[4:7], edge[10:12], (0, 1)),
        (after_ref, edge[3:1:-1], edge[9:6:-1], edge[13:11:-1], (last, last - 1)),
    ):
        order = (0, 1) if ref is before_ref else (1, 0)
        u = [plane_of(ref, d, tiles) for d in order] + own_u
        v = [[HALF_DT * jnp.exp(t) for t in plane_of(ref, 2 + d, tiles)] for d in order] + own_v
        live = ref[4 * tiles]
        weights = [coefficients(masks, v[d], v[d + 1], v[d + 2]) for d in range(3)]
        next_u = [step(masks, weights[d], u[d], u[d + 1], u[d + 2]) for d in range(2)]
        next_u[0] = [value * live for value in next_u[0]]
        next_u = next_u + own_1
        for d in range(2):
            put(u2_ref, where[d], step(masks, weights[d + 1], next_u[d], next_u[d + 1], next_u[d + 2]))

    probe_copy.wait()
    lane = lax.broadcasted_iota(jnp.int32, (ROWS, LANES), 1)
    for part in range(blocks):
        found = jnp.zeros((ROWS, LANES), jnp.float32)
        for p in range(LANES):
            cell = probe_ref[part * LANES + p]
            turned = pltpu.roll(u2_ref[cell >> 7], (p - cell) & (LANES - 1), 1)
            found = jnp.where(lane == p, turned, found)

        observed = obs_ref[blocks, part : part + 1, :]
        variance = obs_ref[blocks, blocks + part : blocks + part + 1, :]
        scaled = (observed + obs_ref[part] - found) / variance
        for slab in range(sent_ref.shape[0]):
            sent_ref[slab, part] = found
            sent_ref[slab, blocks + part] = scaled
    for slab in range(sent_ref.shape[0]):
        for at in range(blocks, obs_ref.shape[0]):
            sent_ref[slab, blocks + at] = obs_ref[at]


def spread_kernel(place_ref, got_ref, sent_ref):
    slabs, (groups, windows, blocks) = got_ref.shape[0], sent_ref.shape[:3]
    for window in range(windows):
        at = window if windows == slabs else jnp.clip(place_ref[0] + window - 2, 0, slabs - 1)
        for b in range(blocks):
            value = got_ref[at, b]
            for group in range(groups):
                sent_ref[group, window, b] = value


def halves(value):
    high = value.astype(jnp.bfloat16)
    return high, (value - high.astype(jnp.float32)).astype(jnp.bfloat16)


def between_kernel(planes, tiles, u2_ref, theta_hbm, out_ref, split_ref, theta_ref, sem):
    copy = pltpu.make_async_copy(theta_hbm, theta_ref, sem)
    copy.start()
    stride = planes * tiles
    members = theta_ref.shape[0] * ROWS

    def store(x, _):
        base = (x // ROWS) * tiles * ROWS + x % ROWS
        for tile in range(tiles):
            out_ref[pl.ds(base + tile * ROWS, ROWS, stride=stride), :] = u2_ref[x * tiles + tile]
        return 0

    lax.fori_loop(0, planes, store, 0)
    copy.wait()

    def split(slot, _):
        high, low = halves(theta_ref[:, slot].reshape(members, LANES))
        split_ref[slot, :members, :] = high
        split_ref[slot, members:, :] = low
        return 0

    lax.fori_loop(0, split_ref.shape[0], split, 0)


def stacked(value):
    high, low = halves(value)
    return jnp.concatenate([high.astype(jnp.float32), low.astype(jnp.float32)], axis=0).astype(jnp.bfloat16)


def fold(both):
    return both[:ROWS] + both[ROWS:]


def dot(left, right, over):
    return lax.dot_general(left, right, (((1,), (over,)), ((), ())), preferred_element_type=jnp.float32)


def update_kernel(slabs, planes, tiles, place_ref, count_ref, cells_hbm, probes_hbm, level_hbm,
                  pred_ref, got_ref, split_hbm, t_hbm, post_ref, gain_ref,
                  reach, cells_ref, probes_ref, level_ref, split_ref, sems):
    groups, windows, blocks = pred_ref.shape[:3]
    members = groups * ROWS
    share = 1.0 / (members - 1)
    copies = [
        pltpu.make_async_copy(source, target, sems.at[at])
        for at, (source, target) in enumerate((
            (cells_hbm, cells_ref), (probes_hbm, probes_ref), (level_hbm, level_ref),
            (split_hbm, split_ref), (t_hbm, post_ref)))
    ]
    for copy in copies:
        copy.start()
    slab = place_ref[0]

    def wide(row):
        return row[:, :members] if members <= LANES else jnp.concatenate([row] * (members // LANES), axis=1)

    anomaly, scaled, matches, places = [], [], [], []
    for d in range(5):
        wanted = slab + d - 2
        at = jnp.clip(wanted, 0, slabs - 1)
        live = jnp.where((wanted >= 0) & (wanted < slabs), 1.0, 0.0)
        places.append(at)
        for b in range(blocks):
            predicted = pred_ref[:, at if windows == slabs else d, b].reshape(members, LANES)
            mean = jnp.sum(predicted, axis=0, keepdims=True) / members
            anomaly.append(halves((predicted - mean) * live))
            scaled.append(got_ref[at, blocks + b] * live)
            left = stacked(scaled[-1])
            high, low = anomaly[-1]
            matches.append(fold(dot(left, high, 1) + dot(left, low, 1)))
    for d in range(1, 4):
        for i in range(blocks):
            total = jnp.zeros((ROWS, members), jnp.float32)
            for j in range(3 * blocks):
                at = 2 * blocks + i * 3 * blocks + j
                level = got_ref[places[d], 2 * blocks + at // ROWS, at % ROWS : at % ROWS + 1, :] / 256.0 * share
                total = total + wide(level) * matches[(d - 1) * blocks + j]
            high, low = anomaly[d * blocks + i]
            left = stacked(total)
            correction = fold(dot(left, high, 0) + dot(left, low, 0))
            at = blocks + i
            variance = got_ref[places[d], 2 * blocks + at // ROWS, at % ROWS : at % ROWS + 1, :]
            gain = scaled[d * blocks + i] - correction / variance
            if d == 2:
                gain_ref[:, i * LANES : (i + 1) * LANES] = gain
            left = stacked(gain)
            both = stacked(fold(dot(left, high, 1) + dot(left, low, 1)))
            reach[(d - 1) * blocks + i] = jnp.concatenate([both, both], axis=1)
    for copy in copies:
        copy.wait()
    for slot in range(split_ref.shape[0]):
        weight = jnp.where(slot < count_ref[0], level_ref[0, slot].astype(jnp.float32) / 256.0, 0.0) * share
        change = fold(dot(reach[probes_ref[0, slot]], split_ref[slot], 0)) * weight
        block = cells_ref[0, slot]
        rows = pl.ds(row_of(block // tiles, block % tiles, tiles), ROWS, stride=planes * tiles)
        post_ref[rows, :] = post_ref[rows, :] + change


def shards(
    starting_speed_field,
    sample_fluidity_exponent,
    observed,
    obs_noise,
    obs_var,
    probe_cells,
    pair_cells,
    pair_probes,
    pair_taper,
    pair_counts,
    probe_taper,
):
    shape = starting_speed_field.shape
    members, planes, cells = shape
    tiles = cells // LANES
    slots = pair_cells.shape[1]
    probes = obs_noise.shape[1]
    blocks = probes // LANES
    slabs, groups = lax.axis_size("space"), lax.axis_size("ens")
    f32, i32 = jnp.float32, jnp.int32
    u_rows = to_rows(starting_speed_field)
    t_rows = to_rows(sample_fluidity_exponent)
    obs_tiles = blocks - (-(2 * blocks + probe_taper.shape[1] * probe_taper.shape[2]) // ROWS)
    edge = jax.ShapeDtypeStruct((4 * tiles + 1, ROWS, LANES), f32)
    obs_shape = jax.ShapeDtypeStruct((obs_tiles, ROWS, LANES), f32)
    params = pltpu.CompilerParams(vmem_limit_bytes=32 * 1024 * 1024)
    stack = pltpu.VMEM((planes * tiles, ROWS, LANES), f32)
    low, high, obs, t_near, picked = pl.pallas_call(
        functools.partial(pack_kernel, planes, tiles),
        out_shape=(
            edge,
            edge,
            obs_shape,
            jax.ShapeDtypeStruct(u_rows.shape, f32),
            pltpu.HBM((groups, slots, ROWS, LANES), f32),
        ),
        in_specs=[HBM] * 7,
        out_specs=(VMEM,) * 4 + (HBM,),
        scratch_shapes=[
            pltpu.SMEM(pair_cells.shape, i32),
            pltpu.SMEM(probe_taper.shape, i32),
            pltpu.VMEM(u_rows.shape, f32),
            pltpu.VMEM((ROWS, probes), f32),
            pltpu.VMEM((2, probes), f32),
            pltpu.VMEM((slots, ROWS, LANES), f32),
            pltpu.SemaphoreType.DMA((7 + groups,)),
        ],
        compiler_params=params,
        name="pack",
    )(*map(stay, (pair_cells, probe_taper, u_rows, t_rows, obs_noise, observed.reshape(1, -1), obs_var.reshape(1, -1))))
    upward = [(i, i + 1) for i in range(slabs - 1)]
    before = lax.ppermute(high, "space", upward)
    after = lax.ppermute(low, "space", [(j, i) for i, j in upward])
    theta_all = lax.all_to_all(picked, "ens", 0, 0)
    inner, edges = pl.pallas_call(
        functools.partial(inner_kernel, planes, tiles),
        out_shape=(
            jax.ShapeDtypeStruct((planes * tiles, ROWS, LANES), f32),
            jax.ShapeDtypeStruct((14 * tiles, ROWS, LANES), f32),
        ),
        in_specs=[HBM, VMEM],
        out_specs=(VMEM,) * 2,
        scratch_shapes=[
            pltpu.VMEM(u_rows.shape, f32),
            stack,
            stack,
            stack,
            pltpu.VMEM((5, planes * tiles, ROWS, LANES), f32),
            pltpu.SemaphoreType.DMA(()),
        ],
        compiler_params=params,
        cost_estimate=pl.CostEstimate(flops=20_000_000, bytes_accessed=20_000_000, transcendentals=0),
        name="inner_planes",
    )(stay(u_rows), t_near)
    u2, sent = pl.pallas_call(
        functools.partial(outer_kernel, planes, tiles),
        out_shape=(
            jax.ShapeDtypeStruct((planes * tiles, ROWS, LANES), f32),
            jax.ShapeDtypeStruct((slabs, blocks + obs_tiles, ROWS, LANES), f32),
        ),
        in_specs=[HBM] + [VMEM] * 5,
        out_specs=(VMEM,) * 2,
        scratch_shapes=[pltpu.SMEM(probe_cells.shape, i32), pltpu.SemaphoreType.DMA(())],
        input_output_aliases={4: 0},
        compiler_params=params,
        name="outer_planes",
    )(stay(probe_cells), before, after, edges, inner, obs)
    got = lax.all_to_all(sent, "space", 0, 0)
    place = lax.axis_index("space").astype(i32).reshape(1)
    windows = min(slabs, 5)
    spread = pl.pallas_call(
        spread_kernel,
        out_shape=jax.ShapeDtypeStruct((groups, windows, blocks, ROWS, LANES), f32),
        in_specs=[SMEM, VMEM],
        out_specs=VMEM,
        compiler_params=params,
        name="spread",
    )(place, got)
    pred_all = lax.all_to_all(spread, "ens", 0, 0)
    u2_rows, split = pl.pallas_call(
        functools.partial(between_kernel, planes, tiles),
        out_shape=(
            jax.ShapeDtypeStruct(u_rows.shape, f32),
            pltpu.HBM((slots, 2 * groups * ROWS, LANES), jnp.bfloat16),
        ),
        in_specs=[VMEM, HBM],
        out_specs=(VMEM,) * 2,
        scratch_shapes=[pltpu.VMEM(theta_all.shape, f32), pltpu.SemaphoreType.DMA(())],
        compiler_params=params,
        cost_estimate=pl.CostEstimate(flops=1_000_000, bytes_accessed=8_000_000, transcendentals=0),
        name="between",
    )(u2, stay(theta_all))
    post_rows, gain = pl.pallas_call(
        functools.partial(update_kernel, slabs, planes, tiles),
        out_shape=(
            jax.ShapeDtypeStruct(u_rows.shape, f32),
            jax.ShapeDtypeStruct((members, probes), f32),
        ),
        in_specs=[SMEM] * 2 + [HBM] * 3 + [VMEM] * 2 + [HBM] * 2,
        out_specs=(VMEM,) * 2,
        scratch_shapes=[
            pltpu.VMEM((probe_taper.shape[2], 2 * ROWS, 2 * groups * ROWS), jnp.bfloat16),
            pltpu.SMEM(pair_cells.shape, i32),
            pltpu.SMEM(pair_cells.shape, i32),
            pltpu.SMEM(pair_cells.shape, i32),
            pltpu.VMEM(split.shape, jnp.bfloat16),
            pltpu.SemaphoreType.DMA((5,)),
        ],
        compiler_params=params,
        name="update",
    )(place, pair_counts, *map(stay, (pair_cells, pair_probes, pair_taper)), pred_all, got,
      stay(split), stay(t_rows))
    return (from_rows(u2_rows, shape), from_rows(post_rows, shape), gain)


def solution(mesh):
    return jax.shard_map(
        shards,
        mesh=mesh,
        in_specs=(
            P("ens", "space", None),
            P("ens", "space", None),
            P("space"),
            P("ens", "space"),
            P("space"),
            P("space"),
            P("space", None),
            P("space", None),
            P("space", None),
            P("space"),
            P("space", None, None),
        ),
        out_specs=(P("ens", "space", None), P("ens", "space", None), P("ens", "space")),
        check_vma=False,
    )
```

```python
import functools

import jax
import jax.numpy as jnp
from jax import lax
from jax.experimental import pallas as pl
from jax.experimental.pallas import tpu as pltpu
from jax.sharding import PartitionSpec as P

LANES = 128
ROWS = 8
NZ = 64
HALF_DT = 0.5 * 0.08

VMEM = pl.BlockSpec(memory_space=pltpu.VMEM)
SMEM = pl.BlockSpec(memory_space=pltpu.SMEM)
HBM = pl.BlockSpec(memory_space=pltpu.HBM)


def stay(array):
    return pltpu.with_memory_space_constraint(array, pltpu.HBM)


def to_rows(array):
    members, planes, cells = array.shape
    split = array.reshape(members, planes // ROWS, ROWS, cells // LANES, LANES)
    return split.transpose(0, 1, 3, 2, 4).reshape(-1, LANES)


def from_rows(rows, shape):
    members, planes, cells = shape
    split = rows.reshape(members, planes // ROWS, cells // LANES, ROWS, LANES)
    return split.transpose(0, 1, 3, 2, 4).reshape(shape)


def row_of(plane, tile, tiles):
    return (plane // ROWS * tiles + tile) * ROWS + plane % ROWS


def pack_kernel(planes, tiles, cells_hbm, taper_hbm, u_hbm, t_hbm, noise_hbm, observed_hbm, var_hbm,
                low_ref, high_ref, obs_ref, t_ref, pick_hbm,
                cells_ref, taper_ref, u_ref, noise_ref, row_ref, pick_ref, sems):
    stride = planes * tiles
    blocks = noise_ref.shape[1] // LANES
    copies = [
        pltpu.make_async_copy(source, target, sems.at[at])
        for at, (source, target) in enumerate((
            (cells_hbm, cells_ref),
            (t_hbm, t_ref),
            (u_hbm, u_ref),
            (taper_hbm, taper_ref),
            (noise_hbm, noise_ref),
            (observed_hbm, row_ref.at[0:1]),
            (var_hbm, row_ref.at[1:2]),
        ))
    ]
    for copy in copies:
        copy.start()
    copies[0].wait()
    copies[1].wait()
    for slot in range(pick_ref.shape[0]):
        block = cells_ref[0, slot]
        row = row_of(block // tiles, block % tiles, tiles)
        pick_ref[slot] = t_ref[pl.ds(row, ROWS, stride=stride), :]
    picks = [
        pltpu.make_async_copy(pick_ref, pick_hbm.at[device], sems.at[len(copies) + device])
        for device in range(pick_hbm.shape[0])
    ]
    for copy in picks:
        copy.start()
    for kind, source in ((1, t_ref), (0, u_ref)):
        if kind == 0:
            copies[2].wait()
        for out_ref, first in ((high_ref, planes - 2), (low_ref, 0)):
            for depth in range(2):
                for tile in range(tiles):
                    out_ref[(kind * 2 + depth) * tiles + tile] = source[
                        pl.ds(row_of(first + depth, tile, tiles), ROWS, stride=stride), :
                    ]
    for ref in (low_ref, high_ref):
        ref[4 * tiles] = jnp.ones((ROWS, LANES), jnp.float32)
    for copy in copies[3:]:
        copy.wait()
    own, window = taper_ref.shape[1:]
    rows = [row_ref[kind : kind + 1, b * LANES : (b + 1) * LANES] for kind in range(2) for b in range(blocks)]
    for i in range(own):
        for j in range(window):
            rows.append(jnp.full((1, LANES), taper_ref[0, i, j].astype(jnp.float32), jnp.float32))
    for b in range(blocks):
        obs_ref[b] = noise_ref[:, b * LANES : (b + 1) * LANES]
    for at, row in enumerate(rows):
        obs_ref[blocks + at // ROWS, at % ROWS : at % ROWS + 1, :] = row
    for ref in (low_ref, high_ref):
        for at in range(obs_ref.shape[0]):
            ref[4 * tiles + 1 + at] = obs_ref[at]
    for copy in picks:
        copy.wait()


def rot(value, by):
    return pltpu.roll(value, by % LANES, 1)


def lane_masks():
    lane = lax.broadcasted_iota(jnp.int32, (ROWS, LANES), 1)
    height = lane & (NZ - 1)
    return lane < NZ, height == 0, height == NZ - 1


def coefficients(masks, low, here, high):
    first_half, floor, roof = masks
    tiles = len(here)
    turned = [rot(value, NZ) for value in here]
    out = []
    for tile in range(tiles):
        mid = here[tile]
        near = mid + turned[tile]
        far = mid + jnp.where(first_half, turned[tile - 1], turned[(tile + 1) % tiles])
        up = mid + jnp.where(roof, HALF_DT, rot(mid, -1))
        down = mid + jnp.where(floor, HALF_DT, rot(mid, 1))
        below = mid + low[tile]
        above = mid + high[tile]
        diag = 1.0 - ((near + far) + (up + down) + (below + above))
        out.append((diag, near, far, jnp.where(roof, 0.0, up), jnp.where(floor, 0.0, down), below, above))
    return out


def step(masks, weights, low, here, high):
    first_half = masks[0]
    tiles = len(here)
    turned = [rot(value, NZ) for value in here]
    out = []
    for tile in range(tiles):
        diag, near, far, up, down, below, above = weights[tile]
        mid = here[tile]
        beyond = jnp.where(first_half, turned[tile - 1], turned[(tile + 1) % tiles])
        out.append(
            (diag * mid + near * turned[tile])
            + (far * beyond + up * rot(mid, -1))
            + (down * rot(mid, 1) + below * low[tile])
            + above * high[tile]
        )
    return out


def plane_of(ref, at, tiles):
    return [ref[at * tiles + tile] for tile in range(tiles)]


def put(ref, at, values):
    for tile, value in enumerate(values):
        ref[at * len(values) + tile] = value


def each(first, last, unroll, body):
    count = (last - first) // unroll

    def several(at, _):
        for d in range(unroll):
            body(first + at * unroll + d)
        return 0

    lax.fori_loop(0, count, several, 0)
    for x in range(first + count * unroll, last):
        body(x)


def inner_kernel(planes, tiles, u_hbm, t_ref, u2_ref, edge_ref, u_ref, u0, hv, u1, held, sem):
    stride = planes * tiles
    masks = lane_masks()
    copy = pltpu.make_async_copy(u_hbm, u_ref, sem)
    copy.start()

    def rows_at(x, tile):
        return pl.ds((x // ROWS) * tiles * ROWS + x % ROWS + tile * ROWS, ROWS, stride=stride)

    def load_t(x):
        for tile in range(tiles):
            hv[x * tiles + tile] = HALF_DT * jnp.exp(t_ref[rows_at(x, tile), :])

    def load_u(x):
        for tile in range(tiles):
            u0[x * tiles + tile] = u_ref[rows_at(x, tile), :]

    def first_step(x):
        weights = coefficients(masks, *[plane_of(hv, x + d, tiles) for d in (-1, 0, 1)])
        for tile in range(tiles):
            for kind in range(5):
                held[kind, x * tiles + tile] = weights[tile][kind]
        put(u1, x, step(masks, weights, *[plane_of(u0, x + d, tiles) for d in (-1, 0, 1)]))

    def second_step(x):
        weights = []
        for tile in range(tiles):
            at = x * tiles + tile
            here = hv[at]
            weights.append([held[kind, at] for kind in range(5)] + [here + hv[at - tiles], here + hv[at + tiles]])
        put(u2_ref, x, step(masks, weights, *[plane_of(u1, x + d, tiles) for d in (-1, 0, 1)]))

    each(0, planes, 4, load_t)
    copy.wait()
    each(0, planes, 4, load_u)
    each(1, planes - 1, 7, first_step)
    each(2, planes - 2, 6, second_step)
    last = planes - 1
    at = 0
    for ref, kept in ((u0, (0, 1, last - 1, last)), (hv, (0, 1, 2, last - 2, last - 1, last)),
                      (u1, (1, 2, last - 2, last - 1))):
        for x in kept:
            put(edge_ref, at, plane_of(ref, x, tiles))
            at += 1


def outer_kernel(planes, tiles, probe_hbm, before_ref, after_ref, edge_ref, inner_ref,
                 u2_ref, sent_ref, probe_ref, sem):
    probe_copy = pltpu.make_async_copy(probe_hbm, probe_ref, sem)
    probe_copy.start()
    masks = lane_masks()
    blocks = probe_ref.shape[0] // LANES
    edge = [plane_of(edge_ref, at, tiles) for at in range(14)]
    last = planes - 1
    for ref, own_u, own_v, own_1, where in (
        (before_ref, edge[0:2], edge[4:7], edge[10:12], (0, 1)),
        (after_ref, edge[3:1:-1], edge[9:6:-1], edge[13:11:-1], (last, last - 1)),
    ):
        order = (0, 1) if ref is before_ref else (1, 0)
        u = [plane_of(ref, d, tiles) for d in order] + own_u
        v = [[HALF_DT * jnp.exp(t) for t in plane_of(ref, 2 + d, tiles)] for d in order] + own_v
        live = ref[4 * tiles]
        weights = [coefficients(masks, v[d], v[d + 1], v[d + 2]) for d in range(3)]
        next_u = [step(masks, weights[d], u[d], u[d + 1], u[d + 2]) for d in range(2)]
        next_u[0] = [value * live for value in next_u[0]]
        next_u = next_u + own_1
        for d in range(2):
            put(u2_ref, where[d], step(masks, weights[d + 1], next_u[d], next_u[d + 1], next_u[d + 2]))

    probe_copy.wait()
    lane = lax.broadcasted_iota(jnp.int32, (ROWS, LANES), 1)
    for part in range(blocks):
        found = jnp.zeros((ROWS, LANES), jnp.float32)
        for p in range(LANES):
            cell = probe_ref[part * LANES + p]
            turned = pltpu.roll(u2_ref[cell >> 7], (p - cell) & (LANES - 1), 1)
            found = jnp.where(lane == p, turned, found)

        def send(at, _):
            for d in range(ROWS):
                sent_ref[at * ROWS + d, part] = found
            return 0

        lax.fori_loop(0, sent_ref.shape[0] // ROWS, send, 0)


def halves(value):
    high = value.astype(jnp.bfloat16)
    return high, (value - high.astype(jnp.float32)).astype(jnp.bfloat16)


def between_kernel(planes, tiles, place_ref, u2_ref, same_hbm, other_hbm, out_ref, split_ref, same_ref, other_ref, sems):
    copies = [
        pltpu.make_async_copy(same_hbm, same_ref, sems.at[0]),
        pltpu.make_async_copy(other_hbm, other_ref, sems.at[1]),
    ]
    for copy in copies:
        copy.start()
    stride = planes * tiles
    members = 2 * same_ref.shape[0] * ROWS
    first_core = jnp.where(place_ref[2] == 0, 1.0, 0.0)

    def store(x, _):
        base = (x // ROWS) * tiles * ROWS + x % ROWS
        for tile in range(tiles):
            out_ref[pl.ds(base + tile * ROWS, ROWS, stride=stride), :] = u2_ref[x * tiles + tile]
        return 0

    lax.fori_loop(0, planes, store, 0)
    for copy in copies:
        copy.wait()

    def split(slot, _):
        parts = []
        for chip in range(same_ref.shape[0]):
            same, other = same_ref[chip, slot], other_ref[chip, slot]
            parts += [jnp.where(first_core > 0.5, same, other), jnp.where(first_core > 0.5, other, same)]
        high, low = halves(jnp.concatenate(parts, axis=0))
        split_ref[slot, :members, :] = high
        split_ref[slot, members:, :] = low
        return 0

    lax.fori_loop(0, split_ref.shape[0], split, 0)


def stacked(value):
    high, low = halves(value)
    return jnp.concatenate([high.astype(jnp.float32), low.astype(jnp.float32)], axis=0).astype(jnp.bfloat16)


def fold(both):
    return both[:ROWS] + both[ROWS:]


def dot(left, right, over):
    return lax.dot_general(left, right, (((1,), (over,)), ((), ())), preferred_element_type=jnp.float32)


def update_kernel(slabs, planes, tiles, place_ref, count_ref, cells_hbm, probes_hbm, level_hbm,
                  pred_ref, before_2_ref, before_ref, own_ref, after_ref, after_2_ref, split_hbm, t_hbm,
                  post_ref, gain_ref, reach, cells_ref, probes_ref, level_ref, split_ref, sems):
    groups, blocks = pred_ref.shape[0] // slabs, pred_ref.shape[1]
    members = groups * ROWS
    share = 1.0 / (members - 1)
    copies = [
        pltpu.make_async_copy(source, target, sems.at[at])
        for at, (source, target) in enumerate((
            (cells_hbm, cells_ref), (probes_hbm, probes_ref), (level_hbm, level_ref),
            (split_hbm, split_ref), (t_hbm, post_ref)))
    ]
    for copy in copies:
        copy.start()
    slab, group = place_ref[0], place_ref[1]
    halo = 4 * tiles + 1
    seen = ((before_2_ref, 0), (before_ref, halo), (own_ref, 0), (after_ref, halo), (after_2_ref, 0))

    def extra(d, at):
        ref, first = seen[d]
        return ref[first + blocks + at // ROWS, at % ROWS : at % ROWS + 1, :]

    def wide(row):
        return row[:, :members] if members <= LANES else jnp.concatenate([row] * (members // LANES), axis=1)

    anomaly, scaled, variance, matches = [], [], [], []
    for d in range(5):
        wanted = slab + d - 2
        at = jnp.clip(wanted, 0, slabs - 1)
        live = jnp.where((wanted >= 0) & (wanted < slabs), 1.0, 0.0)
        for b in range(blocks):
            predicted = pred_ref[pl.ds(at * groups, groups), b].reshape(members, LANES)
            mean = jnp.sum(predicted, axis=0, keepdims=True) / members
            anomaly.append(halves((predicted - mean) * live))
            variance.append(extra(d, blocks + b) + (1.0 - live))
            noise = seen[d][0][seen[d][1] + b]
            scaled.append((extra(d, b) + noise - pred_ref[at * groups + group, b]) / variance[-1] * live)
            left = stacked(scaled[-1])
            high, low = anomaly[-1]
            matches.append(fold(dot(left, high, 1) + dot(left, low, 1)))
    for d in range(1, 4):
        for i in range(blocks):
            total = jnp.zeros((ROWS, members), jnp.float32)
            for j in range(3 * blocks):
                level = extra(d, 2 * blocks + i * 3 * blocks + j) / 256.0 * share
                total = total + wide(level) * matches[(d - 1) * blocks + j]
            high, low = anomaly[d * blocks + i]
            left = stacked(total)
            correction = fold(dot(left, high, 0) + dot(left, low, 0))
            gain = scaled[d * blocks + i] - correction / variance[d * blocks + i]
            if d == 2:
                gain_ref[:, i * LANES : (i + 1) * LANES] = gain
            left = stacked(gain)
            both = stacked(fold(dot(left, high, 1) + dot(left, low, 1)))
            reach[(d - 1) * blocks + i] = jnp.concatenate([both, both], axis=1)
    for copy in copies:
        copy.wait()
    for slot in range(split_ref.shape[0]):
        weight = jnp.where(slot < count_ref[0], level_ref[0, slot].astype(jnp.float32) / 256.0, 0.0) * share
        change = fold(dot(reach[probes_ref[0, slot]], split_ref[slot], 0)) * weight
        block = cells_ref[0, slot]
        rows = pl.ds(row_of(block // tiles, block % tiles, tiles), ROWS, stride=planes * tiles)
        post_ref[rows, :] = post_ref[rows, :] + change


def shards(
    starting_speed_field,
    sample_fluidity_exponent,
    observed,
    obs_noise,
    obs_var,
    probe_cells,
    pair_cells,
    pair_probes,
    pair_taper,
    pair_counts,
    probe_taper,
):
    shape = starting_speed_field.shape
    members, planes, cells = shape
    tiles = cells // LANES
    slots = pair_cells.shape[1]
    probes = obs_noise.shape[1]
    blocks = probes // LANES
    slabs, chips = lax.axis_size("space"), lax.axis_size("chip")
    groups = 2 * chips
    f32, i32 = jnp.float32, jnp.int32
    u_rows = to_rows(starting_speed_field)
    t_rows = to_rows(sample_fluidity_exponent)
    obs_tiles = blocks - (-(2 * blocks + probe_taper.shape[1] * probe_taper.shape[2]) // ROWS)
    edge = jax.ShapeDtypeStruct((4 * tiles + 1 + obs_tiles, ROWS, LANES), f32)
    obs_shape = jax.ShapeDtypeStruct((obs_tiles, ROWS, LANES), f32)
    params = pltpu.CompilerParams(vmem_limit_bytes=32 * 1024 * 1024)
    stack = pltpu.VMEM((planes * tiles, ROWS, LANES), f32)
    low, high, obs, t_near, picked = pl.pallas_call(
        functools.partial(pack_kernel, planes, tiles),
        out_shape=(
            edge,
            edge,
            obs_shape,
            jax.ShapeDtypeStruct(u_rows.shape, f32),
            pltpu.HBM((chips, slots, ROWS, LANES), f32),
        ),
        in_specs=[HBM] * 7,
        out_specs=(VMEM,) * 4 + (HBM,),
        scratch_shapes=[
            pltpu.SMEM(pair_cells.shape, i32),
            pltpu.SMEM(probe_taper.shape, i32),
            pltpu.VMEM(u_rows.shape, f32),
            pltpu.VMEM((ROWS, probes), f32),
            pltpu.VMEM((2, probes), f32),
            pltpu.VMEM((slots, ROWS, LANES), f32),
            pltpu.SemaphoreType.DMA((7 + chips,)),
        ],
        compiler_params=params,
        name="pack",
    )(*map(stay, (pair_cells, probe_taper, u_rows, t_rows, obs_noise, observed.reshape(1, -1), obs_var.reshape(1, -1))))
    upward = [(i, i + 1) for i in range(slabs - 1)]
    before = lax.ppermute(high, "space", upward)
    after = lax.ppermute(low, "space", [(j, i) for i, j in upward])
    if slabs == 4:
        before_2 = after_2 = lax.ppermute(obs, "space", [(i, (i + 2) % 4) for i in range(4)])
    else:
        upward_2 = [(i, i + 2) for i in range(slabs - 2)]
        before_2 = lax.ppermute(obs, "space", upward_2)
        after_2 = lax.ppermute(obs, "space", [(j, i) for i, j in upward_2])
    theta_same = lax.all_to_all(picked, "chip", 0, 0)
    theta_other = lax.ppermute(theta_same, "core", [(0, 1), (1, 0)])
    inner, edges = pl.pallas_call(
        functools.partial(inner_kernel, planes, tiles),
        out_shape=(
            jax.ShapeDtypeStruct((planes * tiles, ROWS, LANES), f32),
            jax.ShapeDtypeStruct((14 * tiles, ROWS, LANES), f32),
        ),
        in_specs=[HBM, VMEM],
        out_specs=(VMEM,) * 2,
        scratch_shapes=[
            pltpu.VMEM(u_rows.shape, f32),
            stack,
            stack,
            stack,
            pltpu.VMEM((5, planes * tiles, ROWS, LANES), f32),
            pltpu.SemaphoreType.DMA(()),
        ],
        compiler_params=params,
        cost_estimate=pl.CostEstimate(flops=20_000_000, bytes_accessed=20_000_000, transcendentals=0),
        name="inner_planes",
    )(stay(u_rows), t_near)
    u2, sent = pl.pallas_call(
        functools.partial(outer_kernel, planes, tiles),
        out_shape=(
            jax.ShapeDtypeStruct((planes * tiles, ROWS, LANES), f32),
            jax.ShapeDtypeStruct((slabs * groups, blocks, ROWS, LANES), f32),
        ),
        in_specs=[HBM] + [VMEM] * 4,
        out_specs=(VMEM,) * 2,
        scratch_shapes=[pltpu.SMEM(probe_cells.shape, i32), pltpu.SemaphoreType.DMA(())],
        input_output_aliases={4: 0},
        compiler_params=params,
        name="outer_planes",
    )(stay(probe_cells), before, after, edges, inner)
    pred_all = lax.all_to_all(sent, ("space", "chip", "core"), 0, 0)
    group = lax.axis_index(("chip", "core"))
    place = jnp.stack([lax.axis_index("space"), group, lax.axis_index("core")]).astype(i32)
    u2_rows, split = pl.pallas_call(
        functools.partial(between_kernel, planes, tiles),
        out_shape=(
            jax.ShapeDtypeStruct(u_rows.shape, f32),
            pltpu.HBM((slots, 2 * groups * ROWS, LANES), jnp.bfloat16),
        ),
        in_specs=[SMEM, VMEM, HBM, HBM],
        out_specs=(VMEM,) * 2,
        scratch_shapes=[pltpu.VMEM(picked.shape, f32)] * 2 + [pltpu.SemaphoreType.DMA((2,))],
        compiler_params=params,
        cost_estimate=pl.CostEstimate(flops=1_000_000, bytes_accessed=8_000_000, transcendentals=0),
        name="between",
    )(place, u2, stay(theta_same), stay(theta_other))
    post_rows, gain = pl.pallas_call(
        functools.partial(update_kernel, slabs, planes, tiles),
        out_shape=(
            jax.ShapeDtypeStruct(u_rows.shape, f32),
            jax.ShapeDtypeStruct((members, probes), f32),
        ),
        in_specs=[SMEM] * 2 + [HBM] * 3 + [VMEM] * 6 + [HBM] * 2,
        out_specs=(VMEM,) * 2,
        scratch_shapes=[
            pltpu.VMEM((probe_taper.shape[2], 2 * ROWS, 2 * groups * ROWS), jnp.bfloat16),
            pltpu.SMEM(pair_cells.shape, i32),
            pltpu.SMEM(pair_cells.shape, i32),
            pltpu.SMEM(pair_cells.shape, i32),
            pltpu.VMEM(split.shape, jnp.bfloat16),
            pltpu.SemaphoreType.DMA((5,)),
        ],
        compiler_params=params,
        name="update",
    )(place, pair_counts, *map(stay, (pair_cells, pair_probes, pair_taper)), pred_all,
      before_2, before, obs, after, after_2, stay(split), stay(t_rows))
    return (from_rows(u2_rows, shape), from_rows(post_rows, shape), gain)


def solution(mesh):
    slabs, groups = mesh.devices.shape
    split = jax.sharding.Mesh(mesh.devices.reshape(slabs, groups // 2, 2), ("space", "chip", "core"))
    members = ("chip", "core")
    return jax.shard_map(
        shards,
        mesh=split,
        in_specs=(
            P(members, "space", None),
            P(members, "space", None),
            P("space"),
            P(members, "space"),
            P("space"),
            P("space"),
            P("space", None),
            P("space", None),
            P("space", None),
            P("space"),
            P("space", None, None),
        ),
        out_specs=(P(members, "space", None), P(members, "space", None), P(members, "space")),
        check_vma=False,
    )
```

```python
import functools

import jax
import jax.numpy as jnp
from jax import lax
from jax.experimental import pallas as pl
from jax.experimental.pallas import tpu as pltpu
from jax.sharding import PartitionSpec as P

LANES = 128
ROWS = 8
NZ = 64
HALF_DT = 0.5 * 0.08

VMEM = pl.BlockSpec(memory_space=pltpu.VMEM)
SMEM = pl.BlockSpec(memory_space=pltpu.SMEM)
HBM = pl.BlockSpec(memory_space=pltpu.HBM)


def stay(array):
    return pltpu.with_memory_space_constraint(array, pltpu.HBM)


def to_rows(array):
    members, planes, cells = array.shape
    split = array.reshape(members, planes // ROWS, ROWS, cells // LANES, LANES)
    return split.transpose(0, 1, 3, 2, 4).reshape(-1, LANES)


def from_rows(rows, shape):
    members, planes, cells = shape
    split = rows.reshape(members, planes // ROWS, cells // LANES, ROWS, LANES)
    return split.transpose(0, 1, 3, 2, 4).reshape(shape)


def row_of(plane, tile, tiles):
    return (plane // ROWS * tiles + tile) * ROWS + plane % ROWS


def pack_kernel(planes, tiles, cells_hbm, taper_hbm, u_hbm, t_hbm, noise_hbm, observed_hbm, var_hbm,
                low_ref, high_ref, obs_ref, t_ref, pick_hbm,
                cells_ref, taper_ref, u_ref, noise_ref, row_ref, pick_ref, sems):
    stride = planes * tiles
    blocks = noise_ref.shape[1] // LANES
    copies = [
        pltpu.make_async_copy(source, target, sems.at[at])
        for at, (source, target) in enumerate((
            (cells_hbm, cells_ref),
            (t_hbm, t_ref),
            (u_hbm, u_ref),
            (taper_hbm, taper_ref),
            (noise_hbm, noise_ref),
            (observed_hbm, row_ref.at[0:1]),
            (var_hbm, row_ref.at[1:2]),
        ))
    ]
    for copy in copies:
        copy.start()
    copies[0].wait()
    copies[1].wait()
    for slot in range(pick_ref.shape[0]):
        block = cells_ref[0, slot]
        row = row_of(block // tiles, block % tiles, tiles)
        pick_ref[slot] = t_ref[pl.ds(row, ROWS, stride=stride), :]
    picks = [
        pltpu.make_async_copy(pick_ref, pick_hbm.at[device], sems.at[len(copies) + device])
        for device in range(pick_hbm.shape[0])
    ]
    for copy in picks:
        copy.start()
    for kind, source in ((1, t_ref), (0, u_ref)):
        if kind == 0:
            copies[2].wait()
        for out_ref, first in ((high_ref, planes - 2), (low_ref, 0)):
            for depth in range(2):
                for tile in range(tiles):
                    out_ref[(kind * 2 + depth) * tiles + tile] = source[
                        pl.ds(row_of(first + depth, tile, tiles), ROWS, stride=stride), :
                    ]
    for ref in (low_ref, high_ref):
        ref[4 * tiles] = jnp.ones((ROWS, LANES), jnp.float32)
    for copy in copies[3:]:
        copy.wait()
    own, window = taper_ref.shape[1:]
    rows = [row_ref[kind : kind + 1, b * LANES : (b + 1) * LANES] for kind in range(2) for b in range(blocks)]
    for i in range(own):
        for j in range(window):
            rows.append(jnp.full((1, LANES), taper_ref[0, i, j].astype(jnp.float32), jnp.float32))
    for b in range(blocks):
        obs_ref[b] = noise_ref[:, b * LANES : (b + 1) * LANES]
    for at, row in enumerate(rows):
        obs_ref[blocks + at // ROWS, at % ROWS : at % ROWS + 1, :] = row
    for ref in (low_ref, high_ref):
        for at in range(obs_ref.shape[0]):
            ref[4 * tiles + 1 + at] = obs_ref[at]
    for copy in picks:
        copy.wait()


def rot(value, by):
    return pltpu.roll(value, by % LANES, 1)


def lane_masks():
    lane = lax.broadcasted_iota(jnp.int32, (ROWS, LANES), 1)
    height = lane & (NZ - 1)
    return lane < NZ, height == 0, height == NZ - 1


def coefficients(masks, low, here, high):
    first_half, floor, roof = masks
    tiles = len(here)
    turned = [rot(value, NZ) for value in here]
    out = []
    for tile in range(tiles):
        mid = here[tile]
        near = mid + turned[tile]
        far = mid + jnp.where(first_half, turned[tile - 1], turned[(tile + 1) % tiles])
        up = mid + jnp.where(roof, HALF_DT, rot(mid, -1))
        down = mid + jnp.where(floor, HALF_DT, rot(mid, 1))
        below = mid + low[tile]
        above = mid + high[tile]
        diag = 1.0 - ((near + far) + (up + down) + (below + above))
        out.append((diag, near, far, jnp.where(roof, 0.0, up), jnp.where(floor, 0.0, down), below, above))
    return out


def step(masks, weights, low, here, high):
    first_half = masks[0]
    tiles = len(here)
    turned = [rot(value, NZ) for value in here]
    out = []
    for tile in range(tiles):
        diag, near, far, up, down, below, above = weights[tile]
        mid = here[tile]
        beyond = jnp.where(first_half, turned[tile - 1], turned[(tile + 1) % tiles])
        out.append(
            (diag * mid + near * turned[tile])
            + (far * beyond + up * rot(mid, -1))
            + (down * rot(mid, 1) + below * low[tile])
            + above * high[tile]
        )
    return out


def plane_of(ref, at, tiles):
    return [ref[at * tiles + tile] for tile in range(tiles)]


def put(ref, at, values):
    for tile, value in enumerate(values):
        ref[at * len(values) + tile] = value


def each(first, last, unroll, body):
    count = (last - first) // unroll

    def several(at, _):
        for d in range(unroll):
            body(first + at * unroll + d)
        return 0

    lax.fori_loop(0, count, several, 0)
    for x in range(first + count * unroll, last):
        body(x)


def inner_kernel(planes, tiles, u_hbm, t_ref, u2_ref, edge_ref, u_ref, u0, hv, u1, held, sem):
    stride = planes * tiles
    masks = lane_masks()
    copy = pltpu.make_async_copy(u_hbm, u_ref, sem)
    copy.start()

    def rows_at(x, tile):
        return pl.ds((x // ROWS) * tiles * ROWS + x % ROWS + tile * ROWS, ROWS, stride=stride)

    def load_t(x):
        for tile in range(tiles):
            hv[x * tiles + tile] = HALF_DT * jnp.exp(t_ref[rows_at(x, tile), :])

    def load_u(x):
        for tile in range(tiles):
            u0[x * tiles + tile] = u_ref[rows_at(x, tile), :]

    def first_step(x):
        weights = coefficients(masks, *[plane_of(hv, x + d, tiles) for d in (-1, 0, 1)])
        for tile in range(tiles):
            for kind in range(5):
                held[kind, x * tiles + tile] = weights[tile][kind]
        put(u1, x, step(masks, weights, *[plane_of(u0, x + d, tiles) for d in (-1, 0, 1)]))

    def second_step(x):
        weights = []
        for tile in range(tiles):
            at = x * tiles + tile
            here = hv[at]
            weights.append([held[kind, at] for kind in range(5)] + [here + hv[at - tiles], here + hv[at + tiles]])
        put(u2_ref, x, step(masks, weights, *[plane_of(u1, x + d, tiles) for d in (-1, 0, 1)]))

    each(0, planes, 4, load_t)
    copy.wait()
    each(0, planes, 4, load_u)
    each(1, planes - 1, 7, first_step)
    each(2, planes - 2, 6, second_step)
    last = planes - 1
    at = 0
    for ref, kept in ((u0, (0, 1, last - 1, last)), (hv, (0, 1, 2, last - 2, last - 1, last)),
                      (u1, (1, 2, last - 2, last - 1))):
        for x in kept:
            put(edge_ref, at, plane_of(ref, x, tiles))
            at += 1


def outer_kernel(planes, tiles, probe_hbm, before_ref, after_ref, edge_ref, inner_ref, same_in,
                 u2_ref, sent_ref, same_out, probe_ref, sem):
    probe_copy = pltpu.make_async_copy(probe_hbm, probe_ref, sem)
    probe_copy.start()
    masks = lane_masks()
    blocks = probe_ref.shape[0] // LANES
    edge = [plane_of(edge_ref, at, tiles) for at in range(14)]
    last = planes - 1
    for ref, own_u, own_v, own_1, where in (
        (before_ref, edge[0:2], edge[4:7], edge[10:12], (0, 1)),
        (after_ref, edge[3:1:-1], edge[9:6:-1], edge[13:11:-1], (last, last - 1)),
    ):
        order = (0, 1) if ref is before_ref else (1, 0)
        u = [plane_of(ref, d, tiles) for d in order] + own_u
        v = [[HALF_DT * jnp.exp(t) for t in plane_of(ref, 2 + d, tiles)] for d in order] + own_v
        live = ref[4 * tiles]
        weights = [coefficients(masks, v[d], v[d + 1], v[d + 2]) for d in range(3)]
        next_u = [step(masks, weights[d], u[d], u[d + 1], u[d + 2]) for d in range(2)]
        next_u[0] = [value * live for value in next_u[0]]
        next_u = next_u + own_1
        for d in range(2):
            put(u2_ref, where[d], step(masks, weights[d + 1], next_u[d], next_u[d + 1], next_u[d + 2]))

    probe_copy.wait()
    lane = lax.broadcasted_iota(jnp.int32, (ROWS, LANES), 1)
    for part in range(blocks):
        found = jnp.zeros((ROWS, LANES), jnp.float32)
        for p in range(LANES):
            cell = probe_ref[part * LANES + p]
            turned = pltpu.roll(u2_ref[cell >> 7], (p - cell) & (LANES - 1), 1)
            found = jnp.where(lane == p, turned, found)

        def send(at, _):
            for d in range(ROWS):
                sent_ref[at * ROWS + d, part] = found
            return 0

        lax.fori_loop(0, sent_ref.shape[0] // ROWS, send, 0)


def halves(value):
    high = value.astype(jnp.bfloat16)
    return high, (value - high.astype(jnp.float32)).astype(jnp.bfloat16)


def between_kernel(planes, tiles, u2_ref, same_hbm, other_hbm, out_ref, split_ref, theta_ref, sems):
    chips = same_hbm.shape[0]
    copies = [
        pltpu.make_async_copy(same_hbm, theta_ref.at[pl.ds(0, chips)], sems.at[0]),
        pltpu.make_async_copy(other_hbm, theta_ref.at[pl.ds(chips, chips)], sems.at[1]),
    ]
    for copy in copies:
        copy.start()
    stride = planes * tiles
    members = theta_ref.shape[0] * ROWS

    def store(x):
        for tile in range(tiles):
            rows = pl.ds((x // ROWS) * tiles * ROWS + x % ROWS + tile * ROWS, ROWS, stride=stride)
            out_ref[rows, :] = u2_ref[x * tiles + tile]

    each(0, planes, 4, store)
    for copy in copies:
        copy.wait()

    def split(slot):
        high, low = halves(theta_ref[:, slot].reshape(members, LANES))
        split_ref[slot, :members, :] = high
        split_ref[slot, members:, :] = low

    each(0, split_ref.shape[0], 4, split)


def stacked(value):
    high, low = halves(value)
    return jnp.concatenate([high.astype(jnp.float32), low.astype(jnp.float32)], axis=0).astype(jnp.bfloat16)


def fold(both):
    return both[:ROWS] + both[ROWS:]


def dot(left, right, over):
    return lax.dot_general(left, right, (((1,), (over,)), ((), ())), preferred_element_type=jnp.float32)


def update_kernel(slabs, planes, tiles, place_ref, count_ref, cells_hbm, probes_hbm, level_hbm,
                  near_ref, far_ref, before_2_ref, before_ref, own_ref, after_ref, after_2_ref, split_hbm, t_hbm,
                  post_ref, gain_ref, reach, cells_ref, probes_ref, level_ref, split_ref, sems):
    chips, blocks = near_ref.shape[0] // slabs, near_ref.shape[1]
    members = 2 * chips * ROWS
    share = 1.0 / (members - 1)
    copies = [
        pltpu.make_async_copy(source, target, sems.at[at])
        for at, (source, target) in enumerate((
            (cells_hbm, cells_ref), (probes_hbm, probes_ref), (level_hbm, level_ref),
            (split_hbm, split_ref), (t_hbm, post_ref)))
    ]
    for copy in copies:
        copy.start()
    slab, chip = place_ref[0], place_ref[1]
    halo = 4 * tiles + 1
    seen = ((before_2_ref, 0), (before_ref, halo), (own_ref, 0), (after_ref, halo), (after_2_ref, 0))

    def extra(d, at):
        ref, first = seen[d]
        return ref[first + blocks + at // ROWS, at % ROWS : at % ROWS + 1, :]

    def wide(row):
        return row[:, :members] if members <= LANES else jnp.concatenate([row] * (members // LANES), axis=1)

    anomaly, scaled, variance, matches = [], [], [], []
    for d in range(5):
        wanted = slab + d - 2
        at = jnp.clip(wanted, 0, slabs - 1)
        live = jnp.where((wanted >= 0) & (wanted < slabs), 1.0, 0.0)
        for b in range(blocks):
            predicted = jnp.concatenate(
                [ref[pl.ds(at * chips, chips), b].reshape(members // 2, LANES) for ref in (near_ref, far_ref)], axis=0
            )
            mean = jnp.sum(predicted, axis=0, keepdims=True) / members
            anomaly.append(halves((predicted - mean) * live))
            variance.append(extra(d, blocks + b) + (1.0 - live))
            noise = seen[d][0][seen[d][1] + b]
            scaled.append((extra(d, b) + noise - near_ref[at * chips + chip, b]) / variance[-1] * live)
            left = stacked(scaled[-1])
            high, low = anomaly[-1]
            matches.append(fold(dot(left, high, 1) + dot(left, low, 1)))
    for d in range(1, 4):
        for i in range(blocks):
            total = jnp.zeros((ROWS, members), jnp.float32)
            for j in range(3 * blocks):
                level = extra(d, 2 * blocks + i * 3 * blocks + j) / 256.0 * share
                total = total + wide(level) * matches[(d - 1) * blocks + j]
            high, low = anomaly[d * blocks + i]
            left = stacked(total)
            correction = fold(dot(left, high, 0) + dot(left, low, 0))
            gain = scaled[d * blocks + i] - correction / variance[d * blocks + i]
            if d == 2:
                gain_ref[:, i * LANES : (i + 1) * LANES] = gain
            left = stacked(gain)
            both = stacked(fold(dot(left, high, 1) + dot(left, low, 1)))
            reach[(d - 1) * blocks + i] = jnp.concatenate([both, both], axis=1)
    for copy in copies:
        copy.wait()
    for slot in range(split_ref.shape[0]):
        weight = jnp.where(slot < count_ref[0], level_ref[0, slot].astype(jnp.float32) / 256.0, 0.0) * share
        change = fold(dot(reach[probes_ref[0, slot]], split_ref[slot], 0)) * weight
        block = cells_ref[0, slot]
        rows = pl.ds(row_of(block // tiles, block % tiles, tiles), ROWS, stride=planes * tiles)
        post_ref[rows, :] = post_ref[rows, :] + change


def shards(
    starting_speed_field,
    sample_fluidity_exponent,
    observed,
    obs_noise,
    obs_var,
    probe_cells,
    pair_cells,
    pair_probes,
    pair_taper,
    pair_counts,
    probe_taper,
):
    shape = starting_speed_field.shape
    members, planes, cells = shape
    tiles = cells // LANES
    slots = pair_cells.shape[1]
    probes = obs_noise.shape[1]
    blocks = probes // LANES
    slabs, chips = lax.axis_size("space"), lax.axis_size("chip")
    groups = 2 * chips
    f32, i32 = jnp.float32, jnp.int32
    u_rows = to_rows(starting_speed_field)
    t_rows = to_rows(sample_fluidity_exponent)
    obs_tiles = blocks - (-(2 * blocks + probe_taper.shape[1] * probe_taper.shape[2]) // ROWS)
    edge = jax.ShapeDtypeStruct((4 * tiles + 1 + obs_tiles, ROWS, LANES), f32)
    obs_shape = jax.ShapeDtypeStruct((obs_tiles, ROWS, LANES), f32)
    params = pltpu.CompilerParams(vmem_limit_bytes=32 * 1024 * 1024)
    stack = pltpu.VMEM((planes * tiles, ROWS, LANES), f32)
    low, high, obs, t_near, picked = pl.pallas_call(
        functools.partial(pack_kernel, planes, tiles),
        out_shape=(
            edge,
            edge,
            obs_shape,
            jax.ShapeDtypeStruct(u_rows.shape, f32),
            pltpu.HBM((chips, slots, ROWS, LANES), f32),
        ),
        in_specs=[HBM] * 7,
        out_specs=(VMEM,) * 4 + (HBM,),
        scratch_shapes=[
            pltpu.SMEM(pair_cells.shape, i32),
            pltpu.SMEM(probe_taper.shape, i32),
            pltpu.VMEM(u_rows.shape, f32),
            pltpu.VMEM((ROWS, probes), f32),
            pltpu.VMEM((2, probes), f32),
            pltpu.VMEM((slots, ROWS, LANES), f32),
            pltpu.SemaphoreType.DMA((7 + chips,)),
        ],
        compiler_params=params,
        name="pack",
    )(*map(stay, (pair_cells, probe_taper, u_rows, t_rows, obs_noise, observed.reshape(1, -1), obs_var.reshape(1, -1))))
    upward = [(i, i + 1) for i in range(slabs - 1)]
    before = lax.ppermute(high, "space", upward)
    after = lax.ppermute(low, "space", [(j, i) for i, j in upward])
    if slabs == 4:
        before_2 = after_2 = lax.ppermute(obs, "space", [(i, (i + 2) % 4) for i in range(4)])
    else:
        upward_2 = [(i, i + 2) for i in range(slabs - 2)]
        before_2 = lax.ppermute(obs, "space", upward_2)
        after_2 = lax.ppermute(obs, "space", [(j, i) for i, j in upward_2])
    theta_same = lax.all_to_all(picked, "chip", 0, 0)
    inner, edges = pl.pallas_call(
        functools.partial(inner_kernel, planes, tiles),
        out_shape=(
            jax.ShapeDtypeStruct((planes * tiles, ROWS, LANES), f32),
            jax.ShapeDtypeStruct((14 * tiles, ROWS, LANES), f32),
        ),
        in_specs=[HBM, VMEM],
        out_specs=(VMEM,) * 2,
        scratch_shapes=[
            pltpu.VMEM(u_rows.shape, f32),
            stack,
            stack,
            stack,
            pltpu.VMEM((5, planes * tiles, ROWS, LANES), f32),
            pltpu.SemaphoreType.DMA(()),
        ],
        compiler_params=params,
        cost_estimate=pl.CostEstimate(flops=0, bytes_accessed=15_000_000, transcendentals=0),
        name="inner_planes",
    )(stay(u_rows), t_near)
    u2, sent, theta_same = pl.pallas_call(
        functools.partial(outer_kernel, planes, tiles),
        out_shape=(
            jax.ShapeDtypeStruct((planes * tiles, ROWS, LANES), f32),
            jax.ShapeDtypeStruct((slabs * chips, blocks, ROWS, LANES), f32),
            pltpu.HBM(picked.shape, f32),
        ),
        in_specs=[HBM] + [VMEM] * 4 + [HBM],
        out_specs=(VMEM, VMEM, HBM),
        scratch_shapes=[pltpu.SMEM(probe_cells.shape, i32), pltpu.SemaphoreType.DMA(())],
        input_output_aliases={4: 0, 5: 2},
        compiler_params=params,
        cost_estimate=pl.CostEstimate(flops=0, bytes_accessed=26_000_000, transcendentals=0),
        name="outer_planes",
    )(stay(probe_cells), before, after, edges, inner, stay(theta_same))
    pred_near = lax.all_to_all(sent, ("space", "chip"), 0, 0)
    swap = [(0, 1), (1, 0)]
    theta_other = lax.ppermute(theta_same, "core", swap)
    pred_far = lax.ppermute(pred_near, "core", swap)
    place = jnp.stack([lax.axis_index("space"), lax.axis_index("chip")]).astype(i32)
    u2_rows, split = pl.pallas_call(
        functools.partial(between_kernel, planes, tiles),
        out_shape=(
            jax.ShapeDtypeStruct(u_rows.shape, f32),
            pltpu.HBM((slots, 2 * groups * ROWS, LANES), jnp.bfloat16),
        ),
        in_specs=[VMEM, HBM, HBM],
        out_specs=(VMEM,) * 2,
        scratch_shapes=[pltpu.VMEM((groups, slots, ROWS, LANES), f32), pltpu.SemaphoreType.DMA((2,))],
        compiler_params=params,
        cost_estimate=pl.CostEstimate(flops=1_000_000, bytes_accessed=8_000_000, transcendentals=0),
        name="between",
    )(u2, stay(theta_same), stay(theta_other))
    post_rows, gain = pl.pallas_call(
        functools.partial(update_kernel, slabs, planes, tiles),
        out_shape=(
            jax.ShapeDtypeStruct(u_rows.shape, f32),
            jax.ShapeDtypeStruct((members, probes), f32),
        ),
        in_specs=[SMEM] * 2 + [HBM] * 3 + [VMEM] * 7 + [HBM] * 2,
        out_specs=(VMEM,) * 2,
        scratch_shapes=[
            pltpu.VMEM((probe_taper.shape[2], 2 * ROWS, 2 * groups * ROWS), jnp.bfloat16),
            pltpu.SMEM(pair_cells.shape, i32),
            pltpu.SMEM(pair_cells.shape, i32),
            pltpu.SMEM(pair_cells.shape, i32),
            pltpu.VMEM(split.shape, jnp.bfloat16),
            pltpu.SemaphoreType.DMA((5,)),
        ],
        compiler_params=params,
        name="update",
    )(place, pair_counts, *map(stay, (pair_cells, pair_probes, pair_taper)), pred_near, pred_far,
      before_2, before, obs, after, after_2, stay(split), stay(t_rows))
    return (from_rows(u2_rows, shape), from_rows(post_rows, shape), gain)


def solution(mesh):
    slabs, groups = mesh.devices.shape
    split = jax.sharding.Mesh(mesh.devices.reshape(slabs, groups // 2, 2), ("space", "chip", "core"))
    members = ("chip", "core")
    return jax.shard_map(
        shards,
        mesh=split,
        in_specs=(
            P(members, "space", None),
            P(members, "space", None),
            P("space"),
            P(members, "space"),
            P("space"),
            P("space"),
            P("space", None),
            P("space", None),
            P("space", None),
            P("space"),
            P("space", None, None),
        ),
        out_specs=(P(members, "space", None), P(members, "space", None), P(members, "space")),
        check_vma=False,
    )
```

```python
import functools

import jax
import jax.numpy as jnp
from jax import lax
from jax.experimental import pallas as pl
from jax.experimental.pallas import tpu as pltpu
from jax.sharding import PartitionSpec as P

LANES = 128
ROWS = 8
NZ = 64
HALF_DT = 0.5 * 0.08

VMEM = pl.BlockSpec(memory_space=pltpu.VMEM)
SMEM = pl.BlockSpec(memory_space=pltpu.SMEM)
HBM = pl.BlockSpec(memory_space=pltpu.HBM)


def stay(array):
    return pltpu.with_memory_space_constraint(array, pltpu.HBM)


def to_rows(array):
    members, planes, cells = array.shape
    split = array.reshape(members, planes // ROWS, ROWS, cells // LANES, LANES)
    return split.transpose(0, 1, 3, 2, 4).reshape(-1, LANES)


def from_rows(rows, shape):
    members, planes, cells = shape
    split = rows.reshape(members, planes // ROWS, cells // LANES, ROWS, LANES)
    return split.transpose(0, 1, 3, 2, 4).reshape(shape)


def row_of(plane, tile, tiles):
    return (plane // ROWS * tiles + tile) * ROWS + plane % ROWS


def pack_kernel(planes, tiles, cells_hbm, taper_hbm, u_hbm, t_hbm, noise_hbm, observed_hbm, var_hbm,
                low_ref, high_ref, obs_ref, t_ref, pick_hbm,
                cells_ref, taper_ref, u_ref, noise_ref, row_ref, pick_ref, sems):
    stride = planes * tiles
    blocks = noise_ref.shape[1] // LANES
    copies = [
        pltpu.make_async_copy(source, target, sems.at[at])
        for at, (source, target) in enumerate((
            (cells_hbm, cells_ref),
            (t_hbm, t_ref),
            (u_hbm, u_ref),
            (taper_hbm, taper_ref),
            (noise_hbm, noise_ref),
            (observed_hbm, row_ref.at[0:1]),
            (var_hbm, row_ref.at[1:2]),
        ))
    ]
    for copy in copies:
        copy.start()
    copies[0].wait()
    copies[1].wait()
    for slot in range(pick_ref.shape[0]):
        block = cells_ref[0, slot]
        row = row_of(block // tiles, block % tiles, tiles)
        pick_ref[slot] = t_ref[pl.ds(row, ROWS, stride=stride), :]
    picks = [
        pltpu.make_async_copy(pick_ref, pick_hbm.at[device], sems.at[len(copies) + device])
        for device in range(pick_hbm.shape[0])
    ]
    for copy in picks:
        copy.start()
    for kind, source in ((1, t_ref), (0, u_ref)):
        if kind == 0:
            copies[2].wait()
        for out_ref, first in ((high_ref, planes - 2), (low_ref, 0)):
            for depth in range(2):
                for tile in range(tiles):
                    out_ref[(kind * 2 + depth) * tiles + tile] = source[
                        pl.ds(row_of(first + depth, tile, tiles), ROWS, stride=stride), :
                    ]
    for ref in (low_ref, high_ref):
        ref[4 * tiles] = jnp.ones((ROWS, LANES), jnp.float32)
    for copy in copies[3:]:
        copy.wait()
    own, window = taper_ref.shape[1:]
    rows = [row_ref[kind : kind + 1, b * LANES : (b + 1) * LANES] for kind in range(2) for b in range(blocks)]
    for i in range(own):
        for j in range(window):
            rows.append(jnp.full((1, LANES), taper_ref[0, i, j].astype(jnp.float32), jnp.float32))
    for b in range(blocks):
        obs_ref[b] = noise_ref[:, b * LANES : (b + 1) * LANES]
    for at, row in enumerate(rows):
        obs_ref[blocks + at // ROWS, at % ROWS : at % ROWS + 1, :] = row
    for ref in (low_ref, high_ref):
        for at in range(obs_ref.shape[0]):
            ref[4 * tiles + 1 + at] = obs_ref[at]
    for copy in picks:
        copy.wait()


def rot(value, by):
    return pltpu.roll(value, by % LANES, 1)


def lane_masks():
    lane = lax.broadcasted_iota(jnp.int32, (ROWS, LANES), 1)
    height = lane & (NZ - 1)
    return lane < NZ, height == 0, height == NZ - 1


def coefficients(masks, low, here, high):
    first_half, floor, roof = masks
    tiles = len(here)
    turned = [rot(value, NZ) for value in here]
    out = []
    for tile in range(tiles):
        mid = here[tile]
        near = mid + turned[tile]
        far = mid + jnp.where(first_half, turned[tile - 1], turned[(tile + 1) % tiles])
        up = mid + jnp.where(roof, HALF_DT, rot(mid, -1))
        down = mid + jnp.where(floor, HALF_DT, rot(mid, 1))
        below = mid + low[tile]
        above = mid + high[tile]
        diag = 1.0 - ((near + far) + (up + down) + (below + above))
        out.append((diag, near, far, jnp.where(roof, 0.0, up), jnp.where(floor, 0.0, down), below, above))
    return out


def step(masks, weights, low, here, high):
    first_half = masks[0]
    tiles = len(here)
    turned = [rot(value, NZ) for value in here]
    out = []
    for tile in range(tiles):
        diag, near, far, up, down, below, above = weights[tile]
        mid = here[tile]
        beyond = jnp.where(first_half, turned[tile - 1], turned[(tile + 1) % tiles])
        out.append(
            (diag * mid + near * turned[tile])
            + (far * beyond + up * rot(mid, -1))
            + (down * rot(mid, 1) + below * low[tile])
            + above * high[tile]
        )
    return out


def plane_of(ref, at, tiles):
    return [ref[at * tiles + tile] for tile in range(tiles)]


def put(ref, at, values):
    for tile, value in enumerate(values):
        ref[at * len(values) + tile] = value


def each(first, last, unroll, body):
    count = (last - first) // unroll

    def several(at, _):
        for d in range(unroll):
            body(first + at * unroll + d)
        return 0

    lax.fori_loop(0, count, several, 0)
    for x in range(first + count * unroll, last):
        body(x)


def inner_kernel(planes, tiles, u_hbm, t_ref, u2_ref, edge_ref, u_ref, u0, hv, u1, held, sem):
    stride = planes * tiles
    masks = lane_masks()
    copy = pltpu.make_async_copy(u_hbm, u_ref, sem)
    copy.start()

    def rows_at(x, tile):
        return pl.ds((x // ROWS) * tiles * ROWS + x % ROWS + tile * ROWS, ROWS, stride=stride)

    def load_t(x):
        for tile in range(tiles):
            hv[x * tiles + tile] = HALF_DT * jnp.exp(t_ref[rows_at(x, tile), :])

    def load_u(x):
        for tile in range(tiles):
            u0[x * tiles + tile] = u_ref[rows_at(x, tile), :]

    def first_step(x):
        weights = coefficients(masks, *[plane_of(hv, x + d, tiles) for d in (-1, 0, 1)])
        for tile in range(tiles):
            for kind in range(5):
                held[kind, x * tiles + tile] = weights[tile][kind]
        put(u1, x, step(masks, weights, *[plane_of(u0, x + d, tiles) for d in (-1, 0, 1)]))

    def second_step(x):
        weights = []
        for tile in range(tiles):
            at = x * tiles + tile
            here = hv[at]
            weights.append([held[kind, at] for kind in range(5)] + [here + hv[at - tiles], here + hv[at + tiles]])
        put(u2_ref, x, step(masks, weights, *[plane_of(u1, x + d, tiles) for d in (-1, 0, 1)]))

    each(0, planes, 4, load_t)
    copy.wait()
    each(0, planes, 4, load_u)
    each(1, planes - 1, 7, first_step)
    each(2, planes - 2, 6, second_step)
    last = planes - 1
    at = 0
    for ref, kept in ((u0, (0, 1, last - 1, last)), (hv, (0, 1, 2, last - 2, last - 1, last)),
                      (u1, (1, 2, last - 2, last - 1))):
        for x in kept:
            put(edge_ref, at, plane_of(ref, x, tiles))
            at += 1


def outer_kernel(planes, tiles, probe_hbm, before_ref, after_ref, edge_ref, inner_ref, same_in,
                 u2_ref, sent_ref, same_out, probe_ref, sem):
    probe_copy = pltpu.make_async_copy(probe_hbm, probe_ref, sem)
    probe_copy.start()
    masks = lane_masks()
    blocks = probe_ref.shape[0] // LANES
    edge = [plane_of(edge_ref, at, tiles) for at in range(14)]
    last = planes - 1
    for ref, own_u, own_v, own_1, where in (
        (before_ref, edge[0:2], edge[4:7], edge[10:12], (0, 1)),
        (after_ref, edge[3:1:-1], edge[9:6:-1], edge[13:11:-1], (last, last - 1)),
    ):
        order = (0, 1) if ref is before_ref else (1, 0)
        u = [plane_of(ref, d, tiles) for d in order] + own_u
        v = [[HALF_DT * jnp.exp(t) for t in plane_of(ref, 2 + d, tiles)] for d in order] + own_v
        live = ref[4 * tiles]
        weights = [coefficients(masks, v[d], v[d + 1], v[d + 2]) for d in range(3)]
        next_u = [step(masks, weights[d], u[d], u[d + 1], u[d + 2]) for d in range(2)]
        next_u[0] = [value * live for value in next_u[0]]
        next_u = next_u + own_1
        for d in range(2):
            put(u2_ref, where[d], step(masks, weights[d + 1], next_u[d], next_u[d + 1], next_u[d + 2]))

    probe_copy.wait()
    lane = lax.broadcasted_iota(jnp.int32, (ROWS, LANES), 1)
    for part in range(blocks):
        found = jnp.zeros((ROWS, LANES), jnp.float32)
        for p in range(LANES):
            cell = probe_ref[part * LANES + p]
            turned = pltpu.roll(u2_ref[cell >> 7], (p - cell) & (LANES - 1), 1)
            found = jnp.where(lane == p, turned, found)

        def send(at, _):
            for d in range(ROWS):
                sent_ref[at * ROWS + d, part] = found
            return 0

        lax.fori_loop(0, sent_ref.shape[0] // ROWS, send, 0)


def halves(value):
    high = value.astype(jnp.bfloat16)
    return high, (value - high.astype(jnp.float32)).astype(jnp.bfloat16)


def between_kernel(planes, tiles, place_ref, u2_ref, same_hbm, other_hbm, out_ref, split_ref, theta_ref, sems):
    core = place_ref[2]
    copies = [
        pltpu.make_async_copy(same_hbm, theta_ref.at[:, core], sems.at[0]),
        pltpu.make_async_copy(other_hbm, theta_ref.at[:, 1 - core], sems.at[1]),
    ]
    for copy in copies:
        copy.start()
    stride = planes * tiles
    members = 2 * theta_ref.shape[0] * ROWS

    def store(x):
        for tile in range(tiles):
            rows = pl.ds((x // ROWS) * tiles * ROWS + x % ROWS + tile * ROWS, ROWS, stride=stride)
            out_ref[rows, :] = u2_ref[x * tiles + tile]

    each(0, planes, 4, store)
    for copy in copies:
        copy.wait()

    def split(slot):
        high, low = halves(theta_ref[:, :, slot].reshape(members, LANES))
        split_ref[slot, :members, :] = high
        split_ref[slot, members:, :] = low

    each(0, split_ref.shape[0], 4, split)


def stacked(value):
    high, low = halves(value)
    return jnp.concatenate([high.astype(jnp.float32), low.astype(jnp.float32)], axis=0).astype(jnp.bfloat16)


def fold(both):
    return both[:ROWS] + both[ROWS:]


def dot(left, right, over):
    return lax.dot_general(left, right, (((1,), (over,)), ((), ())), preferred_element_type=jnp.float32)


def update_kernel(slabs, planes, tiles, place_ref, count_ref, cells_hbm, probes_hbm, level_hbm,
                  pred_ref, before_2_ref, before_ref, own_ref, after_ref, after_2_ref, split_hbm, t_hbm,
                  post_ref, gain_ref, reach, cells_ref, probes_ref, level_ref, split_ref, sems):
    groups, blocks = pred_ref.shape[0] // slabs, pred_ref.shape[1]
    members = groups * ROWS
    share = 1.0 / (members - 1)
    copies = [
        pltpu.make_async_copy(source, target, sems.at[at])
        for at, (source, target) in enumerate((
            (cells_hbm, cells_ref), (probes_hbm, probes_ref), (level_hbm, level_ref),
            (split_hbm, split_ref), (t_hbm, post_ref)))
    ]
    for copy in copies:
        copy.start()
    slab, group = place_ref[0], place_ref[1]
    halo = 4 * tiles + 1
    seen = ((before_2_ref, 0), (before_ref, halo), (own_ref, 0), (after_ref, halo), (after_2_ref, 0))

    def extra(d, at):
        ref, first = seen[d]
        return ref[first + blocks + at // ROWS, at % ROWS : at % ROWS + 1, :]

    def wide(row):
        return row[:, :members] if members <= LANES else jnp.concatenate([row] * (members // LANES), axis=1)

    anomaly, scaled, variance, matches = [], [], [], []
    for d in range(5):
        wanted = slab + d - 2
        at = jnp.clip(wanted, 0, slabs - 1)
        live = jnp.where((wanted >= 0) & (wanted < slabs), 1.0, 0.0)
        for b in range(blocks):
            predicted = pred_ref[pl.ds(at * groups, groups), b].reshape(members, LANES)
            mean = jnp.sum(predicted, axis=0, keepdims=True) / members
            anomaly.append(halves((predicted - mean) * live))
            variance.append(extra(d, blocks + b) + (1.0 - live))
            noise = seen[d][0][seen[d][1] + b]
            scaled.append((extra(d, b) + noise - pred_ref[at * groups + group, b]) / variance[-1] * live)
            left = stacked(scaled[-1])
            high, low = anomaly[-1]
            matches.append(fold(dot(left, high, 1) + dot(left, low, 1)))
    for d in range(1, 4):
        for i in range(blocks):
            total = jnp.zeros((ROWS, members), jnp.float32)
            for j in range(3 * blocks):
                level = extra(d, 2 * blocks + i * 3 * blocks + j) / 256.0 * share
                total = total + wide(level) * matches[(d - 1) * blocks + j]
            high, low = anomaly[d * blocks + i]
            left = stacked(total)
            correction = fold(dot(left, high, 0) + dot(left, low, 0))
            gain = scaled[d * blocks + i] - correction / variance[d * blocks + i]
            if d == 2:
                gain_ref[:, i * LANES : (i + 1) * LANES] = gain
            left = stacked(gain)
            both = stacked(fold(dot(left, high, 1) + dot(left, low, 1)))
            reach[(d - 1) * blocks + i] = jnp.concatenate([both, both], axis=1)
    for copy in copies:
        copy.wait()
    for slot in range(split_ref.shape[0]):
        weight = jnp.where(slot < count_ref[0], level_ref[0, slot].astype(jnp.float32) / 256.0, 0.0) * share
        change = fold(dot(reach[probes_ref[0, slot]], split_ref[slot], 0)) * weight
        block = cells_ref[0, slot]
        rows = pl.ds(row_of(block // tiles, block % tiles, tiles), ROWS, stride=planes * tiles)
        post_ref[rows, :] = post_ref[rows, :] + change


def shards(
    starting_speed_field,
    sample_fluidity_exponent,
    observed,
    obs_noise,
    obs_var,
    probe_cells,
    pair_cells,
    pair_probes,
    pair_taper,
    pair_counts,
    probe_taper,
):
    shape = starting_speed_field.shape
    members, planes, cells = shape
    tiles = cells // LANES
    slots = pair_cells.shape[1]
    probes = obs_noise.shape[1]
    blocks = probes // LANES
    slabs, chips = lax.axis_size("space"), lax.axis_size("chip")
    groups = 2 * chips
    f32, i32 = jnp.float32, jnp.int32
    u_rows = to_rows(starting_speed_field)
    t_rows = to_rows(sample_fluidity_exponent)
    obs_tiles = blocks - (-(2 * blocks + probe_taper.shape[1] * probe_taper.shape[2]) // ROWS)
    edge = jax.ShapeDtypeStruct((4 * tiles + 1 + obs_tiles, ROWS, LANES), f32)
    obs_shape = jax.ShapeDtypeStruct((obs_tiles, ROWS, LANES), f32)
    params = pltpu.CompilerParams(vmem_limit_bytes=32 * 1024 * 1024)
    stack = pltpu.VMEM((planes * tiles, ROWS, LANES), f32)
    low, high, obs, t_near, picked = pl.pallas_call(
        functools.partial(pack_kernel, planes, tiles),
        out_shape=(
            edge,
            edge,
            obs_shape,
            jax.ShapeDtypeStruct(u_rows.shape, f32),
            pltpu.HBM((chips, slots, ROWS, LANES), f32),
        ),
        in_specs=[HBM] * 7,
        out_specs=(VMEM,) * 4 + (HBM,),
        scratch_shapes=[
            pltpu.SMEM(pair_cells.shape, i32),
            pltpu.SMEM(probe_taper.shape, i32),
            pltpu.VMEM(u_rows.shape, f32),
            pltpu.VMEM((ROWS, probes), f32),
            pltpu.VMEM((2, probes), f32),
            pltpu.VMEM((slots, ROWS, LANES), f32),
            pltpu.SemaphoreType.DMA((7 + chips,)),
        ],
        compiler_params=params,
        name="pack",
    )(*map(stay, (pair_cells, probe_taper, u_rows, t_rows, obs_noise, observed.reshape(1, -1), obs_var.reshape(1, -1))))
    upward = [(i, i + 1) for i in range(slabs - 1)]
    before = lax.ppermute(high, "space", upward)
    after = lax.ppermute(low, "space", [(j, i) for i, j in upward])
    if slabs == 4:
        before_2 = after_2 = lax.ppermute(obs, "space", [(i, (i + 2) % 4) for i in range(4)])
    else:
        upward_2 = [(i, i + 2) for i in range(slabs - 2)]
        before_2 = lax.ppermute(obs, "space", upward_2)
        after_2 = lax.ppermute(obs, "space", [(j, i) for i, j in upward_2])
    theta_same = lax.all_to_all(picked, "chip", 0, 0)
    inner, edges = pl.pallas_call(
        functools.partial(inner_kernel, planes, tiles),
        out_shape=(
            jax.ShapeDtypeStruct((planes * tiles, ROWS, LANES), f32),
            jax.ShapeDtypeStruct((14 * tiles, ROWS, LANES), f32),
        ),
        in_specs=[HBM, VMEM],
        out_specs=(VMEM,) * 2,
        scratch_shapes=[
            pltpu.VMEM(u_rows.shape, f32),
            stack,
            stack,
            stack,
            pltpu.VMEM((5, planes * tiles, ROWS, LANES), f32),
            pltpu.SemaphoreType.DMA(()),
        ],
        compiler_params=params,
        cost_estimate=pl.CostEstimate(flops=0, bytes_accessed=400_000_000, transcendentals=0),
        name="inner_planes",
    )(stay(u_rows), t_near)
    u2, sent, theta_same = pl.pallas_call(
        functools.partial(outer_kernel, planes, tiles),
        out_shape=(
            jax.ShapeDtypeStruct((planes * tiles, ROWS, LANES), f32),
            jax.ShapeDtypeStruct((slabs * groups, blocks, ROWS, LANES), f32),
            pltpu.HBM(picked.shape, f32),
        ),
        in_specs=[HBM] + [VMEM] * 4 + [HBM],
        out_specs=(VMEM, VMEM, HBM),
        scratch_shapes=[pltpu.SMEM(probe_cells.shape, i32), pltpu.SemaphoreType.DMA(())],
        input_output_aliases={4: 0, 5: 2},
        compiler_params=params,
        cost_estimate=pl.CostEstimate(flops=0, bytes_accessed=26_000_000, transcendentals=0),
        name="outer_planes",
    )(stay(probe_cells), before, after, edges, inner, stay(theta_same))
    pred_all = lax.all_to_all(sent, ("space", "chip", "core"), 0, 0)
    theta_other = lax.ppermute(theta_same, "core", [(0, 1), (1, 0)])
    place = jnp.stack([lax.axis_index("space"), lax.axis_index(("chip", "core")), lax.axis_index("core")]).astype(i32)
    u2_rows, split = pl.pallas_call(
        functools.partial(between_kernel, planes, tiles),
        out_shape=(
            jax.ShapeDtypeStruct(u_rows.shape, f32),
            pltpu.HBM((slots, 2 * groups * ROWS, LANES), jnp.bfloat16),
        ),
        in_specs=[SMEM, VMEM, HBM, HBM],
        out_specs=(VMEM,) * 2,
        scratch_shapes=[pltpu.VMEM((chips, 2, slots, ROWS, LANES), f32), pltpu.SemaphoreType.DMA((2,))],
        compiler_params=params,
        cost_estimate=pl.CostEstimate(flops=1_000_000, bytes_accessed=8_000_000, transcendentals=0),
        name="between",
    )(place, u2, stay(theta_same), stay(theta_other))
    post_rows, gain = pl.pallas_call(
        functools.partial(update_kernel, slabs, planes, tiles),
        out_shape=(
            jax.ShapeDtypeStruct(u_rows.shape, f32),
            jax.ShapeDtypeStruct((members, probes), f32),
        ),
        in_specs=[SMEM] * 2 + [HBM] * 3 + [VMEM] * 6 + [HBM] * 2,
        out_specs=(VMEM,) * 2,
        scratch_shapes=[
            pltpu.VMEM((probe_taper.shape[2], 2 * ROWS, 2 * groups * ROWS), jnp.bfloat16),
            pltpu.SMEM(pair_cells.shape, i32),
            pltpu.SMEM(pair_cells.shape, i32),
            pltpu.SMEM(pair_cells.shape, i32),
            pltpu.VMEM(split.shape, jnp.bfloat16),
            pltpu.SemaphoreType.DMA((5,)),
        ],
        compiler_params=params,
        name="update",
    )(place, pair_counts, *map(stay, (pair_cells, pair_probes, pair_taper)), pred_all,
      before_2, before, obs, after, after_2, stay(split), stay(t_rows))
    return (from_rows(u2_rows, shape), from_rows(post_rows, shape), gain)


def solution(mesh):
    slabs, groups = mesh.devices.shape
    split = jax.sharding.Mesh(mesh.devices.reshape(slabs, groups // 2, 2), ("space", "chip", "core"))
    members = ("chip", "core")
    return jax.shard_map(
        shards,
        mesh=split,
        in_specs=(
            P(members, "space", None),
            P(members, "space", None),
            P("space"),
            P(members, "space"),
            P("space"),
            P("space"),
            P("space", None),
            P("space", None),
            P("space", None),
            P("space"),
            P("space", None, None),
        ),
        out_specs=(P(members, "space", None), P(members, "space", None), P(members, "space")),
        check_vma=False,
    )
```

```python
import functools

import jax
import jax.numpy as jnp
from jax import lax
from jax.experimental import pallas as pl
from jax.experimental.pallas import tpu as pltpu
from jax.sharding import PartitionSpec as P

LANES = 128
ROWS = 8
NZ = 64
HALF_DT = 0.5 * 0.08

VMEM = pl.BlockSpec(memory_space=pltpu.VMEM)
SMEM = pl.BlockSpec(memory_space=pltpu.SMEM)
HBM = pl.BlockSpec(memory_space=pltpu.HBM)
ANY = pl.BlockSpec(memory_space=pl.ANY)


def stay(array):
    return pltpu.with_memory_space_constraint(array, pltpu.HBM)


def to_rows(array):
    members, planes, cells = array.shape
    split = array.reshape(members, planes // ROWS, ROWS, cells // LANES, LANES)
    return split.transpose(0, 1, 3, 2, 4).reshape(-1, LANES)


def from_rows(rows, shape):
    members, planes, cells = shape
    split = rows.reshape(members, planes // ROWS, cells // LANES, ROWS, LANES)
    return split.transpose(0, 1, 3, 2, 4).reshape(shape)


def row_of(plane, tile, tiles):
    return (plane // ROWS * tiles + tile) * ROWS + plane % ROWS


def pack_kernel(planes, tiles, taper_hbm, u_hbm, t_hbm, noise_hbm, observed_hbm, var_hbm,
                low_ref, high_ref, obs_ref, t_ref, taper_ref, u_ref, noise_ref, row_ref, sems):
    stride = planes * tiles
    blocks = noise_ref.shape[1] // LANES
    copies = [
        pltpu.make_async_copy(source, target, sems.at[at])
        for at, (source, target) in enumerate((
            (t_hbm, t_ref),
            (u_hbm, u_ref),
            (taper_hbm, taper_ref),
            (noise_hbm, noise_ref),
            (observed_hbm, row_ref.at[0:1]),
            (var_hbm, row_ref.at[1:2]),
        ))
    ]
    for copy in copies:
        copy.start()
    for kind, source in ((1, t_ref), (0, u_ref)):
        copies[1 - kind].wait()
        for out_ref, first in ((high_ref, planes - 2), (low_ref, 0)):
            for depth in range(2):
                for tile in range(tiles):
                    out_ref[(kind * 2 + depth) * tiles + tile] = source[
                        pl.ds(row_of(first + depth, tile, tiles), ROWS, stride=stride), :
                    ]
    for ref in (low_ref, high_ref):
        ref[4 * tiles] = jnp.ones((ROWS, LANES), jnp.float32)
    for copy in copies[2:]:
        copy.wait()
    own, window = taper_ref.shape[1:]
    rows = [row_ref[kind : kind + 1, b * LANES : (b + 1) * LANES] for kind in range(2) for b in range(blocks)]
    for i in range(own):
        for j in range(window):
            rows.append(jnp.full((1, LANES), taper_ref[0, i, j].astype(jnp.float32), jnp.float32))
    for b in range(blocks):
        obs_ref[b] = noise_ref[:, b * LANES : (b + 1) * LANES]
    for at, row in enumerate(rows):
        obs_ref[blocks + at // ROWS, at % ROWS : at % ROWS + 1, :] = row
    for ref in (low_ref, high_ref):
        for at in range(obs_ref.shape[0]):
            ref[4 * tiles + 1 + at] = obs_ref[at]


def rot(value, by):
    return pltpu.roll(value, by % LANES, 1)


def lane_masks():
    lane = lax.broadcasted_iota(jnp.int32, (ROWS, LANES), 1)
    height = lane & (NZ - 1)
    return lane < NZ, height == 0, height == NZ - 1


def coefficients(masks, low, here, high):
    first_half, floor, roof = masks
    tiles = len(here)
    turned = [rot(value, NZ) for value in here]
    out = []
    for tile in range(tiles):
        mid = here[tile]
        near = mid + turned[tile]
        far = mid + jnp.where(first_half, turned[tile - 1], turned[(tile + 1) % tiles])
        up = mid + jnp.where(roof, HALF_DT, rot(mid, -1))
        down = mid + jnp.where(floor, HALF_DT, rot(mid, 1))
        below = mid + low[tile]
        above = mid + high[tile]
        diag = 1.0 - ((near + far) + (up + down) + (below + above))
        out.append((diag, near, far, jnp.where(roof, 0.0, up), jnp.where(floor, 0.0, down), below, above))
    return out


def step(masks, weights, low, here, high):
    first_half = masks[0]
    tiles = len(here)
    turned = [rot(value, NZ) for value in here]
    out = []
    for tile in range(tiles):
        diag, near, far, up, down, below, above = weights[tile]
        mid = here[tile]
        beyond = jnp.where(first_half, turned[tile - 1], turned[(tile + 1) % tiles])
        out.append(
            (diag * mid + near * turned[tile])
            + (far * beyond + up * rot(mid, -1))
            + (down * rot(mid, 1) + below * low[tile])
            + above * high[tile]
        )
    return out


def plane_of(ref, at, tiles):
    return [ref[at * tiles + tile] for tile in range(tiles)]


def put(ref, at, values):
    for tile, value in enumerate(values):
        ref[at * len(values) + tile] = value


def each(first, last, unroll, body):
    count = (last - first) // unroll

    def several(at, _):
        for d in range(unroll):
            body(first + at * unroll + d)
        return 0

    lax.fori_loop(0, count, several, 0)
    for x in range(first + count * unroll, last):
        body(x)


def inner_kernel(planes, tiles, u_hbm, cells_hbm, t_ref, u2_ref, edge_ref, pick_hbm,
                 u_ref, u0, hv, u1, held, cells_ref, pick_ref, sems):
    stride = planes * tiles
    masks = lane_masks()
    copy = pltpu.make_async_copy(u_hbm, u_ref, sems.at[0])
    cells_copy = pltpu.make_async_copy(cells_hbm, cells_ref, sems.at[1])
    picked = pltpu.make_async_copy(pick_ref, pick_hbm, sems.at[2])
    cells_copy.start()
    copy.start()

    def rows_at(x, tile):
        return pl.ds((x // ROWS) * tiles * ROWS + x % ROWS + tile * ROWS, ROWS, stride=stride)

    def load_t(x):
        for tile in range(tiles):
            hv[x * tiles + tile] = HALF_DT * jnp.exp(t_ref[rows_at(x, tile), :])

    def load_u(x):
        for tile in range(tiles):
            u0[x * tiles + tile] = u_ref[rows_at(x, tile), :]

    def first_step(x):
        weights = coefficients(masks, *[plane_of(hv, x + d, tiles) for d in (-1, 0, 1)])
        for tile in range(tiles):
            for kind in range(5):
                held[kind, x * tiles + tile] = weights[tile][kind]
        put(u1, x, step(masks, weights, *[plane_of(u0, x + d, tiles) for d in (-1, 0, 1)]))

    def second_step(x):
        weights = []
        for tile in range(tiles):
            at = x * tiles + tile
            here = hv[at]
            weights.append([held[kind, at] for kind in range(5)] + [here + hv[at - tiles], here + hv[at + tiles]])
        put(u2_ref, x, step(masks, weights, *[plane_of(u1, x + d, tiles) for d in (-1, 0, 1)]))

    each(0, planes, 4, load_t)
    cells_copy.wait()
    for slot in range(pick_ref.shape[0]):
        block = cells_ref[0, slot]
        row = row_of(block // tiles, block % tiles, tiles)
        pick_ref[slot] = t_ref[pl.ds(row, ROWS, stride=stride), :]
    picked.start()
    copy.wait()
    each(0, planes, 4, load_u)
    each(1, planes - 1, 7, first_step)
    each(2, planes - 2, 6, second_step)
    last = planes - 1
    at = 0
    for ref, kept in ((u0, (0, 1, last - 1, last)), (hv, (0, 1, 2, last - 2, last - 1, last)),
                      (u1, (1, 2, last - 2, last - 1))):
        for x in kept:
            put(edge_ref, at, plane_of(ref, x, tiles))
            at += 1
    picked.wait()


def outer_kernel(planes, tiles, probe_hbm, before_ref, after_ref, edge_ref, inner_ref,
                 u2_ref, sent_hbm, probe_ref, found_ref, sems):
    probe_copy = pltpu.make_async_copy(probe_hbm, probe_ref, sems.at[0])
    probe_copy.start()
    masks = lane_masks()
    blocks = probe_ref.shape[0] // LANES
    edge = [plane_of(edge_ref, at, tiles) for at in range(14)]
    last = planes - 1
    for ref, own_u, own_v, own_1, where in (
        (before_ref, edge[0:2], edge[4:7], edge[10:12], (0, 1)),
        (after_ref, edge[3:1:-1], edge[9:6:-1], edge[13:11:-1], (last, last - 1)),
    ):
        order = (0, 1) if ref is before_ref else (1, 0)
        u = [plane_of(ref, d, tiles) for d in order] + own_u
        v = [[HALF_DT * jnp.exp(t) for t in plane_of(ref, 2 + d, tiles)] for d in order] + own_v
        live = ref[4 * tiles]
        weights = [coefficients(masks, v[d], v[d + 1], v[d + 2]) for d in range(3)]
        next_u = [step(masks, weights[d], u[d], u[d + 1], u[d + 2]) for d in range(2)]
        next_u[0] = [value * live for value in next_u[0]]
        next_u = next_u + own_1
        for d in range(2):
            put(u2_ref, where[d], step(masks, weights[d + 1], next_u[d], next_u[d + 1], next_u[d + 2]))

    probe_copy.wait()
    lane = lax.broadcasted_iota(jnp.int32, (ROWS, LANES), 1)
    for part in range(blocks):
        found = jnp.zeros((ROWS, LANES), jnp.float32)
        for p in range(LANES):
            cell = probe_ref[part * LANES + p]
            turned = pltpu.roll(u2_ref[cell >> 7], (p - cell) & (LANES - 1), 1)
            found = jnp.where(lane == p, turned, found)

        found_ref[part] = found

    def send(device, _):
        pltpu.make_async_copy(found_ref, sent_hbm.at[device], sems.at[1]).start()
        return 0

    lax.fori_loop(0, sent_hbm.shape[0], send, 0)
    pltpu.make_async_copy(sent_hbm, sent_hbm, sems.at[1]).wait()


def halves(value):
    high = value.astype(jnp.bfloat16)
    return high, (value - high.astype(jnp.float32)).astype(jnp.bfloat16)


def store_kernel(planes, tiles, u2_ref, *refs):
    *parts, out_ref, same_hbm, sems = refs
    copies = [pltpu.make_async_copy(part, same_hbm.at[at], sems.at[at]) for at, part in enumerate(parts)]
    for copy in copies:
        copy.start()

    def store(x):
        for tile in range(tiles):
            rows = pl.ds((x // ROWS) * tiles * ROWS + x % ROWS + tile * ROWS, ROWS, stride=planes * tiles)
            out_ref[rows, :] = u2_ref[x * tiles + tile]

    each(0, planes, 4, store)
    for copy in copies:
        copy.wait()


def split_kernel(by_xor, place_ref, same_hbm, other_hbm, split_ref, theta_ref, sems):
    chip, core = place_ref[2], place_ref[3]
    members = 2 * theta_ref.shape[0] * ROWS
    copies = []
    for at in range(same_hbm.shape[0]):
        where = chip ^ at if by_xor else at
        copies.append(pltpu.make_async_copy(same_hbm.at[at], theta_ref.at[where, core], sems.at[2 * at]))
        copies.append(pltpu.make_async_copy(other_hbm.at[at], theta_ref.at[where, 1 - core], sems.at[2 * at + 1]))
    for copy in copies:
        copy.start()
    for copy in copies:
        copy.wait()

    def split(slot):
        high, low = halves(theta_ref[:, :, slot].reshape(members, LANES))
        split_ref[slot, :members, :] = high
        split_ref[slot, members:, :] = low

    each(0, split_ref.shape[0], 4, split)


def stacked(value):
    high, low = halves(value)
    return jnp.concatenate([high.astype(jnp.float32), low.astype(jnp.float32)], axis=0).astype(jnp.bfloat16)


def fold(both):
    return both[:ROWS] + both[ROWS:]


def dot(left, right, over):
    return lax.dot_general(left, right, (((1,), (over,)), ((), ())), preferred_element_type=jnp.float32)


def update_kernel(slabs, planes, tiles, place_ref, count_ref, cells_hbm, probes_hbm, level_hbm,
                  pred_ref, before_2_ref, before_ref, own_ref, after_ref, after_2_ref, split_hbm, t_hbm,
                  post_ref, gain_ref, reach, cells_ref, probes_ref, level_ref, split_ref, sems):
    groups, blocks = pred_ref.shape[0] // slabs, pred_ref.shape[1]
    members = groups * ROWS
    share = 1.0 / (members - 1)
    copies = [
        pltpu.make_async_copy(source, target, sems.at[at])
        for at, (source, target) in enumerate((
            (cells_hbm, cells_ref), (probes_hbm, probes_ref), (level_hbm, level_ref),
            (split_hbm, split_ref), (t_hbm, post_ref)))
    ]
    for copy in copies:
        copy.start()
    slab, group = place_ref[0], place_ref[1]
    halo = 4 * tiles + 1
    seen = ((before_2_ref, 0), (before_ref, halo), (own_ref, 0), (after_ref, halo), (after_2_ref, 0))

    def extra(d, at):
        ref, first = seen[d]
        return ref[first + blocks + at // ROWS, at % ROWS : at % ROWS + 1, :]

    def wide(row):
        return row[:, :members] if members <= LANES else jnp.concatenate([row] * (members // LANES), axis=1)

    anomaly, scaled, variance, matches = [], [], [], []
    for d in range(5):
        wanted = slab + d - 2
        at = jnp.clip(wanted, 0, slabs - 1)
        live = jnp.where((wanted >= 0) & (wanted < slabs), 1.0, 0.0)
        for b in range(blocks):
            predicted = pred_ref[pl.ds(at * groups, groups), b].reshape(members, LANES)
            mean = jnp.sum(predicted, axis=0, keepdims=True) / members
            anomaly.append(halves((predicted - mean) * live))
            variance.append(extra(d, blocks + b) + (1.0 - live))
            noise = seen[d][0][seen[d][1] + b]
            scaled.append((extra(d, b) + noise - pred_ref[at * groups + group, b]) / variance[-1] * live)
            left = stacked(scaled[-1])
            high, low = anomaly[-1]
            matches.append(fold(dot(left, high, 1) + dot(left, low, 1)))
    for d in range(1, 4):
        for i in range(blocks):
            total = jnp.zeros((ROWS, members), jnp.float32)
            for j in range(3 * blocks):
                level = extra(d, 2 * blocks + i * 3 * blocks + j) / 256.0 * share
                total = total + wide(level) * matches[(d - 1) * blocks + j]
            high, low = anomaly[d * blocks + i]
            left = stacked(total)
            correction = fold(dot(left, high, 0) + dot(left, low, 0))
            gain = scaled[d * blocks + i] - correction / variance[d * blocks + i]
            if d == 2:
                gain_ref[:, i * LANES : (i + 1) * LANES] = gain
            left = stacked(gain)
            both = stacked(fold(dot(left, high, 1) + dot(left, low, 1)))
            reach[(d - 1) * blocks + i] = jnp.concatenate([both, both], axis=1)
    for copy in copies:
        copy.wait()
    for slot in range(split_ref.shape[0]):
        weight = jnp.where(slot < count_ref[0], level_ref[0, slot].astype(jnp.float32) / 256.0, 0.0) * share
        change = fold(dot(reach[probes_ref[0, slot]], split_ref[slot], 0)) * weight
        block = cells_ref[0, slot]
        rows = pl.ds(row_of(block // tiles, block % tiles, tiles), ROWS, stride=planes * tiles)
        post_ref[rows, :] = post_ref[rows, :] + change


def shards(
    starting_speed_field,
    sample_fluidity_exponent,
    observed,
    obs_noise,
    obs_var,
    probe_cells,
    pair_cells,
    pair_probes,
    pair_taper,
    pair_counts,
    probe_taper,
):
    shape = starting_speed_field.shape
    members, planes, cells = shape
    tiles = cells // LANES
    slots = pair_cells.shape[1]
    probes = obs_noise.shape[1]
    blocks = probes // LANES
    slabs, chips = lax.axis_size("space"), lax.axis_size("chip")
    groups = 2 * chips
    f32, i32 = jnp.float32, jnp.int32
    u_rows = to_rows(starting_speed_field)
    t_rows = to_rows(sample_fluidity_exponent)
    obs_tiles = blocks - (-(2 * blocks + probe_taper.shape[1] * probe_taper.shape[2]) // ROWS)
    edge = jax.ShapeDtypeStruct((4 * tiles + 1 + obs_tiles, ROWS, LANES), f32)
    obs_shape = jax.ShapeDtypeStruct((obs_tiles, ROWS, LANES), f32)
    params = pltpu.CompilerParams(vmem_limit_bytes=32 * 1024 * 1024)
    stack = pltpu.VMEM((planes * tiles, ROWS, LANES), f32)
    low, high, obs, t_near = pl.pallas_call(
        functools.partial(pack_kernel, planes, tiles),
        out_shape=(
            edge,
            edge,
            obs_shape,
            jax.ShapeDtypeStruct(u_rows.shape, f32),
        ),
        in_specs=[HBM] * 6,
        out_specs=(VMEM,) * 4,
        scratch_shapes=[
            pltpu.SMEM(probe_taper.shape, i32),
            pltpu.VMEM(u_rows.shape, f32),
            pltpu.VMEM((ROWS, probes), f32),
            pltpu.VMEM((2, probes), f32),
            pltpu.SemaphoreType.DMA((6,)),
        ],
        compiler_params=params,
        name="pack",
    )(*map(stay, (probe_taper, u_rows, t_rows, obs_noise, observed.reshape(1, -1), obs_var.reshape(1, -1))))
    upward = [(i, i + 1) for i in range(slabs - 1)]
    before = lax.ppermute(high, "space", upward)
    after = lax.ppermute(low, "space", [(j, i) for i, j in upward])
    if slabs == 4:
        before_2 = after_2 = lax.ppermute(obs, "space", [(i, (i + 2) % 4) for i in range(4)])
    else:
        upward_2 = [(i, i + 2) for i in range(slabs - 2)]
        before_2 = lax.ppermute(obs, "space", upward_2)
        after_2 = lax.ppermute(obs, "space", [(j, i) for i, j in upward_2])
    inner, edges, picked = pl.pallas_call(
        functools.partial(inner_kernel, planes, tiles),
        out_shape=(
            jax.ShapeDtypeStruct((planes * tiles, ROWS, LANES), f32),
            jax.ShapeDtypeStruct((14 * tiles, ROWS, LANES), f32),
            pltpu.HBM((slots, ROWS, LANES), f32),
        ),
        in_specs=[HBM, HBM, VMEM],
        out_specs=(VMEM, VMEM, HBM),
        scratch_shapes=[
            pltpu.VMEM(u_rows.shape, f32),
            stack,
            stack,
            stack,
            pltpu.VMEM((5, planes * tiles, ROWS, LANES), f32),
            pltpu.SMEM(pair_cells.shape, i32),
            pltpu.VMEM((slots, ROWS, LANES), f32),
            pltpu.SemaphoreType.DMA((3,)),
        ],
        compiler_params=params,
        cost_estimate=pl.CostEstimate(flops=0, bytes_accessed=15_000_000, transcendentals=0),
        name="inner_planes",
    )(stay(u_rows), stay(pair_cells), t_near)
    by_xor = chips <= 4 and chips & (chips - 1) == 0
    if by_xor:
        parts = [picked]
        for d in range(1, chips):
            parts.append(lax.ppermute(picked, "chip", [(i, i ^ d) for i in range(chips)]))
    else:
        spread = lax.all_to_all(jnp.broadcast_to(picked, (chips, *picked.shape)), "chip", 0, 0)
        parts = [spread[i] for i in range(chips)]
    u2, sent = pl.pallas_call(
        functools.partial(outer_kernel, planes, tiles),
        out_shape=(
            jax.ShapeDtypeStruct((planes * tiles, ROWS, LANES), f32),
            pltpu.HBM((slabs * groups, blocks, ROWS, LANES), f32),
        ),
        in_specs=[HBM] + [VMEM] * 4,
        out_specs=(VMEM, HBM),
        scratch_shapes=[
            pltpu.SMEM(probe_cells.shape, i32),
            pltpu.VMEM((blocks, ROWS, LANES), f32),
            pltpu.SemaphoreType.DMA((2,)),
        ],
        input_output_aliases={4: 0},
        compiler_params=params,
        cost_estimate=pl.CostEstimate(flops=0, bytes_accessed=26_000_000, transcendentals=0),
        name="outer_planes",
    )(stay(probe_cells), before, after, edges, inner)
    pred_all = lax.all_to_all(sent, ("space", "chip", "core"), 0, 0)
    u2_rows, theta_same = pl.pallas_call(
        functools.partial(store_kernel, planes, tiles),
        out_shape=(jax.ShapeDtypeStruct(u_rows.shape, f32), pltpu.HBM((chips, slots, ROWS, LANES), f32)),
        in_specs=[VMEM] + [ANY] * chips,
        out_specs=(VMEM, HBM),
        scratch_shapes=[pltpu.SemaphoreType.DMA((chips,))],
        compiler_params=params,
        cost_estimate=pl.CostEstimate(flops=0, bytes_accessed=8_000_000, transcendentals=0),
        name="store",
    )(u2, *parts)
    theta_other = lax.ppermute(theta_same, "core", [(0, 1), (1, 0)])
    where = [lax.axis_index(axes) for axes in ("space", ("chip", "core"), "chip", "core")]
    place = jnp.stack(where).astype(i32)
    split = pl.pallas_call(
        functools.partial(split_kernel, by_xor),
        out_shape=pltpu.HBM((slots, 2 * groups * ROWS, LANES), jnp.bfloat16),
        in_specs=[SMEM, HBM, ANY],
        out_specs=VMEM,
        scratch_shapes=[pltpu.VMEM((chips, 2, slots, ROWS, LANES), f32), pltpu.SemaphoreType.DMA((2 * chips,))],
        compiler_params=params,
        cost_estimate=pl.CostEstimate(flops=0, bytes_accessed=5_000_000, transcendentals=0),
        name="split",
    )(place, stay(theta_same), theta_other)
    post_rows, gain = pl.pallas_call(
        functools.partial(update_kernel, slabs, planes, tiles),
        out_shape=(
            jax.ShapeDtypeStruct(u_rows.shape, f32),
            jax.ShapeDtypeStruct((members, probes), f32),
        ),
        in_specs=[SMEM] * 2 + [HBM] * 3 + [VMEM] * 6 + [HBM] * 2,
        out_specs=(VMEM,) * 2,
        scratch_shapes=[
            pltpu.VMEM((probe_taper.shape[2], 2 * ROWS, 2 * groups * ROWS), jnp.bfloat16),
            pltpu.SMEM(pair_cells.shape, i32),
            pltpu.SMEM(pair_cells.shape, i32),
            pltpu.SMEM(pair_cells.shape, i32),
            pltpu.VMEM(split.shape, jnp.bfloat16),
            pltpu.SemaphoreType.DMA((5,)),
        ],
        compiler_params=params,
        name="update",
    )(place, pair_counts, *map(stay, (pair_cells, pair_probes, pair_taper)), pred_all,
      before_2, before, obs, after, after_2, stay(split), stay(t_rows))
    return (from_rows(u2_rows, shape), from_rows(post_rows, shape), gain)


def solution(mesh):
    slabs, groups = mesh.devices.shape
    split = jax.sharding.Mesh(mesh.devices.reshape(slabs, groups // 2, 2), ("space", "chip", "core"))
    members = ("chip", "core")
    return jax.shard_map(
        shards,
        mesh=split,
        in_specs=(
            P(members, "space", None),
            P(members, "space", None),
            P("space"),
            P(members, "space"),
            P("space"),
            P("space"),
            P("space", None),
            P("space", None),
            P("space", None),
            P("space"),
            P("space", None, None),
        ),
        out_specs=(P(members, "space", None), P(members, "space", None), P(members, "space")),
        check_vma=False,
    )
```

```python
import functools

import jax
import jax.numpy as jnp
from jax import lax
from jax.experimental import pallas as pl
from jax.experimental.pallas import tpu as pltpu
from jax.sharding import PartitionSpec as P

LANES = 128
ROWS = 8
NZ = 64
HALF_DT = 0.5 * 0.08

VMEM = pl.BlockSpec(memory_space=pltpu.VMEM)
SMEM = pl.BlockSpec(memory_space=pltpu.SMEM)
HBM = pl.BlockSpec(memory_space=pltpu.HBM)
ANY = pl.BlockSpec(memory_space=pl.ANY)


def stay(array):
    return pltpu.with_memory_space_constraint(array, pltpu.HBM)


def to_rows(array):
    members, planes, cells = array.shape
    split = array.reshape(members, planes // ROWS, ROWS, cells // LANES, LANES)
    return split.transpose(0, 1, 3, 2, 4).reshape(-1, LANES)


def from_rows(rows, shape):
    members, planes, cells = shape
    split = rows.reshape(members, planes // ROWS, cells // LANES, ROWS, LANES)
    return split.transpose(0, 1, 3, 2, 4).reshape(shape)


def row_of(plane, tile, tiles):
    return (plane // ROWS * tiles + tile) * ROWS + plane % ROWS


def pack_kernel(planes, tiles, taper_hbm, u_hbm, t_hbm, noise_hbm, observed_hbm, var_hbm,
                low_ref, high_ref, obs_ref, t_ref, taper_ref, u_ref, noise_ref, row_ref, sems):
    stride = planes * tiles
    blocks = noise_ref.shape[1] // LANES
    copies = [
        pltpu.make_async_copy(source, target, sems.at[at])
        for at, (source, target) in enumerate((
            (t_hbm, t_ref),
            (u_hbm, u_ref),
            (taper_hbm, taper_ref),
            (noise_hbm, noise_ref),
            (observed_hbm, row_ref.at[0:1]),
            (var_hbm, row_ref.at[1:2]),
        ))
    ]
    for copy in copies:
        copy.start()
    for kind, source in ((1, t_ref), (0, u_ref)):
        copies[1 - kind].wait()
        for out_ref, first in ((high_ref, planes - 2), (low_ref, 0)):
            for depth in range(2):
                for tile in range(tiles):
                    out_ref[(kind * 2 + depth) * tiles + tile] = source[
                        pl.ds(row_of(first + depth, tile, tiles), ROWS, stride=stride), :
                    ]
    for ref in (low_ref, high_ref):
        ref[4 * tiles] = jnp.ones((ROWS, LANES), jnp.float32)
    for copy in copies[2:]:
        copy.wait()
    own, window = taper_ref.shape[1:]
    rows = [row_ref[kind : kind + 1, b * LANES : (b + 1) * LANES] for kind in range(2) for b in range(blocks)]
    for i in range(own):
        for j in range(window):
            rows.append(jnp.full((1, LANES), taper_ref[0, i, j].astype(jnp.float32), jnp.float32))
    for b in range(blocks):
        obs_ref[b] = noise_ref[:, b * LANES : (b + 1) * LANES]
    for at, row in enumerate(rows):
        obs_ref[blocks + at // ROWS, at % ROWS : at % ROWS + 1, :] = row
    for ref in (low_ref, high_ref):
        for at in range(obs_ref.shape[0]):
            ref[4 * tiles + 1 + at] = obs_ref[at]


def rot(value, by):
    return pltpu.roll(value, by % LANES, 1)


def lane_masks():
    lane = lax.broadcasted_iota(jnp.int32, (ROWS, LANES), 1)
    height = lane & (NZ - 1)
    return lane < NZ, height == 0, height == NZ - 1


def coefficients(masks, low, here, high):
    first_half, floor, roof = masks
    tiles = len(here)
    turned = [rot(value, NZ) for value in here]
    out = []
    for tile in range(tiles):
        mid = here[tile]
        near = mid + turned[tile]
        far = mid + jnp.where(first_half, turned[tile - 1], turned[(tile + 1) % tiles])
        up = mid + jnp.where(roof, HALF_DT, rot(mid, -1))
        down = mid + jnp.where(floor, HALF_DT, rot(mid, 1))
        below = mid + low[tile]
        above = mid + high[tile]
        diag = 1.0 - ((near + far) + (up + down) + (below + above))
        out.append((diag, near, far, jnp.where(roof, 0.0, up), jnp.where(floor, 0.0, down), below, above))
    return out


def step(masks, weights, low, here, high):
    first_half = masks[0]
    tiles = len(here)
    turned = [rot(value, NZ) for value in here]
    out = []
    for tile in range(tiles):
        diag, near, far, up, down, below, above = weights[tile]
        mid = here[tile]
        beyond = jnp.where(first_half, turned[tile - 1], turned[(tile + 1) % tiles])
        out.append(
            (diag * mid + near * turned[tile])
            + (far * beyond + up * rot(mid, -1))
            + (down * rot(mid, 1) + below * low[tile])
            + above * high[tile]
        )
    return out


def plane_of(ref, at, tiles):
    return [ref[at * tiles + tile] for tile in range(tiles)]


def put(ref, at, values):
    for tile, value in enumerate(values):
        ref[at * len(values) + tile] = value


def each(first, last, unroll, body):
    count = (last - first) // unroll

    def several(at, _):
        for d in range(unroll):
            body(first + at * unroll + d)
        return 0

    lax.fori_loop(0, count, several, 0)
    for x in range(first + count * unroll, last):
        body(x)


def inner_kernel(planes, tiles, u_hbm, cells_hbm, t_ref, u2_ref, edge_ref, pick_hbm,
                 u_ref, u0, hv, u1, held, cells_ref, pick_ref, sems):
    stride = planes * tiles
    masks = lane_masks()
    copy = pltpu.make_async_copy(u_hbm, u_ref, sems.at[0])
    cells_copy = pltpu.make_async_copy(cells_hbm, cells_ref, sems.at[1])
    picked = pltpu.make_async_copy(pick_ref, pick_hbm, sems.at[2])
    cells_copy.start()
    copy.start()

    def rows_at(x, tile):
        return pl.ds((x // ROWS) * tiles * ROWS + x % ROWS + tile * ROWS, ROWS, stride=stride)

    def load_t(x):
        for tile in range(tiles):
            hv[x * tiles + tile] = HALF_DT * jnp.exp(t_ref[rows_at(x, tile), :])

    def load_u(x):
        for tile in range(tiles):
            u0[x * tiles + tile] = u_ref[rows_at(x, tile), :]

    def first_step(x):
        weights = coefficients(masks, *[plane_of(hv, x + d, tiles) for d in (-1, 0, 1)])
        for tile in range(tiles):
            for kind in range(5):
                held[kind, x * tiles + tile] = weights[tile][kind]
        put(u1, x, step(masks, weights, *[plane_of(u0, x + d, tiles) for d in (-1, 0, 1)]))

    def second_step(x):
        weights = []
        for tile in range(tiles):
            at = x * tiles + tile
            here = hv[at]
            weights.append([held[kind, at] for kind in range(5)] + [here + hv[at - tiles], here + hv[at + tiles]])
        put(u2_ref, x, step(masks, weights, *[plane_of(u1, x + d, tiles) for d in (-1, 0, 1)]))

    each(0, planes, 4, load_t)
    cells_copy.wait()
    for slot in range(pick_ref.shape[0]):
        block = cells_ref[0, slot]
        row = row_of(block // tiles, block % tiles, tiles)
        pick_ref[slot] = t_ref[pl.ds(row, ROWS, stride=stride), :]
    picked.start()
    copy.wait()
    each(0, planes, 4, load_u)
    each(1, planes - 1, 7, first_step)
    each(2, planes - 2, 6, second_step)
    last = planes - 1
    at = 0
    for ref, kept in ((u0, (0, 1, last - 1, last)), (hv, (0, 1, 2, last - 2, last - 1, last)),
                      (u1, (1, 2, last - 2, last - 1))):
        for x in kept:
            put(edge_ref, at, plane_of(ref, x, tiles))
            at += 1
    picked.wait()


def outer_kernel(planes, tiles, probe_hbm, before_ref, after_ref, edge_ref, inner_ref,
                 u2_ref, sent_hbm, seen_ref, probe_ref, found_ref, sems):
    probe_copy = pltpu.make_async_copy(probe_hbm, probe_ref, sems.at[0])
    probe_copy.start()
    masks = lane_masks()
    blocks = probe_ref.shape[0] // LANES
    count = seen_ref.shape[0] // 2
    for at in range(count):
        seen_ref[at] = before_ref[4 * tiles + 1 + at]
        seen_ref[count + at] = after_ref[4 * tiles + 1 + at]
    edge = [plane_of(edge_ref, at, tiles) for at in range(14)]
    last = planes - 1
    for ref, own_u, own_v, own_1, where in (
        (before_ref, edge[0:2], edge[4:7], edge[10:12], (0, 1)),
        (after_ref, edge[3:1:-1], edge[9:6:-1], edge[13:11:-1], (last, last - 1)),
    ):
        order = (0, 1) if ref is before_ref else (1, 0)
        u = [plane_of(ref, d, tiles) for d in order] + own_u
        v = [[HALF_DT * jnp.exp(t) for t in plane_of(ref, 2 + d, tiles)] for d in order] + own_v
        live = ref[4 * tiles]
        weights = [coefficients(masks, v[d], v[d + 1], v[d + 2]) for d in range(3)]
        next_u = [step(masks, weights[d], u[d], u[d + 1], u[d + 2]) for d in range(2)]
        next_u[0] = [value * live for value in next_u[0]]
        next_u = next_u + own_1
        for d in range(2):
            put(u2_ref, where[d], step(masks, weights[d + 1], next_u[d], next_u[d + 1], next_u[d + 2]))

    probe_copy.wait()
    lane = lax.broadcasted_iota(jnp.int32, (ROWS, LANES), 1)
    for part in range(blocks):
        found = jnp.zeros((ROWS, LANES), jnp.float32)
        for p in range(LANES):
            cell = probe_ref[part * LANES + p]
            turned = pltpu.roll(u2_ref[cell >> 7], (p - cell) & (LANES - 1), 1)
            found = jnp.where(lane == p, turned, found)

        found_ref[part] = found

    def send(device, _):
        pltpu.make_async_copy(found_ref, sent_hbm.at[device], sems.at[1]).start()
        return 0

    lax.fori_loop(0, sent_hbm.shape[0], send, 0)
    pltpu.make_async_copy(sent_hbm, sent_hbm, sems.at[1]).wait()


def halves(value):
    high = value.astype(jnp.bfloat16)
    return high, (value - high.astype(jnp.float32)).astype(jnp.bfloat16)


def store_kernel(planes, tiles, u2_ref, *refs):
    out_ref = refs[len(refs) // 2]

    def store(x):
        for tile in range(tiles):
            rows = pl.ds((x // ROWS) * tiles * ROWS + x % ROWS + tile * ROWS, ROWS, stride=planes * tiles)
            out_ref[rows, :] = u2_ref[x * tiles + tile]

    each(0, planes, 4, store)


def split_kernel(by_xor, chips, place_ref, *refs):
    *parts, split_ref, theta_ref, sems = refs
    chip, core = place_ref[2], place_ref[3]
    same, other = parts[: len(parts) // 2], parts[len(parts) // 2 :]
    if not by_xor:
        same, other = ([ref.at[at] for at in range(chips)] for (ref,) in (same, other))
    members = 2 * theta_ref.shape[0] * ROWS
    copies = []
    for at in range(chips):
        where = chip ^ at if by_xor else at
        copies.append(pltpu.make_async_copy(same[at], theta_ref.at[where, core], sems.at[2 * at]))
        copies.append(pltpu.make_async_copy(other[at], theta_ref.at[where, 1 - core], sems.at[2 * at + 1]))
    for copy in copies:
        copy.start()
    for copy in copies:
        copy.wait()

    def split(slot):
        high, low = halves(theta_ref[:, :, slot].reshape(members, LANES))
        split_ref[slot, :members, :] = high
        split_ref[slot, members:, :] = low

    each(0, split_ref.shape[0], 4, split)


def stacked(value):
    high, low = halves(value)
    return jnp.concatenate([high.astype(jnp.float32), low.astype(jnp.float32)], axis=0).astype(jnp.bfloat16)


def fold(both):
    return both[:ROWS] + both[ROWS:]


def dot(left, right, over):
    return lax.dot_general(left, right, (((1,), (over,)), ((), ())), preferred_element_type=jnp.float32)


def update_kernel(slabs, planes, tiles, place_ref, count_ref, cells_hbm, probes_hbm, level_hbm,
                  pred_ref, before_2_ref, seen_ref, own_ref, after_2_ref, split_hbm, t_hbm,
                  post_ref, gain_ref, reach, cells_ref, probes_ref, level_ref, split_ref, sems):
    groups, blocks = pred_ref.shape[0] // slabs, pred_ref.shape[1]
    members = groups * ROWS
    share = 1.0 / (members - 1)
    copies = [
        pltpu.make_async_copy(source, target, sems.at[at])
        for at, (source, target) in enumerate((
            (cells_hbm, cells_ref), (probes_hbm, probes_ref), (level_hbm, level_ref),
            (split_hbm, split_ref), (t_hbm, post_ref)))
    ]
    for copy in copies:
        copy.start()
    slab, group = place_ref[0], place_ref[1]
    seen = ((before_2_ref, 0), (seen_ref, 0), (own_ref, 0), (seen_ref, seen_ref.shape[0] // 2), (after_2_ref, 0))

    def extra(d, at):
        ref, first = seen[d]
        return ref[first + blocks + at // ROWS, at % ROWS : at % ROWS + 1, :]

    def wide(row):
        return row[:, :members] if members <= LANES else jnp.concatenate([row] * (members // LANES), axis=1)

    anomaly, scaled, variance, matches = [], [], [], []
    for d in range(5):
        wanted = slab + d - 2
        at = jnp.clip(wanted, 0, slabs - 1)
        live = jnp.where((wanted >= 0) & (wanted < slabs), 1.0, 0.0)
        for b in range(blocks):
            predicted = pred_ref[pl.ds(at * groups, groups), b].reshape(members, LANES)
            mean = jnp.sum(predicted, axis=0, keepdims=True) / members
            anomaly.append(halves((predicted - mean) * live))
            variance.append(extra(d, blocks + b) + (1.0 - live))
            noise = seen[d][0][seen[d][1] + b]
            scaled.append((extra(d, b) + noise - pred_ref[at * groups + group, b]) / variance[-1] * live)
            left = stacked(scaled[-1])
            high, low = anomaly[-1]
            matches.append(fold(dot(left, high, 1) + dot(left, low, 1)))
    for d in range(1, 4):
        for i in range(blocks):
            total = jnp.zeros((ROWS, members), jnp.float32)
            for j in range(3 * blocks):
                level = extra(d, 2 * blocks + i * 3 * blocks + j) / 256.0 * share
                total = total + wide(level) * matches[(d - 1) * blocks + j]
            high, low = anomaly[d * blocks + i]
            left = stacked(total)
            correction = fold(dot(left, high, 0) + dot(left, low, 0))
            gain = scaled[d * blocks + i] - correction / variance[d * blocks + i]
            if d == 2:
                gain_ref[:, i * LANES : (i + 1) * LANES] = gain
            left = stacked(gain)
            both = stacked(fold(dot(left, high, 1) + dot(left, low, 1)))
            reach[(d - 1) * blocks + i] = jnp.concatenate([both, both], axis=1)
    for copy in copies:
        copy.wait()
    for slot in range(split_ref.shape[0]):
        weight = jnp.where(slot < count_ref[0], level_ref[0, slot].astype(jnp.float32) / 256.0, 0.0) * share
        change = fold(dot(reach[probes_ref[0, slot]], split_ref[slot], 0)) * weight
        block = cells_ref[0, slot]
        rows = pl.ds(row_of(block // tiles, block % tiles, tiles), ROWS, stride=planes * tiles)
        post_ref[rows, :] = post_ref[rows, :] + change


def shards(
    starting_speed_field,
    sample_fluidity_exponent,
    observed,
    obs_noise,
    obs_var,
    probe_cells,
    pair_cells,
    pair_probes,
    pair_taper,
    pair_counts,
    probe_taper,
):
    shape = starting_speed_field.shape
    members, planes, cells = shape
    tiles = cells // LANES
    slots = pair_cells.shape[1]
    probes = obs_noise.shape[1]
    blocks = probes // LANES
    slabs, chips = lax.axis_size("space"), lax.axis_size("chip")
    groups = 2 * chips
    f32, i32 = jnp.float32, jnp.int32
    u_rows = to_rows(starting_speed_field)
    t_rows = to_rows(sample_fluidity_exponent)
    obs_tiles = blocks - (-(2 * blocks + probe_taper.shape[1] * probe_taper.shape[2]) // ROWS)
    edge = jax.ShapeDtypeStruct((4 * tiles + 1 + obs_tiles, ROWS, LANES), f32)
    obs_shape = jax.ShapeDtypeStruct((obs_tiles, ROWS, LANES), f32)
    params = pltpu.CompilerParams(vmem_limit_bytes=32 * 1024 * 1024)
    stack = pltpu.VMEM((planes * tiles, ROWS, LANES), f32)
    low, high, obs, t_near = pl.pallas_call(
        functools.partial(pack_kernel, planes, tiles),
        out_shape=(
            edge,
            edge,
            obs_shape,
            jax.ShapeDtypeStruct(u_rows.shape, f32),
        ),
        in_specs=[HBM] * 6,
        out_specs=(VMEM,) * 4,
        scratch_shapes=[
            pltpu.SMEM(probe_taper.shape, i32),
            pltpu.VMEM(u_rows.shape, f32),
            pltpu.VMEM((ROWS, probes), f32),
            pltpu.VMEM((2, probes), f32),
            pltpu.SemaphoreType.DMA((6,)),
        ],
        compiler_params=params,
        name="pack",
    )(*map(stay, (probe_taper, u_rows, t_rows, obs_noise, observed.reshape(1, -1), obs_var.reshape(1, -1))))
    little = pl.CostEstimate(flops=1000, bytes_accessed=1000, transcendentals=0)
    upward = [(i, i + 1) for i in range(slabs - 1)]
    before = lax.ppermute(high, "space", upward)
    after = lax.ppermute(low, "space", [(j, i) for i, j in upward])
    if slabs == 4:
        before_2 = after_2 = lax.ppermute(obs, "space", [(i, (i + 2) % 4) for i in range(4)])
    else:
        upward_2 = [(i, i + 2) for i in range(slabs - 2)]
        before_2 = lax.ppermute(obs, "space", upward_2)
        after_2 = lax.ppermute(obs, "space", [(j, i) for i, j in upward_2])
    inner, edges, picked = pl.pallas_call(
        functools.partial(inner_kernel, planes, tiles),
        out_shape=(
            jax.ShapeDtypeStruct((planes * tiles, ROWS, LANES), f32),
            jax.ShapeDtypeStruct((14 * tiles, ROWS, LANES), f32),
            pltpu.HBM((slots, ROWS, LANES), f32),
        ),
        in_specs=[HBM, HBM, VMEM],
        out_specs=(VMEM, VMEM, HBM),
        scratch_shapes=[
            pltpu.VMEM(u_rows.shape, f32),
            stack,
            stack,
            stack,
            pltpu.VMEM((5, planes * tiles, ROWS, LANES), f32),
            pltpu.SMEM(pair_cells.shape, i32),
            pltpu.VMEM((slots, ROWS, LANES), f32),
            pltpu.SemaphoreType.DMA((3,)),
        ],
        compiler_params=params,
        cost_estimate=pl.CostEstimate(flops=0, bytes_accessed=15_000_000, transcendentals=0),
        name="inner_planes",
    )(stay(u_rows), stay(pair_cells), t_near)
    by_xor = chips <= 4 and chips & (chips - 1) == 0
    if by_xor:
        parts = [picked]
        for d in range(1, chips):
            parts.append(lax.ppermute(picked, "chip", [(i, i ^ d) for i in range(chips)]))
    else:
        parts = [lax.all_to_all(jnp.broadcast_to(picked, (chips, *picked.shape)), "chip", 0, 0)]
    u2, sent, seen = pl.pallas_call(
        functools.partial(outer_kernel, planes, tiles),
        out_shape=(
            jax.ShapeDtypeStruct((planes * tiles, ROWS, LANES), f32),
            pltpu.HBM((slabs * groups, blocks, ROWS, LANES), f32),
            jax.ShapeDtypeStruct((2 * obs_tiles, ROWS, LANES), f32),
        ),
        in_specs=[HBM] + [VMEM] * 4,
        out_specs=(VMEM, HBM, VMEM),
        scratch_shapes=[
            pltpu.SMEM(probe_cells.shape, i32),
            pltpu.VMEM((blocks, ROWS, LANES), f32),
            pltpu.SemaphoreType.DMA((2,)),
        ],
        input_output_aliases={4: 0},
        compiler_params=params,
        cost_estimate=pl.CostEstimate(flops=0, bytes_accessed=26_000_000, transcendentals=0),
        name="outer_planes",
    )(stay(probe_cells), before, after, edges, inner)
    pred_all = lax.all_to_all(sent, ("space", "chip", "core"), 0, 0)
    u2_rows, *parts = pl.pallas_call(
        functools.partial(store_kernel, planes, tiles),
        out_shape=(jax.ShapeDtypeStruct(u_rows.shape, f32), *(jax.ShapeDtypeStruct(part.shape, f32) for part in parts)),
        in_specs=[VMEM] + [ANY] * len(parts),
        out_specs=(VMEM,) + (ANY,) * len(parts),
        input_output_aliases={1 + at: 1 + at for at in range(len(parts))},
        compiler_params=params,
        cost_estimate=little,
        name="store",
    )(u2, *parts)
    swapped = [lax.ppermute(part, "core", [(0, 1), (1, 0)]) for part in parts]
    where = [lax.axis_index(axes) for axes in ("space", ("chip", "core"), "chip", "core")]
    place = jnp.stack(where).astype(i32)
    split = pl.pallas_call(
        functools.partial(split_kernel, by_xor, chips),
        out_shape=pltpu.HBM((slots, 2 * groups * ROWS, LANES), jnp.bfloat16),
        in_specs=[SMEM] + [ANY] * (2 * len(parts)),
        out_specs=VMEM,
        scratch_shapes=[pltpu.VMEM((chips, 2, slots, ROWS, LANES), f32), pltpu.SemaphoreType.DMA((2 * chips,))],
        compiler_params=params,
        cost_estimate=little,
        name="split",
    )(place, *parts, *swapped)
    post_rows, gain = pl.pallas_call(
        functools.partial(update_kernel, slabs, planes, tiles),
        out_shape=(
            jax.ShapeDtypeStruct(u_rows.shape, f32),
            jax.ShapeDtypeStruct((members, probes), f32),
        ),
        in_specs=[SMEM] * 2 + [HBM] * 3 + [VMEM] * 5 + [HBM] * 2,
        out_specs=(VMEM,) * 2,
        scratch_shapes=[
            pltpu.VMEM((probe_taper.shape[2], 2 * ROWS, 2 * groups * ROWS), jnp.bfloat16),
            pltpu.SMEM(pair_cells.shape, i32),
            pltpu.SMEM(pair_cells.shape, i32),
            pltpu.SMEM(pair_cells.shape, i32),
            pltpu.VMEM(split.shape, jnp.bfloat16),
            pltpu.SemaphoreType.DMA((5,)),
        ],
        compiler_params=params,
        name="update",
    )(place, pair_counts, *map(stay, (pair_cells, pair_probes, pair_taper)), pred_all,
      before_2, seen, obs, after_2, stay(split), stay(t_rows))
    return (from_rows(u2_rows, shape), from_rows(post_rows, shape), gain)


def solution(mesh):
    slabs, groups = mesh.devices.shape
    split = jax.sharding.Mesh(mesh.devices.reshape(slabs, groups // 2, 2), ("space", "chip", "core"))
    members = ("chip", "core")
    return jax.shard_map(
        shards,
        mesh=split,
        in_specs=(
            P(members, "space", None),
            P(members, "space", None),
            P("space"),
            P(members, "space"),
            P("space"),
            P("space"),
            P("space", None),
            P("space", None),
            P("space", None),
            P("space"),
            P("space", None, None),
        ),
        out_specs=(P(members, "space", None), P(members, "space", None), P(members, "space")),
        check_vma=False,
    )
```

```python
import functools

import jax
import jax.numpy as jnp
from jax import lax
from jax.experimental import pallas as pl
from jax.experimental.pallas import tpu as pltpu
from jax.sharding import PartitionSpec as P

LANES = 128
ROWS = 8
NZ = 64
HALF_DT = 0.5 * 0.08

VMEM = pl.BlockSpec(memory_space=pltpu.VMEM)
SMEM = pl.BlockSpec(memory_space=pltpu.SMEM)
HBM = pl.BlockSpec(memory_space=pltpu.HBM)
ANY = pl.BlockSpec(memory_space=pl.ANY)


def stay(array):
    return pltpu.with_memory_space_constraint(array, pltpu.HBM)


def to_rows(array):
    members, planes, cells = array.shape
    split = array.reshape(members, planes // ROWS, ROWS, cells // LANES, LANES)
    return split.transpose(0, 1, 3, 2, 4).reshape(-1, LANES)


def from_rows(rows, shape):
    members, planes, cells = shape
    split = rows.reshape(members, planes // ROWS, cells // LANES, ROWS, LANES)
    return split.transpose(0, 1, 3, 2, 4).reshape(shape)


def row_of(plane, tile, tiles):
    return (plane // ROWS * tiles + tile) * ROWS + plane % ROWS


def pack_kernel(planes, tiles, taper_hbm, u_hbm, t_hbm, noise_hbm, observed_hbm, var_hbm, cells_hbm,
                low_ref, high_ref, obs_ref, t_ref, pick_hbm,
                taper_ref, u_ref, noise_ref, row_ref, cells_ref, pick_ref, sems):
    stride = planes * tiles
    blocks = noise_ref.shape[1] // LANES
    copies = [
        pltpu.make_async_copy(source, target, sems.at[at])
        for at, (source, target) in enumerate((
            (t_hbm, t_ref),
            (u_hbm, u_ref),
            (taper_hbm, taper_ref),
            (noise_hbm, noise_ref),
            (observed_hbm, row_ref.at[0:1]),
            (var_hbm, row_ref.at[1:2]),
            (cells_hbm, cells_ref),
        ))
    ]
    for copy in copies:
        copy.start()
    copies[0].wait()
    copies[6].wait()
    for slot in range(pick_ref.shape[0]):
        block = cells_ref[0, slot]
        row = row_of(block // tiles, block % tiles, tiles)
        pick_ref[slot] = t_ref[pl.ds(row, ROWS, stride=stride), :]
    picked = pltpu.make_async_copy(pick_ref, pick_hbm, sems.at[7])
    picked.start()
    for kind, source in ((1, t_ref), (0, u_ref)):
        if kind == 0:
            copies[1].wait()
        for out_ref, first in ((high_ref, planes - 2), (low_ref, 0)):
            for depth in range(2):
                for tile in range(tiles):
                    out_ref[(kind * 2 + depth) * tiles + tile] = source[
                        pl.ds(row_of(first + depth, tile, tiles), ROWS, stride=stride), :
                    ]
    for ref in (low_ref, high_ref):
        ref[4 * tiles] = jnp.ones((ROWS, LANES), jnp.float32)
    for copy in copies[2:6]:
        copy.wait()
    own, window = taper_ref.shape[1:]
    rows = [row_ref[kind : kind + 1, b * LANES : (b + 1) * LANES] for kind in range(2) for b in range(blocks)]
    for i in range(own):
        for j in range(window):
            rows.append(jnp.full((1, LANES), taper_ref[0, i, j].astype(jnp.float32), jnp.float32))
    for b in range(blocks):
        obs_ref[b] = noise_ref[:, b * LANES : (b + 1) * LANES]
    for at, row in enumerate(rows):
        obs_ref[blocks + at // ROWS, at % ROWS : at % ROWS + 1, :] = row
    for ref in (low_ref, high_ref):
        for at in range(obs_ref.shape[0]):
            ref[4 * tiles + 1 + at] = obs_ref[at]
    picked.wait()


def rot(value, by):
    return pltpu.roll(value, by % LANES, 1)


def lane_masks():
    lane = lax.broadcasted_iota(jnp.int32, (ROWS, LANES), 1)
    height = lane & (NZ - 1)
    return lane < NZ, height == 0, height == NZ - 1


def coefficients(masks, low, here, high):
    first_half, floor, roof = masks
    tiles = len(here)
    turned = [rot(value, NZ) for value in here]
    out = []
    for tile in range(tiles):
        mid = here[tile]
        near = mid + turned[tile]
        far = mid + jnp.where(first_half, turned[tile - 1], turned[(tile + 1) % tiles])
        up = mid + jnp.where(roof, HALF_DT, rot(mid, -1))
        down = mid + jnp.where(floor, HALF_DT, rot(mid, 1))
        below = mid + low[tile]
        above = mid + high[tile]
        diag = 1.0 - ((near + far) + (up + down) + (below + above))
        out.append((diag, near, far, jnp.where(roof, 0.0, up), jnp.where(floor, 0.0, down), below, above))
    return out


def step(masks, weights, low, here, high):
    first_half = masks[0]
    tiles = len(here)
    turned = [rot(value, NZ) for value in here]
    out = []
    for tile in range(tiles):
        diag, near, far, up, down, below, above = weights[tile]
        mid = here[tile]
        beyond = jnp.where(first_half, turned[tile - 1], turned[(tile + 1) % tiles])
        out.append(
            (diag * mid + near * turned[tile])
            + (far * beyond + up * rot(mid, -1))
            + (down * rot(mid, 1) + below * low[tile])
            + above * high[tile]
        )
    return out


def plane_of(ref, at, tiles):
    return [ref[at * tiles + tile] for tile in range(tiles)]


def put(ref, at, values):
    for tile, value in enumerate(values):
        ref[at * len(values) + tile] = value


def each(first, last, unroll, body):
    count = (last - first) // unroll

    def several(at, _):
        for d in range(unroll):
            body(first + at * unroll + d)
        return 0

    lax.fori_loop(0, count, several, 0)
    for x in range(first + count * unroll, last):
        body(x)


def inner_kernel(planes, tiles, u_hbm, t_ref, u2_ref, edge_ref, u_ref, u0, hv, u1, held, sem):
    stride = planes * tiles
    masks = lane_masks()
    copy = pltpu.make_async_copy(u_hbm, u_ref, sem)
    copy.start()

    def rows_at(x, tile):
        return pl.ds((x // ROWS) * tiles * ROWS + x % ROWS + tile * ROWS, ROWS, stride=stride)

    def load_t(x):
        for tile in range(tiles):
            hv[x * tiles + tile] = HALF_DT * jnp.exp(t_ref[rows_at(x, tile), :])

    def load_u(x):
        for tile in range(tiles):
            u0[x * tiles + tile] = u_ref[rows_at(x, tile), :]

    def first_step(x):
        weights = coefficients(masks, *[plane_of(hv, x + d, tiles) for d in (-1, 0, 1)])
        for tile in range(tiles):
            for kind in range(5):
                held[kind, x * tiles + tile] = weights[tile][kind]
        put(u1, x, step(masks, weights, *[plane_of(u0, x + d, tiles) for d in (-1, 0, 1)]))

    def second_step(x):
        weights = []
        for tile in range(tiles):
            at = x * tiles + tile
            here = hv[at]
            weights.append([held[kind, at] for kind in range(5)] + [here + hv[at - tiles], here + hv[at + tiles]])
        put(u2_ref, x, step(masks, weights, *[plane_of(u1, x + d, tiles) for d in (-1, 0, 1)]))

    each(0, planes, 4, load_t)
    copy.wait()
    each(0, planes, 4, load_u)
    each(1, planes - 1, 7, first_step)
    each(2, planes - 2, 6, second_step)
    last = planes - 1
    at = 0
    for ref, kept in ((u0, (0, 1, last - 1, last)), (hv, (0, 1, 2, last - 2, last - 1, last)),
                      (u1, (1, 2, last - 2, last - 1))):
        for x in kept:
            put(edge_ref, at, plane_of(ref, x, tiles))
            at += 1


def outer_kernel(planes, tiles, probe_hbm, before_ref, after_ref, edge_ref, inner_ref,
                 u2_ref, found_ref, seen_ref, probe_ref, sem):
    probe_copy = pltpu.make_async_copy(probe_hbm, probe_ref, sem)
    probe_copy.start()
    masks = lane_masks()
    blocks = probe_ref.shape[0] // LANES
    count = seen_ref.shape[0] // 2
    for at in range(count):
        seen_ref[at] = before_ref[4 * tiles + 1 + at]
        seen_ref[count + at] = after_ref[4 * tiles + 1 + at]
    edge = [plane_of(edge_ref, at, tiles) for at in range(14)]
    last = planes - 1
    for ref, own_u, own_v, own_1, where in (
        (before_ref, edge[0:2], edge[4:7], edge[10:12], (0, 1)),
        (after_ref, edge[3:1:-1], edge[9:6:-1], edge[13:11:-1], (last, last - 1)),
    ):
        order = (0, 1) if ref is before_ref else (1, 0)
        u = [plane_of(ref, d, tiles) for d in order] + own_u
        v = [[HALF_DT * jnp.exp(t) for t in plane_of(ref, 2 + d, tiles)] for d in order] + own_v
        live = ref[4 * tiles]
        weights = [coefficients(masks, v[d], v[d + 1], v[d + 2]) for d in range(3)]
        next_u = [step(masks, weights[d], u[d], u[d + 1], u[d + 2]) for d in range(2)]
        next_u[0] = [value * live for value in next_u[0]]
        next_u = next_u + own_1
        for d in range(2):
            put(u2_ref, where[d], step(masks, weights[d + 1], next_u[d], next_u[d + 1], next_u[d + 2]))

    probe_copy.wait()
    lane = lax.broadcasted_iota(jnp.int32, (ROWS, LANES), 1)
    for part in range(blocks):
        found = jnp.zeros((ROWS, LANES), jnp.float32)
        for p in range(LANES):
            cell = probe_ref[part * LANES + p]
            turned = pltpu.roll(u2_ref[cell >> 7], (p - cell) & (LANES - 1), 1)
            found = jnp.where(lane == p, turned, found)

        found_ref[part] = found


def send_kernel(found_ref, *refs):
    sent_hbm, sem = refs[-2:]

    def send(device, _):
        pltpu.make_async_copy(found_ref, sent_hbm.at[device], sem).start()
        return 0

    lax.fori_loop(0, sent_hbm.shape[0], send, 0)
    pltpu.make_async_copy(sent_hbm, sent_hbm, sem).wait()


def halves(value):
    high = value.astype(jnp.bfloat16)
    return high, (value - high.astype(jnp.float32)).astype(jnp.bfloat16)


def store_kernel(planes, tiles, u2_ref, *refs):
    out_ref = refs[len(refs) // 2]

    def store(x):
        for tile in range(tiles):
            rows = pl.ds((x // ROWS) * tiles * ROWS + x % ROWS + tile * ROWS, ROWS, stride=planes * tiles)
            out_ref[rows, :] = u2_ref[x * tiles + tile]

    each(0, planes, 4, store)


def split_kernel(by_xor, chips, place_ref, *refs):
    *parts, split_ref, theta_ref, sems = refs
    chip, core = place_ref[2], place_ref[3]
    same, other = parts[: len(parts) // 2], parts[len(parts) // 2 :]
    if not by_xor:
        same, other = ([ref.at[at] for at in range(chips)] for (ref,) in (same, other))
    members = 2 * theta_ref.shape[0] * ROWS
    copies = []
    for at in range(chips):
        where = chip ^ at if by_xor else at
        copies.append(pltpu.make_async_copy(same[at], theta_ref.at[where, core], sems.at[2 * at]))
        copies.append(pltpu.make_async_copy(other[at], theta_ref.at[where, 1 - core], sems.at[2 * at + 1]))
    for copy in copies:
        copy.start()
    for copy in copies:
        copy.wait()

    def split(slot):
        high, low = halves(theta_ref[:, :, slot].reshape(members, LANES))
        split_ref[slot, :members, :] = high
        split_ref[slot, members:, :] = low

    each(0, split_ref.shape[0], 4, split)


def stacked(value):
    high, low = halves(value)
    return jnp.concatenate([high.astype(jnp.float32), low.astype(jnp.float32)], axis=0).astype(jnp.bfloat16)


def fold(both):
    return both[:ROWS] + both[ROWS:]


def dot(left, right, over):
    return lax.dot_general(left, right, (((1,), (over,)), ((), ())), preferred_element_type=jnp.float32)


def update_kernel(slabs, planes, tiles, place_ref, count_ref, cells_hbm, probes_hbm, level_hbm,
                  pred_ref, before_2_ref, seen_ref, own_ref, after_2_ref, split_hbm, t_hbm,
                  post_ref, gain_ref, reach, cells_ref, probes_ref, level_ref, split_ref, sems):
    groups, blocks = pred_ref.shape[0] // slabs, pred_ref.shape[1]
    members = groups * ROWS
    share = 1.0 / (members - 1)
    copies = [
        pltpu.make_async_copy(source, target, sems.at[at])
        for at, (source, target) in enumerate((
            (cells_hbm, cells_ref), (probes_hbm, probes_ref), (level_hbm, level_ref),
            (split_hbm, split_ref), (t_hbm, post_ref)))
    ]
    for copy in copies:
        copy.start()
    slab, group = place_ref[0], place_ref[1]
    seen = ((before_2_ref, 0), (seen_ref, 0), (own_ref, 0), (seen_ref, seen_ref.shape[0] // 2), (after_2_ref, 0))

    def extra(d, at):
        ref, first = seen[d]
        return ref[first + blocks + at // ROWS, at % ROWS : at % ROWS + 1, :]

    def wide(row):
        return row[:, :members] if members <= LANES else jnp.concatenate([row] * (members // LANES), axis=1)

    anomaly, scaled, variance, matches = [], [], [], []
    for d in range(5):
        wanted = slab + d - 2
        at = jnp.clip(wanted, 0, slabs - 1)
        live = jnp.where((wanted >= 0) & (wanted < slabs), 1.0, 0.0)
        for b in range(blocks):
            predicted = pred_ref[pl.ds(at * groups, groups), b].reshape(members, LANES)
            mean = jnp.sum(predicted, axis=0, keepdims=True) / members
            anomaly.append(halves((predicted - mean) * live))
            variance.append(extra(d, blocks + b) + (1.0 - live))
            noise = seen[d][0][seen[d][1] + b]
            scaled.append((extra(d, b) + noise - pred_ref[at * groups + group, b]) / variance[-1] * live)
            left = stacked(scaled[-1])
            high, low = anomaly[-1]
            matches.append(fold(dot(left, high, 1) + dot(left, low, 1)))
    for d in range(1, 4):
        for i in range(blocks):
            total = jnp.zeros((ROWS, members), jnp.float32)
            for j in range(3 * blocks):
                level = extra(d, 2 * blocks + i * 3 * blocks + j) / 256.0 * share
                total = total + wide(level) * matches[(d - 1) * blocks + j]
            high, low = anomaly[d * blocks + i]
            left = stacked(total)
            correction = fold(dot(left, high, 0) + dot(left, low, 0))
            gain = scaled[d * blocks + i] - correction / variance[d * blocks + i]
            if d == 2:
                gain_ref[:, i * LANES : (i + 1) * LANES] = gain
            left = stacked(gain)
            both = stacked(fold(dot(left, high, 1) + dot(left, low, 1)))
            reach[(d - 1) * blocks + i] = jnp.concatenate([both, both], axis=1)
    for copy in copies:
        copy.wait()
    for slot in range(split_ref.shape[0]):
        weight = jnp.where(slot < count_ref[0], level_ref[0, slot].astype(jnp.float32) / 256.0, 0.0) * share
        change = fold(dot(reach[probes_ref[0, slot]], split_ref[slot], 0)) * weight
        block = cells_ref[0, slot]
        rows = pl.ds(row_of(block // tiles, block % tiles, tiles), ROWS, stride=planes * tiles)
        post_ref[rows, :] = post_ref[rows, :] + change


def shards(
    starting_speed_field,
    sample_fluidity_exponent,
    observed,
    obs_noise,
    obs_var,
    probe_cells,
    pair_cells,
    pair_probes,
    pair_taper,
    pair_counts,
    probe_taper,
):
    shape = starting_speed_field.shape
    members, planes, cells = shape
    tiles = cells // LANES
    slots = pair_cells.shape[1]
    probes = obs_noise.shape[1]
    blocks = probes // LANES
    slabs, chips = lax.axis_size("space"), lax.axis_size("chip")
    groups = 2 * chips
    f32, i32 = jnp.float32, jnp.int32
    u_rows = to_rows(starting_speed_field)
    t_rows = to_rows(sample_fluidity_exponent)
    obs_tiles = blocks - (-(2 * blocks + probe_taper.shape[1] * probe_taper.shape[2]) // ROWS)
    edge = jax.ShapeDtypeStruct((4 * tiles + 1 + obs_tiles, ROWS, LANES), f32)
    obs_shape = jax.ShapeDtypeStruct((obs_tiles, ROWS, LANES), f32)
    params = pltpu.CompilerParams(vmem_limit_bytes=32 * 1024 * 1024)
    stack = pltpu.VMEM((planes * tiles, ROWS, LANES), f32)
    low, high, obs, t_near, picked = pl.pallas_call(
        functools.partial(pack_kernel, planes, tiles),
        out_shape=(
            edge,
            edge,
            obs_shape,
            jax.ShapeDtypeStruct(u_rows.shape, f32),
            pltpu.HBM((slots, ROWS, LANES), f32),
        ),
        in_specs=[HBM] * 7,
        out_specs=(VMEM,) * 4 + (HBM,),
        scratch_shapes=[
            pltpu.SMEM(probe_taper.shape, i32),
            pltpu.VMEM(u_rows.shape, f32),
            pltpu.VMEM((ROWS, probes), f32),
            pltpu.VMEM((2, probes), f32),
            pltpu.SMEM(pair_cells.shape, i32),
            pltpu.VMEM((slots, ROWS, LANES), f32),
            pltpu.SemaphoreType.DMA((8,)),
        ],
        compiler_params=params,
        name="pack",
    )(*map(stay, (probe_taper, u_rows, t_rows, obs_noise, observed.reshape(1, -1), obs_var.reshape(1, -1), pair_cells)))
    little = pl.CostEstimate(flops=1000, bytes_accessed=1000, transcendentals=0)
    upward = [(i, i + 1) for i in range(slabs - 1)]
    before = lax.ppermute(high, "space", upward)
    after = lax.ppermute(low, "space", [(j, i) for i, j in upward])
    if slabs == 4:
        before_2 = after_2 = lax.ppermute(obs, "space", [(i, (i + 2) % 4) for i in range(4)])
    else:
        upward_2 = [(i, i + 2) for i in range(slabs - 2)]
        before_2 = lax.ppermute(obs, "space", upward_2)
        after_2 = lax.ppermute(obs, "space", [(j, i) for i, j in upward_2])
    inner, edges = pl.pallas_call(
        functools.partial(inner_kernel, planes, tiles),
        out_shape=(
            jax.ShapeDtypeStruct((planes * tiles, ROWS, LANES), f32),
            jax.ShapeDtypeStruct((14 * tiles, ROWS, LANES), f32),
        ),
        in_specs=[HBM, VMEM],
        out_specs=(VMEM, VMEM),
        scratch_shapes=[
            pltpu.VMEM(u_rows.shape, f32),
            stack,
            stack,
            stack,
            pltpu.VMEM((5, planes * tiles, ROWS, LANES), f32),
            pltpu.SemaphoreType.DMA(()),
        ],
        compiler_params=params,
        cost_estimate=pl.CostEstimate(flops=0, bytes_accessed=15_000_000, transcendentals=0),
        name="inner_planes",
    )(stay(u_rows), t_near)
    by_xor = chips <= 4 and chips & (chips - 1) == 0
    if by_xor:
        parts = [picked]
        for d in range(1, chips):
            parts.append(lax.ppermute(picked, "chip", [(i, i ^ d) for i in range(chips)]))
    else:
        parts = [lax.all_to_all(jnp.broadcast_to(picked, (chips, *picked.shape)), "chip", 0, 0)]
    u2, found, seen = pl.pallas_call(
        functools.partial(outer_kernel, planes, tiles),
        out_shape=(
            jax.ShapeDtypeStruct((planes * tiles, ROWS, LANES), f32),
            jax.ShapeDtypeStruct((blocks, ROWS, LANES), f32),
            jax.ShapeDtypeStruct((2 * obs_tiles, ROWS, LANES), f32),
        ),
        in_specs=[HBM] + [VMEM] * 4,
        out_specs=(VMEM,) * 3,
        scratch_shapes=[
            pltpu.SMEM(probe_cells.shape, i32),
            pltpu.SemaphoreType.DMA(()),
        ],
        input_output_aliases={4: 0},
        compiler_params=params,
        cost_estimate=little,
        name="outer_planes",
    )(stay(probe_cells), before, after, edges, inner)
    sent = pl.pallas_call(
        send_kernel,
        out_shape=pltpu.HBM((slabs * groups, blocks, ROWS, LANES), f32),
        in_specs=[VMEM] + [ANY] * len(parts),
        out_specs=HBM,
        scratch_shapes=[pltpu.SemaphoreType.DMA(())],
        compiler_params=params,
        cost_estimate=little,
        name="send",
    )(found, *parts)
    pred_all = lax.all_to_all(sent, ("space", "chip", "core"), 0, 0)
    u2_rows, *parts = pl.pallas_call(
        functools.partial(store_kernel, planes, tiles),
        out_shape=(jax.ShapeDtypeStruct(u_rows.shape, f32), *(jax.ShapeDtypeStruct(part.shape, f32) for part in parts)),
        in_specs=[VMEM] + [ANY] * len(parts),
        out_specs=(VMEM,) + (ANY,) * len(parts),
        input_output_aliases={1 + at: 1 + at for at in range(len(parts))},
        compiler_params=params,
        cost_estimate=little,
        name="store",
    )(u2, *parts)
    swapped = [lax.ppermute(part, "core", [(0, 1), (1, 0)]) for part in parts]
    where = [lax.axis_index(axes) for axes in ("space", ("chip", "core"), "chip", "core")]
    place = jnp.stack(where).astype(i32)
    split = pl.pallas_call(
        functools.partial(split_kernel, by_xor, chips),
        out_shape=pltpu.HBM((slots, 2 * groups * ROWS, LANES), jnp.bfloat16),
        in_specs=[SMEM] + [ANY] * (2 * len(parts)),
        out_specs=VMEM,
        scratch_shapes=[pltpu.VMEM((chips, 2, slots, ROWS, LANES), f32), pltpu.SemaphoreType.DMA((2 * chips,))],
        compiler_params=params,
        cost_estimate=little,
        name="split",
    )(place, *parts, *swapped)
    post_rows, gain = pl.pallas_call(
        functools.partial(update_kernel, slabs, planes, tiles),
        out_shape=(
            jax.ShapeDtypeStruct(u_rows.shape, f32),
            jax.ShapeDtypeStruct((members, probes), f32),
        ),
        in_specs=[SMEM] * 2 + [HBM] * 3 + [VMEM] * 5 + [HBM] * 2,
        out_specs=(VMEM,) * 2,
        scratch_shapes=[
            pltpu.VMEM((probe_taper.shape[2], 2 * ROWS, 2 * groups * ROWS), jnp.bfloat16),
            pltpu.SMEM(pair_cells.shape, i32),
            pltpu.SMEM(pair_cells.shape, i32),
            pltpu.SMEM(pair_cells.shape, i32),
            pltpu.VMEM(split.shape, jnp.bfloat16),
            pltpu.SemaphoreType.DMA((5,)),
        ],
        compiler_params=params,
        name="update",
    )(place, pair_counts, *map(stay, (pair_cells, pair_probes, pair_taper)), pred_all,
      before_2, seen, obs, after_2, stay(split), stay(t_rows))
    return (from_rows(u2_rows, shape), from_rows(post_rows, shape), gain)


def solution(mesh):
    slabs, groups = mesh.devices.shape
    split = jax.sharding.Mesh(mesh.devices.reshape(slabs, groups // 2, 2), ("space", "chip", "core"))
    members = ("chip", "core")
    return jax.shard_map(
        shards,
        mesh=split,
        in_specs=(
            P(members, "space", None),
            P(members, "space", None),
            P("space"),
            P(members, "space"),
            P("space"),
            P("space"),
            P("space", None),
            P("space", None),
            P("space", None),
            P("space"),
            P("space", None, None),
        ),
        out_specs=(P(members, "space", None), P(members, "space", None), P(members, "space")),
        check_vma=False,
    )
```

```python
import functools

import jax
import jax.numpy as jnp
from jax import lax
from jax.experimental import pallas as pl
from jax.experimental.pallas import tpu as pltpu
from jax.sharding import PartitionSpec as P

LANES = 128
ROWS = 8
NZ = 64
HALF_DT = 0.5 * 0.08

VMEM = pl.BlockSpec(memory_space=pltpu.VMEM)
SMEM = pl.BlockSpec(memory_space=pltpu.SMEM)
HBM = pl.BlockSpec(memory_space=pltpu.HBM)
ANY = pl.BlockSpec(memory_space=pl.ANY)


def stay(array):
    return pltpu.with_memory_space_constraint(array, pltpu.HBM)


def to_rows(array):
    members, planes, cells = array.shape
    split = array.reshape(members, planes // ROWS, ROWS, cells // LANES, LANES)
    return split.transpose(0, 1, 3, 2, 4).reshape(-1, LANES)


def from_rows(rows, shape):
    members, planes, cells = shape
    split = rows.reshape(members, planes // ROWS, cells // LANES, ROWS, LANES)
    return split.transpose(0, 1, 3, 2, 4).reshape(shape)


def row_of(plane, tile, tiles):
    return (plane // ROWS * tiles + tile) * ROWS + plane % ROWS


def pack_kernel(planes, tiles, taper_hbm, u_hbm, t_hbm, noise_hbm, observed_hbm, var_hbm, cells_hbm,
                low_ref, high_ref, obs_ref, t_ref, pick_ref,
                taper_ref, u_ref, noise_ref, row_ref, cells_ref, sems):
    stride = planes * tiles
    blocks = noise_ref.shape[1] // LANES
    copies = [
        pltpu.make_async_copy(source, target, sems.at[at])
        for at, (source, target) in enumerate((
            (t_hbm, t_ref),
            (u_hbm, u_ref),
            (taper_hbm, taper_ref),
            (noise_hbm, noise_ref),
            (observed_hbm, row_ref.at[0:1]),
            (var_hbm, row_ref.at[1:2]),
            (cells_hbm, cells_ref),
        ))
    ]
    for copy in copies:
        copy.start()
    copies[0].wait()
    copies[6].wait()
    for slot in range(pick_ref.shape[0]):
        block = cells_ref[0, slot]
        row = row_of(block // tiles, block % tiles, tiles)
        pick_ref[slot] = t_ref[pl.ds(row, ROWS, stride=stride), :]
    for kind, source in ((1, t_ref), (0, u_ref)):
        if kind == 0:
            copies[1].wait()
        for out_ref, first in ((high_ref, planes - 2), (low_ref, 0)):
            for depth in range(2):
                for tile in range(tiles):
                    out_ref[(kind * 2 + depth) * tiles + tile] = source[
                        pl.ds(row_of(first + depth, tile, tiles), ROWS, stride=stride), :
                    ]
    for ref in (low_ref, high_ref):
        ref[4 * tiles] = jnp.ones((ROWS, LANES), jnp.float32)
    for copy in copies[2:6]:
        copy.wait()
    own, window = taper_ref.shape[1:]
    rows = [row_ref[kind : kind + 1, b * LANES : (b + 1) * LANES] for kind in range(2) for b in range(blocks)]
    for i in range(own):
        for j in range(window):
            rows.append(jnp.full((1, LANES), taper_ref[0, i, j].astype(jnp.float32), jnp.float32))
    for b in range(blocks):
        obs_ref[b] = noise_ref[:, b * LANES : (b + 1) * LANES]
    for at, row in enumerate(rows):
        obs_ref[blocks + at // ROWS, at % ROWS : at % ROWS + 1, :] = row
    for ref in (low_ref, high_ref):
        for at in range(obs_ref.shape[0]):
            ref[4 * tiles + 1 + at] = obs_ref[at]


def rot(value, by):
    return pltpu.roll(value, by % LANES, 1)


def lane_masks():
    lane = lax.broadcasted_iota(jnp.int32, (ROWS, LANES), 1)
    height = lane & (NZ - 1)
    return lane < NZ, height == 0, height == NZ - 1


def coefficients(masks, low, here, high):
    first_half, floor, roof = masks
    tiles = len(here)
    turned = [rot(value, NZ) for value in here]
    out = []
    for tile in range(tiles):
        mid = here[tile]
        near = mid + turned[tile]
        far = mid + jnp.where(first_half, turned[tile - 1], turned[(tile + 1) % tiles])
        up = mid + jnp.where(roof, HALF_DT, rot(mid, -1))
        down = mid + jnp.where(floor, HALF_DT, rot(mid, 1))
        below = mid + low[tile]
        above = mid + high[tile]
        diag = 1.0 - ((near + far) + (up + down) + (below + above))
        out.append((diag, near, far, jnp.where(roof, 0.0, up), jnp.where(floor, 0.0, down), below, above))
    return out


def step(masks, weights, low, here, high):
    first_half = masks[0]
    tiles = len(here)
    turned = [rot(value, NZ) for value in here]
    out = []
    for tile in range(tiles):
        diag, near, far, up, down, below, above = weights[tile]
        mid = here[tile]
        beyond = jnp.where(first_half, turned[tile - 1], turned[(tile + 1) % tiles])
        out.append(
            (diag * mid + near * turned[tile])
            + (far * beyond + up * rot(mid, -1))
            + (down * rot(mid, 1) + below * low[tile])
            + above * high[tile]
        )
    return out


def plane_of(ref, at, tiles):
    return [ref[at * tiles + tile] for tile in range(tiles)]


def put(ref, at, values):
    for tile, value in enumerate(values):
        ref[at * len(values) + tile] = value


def each(first, last, unroll, body):
    count = (last - first) // unroll

    def several(at, _):
        for d in range(unroll):
            body(first + at * unroll + d)
        return 0

    lax.fori_loop(0, count, several, 0)
    for x in range(first + count * unroll, last):
        body(x)


def inner_kernel(planes, tiles, u_hbm, t_ref, u2_ref, edge_ref, u_ref, u0, hv, u1, held, sem):
    stride = planes * tiles
    masks = lane_masks()
    copy = pltpu.make_async_copy(u_hbm, u_ref, sem)
    copy.start()

    def rows_at(x, tile):
        return pl.ds((x // ROWS) * tiles * ROWS + x % ROWS + tile * ROWS, ROWS, stride=stride)

    def load_t(x):
        for tile in range(tiles):
            hv[x * tiles + tile] = HALF_DT * jnp.exp(t_ref[rows_at(x, tile), :])

    def load_u(x):
        for tile in range(tiles):
            u0[x * tiles + tile] = u_ref[rows_at(x, tile), :]

    def first_step(x):
        weights = coefficients(masks, *[plane_of(hv, x + d, tiles) for d in (-1, 0, 1)])
        for tile in range(tiles):
            for kind in range(5):
                held[kind, x * tiles + tile] = weights[tile][kind]
        put(u1, x, step(masks, weights, *[plane_of(u0, x + d, tiles) for d in (-1, 0, 1)]))

    def second_step(x):
        weights = []
        for tile in range(tiles):
            at = x * tiles + tile
            here = hv[at]
            weights.append([held[kind, at] for kind in range(5)] + [here + hv[at - tiles], here + hv[at + tiles]])
        put(u2_ref, x, step(masks, weights, *[plane_of(u1, x + d, tiles) for d in (-1, 0, 1)]))

    each(0, planes, 4, load_t)
    copy.wait()
    each(0, planes, 4, load_u)
    each(1, planes - 1, 7, first_step)
    each(2, planes - 2, 6, second_step)
    last = planes - 1
    at = 0
    for ref, kept in ((u0, (0, 1, last - 1, last)), (hv, (0, 1, 2, last - 2, last - 1, last)),
                      (u1, (1, 2, last - 2, last - 1))):
        for x in kept:
            put(edge_ref, at, plane_of(ref, x, tiles))
            at += 1


def outer_kernel(planes, tiles, probe_hbm, before_ref, after_ref, edge_ref, inner_ref,
                 u2_ref, found_ref, seen_ref, probe_ref, sem):
    probe_copy = pltpu.make_async_copy(probe_hbm, probe_ref, sem)
    probe_copy.start()
    masks = lane_masks()
    blocks = probe_ref.shape[0] // LANES
    count = seen_ref.shape[0] // 2
    for at in range(count):
        seen_ref[at] = before_ref[4 * tiles + 1 + at]
        seen_ref[count + at] = after_ref[4 * tiles + 1 + at]
    edge = [plane_of(edge_ref, at, tiles) for at in range(14)]
    last = planes - 1
    for ref, own_u, own_v, own_1, where in (
        (before_ref, edge[0:2], edge[4:7], edge[10:12], (0, 1)),
        (after_ref, edge[3:1:-1], edge[9:6:-1], edge[13:11:-1], (last, last - 1)),
    ):
        order = (0, 1) if ref is before_ref else (1, 0)
        u = [plane_of(ref, d, tiles) for d in order] + own_u
        v = [[HALF_DT * jnp.exp(t) for t in plane_of(ref, 2 + d, tiles)] for d in order] + own_v
        live = ref[4 * tiles]
        weights = [coefficients(masks, v[d], v[d + 1], v[d + 2]) for d in range(3)]
        next_u = [step(masks, weights[d], u[d], u[d + 1], u[d + 2]) for d in range(2)]
        next_u[0] = [value * live for value in next_u[0]]
        next_u = next_u + own_1
        for d in range(2):
            put(u2_ref, where[d], step(masks, weights[d + 1], next_u[d], next_u[d + 1], next_u[d + 2]))

    probe_copy.wait()
    lane = lax.broadcasted_iota(jnp.int32, (ROWS, LANES), 1)
    for part in range(blocks):
        found = jnp.zeros((ROWS, LANES), jnp.float32)
        for p in range(LANES):
            cell = probe_ref[part * LANES + p]
            turned = pltpu.roll(u2_ref[cell >> 7], (p - cell) & (LANES - 1), 1)
            found = jnp.where(lane == p, turned, found)

        found_ref[part] = found


def send_kernel(found_ref, *refs):
    sent_hbm, sem = refs[-2:]

    def send(device, _):
        pltpu.make_async_copy(found_ref, sent_hbm.at[device], sem).start()
        return 0

    lax.fori_loop(0, sent_hbm.shape[0], send, 0)
    pltpu.make_async_copy(sent_hbm, sent_hbm, sem).wait()


def halves(value):
    high = value.astype(jnp.bfloat16)
    return high, (value - high.astype(jnp.float32)).astype(jnp.bfloat16)


def store_kernel(planes, tiles, u2_ref, *refs):
    out_ref = refs[len(refs) // 2]

    def store(x):
        for tile in range(tiles):
            rows = pl.ds((x // ROWS) * tiles * ROWS + x % ROWS + tile * ROWS, ROWS, stride=planes * tiles)
            out_ref[rows, :] = u2_ref[x * tiles + tile]

    each(0, planes, 4, store)


def stacked(value):
    high, low = halves(value)
    return jnp.concatenate([high.astype(jnp.float32), low.astype(jnp.float32)], axis=0).astype(jnp.bfloat16)


def fold(both):
    return both[:ROWS] + both[ROWS:]


def dot(left, right, over):
    return lax.dot_general(left, right, (((1,), (over,)), ((), ())), preferred_element_type=jnp.float32)


def update_kernel(slabs, chips, planes, tiles, place_ref, count_ref, cells_hbm, probes_hbm, level_hbm,
                  pred_ref, before_2_ref, seen_ref, own_ref, after_2_ref, t_hbm, *refs):
    *parts, post_ref, gain_ref, reach, cells_ref, probes_ref, level_ref, theta_ref, sems = refs
    chip, core = place_ref[2], place_ref[3]
    same, other = parts[: len(parts) // 2], parts[len(parts) // 2 :]
    by_xor = len(same) == chips
    if not by_xor:
        same, other = ([ref.at[at] for at in range(chips)] for (ref,) in (same, other))
    groups, blocks = pred_ref.shape[0] // slabs, pred_ref.shape[1]
    members = groups * ROWS
    share = 1.0 / (members - 1)
    copies = [
        pltpu.make_async_copy(source, target, sems.at[at])
        for at, (source, target) in enumerate((
            (cells_hbm, cells_ref), (probes_hbm, probes_ref), (level_hbm, level_ref),
            (t_hbm, post_ref)))
    ]
    for at in range(chips):
        where = chip ^ at if by_xor else at
        for side, source in ((core, same[at]), (1 - core, other[at])):
            copies.append(pltpu.make_async_copy(source, theta_ref.at[where, side], sems.at[len(copies)]))
    for copy in copies:
        copy.start()
    slab, group = place_ref[0], place_ref[1]
    seen = ((before_2_ref, 0), (seen_ref, 0), (own_ref, 0), (seen_ref, seen_ref.shape[0] // 2), (after_2_ref, 0))

    def extra(d, at):
        ref, first = seen[d]
        return ref[first + blocks + at // ROWS, at % ROWS : at % ROWS + 1, :]

    def wide(row):
        return row[:, :members] if members <= LANES else jnp.concatenate([row] * (members // LANES), axis=1)

    anomaly, scaled, variance, matches = [], [], [], []
    for d in range(5):
        wanted = slab + d - 2
        at = jnp.clip(wanted, 0, slabs - 1)
        live = jnp.where((wanted >= 0) & (wanted < slabs), 1.0, 0.0)
        for b in range(blocks):
            predicted = pred_ref[pl.ds(at * groups, groups), b].reshape(members, LANES)
            mean = jnp.sum(predicted, axis=0, keepdims=True) / members
            anomaly.append(halves((predicted - mean) * live))
            variance.append(extra(d, blocks + b) + (1.0 - live))
            noise = seen[d][0][seen[d][1] + b]
            scaled.append((extra(d, b) + noise - pred_ref[at * groups + group, b]) / variance[-1] * live)
            left = stacked(scaled[-1])
            high, low = anomaly[-1]
            matches.append(fold(dot(left, high, 1) + dot(left, low, 1)))
    for d in range(1, 4):
        for i in range(blocks):
            total = jnp.zeros((ROWS, members), jnp.float32)
            for j in range(3 * blocks):
                level = extra(d, 2 * blocks + i * 3 * blocks + j) / 256.0 * share
                total = total + wide(level) * matches[(d - 1) * blocks + j]
            high, low = anomaly[d * blocks + i]
            left = stacked(total)
            correction = fold(dot(left, high, 0) + dot(left, low, 0))
            gain = scaled[d * blocks + i] - correction / variance[d * blocks + i]
            if d == 2:
                gain_ref[:, i * LANES : (i + 1) * LANES] = gain
            left = stacked(gain)
            both = stacked(fold(dot(left, high, 1) + dot(left, low, 1)))
            reach[(d - 1) * blocks + i] = jnp.concatenate([both, both], axis=1)
    for copy in copies:
        copy.wait()
    for slot in range(theta_ref.shape[2]):
        weight = jnp.where(slot < count_ref[0], level_ref[0, slot].astype(jnp.float32) / 256.0, 0.0) * share
        high, low = halves(theta_ref[:, :, slot].reshape(members, LANES))
        both = jnp.concatenate([high, low], axis=0)
        change = fold(dot(reach[probes_ref[0, slot]], both, 0)) * weight
        block = cells_ref[0, slot]
        rows = pl.ds(row_of(block // tiles, block % tiles, tiles), ROWS, stride=planes * tiles)
        post_ref[rows, :] = post_ref[rows, :] + change


def shards(
    starting_speed_field,
    sample_fluidity_exponent,
    observed,
    obs_noise,
    obs_var,
    probe_cells,
    pair_cells,
    pair_probes,
    pair_taper,
    pair_counts,
    probe_taper,
):
    shape = starting_speed_field.shape
    members, planes, cells = shape
    tiles = cells // LANES
    slots = pair_cells.shape[1]
    probes = obs_noise.shape[1]
    blocks = probes // LANES
    slabs, chips = lax.axis_size("space"), lax.axis_size("chip")
    groups = 2 * chips
    f32, i32 = jnp.float32, jnp.int32
    u_rows = to_rows(starting_speed_field)
    t_rows = to_rows(sample_fluidity_exponent)
    obs_tiles = blocks - (-(2 * blocks + probe_taper.shape[1] * probe_taper.shape[2]) // ROWS)
    edge = jax.ShapeDtypeStruct((4 * tiles + 1 + obs_tiles, ROWS, LANES), f32)
    obs_shape = jax.ShapeDtypeStruct((obs_tiles, ROWS, LANES), f32)
    params = pltpu.CompilerParams(vmem_limit_bytes=32 * 1024 * 1024)
    stack = pltpu.VMEM((planes * tiles, ROWS, LANES), f32)
    low, high, obs, t_near, picked = pl.pallas_call(
        functools.partial(pack_kernel, planes, tiles),
        out_shape=(
            edge,
            edge,
            obs_shape,
            jax.ShapeDtypeStruct(u_rows.shape, f32),
            jax.ShapeDtypeStruct((slots, ROWS, LANES), f32),
        ),
        in_specs=[HBM] * 7,
        out_specs=(VMEM,) * 5,
        scratch_shapes=[
            pltpu.SMEM(probe_taper.shape, i32),
            pltpu.VMEM(u_rows.shape, f32),
            pltpu.VMEM((ROWS, probes), f32),
            pltpu.VMEM((2, probes), f32),
            pltpu.SMEM(pair_cells.shape, i32),
            pltpu.SemaphoreType.DMA((7,)),
        ],
        compiler_params=params,
        name="pack",
    )(*map(stay, (probe_taper, u_rows, t_rows, obs_noise, observed.reshape(1, -1), obs_var.reshape(1, -1), pair_cells)))
    little = pl.CostEstimate(flops=1000, bytes_accessed=1000, transcendentals=0)
    upward = [(i, i + 1) for i in range(slabs - 1)]
    before = lax.ppermute(high, "space", upward)
    after = lax.ppermute(low, "space", [(j, i) for i, j in upward])
    if slabs == 4:
        before_2 = after_2 = lax.ppermute(obs, "space", [(i, (i + 2) % 4) for i in range(4)])
    else:
        upward_2 = [(i, i + 2) for i in range(slabs - 2)]
        before_2 = lax.ppermute(obs, "space", upward_2)
        after_2 = lax.ppermute(obs, "space", [(j, i) for i, j in upward_2])
    inner, edges = pl.pallas_call(
        functools.partial(inner_kernel, planes, tiles),
        out_shape=(
            jax.ShapeDtypeStruct((planes * tiles, ROWS, LANES), f32),
            jax.ShapeDtypeStruct((14 * tiles, ROWS, LANES), f32),
        ),
        in_specs=[HBM, VMEM],
        out_specs=(VMEM, VMEM),
        scratch_shapes=[
            pltpu.VMEM(u_rows.shape, f32),
            stack,
            stack,
            stack,
            pltpu.VMEM((5, planes * tiles, ROWS, LANES), f32),
            pltpu.SemaphoreType.DMA(()),
        ],
        compiler_params=params,
        cost_estimate=pl.CostEstimate(flops=0, bytes_accessed=15_000_000, transcendentals=0),
        name="inner_planes",
    )(stay(u_rows), t_near)
    by_xor = chips <= 4 and chips & (chips - 1) == 0
    if by_xor:
        parts = [picked]
        for d in range(1, chips):
            parts.append(lax.ppermute(picked, "chip", [(i, i ^ d) for i in range(chips)]))
    else:
        parts = [lax.all_to_all(jnp.broadcast_to(picked, (chips, *picked.shape)), "chip", 0, 0)]
    u2, found, seen = pl.pallas_call(
        functools.partial(outer_kernel, planes, tiles),
        out_shape=(
            jax.ShapeDtypeStruct((planes * tiles, ROWS, LANES), f32),
            jax.ShapeDtypeStruct((blocks, ROWS, LANES), f32),
            jax.ShapeDtypeStruct((2 * obs_tiles, ROWS, LANES), f32),
        ),
        in_specs=[HBM] + [VMEM] * 4,
        out_specs=(VMEM,) * 3,
        scratch_shapes=[
            pltpu.SMEM(probe_cells.shape, i32),
            pltpu.SemaphoreType.DMA(()),
        ],
        input_output_aliases={4: 0},
        compiler_params=params,
        cost_estimate=little,
        name="outer_planes",
    )(stay(probe_cells), before, after, edges, inner)
    sent = pl.pallas_call(
        send_kernel,
        out_shape=pltpu.HBM((slabs * groups, blocks, ROWS, LANES), f32),
        in_specs=[VMEM] + [ANY] * len(parts),
        out_specs=HBM,
        scratch_shapes=[pltpu.SemaphoreType.DMA(())],
        compiler_params=params,
        cost_estimate=little,
        name="send",
    )(found, *parts)
    pred_all = lax.all_to_all(sent, ("space", "chip", "core"), 0, 0)
    u2_rows, *parts = pl.pallas_call(
        functools.partial(store_kernel, planes, tiles),
        out_shape=(jax.ShapeDtypeStruct(u_rows.shape, f32), *(jax.ShapeDtypeStruct(part.shape, f32) for part in parts)),
        in_specs=[VMEM] + [ANY] * len(parts),
        out_specs=(VMEM,) + (ANY,) * len(parts),
        input_output_aliases={1 + at: 1 + at for at in range(len(parts))},
        compiler_params=params,
        cost_estimate=little,
        name="store",
    )(u2, *parts)
    swapped = [lax.ppermute(part, "core", [(0, 1), (1, 0)]) for part in parts]
    where = [lax.axis_index(axes) for axes in ("space", ("chip", "core"), "chip", "core")]
    place = jnp.stack(where).astype(i32)
    post_rows, gain = pl.pallas_call(
        functools.partial(update_kernel, slabs, chips, planes, tiles),
        out_shape=(
            jax.ShapeDtypeStruct(u_rows.shape, f32),
            jax.ShapeDtypeStruct((members, probes), f32),
        ),
        in_specs=[SMEM] * 2 + [HBM] * 3 + [VMEM] * 5 + [HBM] + [ANY] * (2 * len(parts)),
        out_specs=(VMEM,) * 2,
        scratch_shapes=[
            pltpu.VMEM((probe_taper.shape[2], 2 * ROWS, 2 * groups * ROWS), jnp.bfloat16),
            pltpu.SMEM(pair_cells.shape, i32),
            pltpu.SMEM(pair_cells.shape, i32),
            pltpu.SMEM(pair_cells.shape, i32),
            pltpu.VMEM((chips, 2, slots, ROWS, LANES), f32),
            pltpu.SemaphoreType.DMA((4 + groups,)),
        ],
        compiler_params=params,
        name="update",
    )(place, pair_counts, *map(stay, (pair_cells, pair_probes, pair_taper)), pred_all,
      before_2, seen, obs, after_2, stay(t_rows), *parts, *swapped)
    return (from_rows(u2_rows, shape), from_rows(post_rows, shape), gain)


def solution(mesh):
    slabs, groups = mesh.devices.shape
    split = jax.sharding.Mesh(mesh.devices.reshape(slabs, groups // 2, 2), ("space", "chip", "core"))
    members = ("chip", "core")
    return jax.shard_map(
        shards,
        mesh=split,
        in_specs=(
            P(members, "space", None),
            P(members, "space", None),
            P("space"),
            P(members, "space"),
            P("space"),
            P("space"),
            P("space", None),
            P("space", None),
            P("space", None),
            P("space"),
            P("space", None, None),
        ),
        out_specs=(P(members, "space", None), P(members, "space", None), P(members, "space")),
        check_vma=False,
    )
```

```python
import functools

import jax
import jax.numpy as jnp
from jax import lax
from jax.experimental import pallas as pl
from jax.experimental.pallas import tpu as pltpu
from jax.sharding import PartitionSpec as P

LANES = 128
ROWS = 8
NZ = 64
HALF_DT = 0.5 * 0.08

VMEM = pl.BlockSpec(memory_space=pltpu.VMEM)
SMEM = pl.BlockSpec(memory_space=pltpu.SMEM)
HBM = pl.BlockSpec(memory_space=pltpu.HBM)
ANY = pl.BlockSpec(memory_space=pl.ANY)


def stay(array):
    return pltpu.with_memory_space_constraint(array, pltpu.HBM)


def to_rows(array):
    members, planes, cells = array.shape
    split = array.reshape(members, planes // ROWS, ROWS, cells // LANES, LANES)
    return split.transpose(0, 1, 3, 2, 4).reshape(-1, LANES)


def from_rows(rows, shape):
    members, planes, cells = shape
    split = rows.reshape(members, planes // ROWS, cells // LANES, ROWS, LANES)
    return split.transpose(0, 1, 3, 2, 4).reshape(shape)


def row_of(plane, tile, tiles):
    return (plane // ROWS * tiles + tile) * ROWS + plane % ROWS


def pack_kernel(planes, tiles, taper_hbm, u_hbm, t_hbm, noise_hbm, observed_hbm, var_hbm, cells_hbm,
                low_ref, high_ref, obs_ref, t_ref, pick_ref,
                taper_ref, u_ref, noise_ref, row_ref, cells_ref, sems):
    stride = planes * tiles
    blocks = noise_ref.shape[1] // LANES
    copies = [
        pltpu.make_async_copy(source, target, sems.at[at])
        for at, (source, target) in enumerate((
            (t_hbm, t_ref),
            (u_hbm, u_ref),
            (taper_hbm, taper_ref),
            (noise_hbm, noise_ref),
            (observed_hbm, row_ref.at[0:1]),
            (var_hbm, row_ref.at[1:2]),
            (cells_hbm, cells_ref),
        ))
    ]
    for copy in copies:
        copy.start()
    copies[0].wait()
    copies[6].wait()
    for slot in range(pick_ref.shape[0]):
        block = cells_ref[0, slot]
        row = row_of(block // tiles, block % tiles, tiles)
        pick_ref[slot] = t_ref[pl.ds(row, ROWS, stride=stride), :]
    for kind, source in ((1, t_ref), (0, u_ref)):
        if kind == 0:
            copies[1].wait()
        for out_ref, first in ((high_ref, planes - 2), (low_ref, 0)):
            for depth in range(2):
                for tile in range(tiles):
                    out_ref[(kind * 2 + depth) * tiles + tile] = source[
                        pl.ds(row_of(first + depth, tile, tiles), ROWS, stride=stride), :
                    ]
    for ref in (low_ref, high_ref):
        ref[4 * tiles] = jnp.ones((ROWS, LANES), jnp.float32)
    for copy in copies[2:6]:
        copy.wait()
    own, window = taper_ref.shape[1:]
    rows = [row_ref[kind : kind + 1, b * LANES : (b + 1) * LANES] for kind in range(2) for b in range(blocks)]
    for i in range(own):
        for j in range(window):
            rows.append(jnp.full((1, LANES), taper_ref[0, i, j].astype(jnp.float32), jnp.float32))
    for b in range(blocks):
        obs_ref[b] = noise_ref[:, b * LANES : (b + 1) * LANES]
    for at, row in enumerate(rows):
        obs_ref[blocks + at // ROWS, at % ROWS : at % ROWS + 1, :] = row
    for ref in (low_ref, high_ref):
        for at in range(obs_ref.shape[0]):
            ref[4 * tiles + 1 + at] = obs_ref[at]


def rot(value, by):
    return pltpu.roll(value, by % LANES, 1)


def lane_masks():
    lane = lax.broadcasted_iota(jnp.int32, (ROWS, LANES), 1)
    height = lane & (NZ - 1)
    return lane < NZ, height == 0, height == NZ - 1


def coefficients(masks, low, here, high):
    first_half, floor, roof = masks
    tiles = len(here)
    turned = [rot(value, NZ) for value in here]
    out = []
    for tile in range(tiles):
        mid = here[tile]
        near = mid + turned[tile]
        far = mid + jnp.where(first_half, turned[tile - 1], turned[(tile + 1) % tiles])
        up = mid + jnp.where(roof, HALF_DT, rot(mid, -1))
        down = mid + jnp.where(floor, HALF_DT, rot(mid, 1))
        below = mid + low[tile]
        above = mid + high[tile]
        diag = 1.0 - ((near + far) + (up + down) + (below + above))
        out.append((diag, near, far, jnp.where(roof, 0.0, up), jnp.where(floor, 0.0, down), below, above))
    return out


def step(masks, weights, low, here, high):
    first_half = masks[0]
    tiles = len(here)
    turned = [rot(value, NZ) for value in here]
    out = []
    for tile in range(tiles):
        diag, near, far, up, down, below, above = weights[tile]
        mid = here[tile]
        beyond = jnp.where(first_half, turned[tile - 1], turned[(tile + 1) % tiles])
        out.append(
            (diag * mid + near * turned[tile])
            + (far * beyond + up * rot(mid, -1))
            + (down * rot(mid, 1) + below * low[tile])
            + above * high[tile]
        )
    return out


def plane_of(ref, at, tiles):
    return [ref[at * tiles + tile] for tile in range(tiles)]


def put(ref, at, values):
    for tile, value in enumerate(values):
        ref[at * len(values) + tile] = value


def each(first, last, unroll, body):
    count = (last - first) // unroll

    def several(at, _):
        for d in range(unroll):
            body(first + at * unroll + d)
        return 0

    lax.fori_loop(0, count, several, 0)
    for x in range(first + count * unroll, last):
        body(x)


def inner_kernel(planes, tiles, u_hbm, t_ref, u2_ref, edge_ref, u_ref, u0, hv, u1, held, sem):
    stride = planes * tiles
    masks = lane_masks()
    copy = pltpu.make_async_copy(u_hbm, u_ref, sem)
    copy.start()

    def rows_at(x, tile):
        return pl.ds((x // ROWS) * tiles * ROWS + x % ROWS + tile * ROWS, ROWS, stride=stride)

    def load_t(x):
        for tile in range(tiles):
            hv[x * tiles + tile] = HALF_DT * jnp.exp(t_ref[rows_at(x, tile), :])

    def load_u(x):
        for tile in range(tiles):
            u0[x * tiles + tile] = u_ref[rows_at(x, tile), :]

    def first_step(x):
        weights = coefficients(masks, *[plane_of(hv, x + d, tiles) for d in (-1, 0, 1)])
        for tile in range(tiles):
            for kind in range(5):
                held[kind, x * tiles + tile] = weights[tile][kind]
        put(u1, x, step(masks, weights, *[plane_of(u0, x + d, tiles) for d in (-1, 0, 1)]))

    def second_step(x):
        weights = []
        for tile in range(tiles):
            at = x * tiles + tile
            here = hv[at]
            weights.append([held[kind, at] for kind in range(5)] + [here + hv[at - tiles], here + hv[at + tiles]])
        put(u2_ref, x, step(masks, weights, *[plane_of(u1, x + d, tiles) for d in (-1, 0, 1)]))

    each(0, planes, 4, load_t)
    copy.wait()
    each(0, planes, 4, load_u)
    each(1, planes - 1, 7, first_step)
    each(2, planes - 2, 6, second_step)
    last = planes - 1
    at = 0
    for ref, kept in ((u0, (0, 1, last - 1, last)), (hv, (0, 1, 2, last - 2, last - 1, last)),
                      (u1, (1, 2, last - 2, last - 1))):
        for x in kept:
            put(edge_ref, at, plane_of(ref, x, tiles))
            at += 1


def outer_kernel(planes, tiles, probe_hbm, before_ref, after_ref, edge_ref, inner_ref,
                 u2_ref, found_ref, seen_ref, probe_ref, sem):
    probe_copy = pltpu.make_async_copy(probe_hbm, probe_ref, sem)
    probe_copy.start()
    masks = lane_masks()
    blocks = probe_ref.shape[0] // LANES
    count = seen_ref.shape[0] // 2
    for at in range(count):
        seen_ref[at] = before_ref[4 * tiles + 1 + at]
        seen_ref[count + at] = after_ref[4 * tiles + 1 + at]
    edge = [plane_of(edge_ref, at, tiles) for at in range(14)]
    last = planes - 1
    for ref, own_u, own_v, own_1, where in (
        (before_ref, edge[0:2], edge[4:7], edge[10:12], (0, 1)),
        (after_ref, edge[3:1:-1], edge[9:6:-1], edge[13:11:-1], (last, last - 1)),
    ):
        order = (0, 1) if ref is before_ref else (1, 0)
        u = [plane_of(ref, d, tiles) for d in order] + own_u
        v = [[HALF_DT * jnp.exp(t) for t in plane_of(ref, 2 + d, tiles)] for d in order] + own_v
        live = ref[4 * tiles]
        weights = [coefficients(masks, v[d], v[d + 1], v[d + 2]) for d in range(3)]
        next_u = [step(masks, weights[d], u[d], u[d + 1], u[d + 2]) for d in range(2)]
        next_u[0] = [value * live for value in next_u[0]]
        next_u = next_u + own_1
        for d in range(2):
            put(u2_ref, where[d], step(masks, weights[d + 1], next_u[d], next_u[d + 1], next_u[d + 2]))

    probe_copy.wait()
    lane = lax.broadcasted_iota(jnp.int32, (ROWS, LANES), 1)
    for part in range(blocks):
        found = jnp.zeros((ROWS, LANES), jnp.float32)
        for p in range(LANES):
            cell = probe_ref[part * LANES + p]
            turned = pltpu.roll(u2_ref[cell >> 7], (p - cell) & (LANES - 1), 1)
            found = jnp.where(lane == p, turned, found)

        found_ref[part * ROWS : (part + 1) * ROWS, :] = found


def send_kernel(found_ref, *refs):
    sent_hbm, sem = refs[-2:]

    def send(device, _):
        pltpu.make_async_copy(found_ref, sent_hbm.at[device], sem).start()
        return 0

    lax.fori_loop(0, sent_hbm.shape[0], send, 0)
    pltpu.make_async_copy(sent_hbm, sent_hbm, sem).wait()


def halves(value):
    high = value.astype(jnp.bfloat16)
    return high, (value - high.astype(jnp.float32)).astype(jnp.bfloat16)


def store_kernel(planes, tiles, u2_ref, *refs):
    out_ref = refs[len(refs) // 2]

    def store(x):
        for tile in range(tiles):
            rows = pl.ds((x // ROWS) * tiles * ROWS + x % ROWS + tile * ROWS, ROWS, stride=planes * tiles)
            out_ref[rows, :] = u2_ref[x * tiles + tile]

    each(0, planes, 4, store)


def split_kernel(by_xor, chips, place_ref, *refs):
    *parts, split_hbm, theta_ref, split_ref, sems = refs
    chip, core = place_ref[2], place_ref[3]
    same, other = parts[: len(parts) // 2], parts[len(parts) // 2 :]
    if not by_xor:
        same, other = ([ref.at[at] for at in range(chips)] for (ref,) in (same, other))
    slots, members = theta_ref.shape[2], 2 * chips * ROWS
    half = slots // 2
    arriving, leaving = [[], []], []
    for side in range(2):
        cut = pl.ds(side * half, half)
        for at in range(chips):
            where = chip ^ at if by_xor else at
            for slot, source in ((core, same[at]), (1 - core, other[at])):
                target = theta_ref.at[where, slot, cut]
                sem = sems.at[2 * chips * side + len(arriving[side])]
                arriving[side].append(pltpu.make_async_copy(source.at[cut], target, sem))
        leaving.append(pltpu.make_async_copy(split_ref.at[cut], split_hbm.at[cut], sems.at[4 * chips + side]))
    for copy in arriving[0] + arriving[1]:
        copy.start()

    def split(slot):
        high, low = halves(theta_ref[:, :, slot].reshape(members, LANES))
        split_ref[slot, :members, :] = high
        split_ref[slot, members:, :] = low

    for side in range(2):
        for copy in arriving[side]:
            copy.wait()
        each(side * half, (side + 1) * half, 4, split)
        leaving[side].start()
    for copy in leaving:
        copy.wait()


def stacked(value):
    high, low = halves(value)
    return jnp.concatenate([high.astype(jnp.float32), low.astype(jnp.float32)], axis=0).astype(jnp.bfloat16)


def beside(pair):
    return jnp.concatenate(pair, axis=1)


def fold(both):
    return both[:ROWS] + both[ROWS:]


def dot(left, right, over):
    return lax.dot_general(left, right, (((1,), (over,)), ((), ())), preferred_element_type=jnp.float32)


def update_kernel(slabs, planes, tiles, place_ref, count_ref, cells_hbm, probes_hbm, level_hbm,
                  pred_ref, before_2_ref, seen_ref, own_ref, after_2_ref, t_hbm, split_hbm, pick_hbm,
                  post_ref, gain_ref, reach, cells_ref, probes_ref, level_ref, split_ref, pick_ref, sum_ref, sems):
    groups, blocks = pred_ref.shape[0] // slabs, pred_ref.shape[1] // ROWS
    members = groups * ROWS
    share = 1.0 / (members - 1)
    copies = [
        pltpu.make_async_copy(source, target, sems.at[at])
        for at, (source, target) in enumerate((
            (cells_hbm, cells_ref), (probes_hbm, probes_ref), (level_hbm, level_ref),
            (pick_hbm, pick_ref), (split_hbm, split_ref), (t_hbm, post_ref)))
    ]
    for copy in copies:
        copy.start()
    slab, group = place_ref[0], place_ref[1]
    seen = ((before_2_ref, 0), (seen_ref, 0), (own_ref, 0), (seen_ref, seen_ref.shape[0] // 2), (after_2_ref, 0))

    def extra(d, at):
        ref, first = seen[d]
        return ref[first + blocks + at // ROWS, at % ROWS : at % ROWS + 1, :]

    def wide(row):
        return row[:, :members] if members <= LANES else jnp.concatenate([row] * (members // LANES), axis=1)

    anomaly, scaled, variance, matches = [], [], [], []
    for d in range(5):
        wanted = slab + d - 2
        at = jnp.clip(wanted, 0, slabs - 1)
        live = jnp.where((wanted >= 0) & (wanted < slabs), 1.0, 0.0)
        for b in range(blocks):
            cut = slice(b * ROWS, (b + 1) * ROWS)
            predicted = pred_ref[pl.ds(at * groups, groups), cut].reshape(members, LANES)
            mean = jnp.sum(predicted, axis=0, keepdims=True) / members
            anomaly.append(beside(halves((predicted - mean) * live)))
            variance.append(extra(d, blocks + b) + (1.0 - live))
            noise = seen[d][0][seen[d][1] + b]
            scaled.append((extra(d, b) + noise - pred_ref[at * groups + group, cut]) / variance[-1] * live)
            matches.append(fold(dot(beside([stacked(scaled[-1])] * 2), anomaly[-1], 1)))
    for d in range(1, 4):
        for i in range(blocks):
            total = jnp.zeros((ROWS, members), jnp.float32)
            for j in range(3 * blocks):
                level = extra(d, 2 * blocks + i * 3 * blocks + j) / 256.0 * share
                total = total + wide(level) * matches[(d - 1) * blocks + j]
            both = anomaly[d * blocks + i]
            left = stacked(total)
            correction = fold(dot(left, both[:, :LANES], 0) + dot(left, both[:, LANES:], 0))
            gain = scaled[d * blocks + i] - correction / variance[d * blocks + i]
            if d == 2:
                gain_ref[:, i * LANES : (i + 1) * LANES] = gain
            near = stacked(fold(dot(beside([stacked(gain)] * 2), both, 1)))
            reach[(d - 1) * blocks + i] = beside([near, near])
    for copy in copies[:4]:
        copy.wait()
    slots = split_ref.shape[0]
    blocks_of = [cells_ref[0, slot] for slot in range(slots)]
    for slot in range(slots):
        sum_ref[blocks_of[slot]] = pick_ref[slot]
    copies[4].wait()
    for slot in range(slots):
        weight = jnp.where(slot < count_ref[0], level_ref[0, slot].astype(jnp.float32) / 256.0, 0.0) * share
        change = fold(dot(reach[probes_ref[0, slot]], split_ref[slot], 0)) * weight
        sum_ref[blocks_of[slot]] = sum_ref[blocks_of[slot]] + change
    copies[5].wait()
    for slot in range(slots):
        block = blocks_of[slot]
        rows = pl.ds(row_of(block // tiles, block % tiles, tiles), ROWS, stride=planes * tiles)
        post_ref[rows, :] = sum_ref[block]


def shards(
    starting_speed_field,
    sample_fluidity_exponent,
    observed,
    obs_noise,
    obs_var,
    probe_cells,
    pair_cells,
    pair_probes,
    pair_taper,
    pair_counts,
    probe_taper,
):
    shape = starting_speed_field.shape
    members, planes, cells = shape
    tiles = cells // LANES
    slots = pair_cells.shape[1]
    probes = obs_noise.shape[1]
    blocks = probes // LANES
    slabs, chips = lax.axis_size("space"), lax.axis_size("chip")
    groups = 2 * chips
    f32, i32 = jnp.float32, jnp.int32
    u_rows = to_rows(starting_speed_field)
    t_rows = to_rows(sample_fluidity_exponent)
    obs_tiles = blocks - (-(2 * blocks + probe_taper.shape[1] * probe_taper.shape[2]) // ROWS)
    edge = jax.ShapeDtypeStruct((4 * tiles + 1 + obs_tiles, ROWS, LANES), f32)
    obs_shape = jax.ShapeDtypeStruct((obs_tiles, ROWS, LANES), f32)
    params = pltpu.CompilerParams(vmem_limit_bytes=32 * 1024 * 1024)
    stack = pltpu.VMEM((planes * tiles, ROWS, LANES), f32)
    low, high, obs, t_near, picked = pl.pallas_call(
        functools.partial(pack_kernel, planes, tiles),
        out_shape=(
            edge,
            edge,
            obs_shape,
            jax.ShapeDtypeStruct(u_rows.shape, f32),
            jax.ShapeDtypeStruct((slots, ROWS, LANES), f32),
        ),
        in_specs=[HBM] * 7,
        out_specs=(VMEM,) * 5,
        scratch_shapes=[
            pltpu.SMEM(probe_taper.shape, i32),
            pltpu.VMEM(u_rows.shape, f32),
            pltpu.VMEM((ROWS, probes), f32),
            pltpu.VMEM((2, probes), f32),
            pltpu.SMEM(pair_cells.shape, i32),
            pltpu.SemaphoreType.DMA((7,)),
        ],
        compiler_params=params,
        name="pack",
    )(*map(stay, (probe_taper, u_rows, t_rows, obs_noise, observed.reshape(1, -1), obs_var.reshape(1, -1), pair_cells)))
    little = pl.CostEstimate(flops=1000, bytes_accessed=1000, transcendentals=0)
    upward = [(i, i + 1) for i in range(slabs - 1)]
    before = lax.ppermute(high, "space", upward)
    after = lax.ppermute(low, "space", [(j, i) for i, j in upward])
    if slabs == 4:
        before_2 = after_2 = lax.ppermute(obs, "space", [(i, (i + 2) % 4) for i in range(4)])
    else:
        upward_2 = [(i, i + 2) for i in range(slabs - 2)]
        before_2 = lax.ppermute(obs, "space", upward_2)
        after_2 = lax.ppermute(obs, "space", [(j, i) for i, j in upward_2])
    inner, edges = pl.pallas_call(
        functools.partial(inner_kernel, planes, tiles),
        out_shape=(
            jax.ShapeDtypeStruct((planes * tiles, ROWS, LANES), f32),
            jax.ShapeDtypeStruct((14 * tiles, ROWS, LANES), f32),
        ),
        in_specs=[HBM, VMEM],
        out_specs=(VMEM, VMEM),
        scratch_shapes=[
            pltpu.VMEM(u_rows.shape, f32),
            stack,
            stack,
            stack,
            pltpu.VMEM((5, planes * tiles, ROWS, LANES), f32),
            pltpu.SemaphoreType.DMA(()),
        ],
        compiler_params=params,
        cost_estimate=pl.CostEstimate(flops=0, bytes_accessed=15_000_000, transcendentals=0),
        name="inner_planes",
    )(stay(u_rows), t_near)
    by_xor = chips <= 4 and chips & (chips - 1) == 0
    if by_xor:
        parts = [picked]
        for d in range(1, chips):
            parts.append(lax.ppermute(picked, "chip", [(i, i ^ d) for i in range(chips)]))
    else:
        parts = [lax.all_to_all(jnp.broadcast_to(picked, (chips, *picked.shape)), "chip", 0, 0)]
    u2, found, seen = pl.pallas_call(
        functools.partial(outer_kernel, planes, tiles),
        out_shape=(
            jax.ShapeDtypeStruct((planes * tiles, ROWS, LANES), f32),
            jax.ShapeDtypeStruct((blocks * ROWS, LANES), f32),
            jax.ShapeDtypeStruct((2 * obs_tiles, ROWS, LANES), f32),
        ),
        in_specs=[HBM] + [VMEM] * 4,
        out_specs=(VMEM,) * 3,
        scratch_shapes=[
            pltpu.SMEM(probe_cells.shape, i32),
            pltpu.SemaphoreType.DMA(()),
        ],
        input_output_aliases={4: 0},
        compiler_params=params,
        cost_estimate=little,
        name="outer_planes",
    )(stay(probe_cells), before, after, edges, inner)
    sent = pl.pallas_call(
        send_kernel,
        out_shape=pltpu.HBM((slabs * groups, blocks * ROWS, LANES), f32),
        in_specs=[VMEM] + [ANY] * len(parts),
        out_specs=HBM,
        scratch_shapes=[pltpu.SemaphoreType.DMA(())],
        compiler_params=params,
        cost_estimate=little,
        name="send",
    )(found, *parts)
    pred_all = lax.all_to_all(sent, ("space", "chip", "core"), 0, 0)
    u2_rows, *parts = pl.pallas_call(
        functools.partial(store_kernel, planes, tiles),
        out_shape=(jax.ShapeDtypeStruct(u_rows.shape, f32), *(jax.ShapeDtypeStruct(part.shape, f32) for part in parts)),
        in_specs=[VMEM] + [ANY] * len(parts),
        out_specs=(VMEM,) + (ANY,) * len(parts),
        input_output_aliases={1 + at: 1 + at for at in range(len(parts))},
        compiler_params=params,
        cost_estimate=little,
        name="store",
    )(u2, *parts)
    swapped = [lax.ppermute(part, "core", [(0, 1), (1, 0)]) for part in parts]
    where = [lax.axis_index(axes) for axes in ("space", ("chip", "core"), "chip", "core")]
    place = jnp.stack(where).astype(i32)
    split = pl.pallas_call(
        functools.partial(split_kernel, by_xor, chips),
        out_shape=pltpu.HBM((slots, 2 * groups * ROWS, LANES), jnp.bfloat16),
        in_specs=[SMEM] + [ANY] * (2 * len(parts)),
        out_specs=HBM,
        scratch_shapes=[
            pltpu.VMEM((chips, 2, slots, ROWS, LANES), f32),
            pltpu.VMEM((slots, 2 * groups * ROWS, LANES), jnp.bfloat16),
            pltpu.SemaphoreType.DMA((4 * chips + 2,)),
        ],
        compiler_params=params,
        cost_estimate=little,
        name="split",
    )(place, *parts, *swapped)
    post_rows, gain = pl.pallas_call(
        functools.partial(update_kernel, slabs, planes, tiles),
        out_shape=(
            jax.ShapeDtypeStruct(u_rows.shape, f32),
            jax.ShapeDtypeStruct((members, probes), f32),
        ),
        in_specs=[SMEM] * 2 + [HBM] * 3 + [VMEM] * 5 + [HBM] * 2 + [ANY],
        out_specs=(VMEM,) * 2,
        scratch_shapes=[
            pltpu.VMEM((probe_taper.shape[2], 2 * ROWS, 2 * groups * ROWS), jnp.bfloat16),
            pltpu.SMEM(pair_cells.shape, i32),
            pltpu.SMEM(pair_cells.shape, i32),
            pltpu.SMEM(pair_cells.shape, i32),
            pltpu.VMEM(split.shape, jnp.bfloat16),
            pltpu.VMEM(picked.shape, f32),
            pltpu.VMEM((planes * tiles, ROWS, LANES), f32),
            pltpu.SemaphoreType.DMA((6,)),
        ],
        compiler_params=params,
        name="update",
    )(place, pair_counts, *map(stay, (pair_cells, pair_probes, pair_taper)), pred_all,
      before_2, seen, obs, after_2, stay(t_rows), stay(split), parts[0] if by_xor else picked)
    return (from_rows(u2_rows, shape), from_rows(post_rows, shape), gain)


def solution(mesh):
    slabs, groups = mesh.devices.shape
    split = jax.sharding.Mesh(mesh.devices.reshape(slabs, groups // 2, 2), ("space", "chip", "core"))
    members = ("chip", "core")
    return jax.shard_map(
        shards,
        mesh=split,
        in_specs=(
            P(members, "space", None),
            P(members, "space", None),
            P("space"),
            P(members, "space"),
            P("space"),
            P("space"),
            P("space", None),
            P("space", None),
            P("space", None),
            P("space"),
            P("space", None, None),
        ),
        out_specs=(P(members, "space", None), P(members, "space", None), P(members, "space")),
        check_vma=False,
    )
```

```python
import functools

import jax
import jax.numpy as jnp
from jax import lax
from jax.experimental import pallas as pl
from jax.experimental.pallas import tpu as pltpu
from jax.sharding import PartitionSpec as P

LANES = 128
ROWS = 8
NZ = 64
HALF_DT = 0.5 * 0.08

VMEM = pl.BlockSpec(memory_space=pltpu.VMEM)
SMEM = pl.BlockSpec(memory_space=pltpu.SMEM)
HBM = pl.BlockSpec(memory_space=pltpu.HBM)
ANY = pl.BlockSpec(memory_space=pl.ANY)


def stay(array):
    return pltpu.with_memory_space_constraint(array, pltpu.HBM)


def to_rows(array):
    members, planes, cells = array.shape
    split = array.reshape(members, planes // ROWS, ROWS, cells // LANES, LANES)
    return split.transpose(0, 1, 3, 2, 4).reshape(-1, LANES)


def from_rows(rows, shape):
    members, planes, cells = shape
    split = rows.reshape(members, planes // ROWS, cells // LANES, ROWS, LANES)
    return split.transpose(0, 1, 3, 2, 4).reshape(shape)


def row_of(plane, tile, tiles):
    return (plane // ROWS * tiles + tile) * ROWS + plane % ROWS


def pack_kernel(planes, tiles, taper_hbm, u_hbm, t_hbm, noise_hbm, observed_hbm, var_hbm, cells_hbm,
                low_ref, high_ref, obs_ref, t_ref, pick_ref,
                taper_ref, u_ref, noise_ref, row_ref, cells_ref, sems):
    stride = planes * tiles
    blocks = noise_ref.shape[1] // LANES
    copies = [
        pltpu.make_async_copy(source, target, sems.at[at])
        for at, (source, target) in enumerate((
            (t_hbm, t_ref),
            (u_hbm, u_ref),
            (taper_hbm, taper_ref),
            (noise_hbm, noise_ref),
            (observed_hbm, row_ref.at[0:1]),
            (var_hbm, row_ref.at[1:2]),
            (cells_hbm, cells_ref),
        ))
    ]
    for copy in copies:
        copy.start()
    copies[0].wait()
    copies[6].wait()
    for slot in range(pick_ref.shape[0]):
        block = cells_ref[0, slot]
        row = row_of(block // tiles, block % tiles, tiles)
        pick_ref[slot] = t_ref[pl.ds(row, ROWS, stride=stride), :]
    for kind, source in ((1, t_ref), (0, u_ref)):
        if kind == 0:
            copies[1].wait()
        for out_ref, first in ((high_ref, planes - 2), (low_ref, 0)):
            for depth in range(2):
                for tile in range(tiles):
                    out_ref[(kind * 2 + depth) * tiles + tile] = source[
                        pl.ds(row_of(first + depth, tile, tiles), ROWS, stride=stride), :
                    ]
    for ref in (low_ref, high_ref):
        ref[4 * tiles] = jnp.ones((ROWS, LANES), jnp.float32)
    for copy in copies[2:6]:
        copy.wait()
    own, window = taper_ref.shape[1:]
    rows = [row_ref[kind : kind + 1, b * LANES : (b + 1) * LANES] for kind in range(2) for b in range(blocks)]
    for i in range(own):
        for j in range(window):
            rows.append(jnp.full((1, LANES), taper_ref[0, i, j].astype(jnp.float32), jnp.float32))
    for b in range(blocks):
        obs_ref[b] = noise_ref[:, b * LANES : (b + 1) * LANES]
    for at, row in enumerate(rows):
        obs_ref[blocks + at // ROWS, at % ROWS : at % ROWS + 1, :] = row
    for ref in (low_ref, high_ref):
        for at in range(obs_ref.shape[0]):
            ref[4 * tiles + 1 + at] = obs_ref[at]


def rot(value, by):
    return pltpu.roll(value, by % LANES, 1)


def lane_masks():
    lane = lax.broadcasted_iota(jnp.int32, (ROWS, LANES), 1)
    height = lane & (NZ - 1)
    return lane < NZ, height == 0, height == NZ - 1


def around(tiles, value):
    here = first = value(0)
    before, turned = rot(value(tiles - 1), NZ), rot(here, NZ)
    first_turned = turned
    for tile in range(tiles):
        last = tile == tiles - 1
        ahead = first if last else value(tile + 1)
        after = first_turned if last else rot(ahead, NZ)
        yield here, turned, before, after
        here, before, turned = ahead, turned, after


def weigh(masks, parts, low, high):
    first_half, floor, roof = masks
    mid, turned, before, after = parts
    near = mid + turned
    far = mid + jnp.where(first_half, before, after)
    up = mid + jnp.where(roof, HALF_DT, rot(mid, -1))
    down = mid + jnp.where(floor, HALF_DT, rot(mid, 1))
    below = mid + low
    above = mid + high
    diag = 1.0 - ((near + far) + (up + down) + (below + above))
    return diag, near, far, jnp.where(roof, 0.0, up), jnp.where(floor, 0.0, down), below, above


def blend(masks, weights, parts, low, high):
    diag, near, far, up, down, below, above = weights
    mid, turned, before, after = parts
    beyond = jnp.where(masks[0], before, after)
    return (
        (diag * mid + near * turned)
        + (far * beyond + up * rot(mid, -1))
        + (down * rot(mid, 1) + below * low)
        + above * high
    )


def advance(masks, tiles, v, u, emit):
    pairs = zip(around(tiles, functools.partial(v, 0)), around(tiles, functools.partial(u, 0)))
    for tile, (v_parts, u_parts) in enumerate(pairs):
        weights = weigh(masks, v_parts, v(-1, tile), v(1, tile))
        emit(tile, weights, blend(masks, weights, u_parts, u(-1, tile), u(1, tile)))


def plane_of(ref, at, tiles):
    return [ref[at * tiles + tile] for tile in range(tiles)]


def put(ref, at, values):
    for tile, value in enumerate(values):
        ref[at * len(values) + tile] = value


def each(first, last, unroll, body):
    count = (last - first) // unroll

    def several(at, _):
        for d in range(unroll):
            body(first + at * unroll + d)
        return 0

    lax.fori_loop(0, count, several, 0)
    for x in range(first + count * unroll, last):
        body(x)


def inner_kernel(planes, tiles, u_hbm, t_ref, u2_ref, edge_ref, u_ref, u0, hv, u1, held, sem):
    stride = planes * tiles
    masks = lane_masks()
    copy = pltpu.make_async_copy(u_hbm, u_ref, sem)
    copy.start()

    def rows_at(x, tile):
        return pl.ds((x // ROWS) * tiles * ROWS + x % ROWS + tile * ROWS, ROWS, stride=stride)

    def load_t(x):
        for tile in range(tiles):
            hv[x * tiles + tile] = HALF_DT * jnp.exp(t_ref[rows_at(x, tile), :])

    def load_u(x):
        for tile in range(tiles):
            u0[x * tiles + tile] = u_ref[rows_at(x, tile), :]

    def first_step(x):
        def emit(tile, weights, value):
            for kind in range(5):
                held[kind, x * tiles + tile] = weights[kind]
            u1[x * tiles + tile] = value

        advance(masks, tiles, lambda d, tile: hv[(x + d) * tiles + tile], lambda d, tile: u0[(x + d) * tiles + tile], emit)

    def second_step(x):
        for tile, parts in enumerate(around(tiles, lambda tile: u1[x * tiles + tile])):
            at = x * tiles + tile
            here = hv[at]
            weights = [held[kind, at] for kind in range(5)] + [here + hv[at - tiles], here + hv[at + tiles]]
            u2_ref[at] = blend(masks, weights, parts, u1[at - tiles], u1[at + tiles])

    each(0, planes, 4, load_t)
    copy.wait()
    each(0, planes, 4, load_u)
    each(1, planes - 1, 7, first_step)
    each(2, planes - 2, 6, second_step)
    last = planes - 1
    at = 0
    for ref, kept in ((u0, (0, 1, last - 1, last)), (hv, (0, 1, 2, last - 2, last - 1, last)),
                      (u1, (1, 2, last - 2, last - 1))):
        for x in kept:
            put(edge_ref, at, plane_of(ref, x, tiles))
            at += 1


def outer_kernel(planes, tiles, probe_hbm, before_ref, after_ref, edge_ref, inner_ref,
                 u2_ref, found_ref, seen_ref, probe_ref, v_ref, n_ref, sem):
    probe_copy = pltpu.make_async_copy(probe_hbm, probe_ref, sem)
    probe_copy.start()
    masks = lane_masks()
    blocks = probe_ref.shape[0] // LANES
    count = seen_ref.shape[0] // 2
    for at in range(count):
        seen_ref[at] = before_ref[4 * tiles + 1 + at]
        seen_ref[count + at] = after_ref[4 * tiles + 1 + at]
    last = planes - 1
    for ref, own_u, own_v, own_1, where, order in (
        (before_ref, (0, 1), (4, 5, 6), (10, 11), (0, 1), (0, 1)),
        (after_ref, (3, 2), (9, 8, 7), (13, 12), (last, last - 1), (1, 0)),
    ):
        for d in range(2):
            for tile in range(tiles):
                v_ref[d * tiles + tile] = HALF_DT * jnp.exp(ref[(2 + order[d]) * tiles + tile])
        live = ref[4 * tiles]

        def v(d, tile):
            return v_ref[d * tiles + tile] if d < 2 else edge_ref[own_v[d - 2] * tiles + tile]

        def u(d, tile):
            return ref[order[d] * tiles + tile] if d < 2 else edge_ref[own_u[d - 2] * tiles + tile]

        def u1(d, tile):
            return n_ref[d * tiles + tile] if d < 2 else edge_ref[own_1[d - 2] * tiles + tile]

        def first(d, tile, weights, value):
            n_ref[d * tiles + tile] = value * live if d == 0 else value

        def second(d, tile, weights, value):
            u2_ref[where[d] * tiles + tile] = value

        for d in range(2):
            advance(masks, tiles, lambda s, t: v(d + 1 + s, t), lambda s, t: u(d + 1 + s, t), functools.partial(first, d))
        for d in range(2):
            advance(masks, tiles, lambda s, t: v(d + 2 + s, t), lambda s, t: u1(d + 1 + s, t), functools.partial(second, d))

    probe_copy.wait()
    lane = lax.broadcasted_iota(jnp.int32, (ROWS, LANES), 1)
    for part in range(blocks):
        found = jnp.zeros((ROWS, LANES), jnp.float32)
        for p in range(LANES):
            cell = probe_ref[part * LANES + p]
            turned = pltpu.roll(u2_ref[cell >> 7], (p - cell) & (LANES - 1), 1)
            found = jnp.where(lane == p, turned, found)

        found_ref[part * ROWS : (part + 1) * ROWS, :] = found


def send_kernel(found_ref, *refs):
    sent_hbm, sem = refs[-2:]

    def send(device, _):
        pltpu.make_async_copy(found_ref, sent_hbm.at[device], sem).start()
        return 0

    lax.fori_loop(0, sent_hbm.shape[0], send, 0)
    pltpu.make_async_copy(sent_hbm, sent_hbm, sem).wait()


def halves(value):
    high = value.astype(jnp.bfloat16)
    return high, (value - high.astype(jnp.float32)).astype(jnp.bfloat16)


def store_kernel(planes, tiles, u2_ref, *refs):
    out_ref = refs[len(refs) // 2]

    def store(x):
        for tile in range(tiles):
            rows = pl.ds((x // ROWS) * tiles * ROWS + x % ROWS + tile * ROWS, ROWS, stride=planes * tiles)
            out_ref[rows, :] = u2_ref[x * tiles + tile]

    each(0, planes, 4, store)


def split_kernel(by_xor, chips, place_ref, *refs):
    *parts, split_hbm, theta_ref, split_ref, sems = refs
    chip, core = place_ref[2], place_ref[3]
    same, other = parts[: len(parts) // 2], parts[len(parts) // 2 :]
    if not by_xor:
        same, other = ([ref.at[at] for at in range(chips)] for (ref,) in (same, other))
    slots, members = theta_ref.shape[2], 2 * chips * ROWS
    half = slots // 2
    arriving, leaving = [[], []], []
    for side in range(2):
        cut = pl.ds(side * half, half)
        for at in range(chips):
            where = chip ^ at if by_xor else at
            for slot, source in ((core, same[at]), (1 - core, other[at])):
                target = theta_ref.at[where, slot, cut]
                sem = sems.at[2 * chips * side + len(arriving[side])]
                arriving[side].append(pltpu.make_async_copy(source.at[cut], target, sem))
        leaving.append(pltpu.make_async_copy(split_ref.at[cut], split_hbm.at[cut], sems.at[4 * chips + side]))
    for copy in arriving[0] + arriving[1]:
        copy.start()

    def split(slot):
        high, low = halves(theta_ref[:, :, slot].reshape(members, LANES))
        split_ref[slot, :members, :] = high
        split_ref[slot, members:, :] = low

    for side in range(2):
        for copy in arriving[side]:
            copy.wait()
        each(side * half, (side + 1) * half, 4, split)
        leaving[side].start()
    for copy in leaving:
        copy.wait()


def stacked(value):
    high, low = halves(value)
    return jnp.concatenate([high.astype(jnp.float32), low.astype(jnp.float32)], axis=0).astype(jnp.bfloat16)


def beside(pair):
    return jnp.concatenate(pair, axis=1)


def fold(both):
    return both[:ROWS] + both[ROWS:]


def dot(left, right, over):
    return lax.dot_general(left, right, (((1,), (over,)), ((), ())), preferred_element_type=jnp.float32)


def update_kernel(slabs, planes, tiles, place_ref, count_ref, cells_hbm, probes_hbm, level_hbm,
                  pred_ref, before_2_ref, seen_ref, own_ref, after_2_ref, t_hbm, split_hbm, pick_hbm,
                  post_ref, gain_ref, reach, cells_ref, probes_ref, level_ref, split_ref, pick_ref, sum_ref, sems):
    groups, blocks = pred_ref.shape[0] // slabs, pred_ref.shape[1] // ROWS
    members = groups * ROWS
    share = 1.0 / (members - 1)
    copies = [
        pltpu.make_async_copy(source, target, sems.at[at])
        for at, (source, target) in enumerate((
            (cells_hbm, cells_ref), (probes_hbm, probes_ref), (level_hbm, level_ref),
            (pick_hbm, pick_ref), (split_hbm, split_ref), (t_hbm, post_ref)))
    ]
    for copy in copies:
        copy.start()
    slab, group = place_ref[0], place_ref[1]
    seen = ((before_2_ref, 0), (seen_ref, 0), (own_ref, 0), (seen_ref, seen_ref.shape[0] // 2), (after_2_ref, 0))

    def extra(d, at):
        ref, first = seen[d]
        return ref[first + blocks + at // ROWS, at % ROWS : at % ROWS + 1, :]

    def wide(row):
        return row[:, :members] if members <= LANES else jnp.concatenate([row] * (members // LANES), axis=1)

    anomaly, scaled, variance, matches = [], [], [], []
    for d in range(5):
        wanted = slab + d - 2
        at = jnp.clip(wanted, 0, slabs - 1)
        live = jnp.where((wanted >= 0) & (wanted < slabs), 1.0, 0.0)
        for b in range(blocks):
            cut = slice(b * ROWS, (b + 1) * ROWS)
            predicted = pred_ref[pl.ds(at * groups, groups), cut].reshape(members, LANES)
            mean = jnp.sum(predicted, axis=0, keepdims=True) / members
            anomaly.append(beside(halves((predicted - mean) * live)))
            variance.append(extra(d, blocks + b) + (1.0 - live))
            noise = seen[d][0][seen[d][1] + b]
            scaled.append((extra(d, b) + noise - pred_ref[at * groups + group, cut]) / variance[-1] * live)
            matches.append(fold(dot(beside([stacked(scaled[-1])] * 2), anomaly[-1], 1)))
    for d in range(1, 4):
        for i in range(blocks):
            total = jnp.zeros((ROWS, members), jnp.float32)
            for j in range(3 * blocks):
                level = extra(d, 2 * blocks + i * 3 * blocks + j) / 256.0 * share
                total = total + wide(level) * matches[(d - 1) * blocks + j]
            both = anomaly[d * blocks + i]
            left = stacked(total)
            correction = fold(dot(left, both[:, :LANES], 0) + dot(left, both[:, LANES:], 0))
            gain = scaled[d * blocks + i] - correction / variance[d * blocks + i]
            if d == 2:
                gain_ref[:, i * LANES : (i + 1) * LANES] = gain
            near = stacked(fold(dot(beside([stacked(gain)] * 2), both, 1)))
            reach[(d - 1) * blocks + i] = beside([near, near])
    for copy in copies[:4]:
        copy.wait()
    slots = split_ref.shape[0]
    blocks_of = [cells_ref[0, slot] for slot in range(slots)]
    for slot in range(slots):
        sum_ref[blocks_of[slot]] = pick_ref[slot]
    copies[4].wait()
    for slot in range(slots):
        weight = jnp.where(slot < count_ref[0], level_ref[0, slot].astype(jnp.float32) / 256.0, 0.0) * share
        change = fold(dot(reach[probes_ref[0, slot]], split_ref[slot], 0)) * weight
        sum_ref[blocks_of[slot]] = sum_ref[blocks_of[slot]] + change
    copies[5].wait()
    for slot in range(slots):
        block = blocks_of[slot]
        rows = pl.ds(row_of(block // tiles, block % tiles, tiles), ROWS, stride=planes * tiles)
        post_ref[rows, :] = sum_ref[block]


def shards(
    starting_speed_field,
    sample_fluidity_exponent,
    observed,
    obs_noise,
    obs_var,
    probe_cells,
    pair_cells,
    pair_probes,
    pair_taper,
    pair_counts,
    probe_taper,
):
    shape = starting_speed_field.shape
    members, planes, cells = shape
    tiles = cells // LANES
    slots = pair_cells.shape[1]
    probes = obs_noise.shape[1]
    blocks = probes // LANES
    slabs, chips = lax.axis_size("space"), lax.axis_size("chip")
    groups = 2 * chips
    f32, i32 = jnp.float32, jnp.int32
    u_rows = to_rows(starting_speed_field)
    t_rows = to_rows(sample_fluidity_exponent)
    obs_tiles = blocks - (-(2 * blocks + probe_taper.shape[1] * probe_taper.shape[2]) // ROWS)
    edge = jax.ShapeDtypeStruct((4 * tiles + 1 + obs_tiles, ROWS, LANES), f32)
    obs_shape = jax.ShapeDtypeStruct((obs_tiles, ROWS, LANES), f32)
    params = pltpu.CompilerParams(vmem_limit_bytes=32 * 1024 * 1024)
    stack = pltpu.VMEM((planes * tiles, ROWS, LANES), f32)
    low, high, obs, t_near, picked = pl.pallas_call(
        functools.partial(pack_kernel, planes, tiles),
        out_shape=(
            edge,
            edge,
            obs_shape,
            jax.ShapeDtypeStruct(u_rows.shape, f32),
            jax.ShapeDtypeStruct((slots, ROWS, LANES), f32),
        ),
        in_specs=[HBM] * 7,
        out_specs=(VMEM,) * 5,
        scratch_shapes=[
            pltpu.SMEM(probe_taper.shape, i32),
            pltpu.VMEM(u_rows.shape, f32),
            pltpu.VMEM((ROWS, probes), f32),
            pltpu.VMEM((2, probes), f32),
            pltpu.SMEM(pair_cells.shape, i32),
            pltpu.SemaphoreType.DMA((7,)),
        ],
        compiler_params=params,
        name="pack",
    )(*map(stay, (probe_taper, u_rows, t_rows, obs_noise, observed.reshape(1, -1), obs_var.reshape(1, -1), pair_cells)))
    little = pl.CostEstimate(flops=1000, bytes_accessed=1000, transcendentals=0)
    upward = [(i, i + 1) for i in range(slabs - 1)]
    before = lax.ppermute(high, "space", upward)
    after = lax.ppermute(low, "space", [(j, i) for i, j in upward])
    if slabs == 4:
        before_2 = after_2 = lax.ppermute(obs, "space", [(i, (i + 2) % 4) for i in range(4)])
    else:
        upward_2 = [(i, i + 2) for i in range(slabs - 2)]
        before_2 = lax.ppermute(obs, "space", upward_2)
        after_2 = lax.ppermute(obs, "space", [(j, i) for i, j in upward_2])
    inner, edges = pl.pallas_call(
        functools.partial(inner_kernel, planes, tiles),
        out_shape=(
            jax.ShapeDtypeStruct((planes * tiles, ROWS, LANES), f32),
            jax.ShapeDtypeStruct((14 * tiles, ROWS, LANES), f32),
        ),
        in_specs=[HBM, VMEM],
        out_specs=(VMEM, VMEM),
        scratch_shapes=[
            pltpu.VMEM(u_rows.shape, f32),
            stack,
            stack,
            stack,
            pltpu.VMEM((5, planes * tiles, ROWS, LANES), f32),
            pltpu.SemaphoreType.DMA(()),
        ],
        compiler_params=params,
        cost_estimate=pl.CostEstimate(flops=0, bytes_accessed=15_000_000, transcendentals=0),
        name="inner_planes",
    )(stay(u_rows), t_near)
    by_xor = chips <= 4 and chips & (chips - 1) == 0
    if by_xor:
        parts = [picked]
        for d in range(1, chips):
            parts.append(lax.ppermute(picked, "chip", [(i, i ^ d) for i in range(chips)]))
    else:
        parts = [lax.all_to_all(jnp.broadcast_to(picked, (chips, *picked.shape)), "chip", 0, 0)]
    u2, found, seen = pl.pallas_call(
        functools.partial(outer_kernel, planes, tiles),
        out_shape=(
            jax.ShapeDtypeStruct((planes * tiles, ROWS, LANES), f32),
            jax.ShapeDtypeStruct((blocks * ROWS, LANES), f32),
            jax.ShapeDtypeStruct((2 * obs_tiles, ROWS, LANES), f32),
        ),
        in_specs=[HBM] + [VMEM] * 4,
        out_specs=(VMEM,) * 3,
        scratch_shapes=[
            pltpu.SMEM(probe_cells.shape, i32),
            pltpu.VMEM((2 * tiles, ROWS, LANES), f32),
            pltpu.VMEM((2 * tiles, ROWS, LANES), f32),
            pltpu.SemaphoreType.DMA(()),
        ],
        input_output_aliases={4: 0},
        compiler_params=params,
        cost_estimate=little,
        name="outer_planes",
    )(stay(probe_cells), before, after, edges, inner)
    sent = pl.pallas_call(
        send_kernel,
        out_shape=pltpu.HBM((slabs * groups, blocks * ROWS, LANES), f32),
        in_specs=[VMEM] + [ANY] * len(parts),
        out_specs=HBM,
        scratch_shapes=[pltpu.SemaphoreType.DMA(())],
        compiler_params=params,
        cost_estimate=little,
        name="send",
    )(found, *parts)
    pred_all = lax.all_to_all(sent, ("space", "chip", "core"), 0, 0)
    u2_rows, *parts = pl.pallas_call(
        functools.partial(store_kernel, planes, tiles),
        out_shape=(jax.ShapeDtypeStruct(u_rows.shape, f32), *(jax.ShapeDtypeStruct(part.shape, f32) for part in parts)),
        in_specs=[VMEM] + [ANY] * len(parts),
        out_specs=(VMEM,) + (ANY,) * len(parts),
        input_output_aliases={1 + at: 1 + at for at in range(len(parts))},
        compiler_params=params,
        cost_estimate=little,
        name="store",
    )(u2, *parts)
    swapped = [lax.ppermute(part, "core", [(0, 1), (1, 0)]) for part in parts]
    where = [lax.axis_index(axes) for axes in ("space", ("chip", "core"), "chip", "core")]
    place = jnp.stack(where).astype(i32)
    split = pl.pallas_call(
        functools.partial(split_kernel, by_xor, chips),
        out_shape=pltpu.HBM((slots, 2 * groups * ROWS, LANES), jnp.bfloat16),
        in_specs=[SMEM] + [ANY] * (2 * len(parts)),
        out_specs=HBM,
        scratch_shapes=[
            pltpu.VMEM((chips, 2, slots, ROWS, LANES), f32),
            pltpu.VMEM((slots, 2 * groups * ROWS, LANES), jnp.bfloat16),
            pltpu.SemaphoreType.DMA((4 * chips + 2,)),
        ],
        compiler_params=params,
        cost_estimate=little,
        name="split",
    )(place, *parts, *swapped)
    post_rows, gain = pl.pallas_call(
        functools.partial(update_kernel, slabs, planes, tiles),
        out_shape=(
            jax.ShapeDtypeStruct(u_rows.shape, f32),
            jax.ShapeDtypeStruct((members, probes), f32),
        ),
        in_specs=[SMEM] * 2 + [HBM] * 3 + [VMEM] * 5 + [HBM] * 2 + [ANY],
        out_specs=(VMEM,) * 2,
        scratch_shapes=[
            pltpu.VMEM((probe_taper.shape[2], 2 * ROWS, 2 * groups * ROWS), jnp.bfloat16),
            pltpu.SMEM(pair_cells.shape, i32),
            pltpu.SMEM(pair_cells.shape, i32),
            pltpu.SMEM(pair_cells.shape, i32),
            pltpu.VMEM(split.shape, jnp.bfloat16),
            pltpu.VMEM(picked.shape, f32),
            pltpu.VMEM((planes * tiles, ROWS, LANES), f32),
            pltpu.SemaphoreType.DMA((6,)),
        ],
        compiler_params=params,
        name="update",
    )(place, pair_counts, *map(stay, (pair_cells, pair_probes, pair_taper)), pred_all,
      before_2, seen, obs, after_2, stay(t_rows), stay(split), parts[0] if by_xor else picked)
    return (from_rows(u2_rows, shape), from_rows(post_rows, shape), gain)


def solution(mesh):
    slabs, groups = mesh.devices.shape
    split = jax.sharding.Mesh(mesh.devices.reshape(slabs, groups // 2, 2), ("space", "chip", "core"))
    members = ("chip", "core")
    return jax.shard_map(
        shards,
        mesh=split,
        in_specs=(
            P(members, "space", None),
            P(members, "space", None),
            P("space"),
            P(members, "space"),
            P("space"),
            P("space"),
            P("space", None),
            P("space", None),
            P("space", None),
            P("space"),
            P("space", None, None),
        ),
        out_specs=(P(members, "space", None), P(members, "space", None), P(members, "space")),
        check_vma=False,
    )
```

```python
import functools

import jax
import jax.numpy as jnp
from jax import lax
from jax.experimental import pallas as pl
from jax.experimental.pallas import tpu as pltpu
from jax.sharding import PartitionSpec as P

LANES = 128
ROWS = 8
NZ = 64
HALF_DT = 0.5 * 0.08

VMEM = pl.BlockSpec(memory_space=pltpu.VMEM)
SMEM = pl.BlockSpec(memory_space=pltpu.SMEM)
HBM = pl.BlockSpec(memory_space=pltpu.HBM)
ANY = pl.BlockSpec(memory_space=pl.ANY)


def stay(array):
    return pltpu.with_memory_space_constraint(array, pltpu.HBM)


def to_rows(array):
    members, planes, cells = array.shape
    split = array.reshape(members, planes // ROWS, ROWS, cells // LANES, LANES)
    return split.transpose(0, 1, 3, 2, 4).reshape(-1, LANES)


def from_rows(rows, shape):
    members, planes, cells = shape
    split = rows.reshape(members, planes // ROWS, cells // LANES, ROWS, LANES)
    return split.transpose(0, 1, 3, 2, 4).reshape(shape)


def row_of(plane, tile, tiles):
    return (plane // ROWS * tiles + tile) * ROWS + plane % ROWS


def pack_kernel(planes, tiles, taper_hbm, u_hbm, t_hbm, noise_hbm, observed_hbm, var_hbm, cells_hbm,
                low_ref, high_ref, obs_ref, t_ref, u_ref, pick_ref,
                taper_ref, noise_ref, row_ref, cells_ref, sems):
    stride = planes * tiles
    blocks = noise_ref.shape[1] // LANES
    copies = [
        pltpu.make_async_copy(source, target, sems.at[at])
        for at, (source, target) in enumerate((
            (t_hbm, t_ref),
            (u_hbm, u_ref),
            (taper_hbm, taper_ref),
            (noise_hbm, noise_ref),
            (observed_hbm, row_ref.at[0:1]),
            (var_hbm, row_ref.at[1:2]),
            (cells_hbm, cells_ref),
        ))
    ]
    for copy in copies:
        copy.start()
    copies[0].wait()
    copies[6].wait()
    for slot in range(pick_ref.shape[0]):
        block = cells_ref[0, slot]
        row = row_of(block // tiles, block % tiles, tiles)
        pick_ref[slot] = t_ref[pl.ds(row, ROWS, stride=stride), :]
    for kind, source in ((1, t_ref), (0, u_ref)):
        if kind == 0:
            copies[1].wait()
        for out_ref, first in ((high_ref, planes - 2), (low_ref, 0)):
            for depth in range(2):
                for tile in range(tiles):
                    out_ref[(kind * 2 + depth) * tiles + tile] = source[
                        pl.ds(row_of(first + depth, tile, tiles), ROWS, stride=stride), :
                    ]
    for ref in (low_ref, high_ref):
        ref[4 * tiles] = jnp.ones((ROWS, LANES), jnp.float32)
    for copy in copies[2:6]:
        copy.wait()
    own, window = taper_ref.shape[1:]
    rows = [row_ref[kind : kind + 1, b * LANES : (b + 1) * LANES] for kind in range(2) for b in range(blocks)]
    for i in range(own):
        for j in range(window):
            rows.append(jnp.full((1, LANES), taper_ref[0, i, j].astype(jnp.float32), jnp.float32))
    for b in range(blocks):
        obs_ref[b] = noise_ref[:, b * LANES : (b + 1) * LANES]
    for at, row in enumerate(rows):
        obs_ref[blocks + at // ROWS, at % ROWS : at % ROWS + 1, :] = row
    for ref in (low_ref, high_ref):
        for at in range(obs_ref.shape[0]):
            ref[4 * tiles + 1 + at] = obs_ref[at]


def rot(value, by):
    return pltpu.roll(value, by % LANES, 1)


def lane_masks():
    lane = lax.broadcasted_iota(jnp.int32, (ROWS, LANES), 1)
    height = lane & (NZ - 1)
    return lane < NZ, height == 0, height == NZ - 1


def coefficients(masks, low, here, high):
    first_half, floor, roof = masks
    tiles = len(here)
    turned = [rot(value, NZ) for value in here]
    out = []
    for tile in range(tiles):
        mid = here[tile]
        near = mid + turned[tile]
        far = mid + jnp.where(first_half, turned[tile - 1], turned[(tile + 1) % tiles])
        up = mid + jnp.where(roof, HALF_DT, rot(mid, -1))
        down = mid + jnp.where(floor, HALF_DT, rot(mid, 1))
        below = mid + low[tile]
        above = mid + high[tile]
        diag = 1.0 - ((near + far) + (up + down) + (below + above))
        out.append((diag, near, far, jnp.where(roof, 0.0, up), jnp.where(floor, 0.0, down), below, above))
    return out


def step(masks, weights, low, here, high):
    first_half = masks[0]
    tiles = len(here)
    turned = [rot(value, NZ) for value in here]
    out = []
    for tile in range(tiles):
        diag, near, far, up, down, below, above = weights[tile]
        mid = here[tile]
        beyond = jnp.where(first_half, turned[tile - 1], turned[(tile + 1) % tiles])
        out.append(
            (diag * mid + near * turned[tile])
            + (far * beyond + up * rot(mid, -1))
            + (down * rot(mid, 1) + below * low[tile])
            + above * high[tile]
        )
    return out


def plane_of(ref, at, tiles):
    return [ref[at * tiles + tile] for tile in range(tiles)]


def put(ref, at, values):
    for tile, value in enumerate(values):
        ref[at * len(values) + tile] = value


def each(first, last, unroll, body):
    count = (last - first) // unroll

    def several(at, _):
        for d in range(unroll):
            body(first + at * unroll + d)
        return 0

    lax.fori_loop(0, count, several, 0)
    for x in range(first + count * unroll, last):
        body(x)


def inner_kernel(planes, tiles, u_ref, t_ref, u2_ref, edge_ref, u0, hv, u1, held):
    stride = planes * tiles
    masks = lane_masks()

    def rows_at(x, tile):
        return pl.ds((x // ROWS) * tiles * ROWS + x % ROWS + tile * ROWS, ROWS, stride=stride)

    def load(x):
        for tile in range(tiles):
            hv[x * tiles + tile] = HALF_DT * jnp.exp(t_ref[rows_at(x, tile), :])
            u0[x * tiles + tile] = u_ref[rows_at(x, tile), :]

    def first_step(x):
        weights = coefficients(masks, *[plane_of(hv, x + d, tiles) for d in (-1, 0, 1)])
        for tile in range(tiles):
            for kind in range(5):
                held[kind, x * tiles + tile] = weights[tile][kind]
        put(u1, x, step(masks, weights, *[plane_of(u0, x + d, tiles) for d in (-1, 0, 1)]))

    def second_step(x):
        weights = []
        for tile in range(tiles):
            at = x * tiles + tile
            here = hv[at]
            weights.append([held[kind, at] for kind in range(5)] + [here + hv[at - tiles], here + hv[at + tiles]])
        put(u2_ref, x, step(masks, weights, *[plane_of(u1, x + d, tiles) for d in (-1, 0, 1)]))

    each(0, planes, 4, load)
    each(1, planes - 1, 7, first_step)
    each(2, planes - 2, 6, second_step)
    last = planes - 1
    at = 0
    for ref, kept in ((u0, (0, 1, last - 1, last)), (hv, (0, 1, 2, last - 2, last - 1, last)),
                      (u1, (1, 2, last - 2, last - 1))):
        for x in kept:
            put(edge_ref, at, plane_of(ref, x, tiles))
            at += 1


def outer_kernel(planes, tiles, probe_hbm, before_ref, after_ref, edge_ref, inner_ref,
                 u2_ref, found_ref, seen_ref, probe_ref, sem):
    probe_copy = pltpu.make_async_copy(probe_hbm, probe_ref, sem)
    probe_copy.start()
    masks = lane_masks()
    blocks = probe_ref.shape[0] // LANES
    count = seen_ref.shape[0] // 2
    for at in range(count):
        seen_ref[at] = before_ref[4 * tiles + 1 + at]
        seen_ref[count + at] = after_ref[4 * tiles + 1 + at]
    edge = [plane_of(edge_ref, at, tiles) for at in range(14)]
    last = planes - 1
    for ref, own_u, own_v, own_1, where in (
        (before_ref, edge[0:2], edge[4:7], edge[10:12], (0, 1)),
        (after_ref, edge[3:1:-1], edge[9:6:-1], edge[13:11:-1], (last, last - 1)),
    ):
        order = (0, 1) if ref is before_ref else (1, 0)
        u = [plane_of(ref, d, tiles) for d in order] + own_u
        v = [[HALF_DT * jnp.exp(t) for t in plane_of(ref, 2 + d, tiles)] for d in order] + own_v
        live = ref[4 * tiles]
        weights = [coefficients(masks, v[d], v[d + 1], v[d + 2]) for d in range(3)]
        next_u = [step(masks, weights[d], u[d], u[d + 1], u[d + 2]) for d in range(2)]
        next_u[0] = [value * live for value in next_u[0]]
        next_u = next_u + own_1
        for d in range(2):
            put(u2_ref, where[d], step(masks, weights[d + 1], next_u[d], next_u[d + 1], next_u[d + 2]))

    probe_copy.wait()
    lane = lax.broadcasted_iota(jnp.int32, (ROWS, LANES), 1)
    for part in range(blocks):
        found = jnp.zeros((ROWS, LANES), jnp.float32)
        for p in range(LANES):
            cell = probe_ref[part * LANES + p]
            turned = pltpu.roll(u2_ref[cell >> 7], (p - cell) & (LANES - 1), 1)
            found = jnp.where(lane == p, turned, found)

        found_ref[part * ROWS : (part + 1) * ROWS, :] = found


def send_kernel(found_ref, *refs):
    sent_hbm, sem = refs[-2:]

    def send(device, _):
        pltpu.make_async_copy(found_ref, sent_hbm.at[device], sem).start()
        return 0

    lax.fori_loop(0, sent_hbm.shape[0], send, 0)
    pltpu.make_async_copy(sent_hbm, sent_hbm, sem).wait()


def halves(value):
    high = value.astype(jnp.bfloat16)
    return high, (value - high.astype(jnp.float32)).astype(jnp.bfloat16)


def store_kernel(planes, tiles, u2_ref, *refs):
    out_ref = refs[len(refs) // 2]

    def store(x):
        for tile in range(tiles):
            rows = pl.ds((x // ROWS) * tiles * ROWS + x % ROWS + tile * ROWS, ROWS, stride=planes * tiles)
            out_ref[rows, :] = u2_ref[x * tiles + tile]

    each(0, planes, 4, store)


def split_kernel(by_xor, chips, place_ref, *refs):
    *parts, split_hbm, theta_ref, split_ref, sems = refs
    chip, core = place_ref[2], place_ref[3]
    same, other = parts[: len(parts) // 2], parts[len(parts) // 2 :]
    if not by_xor:
        same, other = ([ref.at[at] for at in range(chips)] for (ref,) in (same, other))
    slots, members = theta_ref.shape[2], 2 * chips * ROWS
    half = slots // 2
    arriving, leaving = [[], []], []
    for side in range(2):
        cut = pl.ds(side * half, half)
        for at in range(chips):
            where = chip ^ at if by_xor else at
            for slot, source in ((core, same[at]), (1 - core, other[at])):
                target = theta_ref.at[where, slot, cut]
                sem = sems.at[2 * chips * side + len(arriving[side])]
                arriving[side].append(pltpu.make_async_copy(source.at[cut], target, sem))
        leaving.append(pltpu.make_async_copy(split_ref.at[cut], split_hbm.at[cut], sems.at[4 * chips + side]))
    for copy in arriving[0] + arriving[1]:
        copy.start()

    def split(slot):
        high, low = halves(theta_ref[:, :, slot].reshape(members, LANES))
        split_ref[slot, :members, :] = high
        split_ref[slot, members:, :] = low

    for side in range(2):
        for copy in arriving[side]:
            copy.wait()
        each(side * half, (side + 1) * half, 4, split)
        leaving[side].start()
    for copy in leaving:
        copy.wait()


def stacked(value):
    high, low = halves(value)
    return jnp.concatenate([high.astype(jnp.float32), low.astype(jnp.float32)], axis=0).astype(jnp.bfloat16)


def beside(pair):
    return jnp.concatenate(pair, axis=1)


def fold(both):
    return both[:ROWS] + both[ROWS:]


def dot(left, right, over):
    return lax.dot_general(left, right, (((1,), (over,)), ((), ())), preferred_element_type=jnp.float32)


def update_kernel(slabs, planes, tiles, place_ref, count_ref, cells_hbm, probes_hbm, level_hbm,
                  pred_ref, before_2_ref, seen_ref, own_ref, after_2_ref, t_hbm, split_hbm, pick_hbm,
                  post_ref, gain_ref, reach, cells_ref, probes_ref, level_ref, split_ref, pick_ref, sum_ref, sems):
    groups, blocks = pred_ref.shape[0] // slabs, pred_ref.shape[1] // ROWS
    members = groups * ROWS
    share = 1.0 / (members - 1)
    copies = [
        pltpu.make_async_copy(source, target, sems.at[at])
        for at, (source, target) in enumerate((
            (cells_hbm, cells_ref), (probes_hbm, probes_ref), (level_hbm, level_ref),
            (pick_hbm, pick_ref), (split_hbm, split_ref), (t_hbm, post_ref)))
    ]
    for copy in copies:
        copy.start()
    slab, group = place_ref[0], place_ref[1]
    seen = ((before_2_ref, 0), (seen_ref, 0), (own_ref, 0), (seen_ref, seen_ref.shape[0] // 2), (after_2_ref, 0))

    def extra(d, at):
        ref, first = seen[d]
        return ref[first + blocks + at // ROWS, at % ROWS : at % ROWS + 1, :]

    def wide(row):
        return row[:, :members] if members <= LANES else jnp.concatenate([row] * (members // LANES), axis=1)

    anomaly, scaled, variance, matches = [], [], [], []
    for d in range(5):
        wanted = slab + d - 2
        at = jnp.clip(wanted, 0, slabs - 1)
        live = jnp.where((wanted >= 0) & (wanted < slabs), 1.0, 0.0)
        for b in range(blocks):
            cut = slice(b * ROWS, (b + 1) * ROWS)
            predicted = pred_ref[pl.ds(at * groups, groups), cut].reshape(members, LANES)
            mean = jnp.sum(predicted, axis=0, keepdims=True) / members
            anomaly.append(beside(halves((predicted - mean) * live)))
            variance.append(extra(d, blocks + b) + (1.0 - live))
            noise = seen[d][0][seen[d][1] + b]
            scaled.append((extra(d, b) + noise - pred_ref[at * groups + group, cut]) / variance[-1] * live)
            matches.append(fold(dot(beside([stacked(scaled[-1])] * 2), anomaly[-1], 1)))
    for d in range(1, 4):
        for i in range(blocks):
            total = jnp.zeros((ROWS, members), jnp.float32)
            for j in range(3 * blocks):
                level = extra(d, 2 * blocks + i * 3 * blocks + j) / 256.0 * share
                total = total + wide(level) * matches[(d - 1) * blocks + j]
            both = anomaly[d * blocks + i]
            left = stacked(total)
            correction = fold(dot(left, both[:, :LANES], 0) + dot(left, both[:, LANES:], 0))
            gain = scaled[d * blocks + i] - correction / variance[d * blocks + i]
            if d == 2:
                gain_ref[:, i * LANES : (i + 1) * LANES] = gain
            near = stacked(fold(dot(beside([stacked(gain)] * 2), both, 1)))
            reach[(d - 1) * blocks + i] = beside([near, near])
    for copy in copies[:4]:
        copy.wait()
    slots = split_ref.shape[0]

    def begin(slot):
        sum_ref[cells_ref[0, slot]] = pick_ref[slot]

    def add(slot):
        weight = jnp.where(slot < count_ref[0], level_ref[0, slot].astype(jnp.float32) / 256.0, 0.0) * share
        change = fold(dot(reach[probes_ref[0, slot]], split_ref[slot], 0)) * weight
        sum_ref[cells_ref[0, slot]] = sum_ref[cells_ref[0, slot]] + change

    def finish(slot):
        block = cells_ref[0, slot]
        rows = pl.ds(row_of(block // tiles, block % tiles, tiles), ROWS, stride=planes * tiles)
        post_ref[rows, :] = sum_ref[block]

    each(0, slots, 8, begin)
    copies[4].wait()
    each(0, slots, 8, add)
    copies[5].wait()
    each(0, slots, 8, finish)


def shards(
    starting_speed_field,
    sample_fluidity_exponent,
    observed,
    obs_noise,
    obs_var,
    probe_cells,
    pair_cells,
    pair_probes,
    pair_taper,
    pair_counts,
    probe_taper,
):
    shape = starting_speed_field.shape
    members, planes, cells = shape
    tiles = cells // LANES
    slots = pair_cells.shape[1]
    probes = obs_noise.shape[1]
    blocks = probes // LANES
    slabs, chips = lax.axis_size("space"), lax.axis_size("chip")
    groups = 2 * chips
    f32, i32 = jnp.float32, jnp.int32
    u_rows = to_rows(starting_speed_field)
    t_rows = to_rows(sample_fluidity_exponent)
    obs_tiles = blocks - (-(2 * blocks + probe_taper.shape[1] * probe_taper.shape[2]) // ROWS)
    edge = jax.ShapeDtypeStruct((4 * tiles + 1 + obs_tiles, ROWS, LANES), f32)
    obs_shape = jax.ShapeDtypeStruct((obs_tiles, ROWS, LANES), f32)
    params = pltpu.CompilerParams(vmem_limit_bytes=32 * 1024 * 1024)
    stack = pltpu.VMEM((planes * tiles, ROWS, LANES), f32)
    low, high, obs, t_near, u_near, picked = pl.pallas_call(
        functools.partial(pack_kernel, planes, tiles),
        out_shape=(
            edge,
            edge,
            obs_shape,
            jax.ShapeDtypeStruct(u_rows.shape, f32),
            jax.ShapeDtypeStruct(u_rows.shape, f32),
            jax.ShapeDtypeStruct((slots, ROWS, LANES), f32),
        ),
        in_specs=[HBM] * 7,
        out_specs=(VMEM,) * 6,
        scratch_shapes=[
            pltpu.SMEM(probe_taper.shape, i32),
            pltpu.VMEM((ROWS, probes), f32),
            pltpu.VMEM((2, probes), f32),
            pltpu.SMEM(pair_cells.shape, i32),
            pltpu.SemaphoreType.DMA((7,)),
        ],
        compiler_params=params,
        name="pack",
    )(*map(stay, (probe_taper, u_rows, t_rows, obs_noise, observed.reshape(1, -1), obs_var.reshape(1, -1), pair_cells)))
    little = pl.CostEstimate(flops=1000, bytes_accessed=1000, transcendentals=0)
    upward = [(i, i + 1) for i in range(slabs - 1)]
    before = lax.ppermute(high, "space", upward)
    after = lax.ppermute(low, "space", [(j, i) for i, j in upward])
    if slabs == 4:
        before_2 = after_2 = lax.ppermute(obs, "space", [(i, (i + 2) % 4) for i in range(4)])
    else:
        upward_2 = [(i, i + 2) for i in range(slabs - 2)]
        before_2 = lax.ppermute(obs, "space", upward_2)
        after_2 = lax.ppermute(obs, "space", [(j, i) for i, j in upward_2])
    inner, edges = pl.pallas_call(
        functools.partial(inner_kernel, planes, tiles),
        out_shape=(
            jax.ShapeDtypeStruct((planes * tiles, ROWS, LANES), f32),
            jax.ShapeDtypeStruct((14 * tiles, ROWS, LANES), f32),
        ),
        in_specs=[VMEM, VMEM],
        out_specs=(VMEM, VMEM),
        scratch_shapes=[stack, stack, stack, pltpu.VMEM((5, planes * tiles, ROWS, LANES), f32)],
        compiler_params=params,
        cost_estimate=pl.CostEstimate(flops=0, bytes_accessed=15_000_000, transcendentals=0),
        name="inner_planes",
    )(u_near, t_near)
    by_xor = chips <= 4 and chips & (chips - 1) == 0
    if by_xor:
        parts = [picked]
        for d in range(1, chips):
            parts.append(lax.ppermute(picked, "chip", [(i, i ^ d) for i in range(chips)]))
    else:
        parts = [lax.all_to_all(jnp.broadcast_to(picked, (chips, *picked.shape)), "chip", 0, 0)]
    u2, found, seen = pl.pallas_call(
        functools.partial(outer_kernel, planes, tiles),
        out_shape=(
            jax.ShapeDtypeStruct((planes * tiles, ROWS, LANES), f32),
            jax.ShapeDtypeStruct((blocks * ROWS, LANES), f32),
            jax.ShapeDtypeStruct((2 * obs_tiles, ROWS, LANES), f32),
        ),
        in_specs=[HBM] + [VMEM] * 4,
        out_specs=(VMEM,) * 3,
        scratch_shapes=[
            pltpu.SMEM(probe_cells.shape, i32),
            pltpu.SemaphoreType.DMA(()),
        ],
        input_output_aliases={4: 0},
        compiler_params=params,
        cost_estimate=little,
        name="outer_planes",
    )(stay(probe_cells), before, after, edges, inner)
    sent = pl.pallas_call(
        send_kernel,
        out_shape=pltpu.HBM((slabs * groups, blocks * ROWS, LANES), f32),
        in_specs=[VMEM] + [ANY] * len(parts),
        out_specs=HBM,
        scratch_shapes=[pltpu.SemaphoreType.DMA(())],
        compiler_params=params,
        cost_estimate=little,
        name="send",
    )(found, *parts)
    pred_all = lax.all_to_all(sent, ("space", "chip", "core"), 0, 0)
    u2_rows, *parts = pl.pallas_call(
        functools.partial(store_kernel, planes, tiles),
        out_shape=(jax.ShapeDtypeStruct(u_rows.shape, f32), *(jax.ShapeDtypeStruct(part.shape, f32) for part in parts)),
        in_specs=[VMEM] + [ANY] * len(parts),
        out_specs=(VMEM,) + (ANY,) * len(parts),
        input_output_aliases={1 + at: 1 + at for at in range(len(parts))},
        compiler_params=params,
        cost_estimate=little,
        name="store",
    )(u2, *parts)
    swapped = [lax.ppermute(part, "core", [(0, 1), (1, 0)]) for part in parts]
    where = [lax.axis_index(axes) for axes in ("space", ("chip", "core"), "chip", "core")]
    place = jnp.stack(where).astype(i32)
    split = pl.pallas_call(
        functools.partial(split_kernel, by_xor, chips),
        out_shape=pltpu.HBM((slots, 2 * groups * ROWS, LANES), jnp.bfloat16),
        in_specs=[SMEM] + [ANY] * (2 * len(parts)),
        out_specs=HBM,
        scratch_shapes=[
            pltpu.VMEM((chips, 2, slots, ROWS, LANES), f32),
            pltpu.VMEM((slots, 2 * groups * ROWS, LANES), jnp.bfloat16),
            pltpu.SemaphoreType.DMA((4 * chips + 2,)),
        ],
        compiler_params=params,
        cost_estimate=little,
        name="split",
    )(place, *parts, *swapped)
    post_rows, gain = pl.pallas_call(
        functools.partial(update_kernel, slabs, planes, tiles),
        out_shape=(
            jax.ShapeDtypeStruct(u_rows.shape, f32),
            jax.ShapeDtypeStruct((members, probes), f32),
        ),
        in_specs=[SMEM] * 2 + [HBM] * 3 + [VMEM] * 5 + [HBM] * 2 + [ANY],
        out_specs=(VMEM,) * 2,
        scratch_shapes=[
            pltpu.VMEM((probe_taper.shape[2], 2 * ROWS, 2 * groups * ROWS), jnp.bfloat16),
            pltpu.SMEM(pair_cells.shape, i32),
            pltpu.SMEM(pair_cells.shape, i32),
            pltpu.SMEM(pair_cells.shape, i32),
            pltpu.VMEM(split.shape, jnp.bfloat16),
            pltpu.VMEM(picked.shape, f32),
            pltpu.VMEM((planes * tiles, ROWS, LANES), f32),
            pltpu.SemaphoreType.DMA((6,)),
        ],
        compiler_params=params,
        name="update",
    )(place, pair_counts, *map(stay, (pair_cells, pair_probes, pair_taper)), pred_all,
      before_2, seen, obs, after_2, stay(t_rows), stay(split), parts[0] if by_xor else picked)
    return (from_rows(u2_rows, shape), from_rows(post_rows, shape), gain)


def solution(mesh):
    slabs, groups = mesh.devices.shape
    split = jax.sharding.Mesh(mesh.devices.reshape(slabs, groups // 2, 2), ("space", "chip", "core"))
    members = ("chip", "core")
    return jax.shard_map(
        shards,
        mesh=split,
        in_specs=(
            P(members, "space", None),
            P(members, "space", None),
            P("space"),
            P(members, "space"),
            P("space"),
            P("space"),
            P("space", None),
            P("space", None),
            P("space", None),
            P("space"),
            P("space", None, None),
        ),
        out_specs=(P(members, "space", None), P(members, "space", None), P(members, "space")),
        check_vma=False,
    )
```

```python
import functools

import jax
import jax.numpy as jnp
from jax import lax
from jax.experimental import pallas as pl
from jax.experimental.pallas import tpu as pltpu
from jax.sharding import PartitionSpec as P

LANES = 128
ROWS = 8
NZ = 64
HALF_DT = 0.5 * 0.08

VMEM = pl.BlockSpec(memory_space=pltpu.VMEM)
SMEM = pl.BlockSpec(memory_space=pltpu.SMEM)
HBM = pl.BlockSpec(memory_space=pltpu.HBM)
ANY = pl.BlockSpec(memory_space=pl.ANY)


def stay(array):
    return pltpu.with_memory_space_constraint(array, pltpu.HBM)


def to_rows(array):
    members, planes, cells = array.shape
    split = array.reshape(members, planes // ROWS, ROWS, cells // LANES, LANES)
    return split.transpose(0, 1, 3, 2, 4).reshape(-1, LANES)


def from_rows(rows, shape):
    members, planes, cells = shape
    split = rows.reshape(members, planes // ROWS, cells // LANES, ROWS, LANES)
    return split.transpose(0, 1, 3, 2, 4).reshape(shape)


def row_of(plane, tile, tiles):
    return (plane // ROWS * tiles + tile) * ROWS + plane % ROWS


def pack_kernel(planes, tiles, taper_hbm, u_hbm, t_hbm, noise_hbm, observed_hbm, var_hbm, cells_hbm,
                low_ref, high_ref, obs_ref, t_ref, u_ref, pick_ref,
                taper_ref, noise_ref, row_ref, cells_ref, sems):
    stride = planes * tiles
    blocks = noise_ref.shape[1] // LANES
    copies = [
        pltpu.make_async_copy(source, target, sems.at[at])
        for at, (source, target) in enumerate((
            (t_hbm, t_ref),
            (u_hbm, u_ref),
            (taper_hbm, taper_ref),
            (noise_hbm, noise_ref),
            (observed_hbm, row_ref.at[0:1]),
            (var_hbm, row_ref.at[1:2]),
            (cells_hbm, cells_ref),
        ))
    ]
    for copy in copies:
        copy.start()
    copies[0].wait()
    copies[6].wait()
    for slot in range(pick_ref.shape[0]):
        block = cells_ref[0, slot]
        row = row_of(block // tiles, block % tiles, tiles)
        pick_ref[slot] = t_ref[pl.ds(row, ROWS, stride=stride), :]
    for kind, source in ((1, t_ref), (0, u_ref)):
        if kind == 0:
            copies[1].wait()
        for out_ref, first in ((high_ref, planes - 2), (low_ref, 0)):
            for depth in range(2):
                for tile in range(tiles):
                    out_ref[(kind * 2 + depth) * tiles + tile] = source[
                        pl.ds(row_of(first + depth, tile, tiles), ROWS, stride=stride), :
                    ]
    for ref in (low_ref, high_ref):
        ref[4 * tiles] = jnp.ones((ROWS, LANES), jnp.float32)
    for copy in copies[2:6]:
        copy.wait()
    own, window = taper_ref.shape[1:]
    rows = [row_ref[kind : kind + 1, b * LANES : (b + 1) * LANES] for kind in range(2) for b in range(blocks)]
    for i in range(own):
        for j in range(window):
            rows.append(jnp.full((1, LANES), taper_ref[0, i, j].astype(jnp.float32), jnp.float32))
    for b in range(blocks):
        obs_ref[b] = noise_ref[:, b * LANES : (b + 1) * LANES]
    for at, row in enumerate(rows):
        obs_ref[blocks + at // ROWS, at % ROWS : at % ROWS + 1, :] = row
    for ref in (low_ref, high_ref):
        for at in range(obs_ref.shape[0]):
            ref[4 * tiles + 1 + at] = obs_ref[at]


def rot(value, by):
    return pltpu.roll(value, by % LANES, 1)


def lane_masks():
    lane = lax.broadcasted_iota(jnp.int32, (ROWS, LANES), 1)
    height = lane & (NZ - 1)
    return lane < NZ, height == 0, height == NZ - 1


def coefficients(masks, low, here, high):
    first_half, floor, roof = masks
    tiles = len(here)
    turned = [rot(value, NZ) for value in here]
    out = []
    for tile in range(tiles):
        mid = here[tile]
        near = mid + turned[tile]
        far = mid + jnp.where(first_half, turned[tile - 1], turned[(tile + 1) % tiles])
        up = mid + jnp.where(roof, HALF_DT, rot(mid, -1))
        down = mid + jnp.where(floor, HALF_DT, rot(mid, 1))
        below = mid + low[tile]
        above = mid + high[tile]
        diag = 1.0 - ((near + far) + (up + down) + (below + above))
        out.append((diag, near, far, jnp.where(roof, 0.0, up), jnp.where(floor, 0.0, down), below, above))
    return out


def step(masks, weights, low, here, high):
    first_half = masks[0]
    tiles = len(here)
    turned = [rot(value, NZ) for value in here]
    out = []
    for tile in range(tiles):
        diag, near, far, up, down, below, above = weights[tile]
        mid = here[tile]
        beyond = jnp.where(first_half, turned[tile - 1], turned[(tile + 1) % tiles])
        out.append(
            (diag * mid + near * turned[tile])
            + (far * beyond + up * rot(mid, -1))
            + (down * rot(mid, 1) + below * low[tile])
            + above * high[tile]
        )
    return out


def plane_of(ref, at, tiles):
    return [ref[at * tiles + tile] for tile in range(tiles)]


def put(ref, at, values):
    for tile, value in enumerate(values):
        ref[at * len(values) + tile] = value


def each(first, last, unroll, body):
    count = (last - first) // unroll

    def several(at, _):
        for d in range(unroll):
            body(first + at * unroll + d)
        return 0

    lax.fori_loop(0, count, several, 0)
    for x in range(first + count * unroll, last):
        body(x)


def inner_kernel(planes, tiles, u_ref, t_ref, u2_ref, edge_ref, u0, hv, u1, held):
    stride = planes * tiles
    masks = lane_masks()

    def rows_at(x, tile):
        return pl.ds((x // ROWS) * tiles * ROWS + x % ROWS + tile * ROWS, ROWS, stride=stride)

    def load(x):
        for tile in range(tiles):
            hv[x * tiles + tile] = HALF_DT * jnp.exp(t_ref[rows_at(x, tile), :])
            u0[x * tiles + tile] = u_ref[rows_at(x, tile), :]

    def first_step(x):
        weights = coefficients(masks, *[plane_of(hv, x + d, tiles) for d in (-1, 0, 1)])
        for tile in range(tiles):
            for kind in range(5):
                held[kind, x * tiles + tile] = weights[tile][kind]
        put(u1, x, step(masks, weights, *[plane_of(u0, x + d, tiles) for d in (-1, 0, 1)]))

    def second_step(x):
        weights = []
        for tile in range(tiles):
            at = x * tiles + tile
            here = hv[at]
            weights.append([held[kind, at] for kind in range(5)] + [here + hv[at - tiles], here + hv[at + tiles]])
        put(u2_ref, x, step(masks, weights, *[plane_of(u1, x + d, tiles) for d in (-1, 0, 1)]))

    each(0, planes, 4, load)
    each(1, planes - 1, 7, first_step)
    each(2, planes - 2, 6, second_step)
    last = planes - 1
    at = 0
    for ref, kept in ((u0, (0, 1, last - 1, last)), (hv, (0, 1, 2, last - 2, last - 1, last)),
                      (u1, (1, 2, last - 2, last - 1))):
        for x in kept:
            put(edge_ref, at, plane_of(ref, x, tiles))
            at += 1


def outer_kernel(planes, tiles, probe_hbm, before_ref, after_ref, edge_ref, inner_ref,
                 u2_ref, found_ref, seen_ref, probe_ref, sem):
    probe_copy = pltpu.make_async_copy(probe_hbm, probe_ref, sem)
    probe_copy.start()
    masks = lane_masks()
    blocks = probe_ref.shape[0] // LANES
    count = seen_ref.shape[0] // 2
    for at in range(count):
        seen_ref[at] = before_ref[4 * tiles + 1 + at]
        seen_ref[count + at] = after_ref[4 * tiles + 1 + at]
    edge = [plane_of(edge_ref, at, tiles) for at in range(14)]
    last = planes - 1
    for ref, own_u, own_v, own_1, where in (
        (before_ref, edge[0:2], edge[4:7], edge[10:12], (0, 1)),
        (after_ref, edge[3:1:-1], edge[9:6:-1], edge[13:11:-1], (last, last - 1)),
    ):
        order = (0, 1) if ref is before_ref else (1, 0)
        u = [plane_of(ref, d, tiles) for d in order] + own_u
        v = [[HALF_DT * jnp.exp(t) for t in plane_of(ref, 2 + d, tiles)] for d in order] + own_v
        live = ref[4 * tiles]
        weights = [coefficients(masks, v[d], v[d + 1], v[d + 2]) for d in range(3)]
        next_u = [step(masks, weights[d], u[d], u[d + 1], u[d + 2]) for d in range(2)]
        next_u[0] = [value * live for value in next_u[0]]
        next_u = next_u + own_1
        for d in range(2):
            put(u2_ref, where[d], step(masks, weights[d + 1], next_u[d], next_u[d + 1], next_u[d + 2]))

    probe_copy.wait()
    lane = lax.broadcasted_iota(jnp.int32, (ROWS, LANES), 1)
    for part in range(blocks):
        found = jnp.zeros((ROWS, LANES), jnp.float32)
        for p in range(LANES):
            cell = probe_ref[part * LANES + p]
            turned = pltpu.roll(u2_ref[cell >> 7], (p - cell) & (LANES - 1), 1)
            found = jnp.where(lane == p, turned, found)

        found_ref[part * ROWS : (part + 1) * ROWS, :] = found


def send_kernel(found_ref, *refs):
    sent_hbm, sem = refs[-2:]

    def send(device, _):
        pltpu.make_async_copy(found_ref, sent_hbm.at[device], sem).start()
        return 0

    lax.fori_loop(0, sent_hbm.shape[0], send, 0)
    pltpu.make_async_copy(sent_hbm, sent_hbm, sem).wait()


def halves(value):
    high = value.astype(jnp.bfloat16)
    return high, (value - high.astype(jnp.float32)).astype(jnp.bfloat16)


def store_kernel(planes, tiles, u2_ref, *refs):
    out_ref = refs[len(refs) // 2]

    def store(x):
        for tile in range(tiles):
            rows = pl.ds((x // ROWS) * tiles * ROWS + x % ROWS + tile * ROWS, ROWS, stride=planes * tiles)
            out_ref[rows, :] = u2_ref[x * tiles + tile]

    each(0, planes, 4, store)


def split_kernel(by_xor, chips, place_ref, *refs):
    *parts, split_hbm, theta_ref, split_ref, sems = refs
    chip, core = place_ref[2], place_ref[3]
    same, other = parts[: len(parts) // 2], parts[len(parts) // 2 :]
    if not by_xor:
        same, other = ([ref.at[at] for at in range(chips)] for (ref,) in (same, other))
    slots, members = theta_ref.shape[2], 2 * chips * ROWS
    half = slots // 2
    arriving, leaving = [[], []], []
    for side in range(2):
        cut = pl.ds(side * half, half)
        for at in range(chips):
            where = chip ^ at if by_xor else at
            for slot, source in ((core, same[at]), (1 - core, other[at])):
                target = theta_ref.at[where, slot, cut]
                sem = sems.at[2 * chips * side + len(arriving[side])]
                arriving[side].append(pltpu.make_async_copy(source.at[cut], target, sem))
        leaving.append(pltpu.make_async_copy(split_ref.at[cut], split_hbm.at[cut], sems.at[4 * chips + side]))
    for copy in arriving[0] + arriving[1]:
        copy.start()

    def split(slot):
        high, low = halves(theta_ref[:, :, slot].reshape(members, LANES))
        split_ref[slot, :members, :] = high
        split_ref[slot, members:, :] = low

    for side in range(2):
        for copy in arriving[side]:
            copy.wait()
        each(side * half, (side + 1) * half, 4, split)
        leaving[side].start()
    for copy in leaving:
        copy.wait()


def stacked(value):
    high, low = halves(value)
    return jnp.concatenate([high.astype(jnp.float32), low.astype(jnp.float32)], axis=0).astype(jnp.bfloat16)


def beside(pair):
    return jnp.concatenate(pair, axis=1)


def fold(both):
    return both[:ROWS] + both[ROWS:]


def dot(left, right, over):
    return lax.dot_general(left, right, (((1,), (over,)), ((), ())), preferred_element_type=jnp.float32)


def update_kernel(slabs, planes, tiles, place_ref, count_ref, cells_hbm, probes_hbm, level_hbm,
                  pred_ref, before_2_ref, seen_ref, own_ref, after_2_ref, t_hbm, split_hbm, pick_hbm,
                  post_ref, gain_ref, reach, cells_ref, probes_ref, level_ref, split_ref, pick_ref, sum_ref, sems):
    groups, blocks = pred_ref.shape[0] // slabs, pred_ref.shape[1] // ROWS
    members = groups * ROWS
    share = 1.0 / (members - 1)
    copies = [
        pltpu.make_async_copy(source, target, sems.at[at])
        for at, (source, target) in enumerate((
            (cells_hbm, cells_ref), (probes_hbm, probes_ref), (level_hbm, level_ref),
            (pick_hbm, pick_ref), (split_hbm, split_ref), (t_hbm, post_ref)))
    ]
    for copy in copies:
        copy.start()
    slab, group = place_ref[0], place_ref[1]
    seen = ((before_2_ref, 0), (seen_ref, 0), (own_ref, 0), (seen_ref, seen_ref.shape[0] // 2), (after_2_ref, 0))

    def extra(d, at):
        ref, first = seen[d]
        return ref[first + blocks + at // ROWS, at % ROWS : at % ROWS + 1, :]

    def wide(row):
        return row[:, :members] if members <= LANES else jnp.concatenate([row] * (members // LANES), axis=1)

    anomaly, scaled, variance, matches = [], [], [], []
    for d in range(5):
        wanted = slab + d - 2
        at = jnp.clip(wanted, 0, slabs - 1)
        live = jnp.where((wanted >= 0) & (wanted < slabs), 1.0, 0.0)
        for b in range(blocks):
            cut = slice(b * ROWS, (b + 1) * ROWS)
            predicted = pred_ref[pl.ds(at * groups, groups), cut].reshape(members, LANES)
            mean = jnp.sum(predicted, axis=0, keepdims=True) / members
            anomaly.append(beside(halves((predicted - mean) * live)))
            variance.append(extra(d, blocks + b) + (1.0 - live))
            noise = seen[d][0][seen[d][1] + b]
            scaled.append((extra(d, b) + noise - pred_ref[at * groups + group, cut]) / variance[-1] * live)
            matches.append(fold(dot(beside([stacked(scaled[-1])] * 2), anomaly[-1], 1)))
    for d in range(1, 4):
        for i in range(blocks):
            total = jnp.zeros((ROWS, members), jnp.float32)
            for j in range(3 * blocks):
                level = extra(d, 2 * blocks + i * 3 * blocks + j) / 256.0 * share
                total = total + wide(level) * matches[(d - 1) * blocks + j]
            both = anomaly[d * blocks + i]
            left = stacked(total)
            correction = fold(dot(left, both[:, :LANES], 0) + dot(left, both[:, LANES:], 0))
            gain = scaled[d * blocks + i] - correction / variance[d * blocks + i]
            if d == 2:
                gain_ref[:, i * LANES : (i + 1) * LANES] = gain
            near = stacked(fold(dot(beside([stacked(gain)] * 2), both, 1)))
            reach[(d - 1) * blocks + i] = beside([near, near])
    for copy in copies[:4]:
        copy.wait()
    slots = split_ref.shape[0]

    blocks_of = [cells_ref[0, slot] for slot in range(slots)]
    for slot in range(slots):
        sum_ref[blocks_of[slot]] = pick_ref[slot]
    copies[4].wait()

    def add(slot, both):
        weight = jnp.where(slot < count_ref[0], level_ref[0, slot].astype(jnp.float32) / 256.0, 0.0) * share
        sum_ref[blocks_of[slot]] = sum_ref[blocks_of[slot]] + fold(both) * weight

    nothing = jnp.zeros(reach.shape[1:], jnp.bfloat16)
    for slot in range(0, slots - slots % 4, 4):
        gains = [reach[probes_ref[0, slot + k]] for k in range(4)]
        left = [beside([gain, nothing] if k % 2 == 0 else [nothing, gain]) for k, gain in enumerate(gains)]
        right = [jnp.concatenate([split_ref[slot + k], split_ref[slot + k + 1]], axis=0) for k in (0, 2)]
        both = dot(jnp.concatenate(left, axis=0), beside(right), 0)
        for k in range(4):
            columns = slice(k // 2 * LANES, (k // 2 + 1) * LANES)
            add(slot + k, both[k * 2 * ROWS : (k + 1) * 2 * ROWS, columns])
    for slot in range(slots - slots % 4, slots):
        add(slot, dot(reach[probes_ref[0, slot]], split_ref[slot], 0))
    copies[5].wait()
    for slot in range(slots):
        block = blocks_of[slot]
        rows = pl.ds(row_of(block // tiles, block % tiles, tiles), ROWS, stride=planes * tiles)
        post_ref[rows, :] = sum_ref[block]


def shards(
    starting_speed_field,
    sample_fluidity_exponent,
    observed,
    obs_noise,
    obs_var,
    probe_cells,
    pair_cells,
    pair_probes,
    pair_taper,
    pair_counts,
    probe_taper,
):
    shape = starting_speed_field.shape
    members, planes, cells = shape
    tiles = cells // LANES
    slots = pair_cells.shape[1]
    probes = obs_noise.shape[1]
    blocks = probes // LANES
    slabs, chips = lax.axis_size("space"), lax.axis_size("chip")
    groups = 2 * chips
    f32, i32 = jnp.float32, jnp.int32
    u_rows = to_rows(starting_speed_field)
    t_rows = to_rows(sample_fluidity_exponent)
    obs_tiles = blocks - (-(2 * blocks + probe_taper.shape[1] * probe_taper.shape[2]) // ROWS)
    edge = jax.ShapeDtypeStruct((4 * tiles + 1 + obs_tiles, ROWS, LANES), f32)
    obs_shape = jax.ShapeDtypeStruct((obs_tiles, ROWS, LANES), f32)
    params = pltpu.CompilerParams(vmem_limit_bytes=32 * 1024 * 1024)
    stack = pltpu.VMEM((planes * tiles, ROWS, LANES), f32)
    low, high, obs, t_near, u_near, picked = pl.pallas_call(
        functools.partial(pack_kernel, planes, tiles),
        out_shape=(
            edge,
            edge,
            obs_shape,
            jax.ShapeDtypeStruct(u_rows.shape, f32),
            jax.ShapeDtypeStruct(u_rows.shape, f32),
            jax.ShapeDtypeStruct((slots, ROWS, LANES), f32),
        ),
        in_specs=[HBM] * 7,
        out_specs=(VMEM,) * 6,
        scratch_shapes=[
            pltpu.SMEM(probe_taper.shape, i32),
            pltpu.VMEM((ROWS, probes), f32),
            pltpu.VMEM((2, probes), f32),
            pltpu.SMEM(pair_cells.shape, i32),
            pltpu.SemaphoreType.DMA((7,)),
        ],
        compiler_params=params,
        name="pack",
    )(*map(stay, (probe_taper, u_rows, t_rows, obs_noise, observed.reshape(1, -1), obs_var.reshape(1, -1), pair_cells)))
    little = pl.CostEstimate(flops=1000, bytes_accessed=1000, transcendentals=0)
    upward = [(i, i + 1) for i in range(slabs - 1)]
    before = lax.ppermute(high, "space", upward)
    after = lax.ppermute(low, "space", [(j, i) for i, j in upward])
    if slabs == 4:
        before_2 = after_2 = lax.ppermute(obs, "space", [(i, (i + 2) % 4) for i in range(4)])
    else:
        upward_2 = [(i, i + 2) for i in range(slabs - 2)]
        before_2 = lax.ppermute(obs, "space", upward_2)
        after_2 = lax.ppermute(obs, "space", [(j, i) for i, j in upward_2])
    inner, edges = pl.pallas_call(
        functools.partial(inner_kernel, planes, tiles),
        out_shape=(
            jax.ShapeDtypeStruct((planes * tiles, ROWS, LANES), f32),
            jax.ShapeDtypeStruct((14 * tiles, ROWS, LANES), f32),
        ),
        in_specs=[VMEM, VMEM],
        out_specs=(VMEM, VMEM),
        scratch_shapes=[stack, stack, stack, pltpu.VMEM((5, planes * tiles, ROWS, LANES), f32)],
        compiler_params=params,
        cost_estimate=pl.CostEstimate(flops=0, bytes_accessed=15_000_000, transcendentals=0),
        name="inner_planes",
    )(u_near, t_near)
    by_xor = chips <= 4 and chips & (chips - 1) == 0
    if by_xor:
        parts = [picked]
        for d in range(1, chips):
            parts.append(lax.ppermute(picked, "chip", [(i, i ^ d) for i in range(chips)]))
    else:
        parts = [lax.all_to_all(jnp.broadcast_to(picked, (chips, *picked.shape)), "chip", 0, 0)]
    u2, found, seen = pl.pallas_call(
        functools.partial(outer_kernel, planes, tiles),
        out_shape=(
            jax.ShapeDtypeStruct((planes * tiles, ROWS, LANES), f32),
            jax.ShapeDtypeStruct((blocks * ROWS, LANES), f32),
            jax.ShapeDtypeStruct((2 * obs_tiles, ROWS, LANES), f32),
        ),
        in_specs=[HBM] + [VMEM] * 4,
        out_specs=(VMEM,) * 3,
        scratch_shapes=[
            pltpu.SMEM(probe_cells.shape, i32),
            pltpu.SemaphoreType.DMA(()),
        ],
        input_output_aliases={4: 0},
        compiler_params=params,
        cost_estimate=little,
        name="outer_planes",
    )(stay(probe_cells), before, after, edges, inner)
    sent = pl.pallas_call(
        send_kernel,
        out_shape=pltpu.HBM((slabs * groups, blocks * ROWS, LANES), f32),
        in_specs=[VMEM] + [ANY] * len(parts),
        out_specs=HBM,
        scratch_shapes=[pltpu.SemaphoreType.DMA(())],
        compiler_params=params,
        cost_estimate=little,
        name="send",
    )(found, *parts)
    pred_all = lax.all_to_all(sent, ("space", "chip", "core"), 0, 0)
    u2_rows, *parts = pl.pallas_call(
        functools.partial(store_kernel, planes, tiles),
        out_shape=(jax.ShapeDtypeStruct(u_rows.shape, f32), *(jax.ShapeDtypeStruct(part.shape, f32) for part in parts)),
        in_specs=[VMEM] + [ANY] * len(parts),
        out_specs=(VMEM,) + (ANY,) * len(parts),
        input_output_aliases={1 + at: 1 + at for at in range(len(parts))},
        compiler_params=params,
        cost_estimate=little,
        name="store",
    )(u2, *parts)
    swapped = [lax.ppermute(part, "core", [(0, 1), (1, 0)]) for part in parts]
    where = [lax.axis_index(axes) for axes in ("space", ("chip", "core"), "chip", "core")]
    place = jnp.stack(where).astype(i32)
    split = pl.pallas_call(
        functools.partial(split_kernel, by_xor, chips),
        out_shape=pltpu.HBM((slots, 2 * groups * ROWS, LANES), jnp.bfloat16),
        in_specs=[SMEM] + [ANY] * (2 * len(parts)),
        out_specs=HBM,
        scratch_shapes=[
            pltpu.VMEM((chips, 2, slots, ROWS, LANES), f32),
            pltpu.VMEM((slots, 2 * groups * ROWS, LANES), jnp.bfloat16),
            pltpu.SemaphoreType.DMA((4 * chips + 2,)),
        ],
        compiler_params=params,
        cost_estimate=little,
        name="split",
    )(place, *parts, *swapped)
    post_rows, gain = pl.pallas_call(
        functools.partial(update_kernel, slabs, planes, tiles),
        out_shape=(
            jax.ShapeDtypeStruct(u_rows.shape, f32),
            jax.ShapeDtypeStruct((members, probes), f32),
        ),
        in_specs=[SMEM] * 2 + [HBM] * 3 + [VMEM] * 5 + [HBM] * 2 + [ANY],
        out_specs=(VMEM,) * 2,
        scratch_shapes=[
            pltpu.VMEM((probe_taper.shape[2], 2 * ROWS, 2 * groups * ROWS), jnp.bfloat16),
            pltpu.SMEM(pair_cells.shape, i32),
            pltpu.SMEM(pair_cells.shape, i32),
            pltpu.SMEM(pair_cells.shape, i32),
            pltpu.VMEM(split.shape, jnp.bfloat16),
            pltpu.VMEM(picked.shape, f32),
            pltpu.VMEM((planes * tiles, ROWS, LANES), f32),
            pltpu.SemaphoreType.DMA((6,)),
        ],
        compiler_params=params,
        name="update",
    )(place, pair_counts, *map(stay, (pair_cells, pair_probes, pair_taper)), pred_all,
      before_2, seen, obs, after_2, stay(t_rows), stay(split), parts[0] if by_xor else picked)
    return (from_rows(u2_rows, shape), from_rows(post_rows, shape), gain)


def solution(mesh):
    slabs, groups = mesh.devices.shape
    split = jax.sharding.Mesh(mesh.devices.reshape(slabs, groups // 2, 2), ("space", "chip", "core"))
    members = ("chip", "core")
    return jax.shard_map(
        shards,
        mesh=split,
        in_specs=(
            P(members, "space", None),
            P(members, "space", None),
            P("space"),
            P(members, "space"),
            P("space"),
            P("space"),
            P("space", None),
            P("space", None),
            P("space", None),
            P("space"),
            P("space", None, None),
        ),
        out_specs=(P(members, "space", None), P(members, "space", None), P(members, "space")),
        check_vma=False,
    )
```

```python
import functools

import jax
import jax.numpy as jnp
from jax import lax
from jax.experimental import pallas as pl
from jax.experimental.pallas import tpu as pltpu
from jax.sharding import PartitionSpec as P

LANES = 128
ROWS = 8
NZ = 64
HALF_DT = 0.5 * 0.08

VMEM = pl.BlockSpec(memory_space=pltpu.VMEM)
SMEM = pl.BlockSpec(memory_space=pltpu.SMEM)
HBM = pl.BlockSpec(memory_space=pltpu.HBM)
ANY = pl.BlockSpec(memory_space=pl.ANY)


def stay(array):
    return pltpu.with_memory_space_constraint(array, pltpu.HBM)


def to_rows(array):
    members, planes, cells = array.shape
    split = array.reshape(members, planes // ROWS, ROWS, cells // LANES, LANES)
    return split.transpose(0, 1, 3, 2, 4).reshape(-1, LANES)


def from_rows(rows, shape):
    members, planes, cells = shape
    split = rows.reshape(members, planes // ROWS, cells // LANES, ROWS, LANES)
    return split.transpose(0, 1, 3, 2, 4).reshape(shape)


def row_of(plane, tile, tiles):
    return (plane // ROWS * tiles + tile) * ROWS + plane % ROWS


def pack_kernel(planes, tiles, taper_hbm, u_hbm, t_hbm, noise_hbm, observed_hbm, var_hbm, cells_hbm,
                low_ref, high_ref, obs_ref, t_ref, u_ref, pick_ref,
                taper_ref, noise_ref, row_ref, cells_ref, sems):
    stride = planes * tiles
    blocks = noise_ref.shape[1] // LANES
    copies = [
        pltpu.make_async_copy(source, target, sems.at[at])
        for at, (source, target) in enumerate((
            (t_hbm, t_ref),
            (u_hbm, u_ref),
            (taper_hbm, taper_ref),
            (noise_hbm, noise_ref),
            (observed_hbm, row_ref.at[0:1]),
            (var_hbm, row_ref.at[1:2]),
            (cells_hbm, cells_ref),
        ))
    ]
    for copy in copies:
        copy.start()
    copies[0].wait()
    copies[6].wait()
    for slot in range(pick_ref.shape[0]):
        block = cells_ref[0, slot]
        row = row_of(block // tiles, block % tiles, tiles)
        pick_ref[slot] = t_ref[pl.ds(row, ROWS, stride=stride), :]
    for kind, source in ((1, t_ref), (0, u_ref)):
        if kind == 0:
            copies[1].wait()
        for out_ref, first in ((high_ref, planes - 2), (low_ref, 0)):
            for depth in range(2):
                for tile in range(tiles):
                    out_ref[(kind * 2 + depth) * tiles + tile] = source[
                        pl.ds(row_of(first + depth, tile, tiles), ROWS, stride=stride), :
                    ]
    for ref in (low_ref, high_ref):
        ref[4 * tiles] = jnp.ones((ROWS, LANES), jnp.float32)
    for copy in copies[2:6]:
        copy.wait()
    own, window = taper_ref.shape[1:]
    rows = [row_ref[kind : kind + 1, b * LANES : (b + 1) * LANES] for kind in range(2) for b in range(blocks)]
    for i in range(own):
        for j in range(window):
            rows.append(jnp.full((1, LANES), taper_ref[0, i, j].astype(jnp.float32), jnp.float32))
    for b in range(blocks):
        obs_ref[b] = noise_ref[:, b * LANES : (b + 1) * LANES]
    for at, row in enumerate(rows):
        obs_ref[blocks + at // ROWS, at % ROWS : at % ROWS + 1, :] = row
    for ref in (low_ref, high_ref):
        for at in range(obs_ref.shape[0]):
            ref[4 * tiles + 1 + at] = obs_ref[at]


def rot(value, by):
    return pltpu.roll(value, by % LANES, 1)


def lane_masks():
    lane = lax.broadcasted_iota(jnp.int32, (ROWS, LANES), 1)
    height = lane & (NZ - 1)
    return lane < NZ, height == 0, height == NZ - 1


def coefficients(masks, low, here, high):
    first_half, floor, roof = masks
    tiles = len(here)
    turned = [rot(value, NZ) for value in here]
    out = []
    for tile in range(tiles):
        mid = here[tile]
        near = mid + turned[tile]
        far = mid + jnp.where(first_half, turned[tile - 1], turned[(tile + 1) % tiles])
        up = mid + jnp.where(roof, HALF_DT, rot(mid, -1))
        down = mid + jnp.where(floor, HALF_DT, rot(mid, 1))
        below = mid + low[tile]
        above = mid + high[tile]
        diag = 1.0 - ((near + far) + (up + down) + (below + above))
        out.append((diag, near, far, jnp.where(roof, 0.0, up), jnp.where(floor, 0.0, down), below, above))
    return out


def step(masks, weights, low, here, high):
    first_half = masks[0]
    tiles = len(here)
    turned = [rot(value, NZ) for value in here]
    out = []
    for tile in range(tiles):
        diag, near, far, up, down, below, above = weights[tile]
        mid = here[tile]
        beyond = jnp.where(first_half, turned[tile - 1], turned[(tile + 1) % tiles])
        out.append(
            (diag * mid + near * turned[tile])
            + (far * beyond + up * rot(mid, -1))
            + (down * rot(mid, 1) + below * low[tile])
            + above * high[tile]
        )
    return out


def plane_of(ref, at, tiles):
    return [ref[at * tiles + tile] for tile in range(tiles)]


def put(ref, at, values):
    for tile, value in enumerate(values):
        ref[at * len(values) + tile] = value


def each(first, last, unroll, body):
    count = (last - first) // unroll

    def several(at, _):
        for d in range(unroll):
            body(first + at * unroll + d)
        return 0

    lax.fori_loop(0, count, several, 0)
    for x in range(first + count * unroll, last):
        body(x)


def inner_kernel(planes, tiles, u_ref, t_ref, u2_ref, edge_ref, u0, hv, u1, held):
    stride = planes * tiles
    masks = lane_masks()

    def rows_at(x, tile):
        return pl.ds((x // ROWS) * tiles * ROWS + x % ROWS + tile * ROWS, ROWS, stride=stride)

    def load(x):
        for tile in range(tiles):
            hv[x * tiles + tile] = HALF_DT * jnp.exp(t_ref[rows_at(x, tile), :])
            u0[x * tiles + tile] = u_ref[rows_at(x, tile), :]

    def first_step(x):
        weights = coefficients(masks, *[plane_of(hv, x + d, tiles) for d in (-1, 0, 1)])
        for tile in range(tiles):
            for kind in range(5):
                held[kind, x * tiles + tile] = weights[tile][kind]
        put(u1, x, step(masks, weights, *[plane_of(u0, x + d, tiles) for d in (-1, 0, 1)]))

    def second_step(x):
        weights = []
        for tile in range(tiles):
            at = x * tiles + tile
            here = hv[at]
            weights.append([held[kind, at] for kind in range(5)] + [here + hv[at - tiles], here + hv[at + tiles]])
        put(u2_ref, x, step(masks, weights, *[plane_of(u1, x + d, tiles) for d in (-1, 0, 1)]))

    each(0, planes, 4, load)
    each(1, planes - 1, 7, first_step)
    each(2, planes - 2, 6, second_step)
    last = planes - 1
    at = 0
    for ref, kept in ((u0, (0, 1, last - 1, last)), (hv, (0, 1, 2, last - 2, last - 1, last)),
                      (u1, (1, 2, last - 2, last - 1))):
        for x in kept:
            put(edge_ref, at, plane_of(ref, x, tiles))
            at += 1


def outer_kernel(planes, tiles, probe_hbm, before_ref, after_ref, edge_ref, inner_ref,
                 u2_ref, found_ref, seen_ref, probe_ref, sem):
    probe_copy = pltpu.make_async_copy(probe_hbm, probe_ref, sem)
    probe_copy.start()
    masks = lane_masks()
    blocks = probe_ref.shape[0] // LANES
    count = seen_ref.shape[0] // 2
    for at in range(count):
        seen_ref[at] = before_ref[4 * tiles + 1 + at]
        seen_ref[count + at] = after_ref[4 * tiles + 1 + at]
    edge = [plane_of(edge_ref, at, tiles) for at in range(14)]
    last = planes - 1
    for ref, own_u, own_v, own_1, where in (
        (before_ref, edge[0:2], edge[4:7], edge[10:12], (0, 1)),
        (after_ref, edge[3:1:-1], edge[9:6:-1], edge[13:11:-1], (last, last - 1)),
    ):
        order = (0, 1) if ref is before_ref else (1, 0)
        u = [plane_of(ref, d, tiles) for d in order] + own_u
        v = [[HALF_DT * jnp.exp(t) for t in plane_of(ref, 2 + d, tiles)] for d in order] + own_v
        live = ref[4 * tiles]
        weights = [coefficients(masks, v[d], v[d + 1], v[d + 2]) for d in range(3)]
        next_u = [step(masks, weights[d], u[d], u[d + 1], u[d + 2]) for d in range(2)]
        next_u[0] = [value * live for value in next_u[0]]
        next_u = next_u + own_1
        for d in range(2):
            put(u2_ref, where[d], step(masks, weights[d + 1], next_u[d], next_u[d + 1], next_u[d + 2]))

    probe_copy.wait()
    lane = lax.broadcasted_iota(jnp.int32, (ROWS, LANES), 1)
    for part in range(blocks):
        found = jnp.zeros((ROWS, LANES), jnp.float32)
        for p in range(LANES):
            cell = probe_ref[part * LANES + p]
            turned = pltpu.roll(u2_ref[cell >> 7], (p - cell) & (LANES - 1), 1)
            found = jnp.where(lane == p, turned, found)

        found_ref[part * ROWS : (part + 1) * ROWS, :] = found


def send_kernel(found_ref, *refs):
    sent_hbm, many_ref, sem = refs[-3:]
    many = many_ref.shape[0]
    for device in range(many):
        many_ref[device] = found_ref[...]

    def send(at):
        pltpu.make_async_copy(many_ref, sent_hbm.at[pl.ds(at * many, many)], sem).start()

    each(0, sent_hbm.shape[0] // many, 4, send)
    pltpu.make_async_copy(sent_hbm, sent_hbm, sem).wait()


def halves(value):
    high = value.astype(jnp.bfloat16)
    return high, (value - high.astype(jnp.float32)).astype(jnp.bfloat16)


def store_kernel(planes, tiles, u2_ref, *refs):
    out_ref = refs[len(refs) // 2]

    def store(x):
        for tile in range(tiles):
            rows = pl.ds((x // ROWS) * tiles * ROWS + x % ROWS + tile * ROWS, ROWS, stride=planes * tiles)
            out_ref[rows, :] = u2_ref[x * tiles + tile]

    each(0, planes, 4, store)


def split_kernel(by_xor, chips, place_ref, *refs):
    *parts, split_hbm, theta_ref, split_ref, sems = refs
    chip, core = place_ref[2], place_ref[3]
    same, other = parts[: len(parts) // 2], parts[len(parts) // 2 :]
    if not by_xor:
        same, other = ([ref.at[at] for at in range(chips)] for (ref,) in (same, other))
    slots, members = theta_ref.shape[2], 2 * chips * ROWS
    half = slots // 2
    arriving, leaving = [[], []], []
    for side in range(2):
        cut = pl.ds(side * half, half)
        for at in range(chips):
            where = chip ^ at if by_xor else at
            for slot, source in ((core, same[at]), (1 - core, other[at])):
                target = theta_ref.at[where, slot, cut]
                sem = sems.at[2 * chips * side + len(arriving[side])]
                arriving[side].append(pltpu.make_async_copy(source.at[cut], target, sem))
        leaving.append(pltpu.make_async_copy(split_ref.at[cut], split_hbm.at[cut], sems.at[4 * chips + side]))
    for copy in arriving[0] + arriving[1]:
        copy.start()

    def split(slot):
        high, low = halves(theta_ref[:, :, slot].reshape(members, LANES))
        split_ref[slot, :members, :] = high
        split_ref[slot, members:, :] = low

    for side in range(2):
        for copy in arriving[side]:
            copy.wait()
        each(side * half, (side + 1) * half, 4, split)
        leaving[side].start()
    for copy in leaving:
        copy.wait()


def stacked(value):
    high, low = halves(value)
    return jnp.concatenate([high.astype(jnp.float32), low.astype(jnp.float32)], axis=0).astype(jnp.bfloat16)


def beside(pair):
    return jnp.concatenate(pair, axis=1)


def fold(both):
    return both[:ROWS] + both[ROWS:]


def dot(left, right, over):
    return lax.dot_general(left, right, (((1,), (over,)), ((), ())), preferred_element_type=jnp.float32)


def update_kernel(slabs, planes, tiles, place_ref, count_ref, cells_hbm, probes_hbm, level_hbm,
                  pred_ref, before_2_ref, seen_ref, own_ref, after_2_ref, t_hbm, split_hbm, pick_hbm,
                  post_ref, gain_ref, reach, cells_ref, probes_ref, level_ref, split_ref, pick_ref, sum_ref, sems):
    groups, blocks = pred_ref.shape[0] // slabs, pred_ref.shape[1] // ROWS
    members = groups * ROWS
    share = 1.0 / (members - 1)
    copies = [
        pltpu.make_async_copy(source, target, sems.at[at])
        for at, (source, target) in enumerate((
            (cells_hbm, cells_ref), (probes_hbm, probes_ref), (level_hbm, level_ref),
            (pick_hbm, pick_ref), (split_hbm, split_ref), (t_hbm, post_ref)))
    ]
    for copy in copies:
        copy.start()
    slab, group = place_ref[0], place_ref[1]
    seen = ((before_2_ref, 0), (seen_ref, 0), (own_ref, 0), (seen_ref, seen_ref.shape[0] // 2), (after_2_ref, 0))

    def extra(d, at):
        ref, first = seen[d]
        return ref[first + blocks + at // ROWS, at % ROWS : at % ROWS + 1, :]

    def wide(row):
        return row[:, :members] if members <= LANES else jnp.concatenate([row] * (members // LANES), axis=1)

    anomaly, scaled, variance, matches = [], [], [], []
    for d in range(5):
        wanted = slab + d - 2
        at = jnp.clip(wanted, 0, slabs - 1)
        live = jnp.where((wanted >= 0) & (wanted < slabs), 1.0, 0.0)
        for b in range(blocks):
            cut = slice(b * ROWS, (b + 1) * ROWS)
            predicted = pred_ref[pl.ds(at * groups, groups), cut].reshape(members, LANES)
            mean = jnp.sum(predicted, axis=0, keepdims=True) / members
            anomaly.append(beside(halves((predicted - mean) * live)))
            variance.append(extra(d, blocks + b) + (1.0 - live))
            noise = seen[d][0][seen[d][1] + b]
            scaled.append((extra(d, b) + noise - pred_ref[at * groups + group, cut]) / variance[-1] * live)
            matches.append(fold(dot(beside([stacked(scaled[-1])] * 2), anomaly[-1], 1)))
    for d in range(1, 4):
        for i in range(blocks):
            total = jnp.zeros((ROWS, members), jnp.float32)
            for j in range(3 * blocks):
                level = extra(d, 2 * blocks + i * 3 * blocks + j) / 256.0 * share
                total = total + wide(level) * matches[(d - 1) * blocks + j]
            both = anomaly[d * blocks + i]
            left = stacked(total)
            correction = fold(dot(left, both[:, :LANES], 0) + dot(left, both[:, LANES:], 0))
            gain = scaled[d * blocks + i] - correction / variance[d * blocks + i]
            if d == 2:
                gain_ref[:, i * LANES : (i + 1) * LANES] = gain
            near = stacked(fold(dot(beside([stacked(gain)] * 2), both, 1)))
            reach[(d - 1) * blocks + i] = beside([near, near])
    for copy in copies[:4]:
        copy.wait()
    slots = split_ref.shape[0]

    blocks_of = [cells_ref[0, slot] for slot in range(slots)]
    for slot in range(slots):
        sum_ref[blocks_of[slot]] = pick_ref[slot]
    copies[4].wait()

    def add(slot, both):
        weight = jnp.where(slot < count_ref[0], level_ref[0, slot].astype(jnp.float32) / 256.0, 0.0) * share
        sum_ref[blocks_of[slot]] = sum_ref[blocks_of[slot]] + fold(both) * weight

    nothing = jnp.zeros(reach.shape[1:], jnp.bfloat16)
    for slot in range(0, slots - slots % 4, 4):
        gains = [reach[probes_ref[0, slot + k]] for k in range(4)]
        left = [beside([gain, nothing] if k % 2 == 0 else [nothing, gain]) for k, gain in enumerate(gains)]
        right = [jnp.concatenate([split_ref[slot + k], split_ref[slot + k + 1]], axis=0) for k in (0, 2)]
        both = dot(jnp.concatenate(left, axis=0), beside(right), 0)
        for k in range(4):
            columns = slice(k // 2 * LANES, (k // 2 + 1) * LANES)
            add(slot + k, both[k * 2 * ROWS : (k + 1) * 2 * ROWS, columns])
    for slot in range(slots - slots % 4, slots):
        add(slot, dot(reach[probes_ref[0, slot]], split_ref[slot], 0))
    copies[5].wait()
    for slot in range(slots):
        block = blocks_of[slot]
        rows = pl.ds(row_of(block // tiles, block % tiles, tiles), ROWS, stride=planes * tiles)
        post_ref[rows, :] = sum_ref[block]


def shards(
    starting_speed_field,
    sample_fluidity_exponent,
    observed,
    obs_noise,
    obs_var,
    probe_cells,
    pair_cells,
    pair_probes,
    pair_taper,
    pair_counts,
    probe_taper,
):
    shape = starting_speed_field.shape
    members, planes, cells = shape
    tiles = cells // LANES
    slots = pair_cells.shape[1]
    probes = obs_noise.shape[1]
    blocks = probes // LANES
    slabs, chips = lax.axis_size("space"), lax.axis_size("chip")
    groups = 2 * chips
    f32, i32 = jnp.float32, jnp.int32
    u_rows = to_rows(starting_speed_field)
    t_rows = to_rows(sample_fluidity_exponent)
    obs_tiles = blocks - (-(2 * blocks + probe_taper.shape[1] * probe_taper.shape[2]) // ROWS)
    edge = jax.ShapeDtypeStruct((4 * tiles + 1 + obs_tiles, ROWS, LANES), f32)
    obs_shape = jax.ShapeDtypeStruct((obs_tiles, ROWS, LANES), f32)
    params = pltpu.CompilerParams(vmem_limit_bytes=32 * 1024 * 1024)
    stack = pltpu.VMEM((planes * tiles, ROWS, LANES), f32)
    low, high, obs, t_near, u_near, picked = pl.pallas_call(
        functools.partial(pack_kernel, planes, tiles),
        out_shape=(
            edge,
            edge,
            obs_shape,
            jax.ShapeDtypeStruct(u_rows.shape, f32),
            jax.ShapeDtypeStruct(u_rows.shape, f32),
            jax.ShapeDtypeStruct((slots, ROWS, LANES), f32),
        ),
        in_specs=[HBM] * 7,
        out_specs=(VMEM,) * 6,
        scratch_shapes=[
            pltpu.SMEM(probe_taper.shape, i32),
            pltpu.VMEM((ROWS, probes), f32),
            pltpu.VMEM((2, probes), f32),
            pltpu.SMEM(pair_cells.shape, i32),
            pltpu.SemaphoreType.DMA((7,)),
        ],
        compiler_params=params,
        name="pack",
    )(*map(stay, (probe_taper, u_rows, t_rows, obs_noise, observed.reshape(1, -1), obs_var.reshape(1, -1), pair_cells)))
    little = pl.CostEstimate(flops=1000, bytes_accessed=1000, transcendentals=0)
    upward = [(i, i + 1) for i in range(slabs - 1)]
    before = lax.ppermute(high, "space", upward)
    after = lax.ppermute(low, "space", [(j, i) for i, j in upward])
    if slabs == 4:
        before_2 = after_2 = lax.ppermute(obs, "space", [(i, (i + 2) % 4) for i in range(4)])
    else:
        upward_2 = [(i, i + 2) for i in range(slabs - 2)]
        before_2 = lax.ppermute(obs, "space", upward_2)
        after_2 = lax.ppermute(obs, "space", [(j, i) for i, j in upward_2])
    inner, edges = pl.pallas_call(
        functools.partial(inner_kernel, planes, tiles),
        out_shape=(
            jax.ShapeDtypeStruct((planes * tiles, ROWS, LANES), f32),
            jax.ShapeDtypeStruct((14 * tiles, ROWS, LANES), f32),
        ),
        in_specs=[VMEM, VMEM],
        out_specs=(VMEM, VMEM),
        scratch_shapes=[stack, stack, stack, pltpu.VMEM((5, planes * tiles, ROWS, LANES), f32)],
        compiler_params=params,
        cost_estimate=pl.CostEstimate(flops=0, bytes_accessed=15_000_000, transcendentals=0),
        name="inner_planes",
    )(u_near, t_near)
    by_xor = chips <= 4 and chips & (chips - 1) == 0
    if by_xor:
        parts = [picked]
        for d in range(1, chips):
            parts.append(lax.ppermute(picked, "chip", [(i, i ^ d) for i in range(chips)]))
    else:
        parts = [lax.all_to_all(jnp.broadcast_to(picked, (chips, *picked.shape)), "chip", 0, 0)]
    u2, found, seen = pl.pallas_call(
        functools.partial(outer_kernel, planes, tiles),
        out_shape=(
            jax.ShapeDtypeStruct((planes * tiles, ROWS, LANES), f32),
            jax.ShapeDtypeStruct((blocks * ROWS, LANES), f32),
            jax.ShapeDtypeStruct((2 * obs_tiles, ROWS, LANES), f32),
        ),
        in_specs=[HBM] + [VMEM] * 4,
        out_specs=(VMEM,) * 3,
        scratch_shapes=[
            pltpu.SMEM(probe_cells.shape, i32),
            pltpu.SemaphoreType.DMA(()),
        ],
        input_output_aliases={4: 0},
        compiler_params=params,
        cost_estimate=little,
        name="outer_planes",
    )(stay(probe_cells), before, after, edges, inner)
    sent = pl.pallas_call(
        send_kernel,
        out_shape=pltpu.HBM((slabs * groups, blocks * ROWS, LANES), f32),
        in_specs=[VMEM] + [ANY] * len(parts),
        out_specs=HBM,
        scratch_shapes=[pltpu.VMEM((groups, blocks * ROWS, LANES), f32), pltpu.SemaphoreType.DMA(())],
        compiler_params=params,
        cost_estimate=little,
        name="send",
    )(found, *parts)
    pred_all = lax.all_to_all(sent, ("space", "chip", "core"), 0, 0)
    u2_rows, *parts = pl.pallas_call(
        functools.partial(store_kernel, planes, tiles),
        out_shape=(jax.ShapeDtypeStruct(u_rows.shape, f32), *(jax.ShapeDtypeStruct(part.shape, f32) for part in parts)),
        in_specs=[VMEM] + [ANY] * len(parts),
        out_specs=(VMEM,) + (ANY,) * len(parts),
        input_output_aliases={1 + at: 1 + at for at in range(len(parts))},
        compiler_params=params,
        cost_estimate=little,
        name="store",
    )(u2, *parts)
    swapped = [lax.ppermute(part, "core", [(0, 1), (1, 0)]) for part in parts]
    where = [lax.axis_index(axes) for axes in ("space", ("chip", "core"), "chip", "core")]
    place = jnp.stack(where).astype(i32)
    split = pl.pallas_call(
        functools.partial(split_kernel, by_xor, chips),
        out_shape=pltpu.HBM((slots, 2 * groups * ROWS, LANES), jnp.bfloat16),
        in_specs=[SMEM] + [ANY] * (2 * len(parts)),
        out_specs=HBM,
        scratch_shapes=[
            pltpu.VMEM((chips, 2, slots, ROWS, LANES), f32),
            pltpu.VMEM((slots, 2 * groups * ROWS, LANES), jnp.bfloat16),
            pltpu.SemaphoreType.DMA((4 * chips + 2,)),
        ],
        compiler_params=params,
        cost_estimate=little,
        name="split",
    )(place, *parts, *swapped)
    post_rows, gain = pl.pallas_call(
        functools.partial(update_kernel, slabs, planes, tiles),
        out_shape=(
            jax.ShapeDtypeStruct(u_rows.shape, f32),
            jax.ShapeDtypeStruct((members, probes), f32),
        ),
        in_specs=[SMEM] * 2 + [HBM] * 3 + [VMEM] * 5 + [HBM] * 2 + [ANY],
        out_specs=(VMEM,) * 2,
        scratch_shapes=[
            pltpu.VMEM((probe_taper.shape[2], 2 * ROWS, 2 * groups * ROWS), jnp.bfloat16),
            pltpu.SMEM(pair_cells.shape, i32),
            pltpu.SMEM(pair_cells.shape, i32),
            pltpu.SMEM(pair_cells.shape, i32),
            pltpu.VMEM(split.shape, jnp.bfloat16),
            pltpu.VMEM(picked.shape, f32),
            pltpu.VMEM((planes * tiles, ROWS, LANES), f32),
            pltpu.SemaphoreType.DMA((6,)),
        ],
        compiler_params=params,
        name="update",
    )(place, pair_counts, *map(stay, (pair_cells, pair_probes, pair_taper)), pred_all,
      before_2, seen, obs, after_2, stay(t_rows), stay(split), parts[0] if by_xor else picked)
    return (from_rows(u2_rows, shape), from_rows(post_rows, shape), gain)


def solution(mesh):
    slabs, groups = mesh.devices.shape
    split = jax.sharding.Mesh(mesh.devices.reshape(slabs, groups // 2, 2), ("space", "chip", "core"))
    members = ("chip", "core")
    return jax.shard_map(
        shards,
        mesh=split,
        in_specs=(
            P(members, "space", None),
            P(members, "space", None),
            P("space"),
            P(members, "space"),
            P("space"),
            P("space"),
            P("space", None),
            P("space", None),
            P("space", None),
            P("space"),
            P("space", None, None),
        ),
        out_specs=(P(members, "space", None), P(members, "space", None), P(members, "space")),
        check_vma=False,
    )
```

```python
import functools

import jax
import jax.numpy as jnp
from jax import lax
from jax.experimental import pallas as pl
from jax.experimental.pallas import tpu as pltpu
from jax.sharding import PartitionSpec as P

LANES = 128
ROWS = 8
NZ = 64
HALF_DT = 0.5 * 0.08

VMEM = pl.BlockSpec(memory_space=pltpu.VMEM)
SMEM = pl.BlockSpec(memory_space=pltpu.SMEM)
HBM = pl.BlockSpec(memory_space=pltpu.HBM)
ANY = pl.BlockSpec(memory_space=pl.ANY)


def stay(array):
    return pltpu.with_memory_space_constraint(array, pltpu.HBM)


def to_rows(array):
    members, planes, cells = array.shape
    split = array.reshape(members, planes // ROWS, ROWS, cells // LANES, LANES)
    return split.transpose(0, 1, 3, 2, 4).reshape(-1, LANES)


def from_rows(rows, shape):
    members, planes, cells = shape
    split = rows.reshape(members, planes // ROWS, cells // LANES, ROWS, LANES)
    return split.transpose(0, 1, 3, 2, 4).reshape(shape)


def row_of(plane, tile, tiles):
    return (plane // ROWS * tiles + tile) * ROWS + plane % ROWS


def pack_kernel(planes, tiles, taper_hbm, u_hbm, t_hbm, noise_hbm, observed_hbm, var_hbm, cells_hbm,
                low_ref, high_ref, obs_ref, t_ref, u_ref, pick_ref,
                taper_ref, noise_ref, row_ref, cells_ref, sems):
    stride = planes * tiles
    blocks = noise_ref.shape[1] // LANES
    copies = [
        pltpu.make_async_copy(source, target, sems.at[at])
        for at, (source, target) in enumerate((
            (t_hbm, t_ref),
            (u_hbm, u_ref),
            (taper_hbm, taper_ref),
            (noise_hbm, noise_ref),
            (observed_hbm, row_ref.at[0:1]),
            (var_hbm, row_ref.at[1:2]),
            (cells_hbm, cells_ref),
        ))
    ]
    for copy in copies:
        copy.start()
    copies[0].wait()
    copies[6].wait()
    for slot in range(pick_ref.shape[0]):
        block = cells_ref[0, slot]
        row = row_of(block // tiles, block % tiles, tiles)
        pick_ref[slot] = t_ref[pl.ds(row, ROWS, stride=stride), :]
    for kind, source in ((1, t_ref), (0, u_ref)):
        if kind == 0:
            copies[1].wait()
        for out_ref, first in ((high_ref, planes - 2), (low_ref, 0)):
            for depth in range(2):
                for tile in range(tiles):
                    out_ref[(kind * 2 + depth) * tiles + tile] = source[
                        pl.ds(row_of(first + depth, tile, tiles), ROWS, stride=stride), :
                    ]
    for ref in (low_ref, high_ref):
        ref[4 * tiles] = jnp.ones((ROWS, LANES), jnp.float32)
    for copy in copies[2:6]:
        copy.wait()
    own, window = taper_ref.shape[1:]
    rows = [row_ref[kind : kind + 1, b * LANES : (b + 1) * LANES] for kind in range(2) for b in range(blocks)]
    for i in range(own):
        for j in range(window):
            rows.append(jnp.full((1, LANES), taper_ref[0, i, j].astype(jnp.float32), jnp.float32))
    for b in range(blocks):
        obs_ref[b] = noise_ref[:, b * LANES : (b + 1) * LANES]
    for at, row in enumerate(rows):
        obs_ref[blocks + at // ROWS, at % ROWS : at % ROWS + 1, :] = row
    for ref in (low_ref, high_ref):
        for at in range(obs_ref.shape[0]):
            ref[4 * tiles + 1 + at] = obs_ref[at]


def rot(value, by):
    return pltpu.roll(value, by % LANES, 1)


def lane_masks():
    lane = lax.broadcasted_iota(jnp.int32, (ROWS, LANES), 1)
    height = lane & (NZ - 1)
    return lane < NZ, height == 0, height == NZ - 1


def coefficients(masks, low, here, high):
    first_half, floor, roof = masks
    tiles = len(here)
    turned = [rot(value, NZ) for value in here]
    out = []
    for tile in range(tiles):
        mid = here[tile]
        near = mid + turned[tile]
        far = mid + jnp.where(first_half, turned[tile - 1], turned[(tile + 1) % tiles])
        up = mid + jnp.where(roof, HALF_DT, rot(mid, -1))
        down = mid + jnp.where(floor, HALF_DT, rot(mid, 1))
        below = mid + low[tile]
        above = mid + high[tile]
        diag = 1.0 - ((near + far) + (up + down) + (below + above))
        out.append((diag, near, far, jnp.where(roof, 0.0, up), jnp.where(floor, 0.0, down), below, above))
    return out


def step(masks, weights, low, here, high):
    first_half = masks[0]
    tiles = len(here)
    turned = [rot(value, NZ) for value in here]
    out = []
    for tile in range(tiles):
        diag, near, far, up, down, below, above = weights[tile]
        mid = here[tile]
        beyond = jnp.where(first_half, turned[tile - 1], turned[(tile + 1) % tiles])
        out.append(
            (diag * mid + near * turned[tile])
            + (far * beyond + up * rot(mid, -1))
            + (down * rot(mid, 1) + below * low[tile])
            + above * high[tile]
        )
    return out


def plane_of(ref, at, tiles):
    return [ref[at * tiles + tile] for tile in range(tiles)]


def put(ref, at, values):
    for tile, value in enumerate(values):
        ref[at * len(values) + tile] = value


def each(first, last, unroll, body):
    count = (last - first) // unroll

    def several(at, _):
        for d in range(unroll):
            body(first + at * unroll + d)
        return 0

    lax.fori_loop(0, count, several, 0)
    for x in range(first + count * unroll, last):
        body(x)


def inner_kernel(planes, tiles, u_ref, t_ref, u2_ref, edge_ref, u0, hv, u1, held):
    stride = planes * tiles
    masks = lane_masks()

    def rows_at(x, tile):
        return pl.ds((x // ROWS) * tiles * ROWS + x % ROWS + tile * ROWS, ROWS, stride=stride)

    def load(x):
        for tile in range(tiles):
            hv[x * tiles + tile] = HALF_DT * jnp.exp(t_ref[rows_at(x, tile), :])
            u0[x * tiles + tile] = u_ref[rows_at(x, tile), :]

    def first_step(x):
        weights = coefficients(masks, *[plane_of(hv, x + d, tiles) for d in (-1, 0, 1)])
        for tile in range(tiles):
            for kind in range(5):
                held[kind, x * tiles + tile] = weights[tile][kind]
        put(u1, x, step(masks, weights, *[plane_of(u0, x + d, tiles) for d in (-1, 0, 1)]))

    def second_step(x):
        weights = []
        for tile in range(tiles):
            at = x * tiles + tile
            here = hv[at]
            weights.append([held[kind, at] for kind in range(5)] + [here + hv[at - tiles], here + hv[at + tiles]])
        put(u2_ref, x, step(masks, weights, *[plane_of(u1, x + d, tiles) for d in (-1, 0, 1)]))

    each(0, planes, 4, load)
    each(1, planes - 1, 7, first_step)
    each(2, planes - 2, 6, second_step)
    last = planes - 1
    nothing = [jnp.zeros((ROWS, LANES), jnp.float32)] * tiles
    for x, low, high, at in ((0, None, 1, 34), (last, last - 1, None, 35)):
        sides = [[nothing if near is None else plane_of(ref, near, tiles) for near in (low, high)] for ref in (hv, u0)]
        weights = coefficients(masks, sides[0][0], plane_of(hv, x, tiles), sides[0][1])
        for tile in range(tiles):
            for kind in range(5):
                held[kind, x * tiles + tile] = weights[tile][kind]
        put(edge_ref, at, step(masks, weights, sides[1][0], plane_of(u0, x, tiles), sides[1][1]))
    for number, x in enumerate((0, 1, last - 1, last)):
        for kind in range(5):
            for tile in range(tiles):
                edge_ref[(14 + number * 5 + kind) * tiles + tile] = held[kind, x * tiles + tile]
    at = 0
    for ref, kept in ((u0, (0, 1, last - 1, last)), (hv, (0, 1, 2, last - 2, last - 1, last)),
                      (u1, (1, 2, last - 2, last - 1))):
        for x in kept:
            put(edge_ref, at, plane_of(ref, x, tiles))
            at += 1


def outer_kernel(planes, tiles, probe_hbm, before_ref, after_ref, edge_ref, inner_ref,
                 u2_ref, found_ref, seen_ref, probe_ref, sem):
    probe_copy = pltpu.make_async_copy(probe_hbm, probe_ref, sem)
    probe_copy.start()
    masks = lane_masks()
    blocks = probe_ref.shape[0] // LANES
    count = seen_ref.shape[0] // 2
    for at in range(count):
        seen_ref[at] = before_ref[4 * tiles + 1 + at]
        seen_ref[count + at] = after_ref[4 * tiles + 1 + at]
    edge = [plane_of(edge_ref, at, tiles) for at in range(36)]
    last = planes - 1
    for ref, own_u, own_v, own_1, own_w, partial, where in (
        (before_ref, edge[0:2], edge[4:7], edge[10:12], (14, 19), edge[34], (0, 1)),
        (after_ref, edge[3:1:-1], edge[9:6:-1], edge[13:11:-1], (29, 24), edge[35], (last, last - 1)),
    ):
        order = (0, 1) if ref is before_ref else (1, 0)
        u = [plane_of(ref, d, tiles) for d in order] + own_u
        v = [[HALF_DT * jnp.exp(t) for t in plane_of(ref, 2 + d, tiles)] for d in order] + own_v
        live = ref[4 * tiles]
        weights = [coefficients(masks, v[0], v[1], v[2])]
        for d in (1, 2):
            kinds = edge[own_w[d - 1] : own_w[d - 1] + 5]
            weights.append([
                (kinds[0][t] - v[1][t] if d == 1 else kinds[0][t], *(kinds[k][t] for k in range(1, 5)),
                 v[d + 1][t] + v[d][t], v[d + 1][t] + v[d + 2][t])
                for t in range(tiles)
            ])
        next_u = [[value * live for value in step(masks, weights[0], u[0], u[1], u[2])]]
        next_u.append([
            partial[t] - v[1][t] * u[2][t] + (v[2][t] + v[1][t]) * u[1][t] for t in range(tiles)
        ])
        next_u = next_u + own_1
        for d in range(2):
            put(u2_ref, where[d], step(masks, weights[d + 1], next_u[d], next_u[d + 1], next_u[d + 2]))

    probe_copy.wait()
    lane = lax.broadcasted_iota(jnp.int32, (ROWS, LANES), 1)
    for part in range(blocks):
        found = jnp.zeros((ROWS, LANES), jnp.float32)
        for p in range(LANES):
            cell = probe_ref[part * LANES + p]
            turned = pltpu.roll(u2_ref[cell >> 7], (p - cell) & (LANES - 1), 1)
            found = jnp.where(lane == p, turned, found)

        found_ref[part * ROWS : (part + 1) * ROWS, :] = found


def send_kernel(found_ref, *refs):
    sent_hbm, many_ref, sem = refs[-3:]
    many = many_ref.shape[0]
    for device in range(many):
        many_ref[device] = found_ref[...]

    def send(at):
        pltpu.make_async_copy(many_ref, sent_hbm.at[pl.ds(at * many, many)], sem).start()

    each(0, sent_hbm.shape[0] // many, 4, send)
    pltpu.make_async_copy(sent_hbm, sent_hbm, sem).wait()


def halves(value):
    high = value.astype(jnp.bfloat16)
    return high, (value - high.astype(jnp.float32)).astype(jnp.bfloat16)


def store_kernel(planes, tiles, u2_ref, *refs):
    out_ref = refs[len(refs) // 2]

    def store(x):
        for tile in range(tiles):
            rows = pl.ds((x // ROWS) * tiles * ROWS + x % ROWS + tile * ROWS, ROWS, stride=planes * tiles)
            out_ref[rows, :] = u2_ref[x * tiles + tile]

    each(0, planes, 4, store)


def split_kernel(by_xor, chips, place_ref, *refs):
    *parts, split_hbm, theta_ref, split_ref, sems = refs
    chip, core = place_ref[2], place_ref[3]
    same, other = parts[: len(parts) // 2], parts[len(parts) // 2 :]
    if not by_xor:
        same, other = ([ref.at[at] for at in range(chips)] for (ref,) in (same, other))
    slots, members = theta_ref.shape[2], 2 * chips * ROWS
    half = slots // 2
    arriving, leaving = [[], []], []
    for side in range(2):
        cut = pl.ds(side * half, half)
        for at in range(chips):
            where = chip ^ at if by_xor else at
            for slot, source in ((core, same[at]), (1 - core, other[at])):
                target = theta_ref.at[where, slot, cut]
                sem = sems.at[2 * chips * side + len(arriving[side])]
                arriving[side].append(pltpu.make_async_copy(source.at[cut], target, sem))
        leaving.append(pltpu.make_async_copy(split_ref.at[cut], split_hbm.at[cut], sems.at[4 * chips + side]))
    for copy in arriving[0] + arriving[1]:
        copy.start()

    def split(slot):
        high, low = halves(theta_ref[:, :, slot].reshape(members, LANES))
        split_ref[slot, :members, :] = high
        split_ref[slot, members:, :] = low

    for side in range(2):
        for copy in arriving[side]:
            copy.wait()
        each(side * half, (side + 1) * half, 4, split)
        leaving[side].start()
    for copy in leaving:
        copy.wait()


def stacked(value):
    high, low = halves(value)
    return jnp.concatenate([high.astype(jnp.float32), low.astype(jnp.float32)], axis=0).astype(jnp.bfloat16)


def beside(pair):
    return jnp.concatenate(pair, axis=1)


def fold(both):
    return both[:ROWS] + both[ROWS:]


def dot(left, right, over):
    return lax.dot_general(left, right, (((1,), (over,)), ((), ())), preferred_element_type=jnp.float32)


def update_kernel(slabs, planes, tiles, place_ref, count_ref, cells_hbm, probes_hbm, level_hbm,
                  pred_ref, before_2_ref, seen_ref, own_ref, after_2_ref, t_hbm, split_hbm, pick_hbm,
                  post_ref, gain_ref, reach, cells_ref, probes_ref, level_ref, split_ref, pick_ref, sum_ref, sems):
    groups, blocks = pred_ref.shape[0] // slabs, pred_ref.shape[1] // ROWS
    members = groups * ROWS
    share = 1.0 / (members - 1)
    copies = [
        pltpu.make_async_copy(source, target, sems.at[at])
        for at, (source, target) in enumerate((
            (cells_hbm, cells_ref), (probes_hbm, probes_ref), (level_hbm, level_ref),
            (pick_hbm, pick_ref), (split_hbm, split_ref), (t_hbm, post_ref)))
    ]
    for copy in copies:
        copy.start()
    slab, group = place_ref[0], place_ref[1]
    seen = ((before_2_ref, 0), (seen_ref, 0), (own_ref, 0), (seen_ref, seen_ref.shape[0] // 2), (after_2_ref, 0))

    def extra(d, at):
        ref, first = seen[d]
        return ref[first + blocks + at // ROWS, at % ROWS : at % ROWS + 1, :]

    def wide(row):
        return row[:, :members] if members <= LANES else jnp.concatenate([row] * (members // LANES), axis=1)

    anomaly, scaled, variance, matches = [], [], [], []
    for d in range(5):
        wanted = slab + d - 2
        at = jnp.clip(wanted, 0, slabs - 1)
        live = jnp.where((wanted >= 0) & (wanted < slabs), 1.0, 0.0)
        for b in range(blocks):
            cut = slice(b * ROWS, (b + 1) * ROWS)
            predicted = pred_ref[pl.ds(at * groups, groups), cut].reshape(members, LANES)
            mean = jnp.sum(predicted, axis=0, keepdims=True) / members
            anomaly.append(beside(halves((predicted - mean) * live)))
            variance.append(extra(d, blocks + b) + (1.0 - live))
            noise = seen[d][0][seen[d][1] + b]
            scaled.append((extra(d, b) + noise - pred_ref[at * groups + group, cut]) / variance[-1] * live)
            matches.append(fold(dot(beside([stacked(scaled[-1])] * 2), anomaly[-1], 1)))
    for d in range(1, 4):
        for i in range(blocks):
            total = jnp.zeros((ROWS, members), jnp.float32)
            for j in range(3 * blocks):
                level = extra(d, 2 * blocks + i * 3 * blocks + j) / 256.0 * share
                total = total + wide(level) * matches[(d - 1) * blocks + j]
            both = anomaly[d * blocks + i]
            left = stacked(total)
            correction = fold(dot(left, both[:, :LANES], 0) + dot(left, both[:, LANES:], 0))
            gain = scaled[d * blocks + i] - correction / variance[d * blocks + i]
            if d == 2:
                gain_ref[:, i * LANES : (i + 1) * LANES] = gain
            near = stacked(fold(dot(beside([stacked(gain)] * 2), both, 1)))
            reach[(d - 1) * blocks + i] = beside([near, near])
    for copy in copies[:4]:
        copy.wait()
    slots = split_ref.shape[0]

    blocks_of = [cells_ref[0, slot] for slot in range(slots)]
    for slot in range(slots):
        sum_ref[blocks_of[slot]] = pick_ref[slot]
    copies[4].wait()

    def add(slot, both):
        weight = jnp.where(slot < count_ref[0], level_ref[0, slot].astype(jnp.float32) / 256.0, 0.0) * share
        sum_ref[blocks_of[slot]] = sum_ref[blocks_of[slot]] + fold(both) * weight

    nothing = jnp.zeros(reach.shape[1:], jnp.bfloat16)
    for slot in range(0, slots - slots % 4, 4):
        gains = [reach[probes_ref[0, slot + k]] for k in range(4)]
        left = [beside([gain, nothing] if k % 2 == 0 else [nothing, gain]) for k, gain in enumerate(gains)]
        right = [jnp.concatenate([split_ref[slot + k], split_ref[slot + k + 1]], axis=0) for k in (0, 2)]
        both = dot(jnp.concatenate(left, axis=0), beside(right), 0)
        for k in range(4):
            columns = slice(k // 2 * LANES, (k // 2 + 1) * LANES)
            add(slot + k, both[k * 2 * ROWS : (k + 1) * 2 * ROWS, columns])
    for slot in range(slots - slots % 4, slots):
        add(slot, dot(reach[probes_ref[0, slot]], split_ref[slot], 0))
    copies[5].wait()
    for slot in range(slots):
        block = blocks_of[slot]
        rows = pl.ds(row_of(block // tiles, block % tiles, tiles), ROWS, stride=planes * tiles)
        post_ref[rows, :] = sum_ref[block]


def shards(
    starting_speed_field,
    sample_fluidity_exponent,
    observed,
    obs_noise,
    obs_var,
    probe_cells,
    pair_cells,
    pair_probes,
    pair_taper,
    pair_counts,
    probe_taper,
):
    shape = starting_speed_field.shape
    members, planes, cells = shape
    tiles = cells // LANES
    slots = pair_cells.shape[1]
    probes = obs_noise.shape[1]
    blocks = probes // LANES
    slabs, chips = lax.axis_size("space"), lax.axis_size("chip")
    groups = 2 * chips
    f32, i32 = jnp.float32, jnp.int32
    u_rows = to_rows(starting_speed_field)
    t_rows = to_rows(sample_fluidity_exponent)
    obs_tiles = blocks - (-(2 * blocks + probe_taper.shape[1] * probe_taper.shape[2]) // ROWS)
    edge = jax.ShapeDtypeStruct((4 * tiles + 1 + obs_tiles, ROWS, LANES), f32)
    obs_shape = jax.ShapeDtypeStruct((obs_tiles, ROWS, LANES), f32)
    params = pltpu.CompilerParams(vmem_limit_bytes=32 * 1024 * 1024)
    stack = pltpu.VMEM((planes * tiles, ROWS, LANES), f32)
    low, high, obs, t_near, u_near, picked = pl.pallas_call(
        functools.partial(pack_kernel, planes, tiles),
        out_shape=(
            edge,
            edge,
            obs_shape,
            jax.ShapeDtypeStruct(u_rows.shape, f32),
            jax.ShapeDtypeStruct(u_rows.shape, f32),
            jax.ShapeDtypeStruct((slots, ROWS, LANES), f32),
        ),
        in_specs=[HBM] * 7,
        out_specs=(VMEM,) * 6,
        scratch_shapes=[
            pltpu.SMEM(probe_taper.shape, i32),
            pltpu.VMEM((ROWS, probes), f32),
            pltpu.VMEM((2, probes), f32),
            pltpu.SMEM(pair_cells.shape, i32),
            pltpu.SemaphoreType.DMA((7,)),
        ],
        compiler_params=params,
        name="pack",
    )(*map(stay, (probe_taper, u_rows, t_rows, obs_noise, observed.reshape(1, -1), obs_var.reshape(1, -1), pair_cells)))
    little = pl.CostEstimate(flops=1000, bytes_accessed=1000, transcendentals=0)
    upward = [(i, i + 1) for i in range(slabs - 1)]
    before = lax.ppermute(high, "space", upward)
    after = lax.ppermute(low, "space", [(j, i) for i, j in upward])
    if slabs == 4:
        before_2 = after_2 = lax.ppermute(obs, "space", [(i, (i + 2) % 4) for i in range(4)])
    else:
        upward_2 = [(i, i + 2) for i in range(slabs - 2)]
        before_2 = lax.ppermute(obs, "space", upward_2)
        after_2 = lax.ppermute(obs, "space", [(j, i) for i, j in upward_2])
    inner, edges = pl.pallas_call(
        functools.partial(inner_kernel, planes, tiles),
        out_shape=(
            jax.ShapeDtypeStruct((planes * tiles, ROWS, LANES), f32),
            jax.ShapeDtypeStruct((36 * tiles, ROWS, LANES), f32),
        ),
        in_specs=[VMEM, VMEM],
        out_specs=(VMEM, VMEM),
        scratch_shapes=[stack, stack, stack, pltpu.VMEM((5, planes * tiles, ROWS, LANES), f32)],
        compiler_params=params,
        cost_estimate=pl.CostEstimate(flops=0, bytes_accessed=15_000_000, transcendentals=0),
        name="inner_planes",
    )(u_near, t_near)
    by_xor = chips <= 4 and chips & (chips - 1) == 0
    if by_xor:
        parts = [picked]
        for d in range(1, chips):
            parts.append(lax.ppermute(picked, "chip", [(i, i ^ d) for i in range(chips)]))
    else:
        parts = [lax.all_to_all(jnp.broadcast_to(picked, (chips, *picked.shape)), "chip", 0, 0)]
    u2, found, seen = pl.pallas_call(
        functools.partial(outer_kernel, planes, tiles),
        out_shape=(
            jax.ShapeDtypeStruct((planes * tiles, ROWS, LANES), f32),
            jax.ShapeDtypeStruct((blocks * ROWS, LANES), f32),
            jax.ShapeDtypeStruct((2 * obs_tiles, ROWS, LANES), f32),
        ),
        in_specs=[HBM] + [VMEM] * 4,
        out_specs=(VMEM,) * 3,
        scratch_shapes=[
            pltpu.SMEM(probe_cells.shape, i32),
            pltpu.SemaphoreType.DMA(()),
        ],
        input_output_aliases={4: 0},
        compiler_params=params,
        cost_estimate=little,
        name="outer_planes",
    )(stay(probe_cells), before, after, edges, inner)
    sent = pl.pallas_call(
        send_kernel,
        out_shape=pltpu.HBM((slabs * groups, blocks * ROWS, LANES), f32),
        in_specs=[VMEM] + [ANY] * len(parts),
        out_specs=HBM,
        scratch_shapes=[pltpu.VMEM((groups, blocks * ROWS, LANES), f32), pltpu.SemaphoreType.DMA(())],
        compiler_params=params,
        cost_estimate=little,
        name="send",
    )(found, *parts)
    pred_all = lax.all_to_all(sent, ("space", "chip", "core"), 0, 0)
    u2_rows, *parts = pl.pallas_call(
        functools.partial(store_kernel, planes, tiles),
        out_shape=(jax.ShapeDtypeStruct(u_rows.shape, f32), *(jax.ShapeDtypeStruct(part.shape, f32) for part in parts)),
        in_specs=[VMEM] + [ANY] * len(parts),
        out_specs=(VMEM,) + (ANY,) * len(parts),
        input_output_aliases={1 + at: 1 + at for at in range(len(parts))},
        compiler_params=params,
        cost_estimate=little,
        name="store",
    )(u2, *parts)
    swapped = [lax.ppermute(part, "core", [(0, 1), (1, 0)]) for part in parts]
    where = [lax.axis_index(axes) for axes in ("space", ("chip", "core"), "chip", "core")]
    place = jnp.stack(where).astype(i32)
    split = pl.pallas_call(
        functools.partial(split_kernel, by_xor, chips),
        out_shape=pltpu.HBM((slots, 2 * groups * ROWS, LANES), jnp.bfloat16),
        in_specs=[SMEM] + [ANY] * (2 * len(parts)),
        out_specs=HBM,
        scratch_shapes=[
            pltpu.VMEM((chips, 2, slots, ROWS, LANES), f32),
            pltpu.VMEM((slots, 2 * groups * ROWS, LANES), jnp.bfloat16),
            pltpu.SemaphoreType.DMA((4 * chips + 2,)),
        ],
        compiler_params=params,
        cost_estimate=little,
        name="split",
    )(place, *parts, *swapped)
    post_rows, gain = pl.pallas_call(
        functools.partial(update_kernel, slabs, planes, tiles),
        out_shape=(
            jax.ShapeDtypeStruct(u_rows.shape, f32),
            jax.ShapeDtypeStruct((members, probes), f32),
        ),
        in_specs=[SMEM] * 2 + [HBM] * 3 + [VMEM] * 5 + [HBM] * 2 + [ANY],
        out_specs=(VMEM,) * 2,
        scratch_shapes=[
            pltpu.VMEM((probe_taper.shape[2], 2 * ROWS, 2 * groups * ROWS), jnp.bfloat16),
            pltpu.SMEM(pair_cells.shape, i32),
            pltpu.SMEM(pair_cells.shape, i32),
            pltpu.SMEM(pair_cells.shape, i32),
            pltpu.VMEM(split.shape, jnp.bfloat16),
            pltpu.VMEM(picked.shape, f32),
            pltpu.VMEM((planes * tiles, ROWS, LANES), f32),
            pltpu.SemaphoreType.DMA((6,)),
        ],
        compiler_params=params,
        name="update",
    )(place, pair_counts, *map(stay, (pair_cells, pair_probes, pair_taper)), pred_all,
      before_2, seen, obs, after_2, stay(t_rows), stay(split), parts[0] if by_xor else picked)
    return (from_rows(u2_rows, shape), from_rows(post_rows, shape), gain)


def solution(mesh):
    slabs, groups = mesh.devices.shape
    split = jax.sharding.Mesh(mesh.devices.reshape(slabs, groups // 2, 2), ("space", "chip", "core"))
    members = ("chip", "core")
    return jax.shard_map(
        shards,
        mesh=split,
        in_specs=(
            P(members, "space", None),
            P(members, "space", None),
            P("space"),
            P(members, "space"),
            P("space"),
            P("space"),
            P("space", None),
            P("space", None),
            P("space", None),
            P("space"),
            P("space", None, None),
        ),
        out_specs=(P(members, "space", None), P(members, "space", None), P(members, "space")),
        check_vma=False,
    )
```
